32 devices in a mesh: traj: 4 (over x, core), tx: 2 (over y), ty: 4 (over z).
Axes of the slice: x: 2, y: 2, z: 4, core: 2. Of those that a mesh axis runs over, the one named last changes fastest.
Arguments:
- density: float32 [4, 256, 1024], P('traj', None, ('tx', 'ty')), may hold values from 1 to 2
- momentum: float32 [4, 2, 256, 1024], P('traj', None, None, ('tx', 'ty')), may hold values from -0.5 to 0.5
- tracer: float32 [4, 256, 1024], P('traj', None, ('tx', 'ty')), may hold values from -1 to 1
- cotangent: float32 [4, 4, 256, 1024], P('traj', None, None, ('tx', 'ty')), may hold values from -6 to 6
- w_in: float32 [32, 16], replicated, may hold values from -1.5 to 1.5
- b_in: float32 [32], replicated, may hold values from -3 to 3
- w_mid: float32 [32, 32], replicated, may hold values from -1 to 1
- b_mid: float32 [32], replicated, may hold values from -3 to 3
- w_out: float32 [8, 32], replicated, may hold values from -1 to 1
- b_out: float32 [8], replicated, may hold values from -3 to 3
Outputs:
- grad_density: float32 [4, 256, 1024], P('traj', None, ('tx', 'ty'))
- grad_momentum: float32 [4, 2, 256, 1024], P('traj', None, None, ('tx', 'ty'))
- grad_tracer: float32 [4, 256, 1024], P('traj', None, ('tx', 'ty'))
- grad_w_in: float32 [32, 16], replicated
- grad_b_in: float32 [32], replicated
- grad_w_mid: float32 [32, 32], replicated
- grad_b_mid: float32 [32], replicated
- grad_w_out: float32 [8, 32], replicated
- grad_b_out: float32 [8], replicated
The draws below stay inside these ranges and needn't reach their ends.
All inputs are finite; a program needn't handle non-finite values.
Results may differ from the reference program's by a relative error of at most 0.0003.
Values sent between devices are 32-bit elements; how exact they have to be, the bound alone decides.
No kernel may reach another device: no remote copies, remote signals or barrier semaphores. Data moves between devices by JAX's collectives and lax.ppermute only.
A program may use at most 128 MiB of HBM per device.

```python
import jax
import jax.numpy as jnp
from jax import lax

NX = 256
HID = 32
TRAJ = 4
NY = 1024


def steps_of(rng, extent, cuts, low, top_value):
    level, own = 1.0, jax.random.fold_in(rng, 6)
    for axis_at, shards_of in cuts:
        draws = jnp.exp(jax.random.uniform(jax.random.fold_in(own, axis_at), (shards_of,), jnp.float32, low / len(cuts), top_value / len(cuts)))
        level = level * jnp.repeat(draws, extent[axis_at] // shards_of).reshape([-1 if axis == axis_at else 1 for axis in range(len(extent))])
    return level


def scatter_about(stream_key, shape, spread, bound, cuts=(), dtype=jnp.bfloat16):
    level = steps_of(stream_key, shape, cuts, -0.22, 0.18) if cuts else 1.0
    entries = jax.random.normal(stream_key, shape, jnp.float32) * spread * level
    return jnp.minimum(jnp.maximum(entries, -bound), bound).astype(dtype)


def setup_inputs(seed: int = 0) -> dict:
    arg_keys = jax.random.split(jax.random.key(seed), 11)
    density = jnp.clip(1.0 + 1.0 * jax.random.uniform(arg_keys[0], (TRAJ, NX, NY), jnp.float32) ** steps_of(arg_keys[0], (TRAJ, NX, NY), ((0, 4), (2, 8)), -0.2, 0.2), 1.0, 2.0)
    momentum = jnp.clip(jax.random.uniform(arg_keys[1], (TRAJ, 2, NX, NY), jnp.float32, -0.5, 0.5) * steps_of(arg_keys[1], (TRAJ, 2, NX, NY), ((0, 4), (3, 8)), -0.4, 0.0), -0.5, 0.5)
    tracer = jnp.clip(jax.random.uniform(arg_keys[2], (TRAJ, NX, NY), jnp.float32, -1.0, 1.0) * steps_of(arg_keys[2], (TRAJ, NX, NY), ((0, 4), (2, 8)), -0.4, 0.0), -1.0, 1.0)
    cotangent = scatter_about(arg_keys[3], (TRAJ, 4, NX, NY), 1.0, 6.0, ((0, 4), (3, 8)), jnp.float32)
    w_in = scatter_about(arg_keys[4], (HID, 16), 16 ** -0.5, 1.5, (), jnp.float32)
    b_in = scatter_about(arg_keys[5], (HID,), 0.5, 3.0, (), jnp.float32)
    w_mid = scatter_about(arg_keys[6], (HID, HID), HID ** -0.5, 1.0, (), jnp.float32)
    b_mid = scatter_about(arg_keys[7], (HID,), 0.5, 3.0, (), jnp.float32)
    w_out = scatter_about(arg_keys[8], (8, HID), HID ** -0.5, 1.0, (), jnp.float32)
    b_out = scatter_about(arg_keys[9], (8,), 0.5, 3.0, (), jnp.float32)
    return {"density": density, "momentum": momentum, "tracer": tracer, "cotangent": cotangent, "w_in": w_in, "b_in": b_in, "w_mid": w_mid, "b_mid": b_mid, "w_out": w_out, "b_out": b_out}


courant = 0.1
slope_gain = 0.25

def take_cells(values, sweep_dim, first_index, cell_count):
    return lax.slice_in_dim(values, first_index, first_index + cell_count, axis=sweep_dim)

def wrap_pad(values, sweep_dim, rim_width):
    total = values.shape[sweep_dim]
    return jnp.concatenate([take_cells(values, sweep_dim, total - rim_width, rim_width), values, take_cells(values, sweep_dim, 0, rim_width)], sweep_dim)

def expand(vector):
    return vector.reshape(vector.shape + (1, 1))

def limiter(window, weights):
    w_in, b_in, w_mid, b_mid, w_out, b_out = weights
    highest = lax.Precision.HIGHEST
    hidden_first = jnp.tanh(jnp.einsum('hc,cxy->hxy', w_in, window, precision=highest) + expand(b_in))
    hidden_second = jnp.tanh(jnp.einsum('hc,cxy->hxy', w_mid, hidden_first, precision=highest) + expand(b_mid))
    return jnp.tanh(jnp.einsum('hc,cxy->hxy', w_out, hidden_second, precision=highest) + expand(b_out))

def physical_flux(states, velocity):
    return jnp.stack([states[1], states[1] * velocity + states[0], states[2] * velocity, states[3] * velocity])

def face_flux(left_state, right_state):
    velocity_left = left_state[1] / left_state[0]
    velocity_right = right_state[1] / right_state[0]
    wave_speed = jnp.maximum(jnp.abs(velocity_left), jnp.abs(velocity_right)) + 1.0
    mean_flux = 0.5 * (physical_flux(left_state, velocity_left) + physical_flux(right_state, velocity_right))
    return mean_flux - 0.5 * wave_speed * (right_state - left_state)

def swap_momenta(values):
    return jnp.stack([values[0], values[2], values[1], values[3]])

def sweep(padded, sweep_dim, rotate, weights):
    if rotate:
        padded = swap_momenta(padded)
    length = padded.shape[sweep_dim] - 4
    face_count = length + 1
    shifted = [take_cells(padded, sweep_dim, offset, face_count) for offset in range(4)]
    window = jnp.concatenate(shifted, 0)
    gate_values = limiter(window, weights)
    left_state = shifted[1] + slope_gain * gate_values[:4] * (shifted[2] - shifted[0])
    right_state = shifted[2] - slope_gain * gate_values[4:] * (shifted[3] - shifted[1])
    fluxes = face_flux(left_state, right_state)
    cell_values = take_cells(padded, sweep_dim, 2, length)
    updated = cell_values - courant * (take_cells(fluxes, sweep_dim, 1, length) - take_cells(fluxes, sweep_dim, 0, length))
    if rotate:
        updated = swap_momenta(updated)
    return updated

def forward(states, weights):
    middle = sweep(wrap_pad(states, 1, 2), 1, False, weights)
    return sweep(wrap_pad(middle, 2, 2), 2, True, weights)

def reference(density, momentum, tracer, cotangent, w_in, b_in, w_mid, b_mid, w_out, b_out):
    weights = (w_in, b_in, w_mid, b_mid, w_out, b_out)
    states = jnp.concatenate([density[:, None], momentum, tracer[:, None]], 1)

    def single_flow(flow_pair):
        flow_state, flow_cot = flow_pair
        _, pull_back = jax.vjp(forward, flow_state, weights)
        return pull_back(flow_cot)
    grad_state, grad_weights = lax.map(single_flow, (states, cotangent))
    grad_weights = jax.tree.map(lambda stacked: lax.optimization_barrier(jnp.sum(stacked, 0)), grad_weights)
    return (grad_state[:, 0], grad_state[:, 1:3], grad_state[:, 3], grad_weights[0], grad_weights[1], grad_weights[2], grad_weights[3], grad_weights[4], grad_weights[5])
```

```python
import functools

import jax
import jax.numpy as jnp
from jax import lax
from jax.experimental import pallas as pl
from jax.experimental.pallas import tpu as pltpu
from jax.sharding import PartitionSpec as P

courant = 0.1
slope_gain = 0.25
F32 = jnp.float32
BF16 = jnp.bfloat16
FACES = 8
SEG = 16
RIM = 4
PAIR = 2
ONES = 16
VMEM_BYTES = 48 * 2**20


def dot(a, b):
    return lax.dot_general(a, b, (((1,), (0,)), ((), ())), preferred_element_type=F32)


def dot_nt(a, b):
    return lax.dot_general(a, b, (((1,), (1,)), ((), ())), preferred_element_type=F32)


def exact(a, b):
    return lax.dot_general(
        a, b, (((1,), (0,)), ((), ())), precision=lax.Precision.HIGHEST, preferred_element_type=F32
    )


def exact_nt(a, b):
    return lax.dot_general(
        a, b, (((1,), (1,)), ((), ())), precision=lax.Precision.HIGHEST, preferred_element_type=F32
    )


def split(values):
    high = values.astype(BF16)
    return high, (values - high.astype(F32)).astype(BF16)


def split3(values):
    high = values.astype(BF16)
    rest = values - high.astype(F32)
    middle = rest.astype(BF16)
    return high, middle, (rest - middle.astype(F32)).astype(BF16)


def rows_cols(shape):
    return lax.broadcasted_iota(jnp.int32, shape, 0), lax.broadcasted_iota(jnp.int32, shape, 1)


def pick(shape, test, dtype=BF16):
    r, c = rows_cols(shape)
    return jnp.where(test(r, c), 1.0, 0.0).astype(dtype)


def stack(parts):
    return jnp.concatenate(parts, 0)


def side(parts):
    return jnp.concatenate(parts, 1)


def place(left, levels, rights):
    total = None
    for values, right in zip(levels, rights):
        values = values if left is None else left(values).astype(BF16)
        part = dot(values, right)
        total = part if total is None else total + part
    return total


STACKED = (0, 0, 0, 1, 1, 2)


def stacked(parts):
    return [parts[0], parts[1], parts[2], parts[0], parts[1], parts[0]]


def level_of(block):
    return jnp.where(block < 3, 0, jnp.where(block < 5, 1, 2))


def build_first_x(w, b, hid):
    wide, cols = FACES * hid, 6 * 64 + ONES
    shape = (wide, cols)
    r, c = rows_cols(shape)
    total = jnp.zeros(shape, F32)
    for s in range(4):
        rights = [
            pick((16, cols), lambda q, n: (n < 384) & (level_of(n >> 6) == lev) & (q == 4 * s + ((n >> 4) & 3)))
            for lev in range(3)
        ]
        part = place(None, w, rights)
        total = total + jnp.where((c & 15) - (r // hid) == s, stack([part] * FACES), 0.0)
    levels = split3(b)
    at, _ = rows_cols((cols, hid))
    rows = jnp.zeros((cols, hid), F32)
    for lev in range(3):
        rows = jnp.where(at == 384 + lev, jnp.broadcast_to(levels[lev].astype(F32), (cols, hid)), rows)
    bias = dot_nt(pick((wide, hid), lambda q, n: (q % hid) == n), rows.astype(BF16))
    return (jnp.where(c < 384, total, 0.0) + bias).astype(BF16)


def build_first_y(w, hid):
    wide, cols = FACES * hid, 6 * 128
    shape = (wide, cols)
    r, c = rows_cols(shape)
    rights = [
        pick((16, cols), lambda q, n: (level_of(n >> 7) == lev) & (q == ((n & 127) >> 3))) for lev in range(3)
    ]
    part = place(None, w, rights)
    return jnp.where((c & 7) == (r // hid), stack([part] * FACES), 0.0).astype(BF16)


def build_mid(w, hid):
    block = 2 * hid
    shape = (2 * block, 4 * block)
    r, c = rows_cols(shape)

    def rights(levels):
        def test(lev):
            def inner(q, n):
                at = jnp.full(n.shape, -1, jnp.int32)
                for k, level in enumerate(levels):
                    at = jnp.where(n // block == k, level, at)
                return (at == lev) & ((n % hid) == q)

            return inner

        return [pick((hid, 4 * block), test(lev)) for lev in range(3)]

    upper = place(None, w, rights((0, 0, 0, 2)))
    lower = place(None, w, rights((1, 1, -1, -1)))
    keep = ((r % block) // hid) == ((c % block) // hid)
    return jnp.where(keep, stack([upper, upper, lower, lower]), 0.0).astype(BF16)


def build_mid_back(w, hid):
    block = 2 * hid
    shape = (block, 3 * block)
    r, c = rows_cols(shape)
    eye = pick((hid, hid), lambda q, n: q == n)
    rights = [
        pick((hid, 3 * block), lambda q, n: ((n // block == 1) == (lev == 1)) & ((n % hid) == q))
        for lev in range(2)
    ]
    part = place(lambda v: dot_nt(eye, v), w[:2], rights)
    return jnp.where((r // hid) == ((c % block) // hid), stack([part] * 2), 0.0).astype(BF16)


def build_out(w, hid):
    wide = FACES * hid
    shape = (64, wide)
    r, c = rows_cols(shape)
    right = pick((hid, wide), lambda q, n: (n % hid) == q)
    left = pick((64, 8), lambda q, n: (q >> 3) == n)
    keep = (r & 7) == (c // hid)
    return stack([jnp.where(keep, dot(dot(left, v).astype(BF16), right), 0.0) for v in w]).astype(BF16)


def spread_bias(b, rows, lanes, unit):
    n = b.shape[1]
    return exact_nt(pick((rows, n), lambda q, m: unit(q) == m, F32), jnp.broadcast_to(b, (lanes, n)))


def build_out_back(w, hid):
    wide = FACES * hid
    shape = (wide, 192)
    r, c = rows_cols(shape)
    left = pick((wide, hid), lambda q, n: (q % hid) == n)

    rights = [
        pick((8, 192), lambda q, n: (((n >> 6) == 1) == (lev == 1)) & (((n & 63) >> 3) == q)) for lev in range(2)
    ]
    part = place(lambda v: dot_nt(left, v), w[:2], rights)
    return jnp.where((r // hid) == (c & 7), part, 0.0).astype(BF16)


def build_first_x_back(w, hid):
    wide = FACES * hid
    shape = (128, 2 * wide)
    r, c = rows_cols(shape)
    right = pick((hid, 2 * wide), lambda q, n: (n % hid) == q)
    total = jnp.zeros(shape, F32)
    for s in range(4):
        left = pick((128, 16), lambda q, n: n == 4 * s + ((q & 63) >> 4))

        def one(values):
            return dot(dot_nt(left, values).astype(BF16), right)

        value = jnp.where(r < 64, one(w[0]), jnp.where(c < wide, one(w[1]), 0.0))
        total = total + jnp.where((r & 15) - ((c % wide) // hid) == s, value, 0.0)
    return total.astype(BF16)


def build_first_y_back(w, hid):
    wide = FACES * hid
    shape = (256, 2 * wide)
    r, c = rows_cols(shape)
    right = pick((hid, 2 * wide), lambda q, n: (n % hid) == q)
    left = pick((256, 16), lambda q, n: n == ((q & 127) >> 3))

    def one(values):
        return dot(dot_nt(left, values).astype(BF16), right)

    value = jnp.where(r < 128, one(w[0]), jnp.where(c < wide, one(w[1]), 0.0))
    return jnp.where((r & 7) == ((c % wide) // hid), value, 0.0).astype(BF16)


def limiter_forward(first, weights, hid):
    first_ref, first_bias_ref, mid_ref, mid_bias_ref, out_ref, out_bias_ref = weights
    width = first[0].shape[1]
    if first_bias_ref is None:
        h1 = jnp.tanh(dot(first_ref[...], stack(stacked(first) + [jnp.ones((ONES, width), BF16)])))
    else:
        h1 = jnp.tanh(dot(first_ref[...], stack(stacked(first))) + first_bias_ref[...])
    h1_parts = split3(h1)
    block = 2 * hid
    parts = []
    for at in range(0, FACES * hid, block):
        high, middle, low = (p[at : at + block] for p in h1_parts)
        both = dot(mid_ref[...], stack([high, middle, low, high]))
        parts.append(jnp.tanh(both[:block] + both[block:] + mid_bias_ref[...]))
    h2 = stack(parts)
    h2_parts = split3(h2)
    rows = 8 * FACES
    a = dot(out_ref[...], h2_parts[0])
    b = dot(out_ref[: 2 * rows, :], h2_parts[1])
    c = dot(out_ref[:rows, :], h2_parts[2])
    gates = jnp.tanh(
        ((a[2 * rows :] + b[rows:] + c) + (a[rows : 2 * rows] + b[:rows])) + a[:rows] + out_bias_ref[...]
    )
    return h1, h1_parts[:2], h2, h2_parts[:2], gates


def limiter_backward(d3, h1, h2, out_back_ref, mid_back_ref, hid):
    d3_hi, d3_lo = split(d3)
    d2 = dot(out_back_ref[...], stack([d3_hi, d3_hi, d3_lo])) * (1.0 - h2 * h2)
    d2_hi, d2_lo = split(d2)
    block = 2 * hid
    parts = []
    for at in range(0, FACES * hid, block):
        hi, lo = d2_hi[at : at + block], d2_lo[at : at + block]
        parts.append(dot(mid_back_ref[...], stack([hi, hi, lo])))
    d1 = stack(parts) * (1.0 - h1 * h1)
    return (d3_hi, d3_lo), (d2_hi, d2_lo), split(d1)


def first_backward(d1, back_ref):
    both = dot(back_ref[...], stack([d1[0], d1[1]]))
    half = both.shape[0] // 2
    return both[:half] + both[half:]


def add_weight_grads(first, h1, h2, d1, d2, d3, d3_full, acc, hid):
    acc_in, acc_mid, acc_out, acc_out_bias = acc
    width = d3_full.shape[1]
    ones = jnp.ones((ONES, width), BF16)
    nothing = jnp.zeros((ONES, width), BF16)
    acc_in[...] += dot_nt(
        side([stack([first[0], ones]), stack([first[0], ones]), stack([first[1], nothing])]),
        side([d1[0], d1[1], d1[0]]),
    )
    lefts, rights = [], []
    for at in range(0, FACES * hid, hid):
        lefts.append(stack([h1[0][at : at + hid], h1[1][at : at + hid], ones]))
        rights.append(stack([d2[0][at : at + hid], d2[1][at : at + hid]]))
    acc_mid[...] += dot_nt(side(lefts), side(rights))
    acc_out[...] += dot_nt(side([d3[0], d3[0], d3[1]]), side([h2[0], h2[1], h2[0]]))
    acc_out_bias[...] += d3_full


def edge_states(cells, gates):
    left, right = [], []
    for c in range(4):
        low = gates[FACES * c : FACES * (c + 1)]
        high = gates[FACES * (c + 4) : FACES * (c + 5)]
        left.append(cells[1][c] + slope_gain * low * (cells[2][c] - cells[0][c]))
        right.append(cells[2][c] - slope_gain * high * (cells[3][c] - cells[1][c]))
    return left, right


def face_flux(left, right):
    ul = left[1] / left[0]
    ur = right[1] / right[0]
    half_speed = 0.5 * (jnp.maximum(jnp.abs(ul), jnp.abs(ur)) + 1.0)
    fl = [left[1], left[1] * ul + left[0], left[2] * ul, left[3] * ul]
    fr = [right[1], right[1] * ur + right[0], right[2] * ur, right[3] * ur]
    return [0.5 * (fl[c] + fr[c]) - half_speed * (right[c] - left[c]) for c in range(4)]


def sign_of(values):
    return jnp.where(values > 0.0, 1.0, jnp.where(values < 0.0, -1.0, 0.0))


def face_flux_backward(left, right, d_flux):
    inv_l, inv_r = 1.0 / left[0], 1.0 / right[0]
    ul, ur = left[1] / left[0], right[1] / right[0]
    al, ar = jnp.abs(ul), jnp.abs(ur)
    half_speed = 0.5 * (jnp.maximum(al, ar) + 1.0)
    d_speed = -0.5 * sum(d_flux[c] * (right[c] - left[c]) for c in range(4))
    share = jnp.where(al > ar, 1.0, jnp.where(al < ar, 0.0, 0.5))
    half = [0.5 * d for d in d_flux]
    spread = [half_speed * d for d in d_flux]

    def one(state, u, inv, speed_part, sign):
        du = half[1] * state[1] + half[2] * state[2] + half[3] * state[3] + speed_part * sign_of(u)
        over = du * inv
        return [
            half[1] - over * u + sign * spread[0],
            half[0] + half[1] * u + over + sign * spread[1],
            half[2] * u + sign * spread[2],
            half[3] * u + sign * spread[3],
        ]

    return (
        one(left, ul, inv_l, d_speed * share, 1.0),
        one(right, ur, inv_r, d_speed * (1.0 - share), -1.0),
    )


def edge_backward(cells, gates, d_left, d_right):
    lows, highs = [], []
    direct = [[None] * 4 for _ in range(4)]
    for c in range(4):
        low = gates[FACES * c : FACES * (c + 1)]
        high = gates[FACES * (c + 4) : FACES * (c + 5)]
        lows.append(slope_gain * (cells[2][c] - cells[0][c]) * d_left[c])
        highs.append(-slope_gain * (cells[3][c] - cells[1][c]) * d_right[c])
        low_part = slope_gain * low * d_left[c]
        high_part = slope_gain * high * d_right[c]
        direct[0][c] = -low_part
        direct[1][c] = d_left[c] + high_part
        direct[2][c] = d_right[c] + low_part
        direct[3][c] = -high_part
    return stack(lows + highs) * (1.0 - gates * gates), direct


def turn(values, shift, axis):
    size = values.shape[axis]
    return values if shift % size == 0 else pltpu.roll(values, shift % size, axis)


def x_cells(tiles):
    return [[turn(t, -s, 0)[:FACES] for t in tiles] for s in range(4)]


def pack_kernel(den, mom, tra, cot, w_in, b_in, w_mid, b_mid, w_out, b_out,
                rim, first_x, first_y, first_bias, mid, mid_bias, out, out_bias,
                out_back, mid_back, first_x_back, first_y_back):
    nx, ny = den.shape[1:]
    segs = ny // SEG
    rows = nx // segs
    hid = w_in.shape[0]
    planes = [den.at[0], mom.at[0, 0], mom.at[0, 1], tra.at[0]] + [cot.at[0, c] for c in range(4)]
    lane = lax.broadcasted_iota(jnp.int32, (FACES, ny), 1)
    for v, plane in enumerate(planes):
        for at in range(0, rows, FACES):
            total = jnp.zeros((FACES, ny), F32)
            for s in range(segs):
                first = s * SEG + RIM
                moved = turn(plane[pl.ds(s * rows + at, FACES), :], first + RIM, 1)
                total = jnp.where((lane >= first) & (lane < first + 2 * RIM), moved, total)
            rim[v, pl.ds(at, FACES), :] = total

    wi, wm, wo = split3(w_in[...]), split3(w_mid[...]), split3(w_out[...])
    lanes = out_bias.shape[1]
    first_x[...] = build_first_x(wi, b_in[...], hid)
    first_y[...] = build_first_y(wi, hid)
    first_bias[...] = spread_bias(b_in[...], FACES * hid, lanes, lambda q: q % hid)
    mid[...] = build_mid(wm, hid)
    mid_bias[...] = spread_bias(b_mid[...], 2 * hid, lanes, lambda q: q % hid)
    out[...] = build_out(wo, hid)
    out_bias[...] = spread_bias(b_out[...], 64, lanes, lambda q: q >> 3)
    out_back[...] = build_out_back(wo, hid)
    mid_back[...] = build_mid_back(wm, hid)
    first_x_back[...] = build_first_x_back(wi, hid)
    first_y_back[...] = build_first_y_back(wi, hid)


def row_block(at):
    return pl.ds(pl.multiple_of(at * FACES, FACES), FACES)


def state_planes(den, mom, tra):
    return [den.at[0], mom.at[0, 0], mom.at[0, 1], tra.at[0]]


def x_tiles(planes, group, groups):
    after = jnp.where(group + 1 == groups, 0, group + 1)
    return [stack([plane[row_block(group), :], plane[row_block(after), :]]) for plane in planes]


def pair_tiles(planes, step, half):
    sets = [x_tiles(planes, step + k * half, PAIR * half) for k in range(PAIR)]
    return [side([one[c] for one in sets]) for c in range(len(planes))]


def x_forward(tiles, weights, hid):
    h1, h1_pair, h2, h2_pair, gates = limiter_forward(split3(stack(tiles)), weights, hid)
    cells = x_cells(tiles)
    return h1_pair, h2_pair, gates, face_flux(*edge_states(cells, gates))


def update_cells(plane_rows, flux_rows):
    upper = turn(flux_rows, -7, 0)[:FACES]
    lower = turn(flux_rows, -6, 0)[:FACES]
    return plane_rows - courant * (upper - lower)


def x_forward_kernel(den, mom, tra, first_x, mid, mid_bias, out, out_bias,
                     middle, h1_hi, h1_lo, h2_hi, h2_lo, gates_out,
                     flux, kept, kept_gates, sems):
    nx, ny = den.shape[1:]
    groups = nx // FACES
    half = groups // PAIR
    hid = mid.shape[0] // 4
    x_weights = (first_x, None, mid, mid_bias, out, out_bias)
    planes = state_planes(den, mom, tra)
    targets = [h1_hi, h1_lo, h2_hi, h2_lo]

    def copies(step):
        all_of = [
            pltpu.make_async_copy(kept.at[k, step], target.at[step], sems.at[k, step])
            for k, target in enumerate(targets)
        ]
        return all_of + [pltpu.make_async_copy(kept_gates.at[step], gates_out.at[step], sems.at[4, step])]

    def step_of(step, _):
        tiles = pair_tiles(planes, step, half)
        h1_pair, h2_pair, gates, fluxes = x_forward(tiles, x_weights, hid)
        for k, value in enumerate(h1_pair + h2_pair):
            kept[k, step] = value
        kept_gates[step] = gates
        for one in copies(step):
            one.start()
        for c in range(4):
            for k in range(PAIR):
                flux[c, row_block(step + k * half + 1), :] = fluxes[c][:, k * ny : (k + 1) * ny]
        return 0

    lax.fori_loop(0, half, step_of, 0)
    for c in range(4):
        flux[c, :FACES, :] = flux[c, nx : nx + FACES, :]

    def update(group, _):
        for c in range(4):
            both = stack([flux[c, row_block(group), :], flux[c, row_block(group + 1), :]])
            middle[c, row_block(group), :] = update_cells(planes[c][row_block(group), :], both)
        return 0

    lax.fori_loop(0, groups, update, 0)

    def finish(step, _):
        for one in copies(step):
            one.wait()
        return 0

    lax.fori_loop(0, half, finish, 0)


def y_order(planes):
    return [planes[0], planes[2], planes[1], planes[3]]


def lane_index(width):
    return lax.broadcasted_iota(jnp.int32, (FACES, width), 1)


def y_step(cells, cots, halo_mask, refs, hid):
    weights, out_back, mid_back, first_y_back = refs
    window = split3(stack([cells[s][c] for s in range(4) for c in range(4)]))
    h1, h1_pair, h2, h2_pair, gates = limiter_forward(window, weights, hid)
    left, right = edge_states(cells, gates)
    d_flux = [courant * (cots[1][c] - cots[0][c]) for c in range(4)]
    d_left, d_right = face_flux_backward(left, right, d_flux)
    if halo_mask is not None:
        d_left = [jnp.where(halo_mask, d, 0.0) for d in d_left]
        d_right = [jnp.where(halo_mask, d, 0.0) for d in d_right]
    d3_full, direct = edge_backward(cells, gates, d_left, d_right)
    d3, d2, d1 = limiter_backward(d3_full, h1, h2, out_back, mid_back, hid)
    d_window = first_backward(d1, first_y_back)
    parts = [
        [d_window[FACES * (4 * s + c) : FACES * (4 * s + c + 1)] + direct[s][c] for c in range(4)]
        for s in range(4)
    ]
    return parts, (window, h1_pair, h2_pair, d1, d2, d3, d3_full)


def y_gather(parts, ny):
    lane = lane_index(ny)
    out = []
    for c in range(4):
        a = turn(jnp.where(lane >= 1, parts[0][c], 0.0), -1, 1)
        b = turn(jnp.where(lane < ny - 1, parts[2][c], 0.0), 1, 1)
        d = turn(jnp.where(lane < ny - 2, parts[3][c], 0.0), 2, 1)
        out.append(parts[1][c] + a + b + d)
    return out


def fold_first_x(acc, hid):
    shape = acc.shape
    r, c = rows_cols(shape)
    fold = pick((shape[1], hid), lambda q, n: (q % hid) == n, F32)
    total = jnp.zeros((24, hid), F32)
    for s in range(4):
        keep = ((r & 15) - (c // hid) == s) & (r < 64)
        sel = lambda q, n: (n < 64) & (q == 4 * s + (n >> 4))
        if s == 0:
            keep = keep | (r >= 64)
            sel = lambda q, n: ((n < 64) & (q == (n >> 4))) | ((n == 64) & (q == 16))
        total = total + exact(pick((24, shape[0]), sel, F32), exact(jnp.where(keep, acc, 0.0), fold))
    return total


def fold_first_y(acc, hid):
    shape = acc.shape
    r, c = rows_cols(shape)
    fold = pick((shape[1], hid), lambda q, n: (q % hid) == n, F32)
    keep = ((r & 7) == (c // hid)) | (r >= 128)
    sel = lambda q, n: ((n < 128) & (q == (n >> 3))) | ((n == 128) & (q == 16))
    return exact(pick((24, shape[0]), sel, F32), exact(jnp.where(keep, acc, 0.0), fold))


def back_kernel(den, mom, tra, cot, middle, own, from_left, from_right,
                first_x, first_y, first_bias, mid, mid_bias, out, out_bias,
                out_back, mid_back, first_x_back, first_y_back,
                h1_hi, h1_lo, h2_hi, h2_lo, gates_in,
                g_den, g_mom, g_tra, g_weights,
                rim_state, rim_cot, rim_flux, rim_middle, rim_grad, d_middle,
                kept, kept_gates, acc_x, acc_y, acc_mid, acc_out, acc_out_bias, sems):
    nx, ny = den.shape[1:]
    groups = nx // FACES
    half = groups // PAIR
    hid = mid.shape[0] // 4
    x_weights = (first_x, None, mid, mid_bias, out, out_bias)
    segs = ny // SEG
    rim_rows = nx // segs
    rim_groups = rim_rows // FACES
    rim_half = rim_groups // PAIR

    fetches = [
        pltpu.make_async_copy(source, kept.at[k], sems.at[k])
        for k, source in enumerate([h1_hi, h1_lo, h2_hi, h2_lo])
    ] + [pltpu.make_async_copy(gates_in, kept_gates, sems.at[4])]
    for one in fetches:
        one.start()

    for acc in (acc_x, acc_y, acc_mid, acc_out, acc_out_bias):
        acc[...] = jnp.zeros(acc.shape, F32)

    lane = lane_index(ny)
    spot = lane & (SEG - 1)
    for v in range(8):
        for g in range(rim_groups):
            rows = pl.ds(g * FACES, FACES)
            mine = own[v, rows, :]
            value = jnp.where(
                spot < RIM,
                turn(from_left[v, rows, :], -RIM, 1),
                jnp.where(
                    spot < 2 * RIM,
                    turn(mine, -RIM, 1),
                    jnp.where(spot < 3 * RIM, turn(mine, RIM, 1), turn(from_right[v, rows, :], RIM, 1)),
                ),
            )
            if v < 4:
                rim_state[v, rows, :] = value
                if g == 0:
                    rim_state[v, pl.ds(rim_rows, FACES), :] = turn(value, -SEG, 1)
            else:
                rim_cot[v - 4, rows, :] = value

    def rim_forward(step, _):
        sets = [
            [
                stack([
                    rim_state[c, row_block(step + k * rim_half), :],
                    rim_state[c, row_block(step + k * rim_half + 1), :],
                ])
                for c in range(4)
            ]
            for k in range(PAIR)
        ]
        tiles = [side([one[c] for one in sets]) for c in range(4)]
        fluxes = x_forward(tiles, x_weights, hid)[3]
        for c in range(4):
            for k in range(PAIR):
                rim_flux[c, row_block(step + k * rim_half + 1), :] = fluxes[c][:, k * ny : (k + 1) * ny]
        return 0

    lax.fori_loop(0, rim_half, rim_forward, 0)
    for c in range(4):
        rim_flux[c, :FACES, :] = turn(rim_flux[c, rim_rows : rim_rows + FACES, :], SEG, 1)
        for g in range(rim_groups):
            rows = pl.ds(g * FACES, FACES)
            both = stack([rim_flux[c, rows, :], rim_flux[c, pl.ds((g + 1) * FACES, FACES), :]])
            rim_middle[c, rows, :] = update_cells(rim_state[c, rows, :], both)

    refs = ((first_y, first_bias, mid, mid_bias, out, out_bias), out_back, mid_back, first_y_back)
    spot_wide = lane_index(PAIR * ny) & (SEG - 1)
    rim_faces = (spot_wide == RIM - 2) | (spot_wide == RIM - 1) | (spot_wide == 3 * RIM)

    def rim_back(step, _):
        cells = [[[] for _ in range(4)] for _ in range(4)]
        cots = [[[] for _ in range(4)] for _ in range(2)]
        for k in range(PAIR):
            rows = row_block(step + k * rim_half)
            for c in range(4):
                value = rim_middle[c, rows, :]
                for s in range(4):
                    cells[s][c].append(turn(value, 1 - s, 1))
                value = rim_cot[c, rows, :]
                for s in range(2):
                    cots[s][c].append(turn(value, -s, 1))
        cells = [y_order([side(one) for one in row]) for row in cells]
        cots = [y_order([side(one) for one in row]) for row in cots]
        parts, _ = y_step(cells, cots, rim_faces, refs, hid)
        for k in range(PAIR):
            own_parts = [[one[:, k * ny : (k + 1) * ny] for one in row] for row in parts]
            gathered = y_order(y_gather(own_parts, ny))
            for c in range(4):
                rim_grad[c, row_block(step + k * rim_half), :] = gathered[c]
        return 0

    lax.fori_loop(0, rim_half, rim_back, 0)

    def main_y(step, _):
        cells = [[[] for _ in range(4)] for _ in range(4)]
        cots = [[[] for _ in range(4)] for _ in range(2)]
        for k in range(PAIR):
            group = step + k * half
            rows = row_block(group)
            seg = group // rim_groups
            rim_at = row_block(group - seg * rim_groups)
            to_low = ny - (seg * SEG + 3 * RIM)
            to_high = lax.rem(ny - 1 - (seg * SEG + RIM - 1) + ny, ny)
            for c in range(4):
                value = middle[c, rows, :]
                rim_value = rim_middle[c, rim_at, :]
                low = jnp.where(lane < 2, pltpu.roll(rim_value, to_low, 1), value)
                high = jnp.where(lane == ny - 1, pltpu.roll(rim_value, to_high, 1), value)
                cells[0][c].append(turn(high, 1, 1))
                cells[1][c].append(value)
                cells[2][c].append(turn(jnp.where(lane < 1, low, value), -1, 1))
                cells[3][c].append(turn(low, -2, 1))
                value = cot[0, c, rows, :]
                rim_value = rim_cot[c, rim_at, :]
                low = jnp.where(lane < 1, pltpu.roll(rim_value, to_low, 1), value)
                cots[0][c].append(value)
                cots[1][c].append(turn(low, -1, 1))
        cells = [y_order([side(one) for one in row]) for row in cells]
        cots = [y_order([side(one) for one in row]) for row in cots]
        parts, (window, h1_pair, h2_pair, d1, d2, d3, d3_full) = y_step(cells, cots, None, refs, hid)
        add_weight_grads(
            window, h1_pair, h2_pair, d1, d2, d3, d3_full, (acc_y, acc_mid, acc_out, acc_out_bias), hid
        )
        for k in range(PAIR):
            group = step + k * half
            rows = row_block(group)
            seg = group // rim_groups
            rim_at = row_block(group - seg * rim_groups)
            own_parts = [[one[:, k * ny : (k + 1) * ny] for one in row] for row in parts]
            gathered = y_order(y_gather(own_parts, ny))
            to_low = ny - (seg * SEG + RIM)
            to_high = lax.rem(ny - 1 - (seg * SEG + 3 * RIM - 1) + ny, ny)
            for c in range(4):
                rim_value = rim_grad[c, rim_at, :]
                from_rim = jnp.where(
                    lane < 2,
                    pltpu.roll(rim_value, to_low, 1),
                    jnp.where(lane == ny - 1, pltpu.roll(rim_value, to_high, 1), 0.0),
                )
                d_middle[c, rows, :] = cot[0, c, rows, :] + gathered[c] + from_rim
        return 0

    lax.fori_loop(0, half, main_y, 0)

    for one in fetches:
        one.wait()
    planes = state_planes(den, mom, tra)
    grads = state_planes(g_den, g_mom, g_tra)
    d_planes = [d_middle.at[c] for c in range(4)]

    def main_x(step, carry):
        tiles = pair_tiles(planes, step, half)
        d_tiles = pair_tiles(d_planes, step, half)
        gates = kept_gates[step]
        h1_pair = (kept[0, step], kept[1, step])
        h2_pair = (kept[2, step], kept[3, step])
        h1 = h1_pair[0].astype(F32) + h1_pair[1].astype(F32)
        h2 = h2_pair[0].astype(F32) + h2_pair[1].astype(F32)
        cells = x_cells(tiles)
        left, right = edge_states(cells, gates)
        d_flux = [courant * (turn(d, -2, 0)[:FACES] - turn(d, -1, 0)[:FACES]) for d in d_tiles]
        d_left, d_right = face_flux_backward(left, right, d_flux)
        d3_full, direct = edge_backward(cells, gates, d_left, d_right)
        d3, d2, d1 = limiter_backward(d3_full, h1, h2, out_back, mid_back, hid)
        d_window = first_backward(d1, first_x_back)
        add_weight_grads(
            split(stack(tiles)), h1_pair, h2_pair, d1, d2, d3, d3_full,
            (acc_x, acc_mid, acc_out, acc_out_bias), hid,
        )
        later = []
        for c in range(4):
            total = d_window[2 * FACES * c : 2 * FACES * (c + 1)]
            for s in range(4):
                total = total + turn(stack([direct[s][c], jnp.zeros_like(direct[s][c])]), s, 0)
            now = total[:FACES] + d_tiles[c][:FACES] + carry[c]
            for k in range(PAIR):
                grads[c][row_block(step + k * half), :] = now[:, k * ny : (k + 1) * ny]
            later.append(total[FACES:])
        return tuple(later)

    start = tuple(jnp.zeros((FACES, PAIR * ny), F32) for _ in range(4))
    last = lax.fori_loop(0, half, main_x, start)
    for c in range(4):
        for k in range(PAIR):
            at = (k + 1) % PAIR * half * FACES
            grads[c][pl.ds(at, FACES), :] += last[c][:, k * ny : (k + 1) * ny]

    g_weights[...] = jnp.zeros(g_weights.shape, F32)
    eye = pick((hid, hid), lambda q, n: q == n, F32)
    grad_first = fold_first_x(acc_x[...], hid) + fold_first_y(acc_y[...], hid)
    g_weights[0:hid, 0:16] = exact_nt(eye, grad_first[:16])
    both = acc_mid[...]
    grad_mid = both[:hid, :hid] + both[:hid, hid:] + both[hid : 2 * hid, :hid]
    g_weights[hid : 2 * hid, 0:hid] = exact_nt(eye, grad_mid)
    grad_mid_bias = both[2 * hid :, :hid] + both[2 * hid :, hid:]
    r, c = rows_cols(acc_out.shape)
    fold = pick((acc_out.shape[1], hid), lambda q, n: (q % hid) == n, F32)
    rows = pick((8, 64), lambda q, n: (n >> 3) == q, F32)
    g_weights[2 * hid : 2 * hid + 8, 0:hid] = exact(
        rows, exact(jnp.where((r & 7) == (c // hid), acc_out[...], 0.0), fold)
    )
    out_bias_rows = exact_nt(jnp.ones((8, acc_out_bias.shape[1]), F32), acc_out_bias[...])
    r, c = rows_cols((8, hid))
    g_weights[2 * hid + 8 : 2 * hid + 16, 0:hid] = jnp.where(
        r == 0, grad_first[16:24], jnp.where(r == 1, grad_mid_bias[:8], 0.0)
    )
    g_weights[2 * hid + 16 : 2 * hid + 24, 0:8] = exact_nt(out_bias_rows, rows)


def whole(count, space=pltpu.VMEM):
    return [pl.BlockSpec(memory_space=space)] * count


def call(kernel, outs, operands, out_spaces=None, in_spaces=None, scratch=(), flops=0, moved=0):
    return pl.pallas_call(
        kernel,
        out_shape=outs,
        in_specs=in_spaces or whole(len(operands)),
        out_specs=out_spaces or whole(len(outs)),
        scratch_shapes=list(scratch),
        compiler_params=pltpu.CompilerParams(vmem_limit_bytes=VMEM_BYTES),
        cost_estimate=pl.CostEstimate(flops=flops, bytes_accessed=moved, transcendentals=0),
    )(*operands)


def body(ring, density, momentum, tracer, cotangent, w_in, b_in, w_mid, b_mid, w_out, b_out):
    nx, ny = density.shape[1:]
    hid = w_in.shape[0]
    wide = FACES * hid
    groups = nx // FACES
    half = groups // PAIR
    lanes = PAIR * ny
    segs = ny // SEG
    rim_rows = nx // segs
    shape = jax.ShapeDtypeStruct

    rim, *matrices = call(
        pack_kernel,
        [
            shape((8, rim_rows, ny), F32),
            shape((wide, 6 * 64 + ONES), BF16),
            shape((wide, 6 * 128), BF16),
            shape((wide, lanes), F32),
            shape((4 * hid, 8 * hid), BF16),
            shape((2 * hid, lanes), F32),
            shape((192, wide), BF16),
            shape((64, lanes), F32),
            shape((wide, 192), BF16),
            shape((2 * hid, 6 * hid), BF16),
            shape((128, 2 * wide), BF16),
            shape((256, 2 * wide), BF16),
        ],
        [density, momentum, tracer, cotangent, w_in, b_in[None], w_mid, b_mid[None], w_out, b_out[None]],
    )
    axes = ("tx", "ty")
    from_left = lax.ppermute(rim, axes, [(i, (i + 1) % ring) for i in range(ring)])
    from_right = lax.ppermute(rim, axes, [((i + 1) % ring, i) for i in range(ring)])

    middle, h1_hi, h1_lo, h2_hi, h2_lo, gates = call(
        x_forward_kernel,
        [shape((4, nx, ny), F32)]
        + [shape((half, wide, lanes), BF16)] * 4
        + [shape((half, 64, lanes), F32)],
        [density, momentum, tracer, matrices[0]] + matrices[3:7],
        out_spaces=whole(1) + whole(5, pl.ANY),
        scratch=[
            pltpu.VMEM((4, nx + FACES, ny), F32),
            pltpu.VMEM((4, half, wide, lanes), BF16),
            pltpu.VMEM((half, 64, lanes), F32),
            pltpu.SemaphoreType.DMA((5, half)),
        ],
        flops=10**10,
        moved=10**7,
    )
    g_den, g_mom, g_tra, g_weights = call(
        back_kernel,
        [
            shape(density.shape, F32),
            shape(momentum.shape, F32),
            shape(tracer.shape, F32),
            shape((2 * hid + 24, 128), F32),
        ],
        [density, momentum, tracer, cotangent, middle, rim, from_left, from_right]
        + matrices
        + [h1_hi, h1_lo, h2_hi, h2_lo, gates],
        in_spaces=whole(19) + whole(5, pl.ANY),
        scratch=[
            pltpu.VMEM((4, rim_rows + FACES, ny), F32),
            pltpu.VMEM((4, rim_rows, ny), F32),
            pltpu.VMEM((4, rim_rows + FACES, ny), F32),
            pltpu.VMEM((4, rim_rows, ny), F32),
            pltpu.VMEM((4, rim_rows, ny), F32),
            pltpu.VMEM((4, nx, ny), F32),
            pltpu.VMEM((4, half, wide, lanes), BF16),
            pltpu.VMEM((half, 64, lanes), F32),
            pltpu.VMEM((64 + ONES, wide), F32),
            pltpu.VMEM((128 + ONES, wide), F32),
            pltpu.VMEM((2 * hid + ONES, 2 * hid), F32),
            pltpu.VMEM((64, wide), F32),
            pltpu.VMEM((64, lanes), F32),
            pltpu.SemaphoreType.DMA((5,)),
        ],
        flops=4 * 10**10,
        moved=2 * 10**7,
    )
    totals = lax.psum(g_weights, ("traj", "tx", "ty"))
    return (
        g_den,
        g_mom,
        g_tra,
        totals[:hid, :16],
        totals[2 * hid + 8, :hid],
        totals[hid : 2 * hid, :hid],
        totals[2 * hid + 9, :hid],
        totals[2 * hid : 2 * hid + 8, :hid],
        totals[2 * hid + 16, :8],
    )


def solution(mesh):
    flow = P("traj", None, ("tx", "ty"))
    deep = P("traj", None, None, ("tx", "ty"))
    ring = mesh.shape["tx"] * mesh.shape["ty"]
    return jax.shard_map(
        functools.partial(body, ring),
        mesh=mesh,
        in_specs=(flow, deep, flow, deep) + (P(),) * 6,
        out_specs=(flow, deep, flow) + (P(),) * 6,
        check_vma=False,
    )
```

```python
import functools

import jax
import jax.numpy as jnp
from jax import lax
from jax.experimental import pallas as pl
from jax.experimental.pallas import tpu as pltpu
from jax.sharding import PartitionSpec as P

courant = 0.1
slope_gain = 0.25
F32 = jnp.float32
BF16 = jnp.bfloat16
FACES = 8
SEG = 16
RIM = 4
PAIR = 4
ONES = 16
VMEM_BYTES = 32 * 2**20


def dot(a, b):
    return lax.dot_general(a, b, (((1,), (0,)), ((), ())), preferred_element_type=F32)


def dot_nt(a, b):
    return lax.dot_general(a, b, (((1,), (1,)), ((), ())), preferred_element_type=F32)


def exact(a, b):
    return lax.dot_general(
        a, b, (((1,), (0,)), ((), ())), precision=lax.Precision.HIGHEST, preferred_element_type=F32
    )


def exact_nt(a, b):
    return lax.dot_general(
        a, b, (((1,), (1,)), ((), ())), precision=lax.Precision.HIGHEST, preferred_element_type=F32
    )


def split(values):
    high = values.astype(BF16)
    return high, (values - high.astype(F32)).astype(BF16)


def split3(values):
    high = values.astype(BF16)
    rest = values - high.astype(F32)
    middle = rest.astype(BF16)
    return high, middle, (rest - middle.astype(F32)).astype(BF16)


def rows_cols(shape):
    return lax.broadcasted_iota(jnp.int32, shape, 0), lax.broadcasted_iota(jnp.int32, shape, 1)


def pick(shape, test, dtype=BF16):
    r, c = rows_cols(shape)
    return jnp.where(test(r, c), 1.0, 0.0).astype(dtype)


def stack(parts):
    return jnp.concatenate(parts, 0)


def side(parts):
    return jnp.concatenate(parts, 1)


def place(left, levels, rights):
    total = None
    for values, right in zip(levels, rights):
        values = values if left is None else left(values).astype(BF16)
        part = dot(values, right)
        total = part if total is None else total + part
    return total


STACKED = (0, 0, 0, 1, 1, 2)


def stacked(parts):
    return [parts[0], parts[1], parts[2], parts[0], parts[1], parts[0]]


def level_of(block):
    return jnp.where(block < 3, 0, jnp.where(block < 5, 1, 2))


def build_first_x(w, b, hid):
    wide, cols = FACES * hid, 6 * 64 + ONES
    shape = (wide, cols)
    r, c = rows_cols(shape)
    total = jnp.zeros(shape, F32)
    for s in range(4):
        rights = [
            pick((16, cols), lambda q, n: (n < 384) & (level_of(n >> 6) == lev) & (q == 4 * s + ((n >> 4) & 3)))
            for lev in range(3)
        ]
        part = place(None, w, rights)
        total = total + jnp.where((c & 15) - (r // hid) == s, stack([part] * FACES), 0.0)
    levels = split3(b)
    at, _ = rows_cols((cols, hid))
    rows = jnp.zeros((cols, hid), F32)
    for lev in range(3):
        rows = jnp.where(at == 384 + lev, jnp.broadcast_to(levels[lev].astype(F32), (cols, hid)), rows)
    bias = dot_nt(pick((wide, hid), lambda q, n: (q % hid) == n), rows.astype(BF16))
    return (jnp.where(c < 384, total, 0.0) + bias).astype(BF16)


def build_first_y(w, hid):
    wide, cols = FACES * hid, 6 * 128
    shape = (wide, cols)
    r, c = rows_cols(shape)
    rights = [
        pick((16, cols), lambda q, n: (level_of(n >> 7) == lev) & (q == ((n & 127) >> 3))) for lev in range(3)
    ]
    part = place(None, w, rights)
    return jnp.where((c & 7) == (r // hid), stack([part] * FACES), 0.0).astype(BF16)


def build_mid(w, hid):
    block = 2 * hid
    shape = (2 * block, 4 * block)
    r, c = rows_cols(shape)

    def rights(levels):
        def test(lev):
            def inner(q, n):
                at = jnp.full(n.shape, -1, jnp.int32)
                for k, level in enumerate(levels):
                    at = jnp.where(n // block == k, level, at)
                return (at == lev) & ((n % hid) == q)

            return inner

        return [pick((hid, 4 * block), test(lev)) for lev in range(3)]

    upper = place(None, w, rights((0, 0, 0, 2)))
    lower = place(None, w, rights((1, 1, -1, -1)))
    keep = ((r % block) // hid) == ((c % block) // hid)
    return jnp.where(keep, stack([upper, upper, lower, lower]), 0.0).astype(BF16)


def build_mid_back(w, hid):
    block = 2 * hid
    shape = (block, 3 * block)
    r, c = rows_cols(shape)
    eye = pick((hid, hid), lambda q, n: q == n)
    rights = [
        pick((hid, 3 * block), lambda q, n: ((n // block == 1) == (lev == 1)) & ((n % hid) == q))
        for lev in range(2)
    ]
    part = place(lambda v: dot_nt(eye, v), w[:2], rights)
    return jnp.where((r // hid) == ((c % block) // hid), stack([part] * 2), 0.0).astype(BF16)


def build_out(w, hid):
    wide = FACES * hid
    shape = (64, wide)
    r, c = rows_cols(shape)
    right = pick((hid, wide), lambda q, n: (n % hid) == q)
    left = pick((64, 8), lambda q, n: (q >> 3) == n)
    keep = (r & 7) == (c // hid)
    return stack([jnp.where(keep, dot(dot(left, v).astype(BF16), right), 0.0) for v in w]).astype(BF16)


def spread_bias(b, rows, lanes, unit):
    n = b.shape[1]
    return exact_nt(pick((rows, n), lambda q, m: unit(q) == m, F32), jnp.broadcast_to(b, (lanes, n)))


def build_out_back(w, hid):
    wide = FACES * hid
    shape = (wide, 192)
    r, c = rows_cols(shape)
    left = pick((wide, hid), lambda q, n: (q % hid) == n)

    rights = [
        pick((8, 192), lambda q, n: (((n >> 6) == 1) == (lev == 1)) & (((n & 63) >> 3) == q)) for lev in range(2)
    ]
    part = place(lambda v: dot_nt(left, v), w[:2], rights)
    return jnp.where((r // hid) == (c & 7), part, 0.0).astype(BF16)


def build_first_x_back(w, hid):
    wide = FACES * hid
    shape = (128, 2 * wide)
    r, c = rows_cols(shape)
    right = pick((hid, 2 * wide), lambda q, n: (n % hid) == q)
    total = jnp.zeros(shape, F32)
    for s in range(4):
        left = pick((128, 16), lambda q, n: n == 4 * s + ((q & 63) >> 4))

        def one(values):
            return dot(dot_nt(left, values).astype(BF16), right)

        value = jnp.where(r < 64, one(w[0]), jnp.where(c < wide, one(w[1]), 0.0))
        total = total + jnp.where((r & 15) - ((c % wide) // hid) == s, value, 0.0)
    return total.astype(BF16)


def build_first_y_back(w, hid):
    wide = FACES * hid
    shape = (256, 2 * wide)
    r, c = rows_cols(shape)
    right = pick((hid, 2 * wide), lambda q, n: (n % hid) == q)
    left = pick((256, 16), lambda q, n: n == ((q & 127) >> 3))

    def one(values):
        return dot(dot_nt(left, values).astype(BF16), right)

    value = jnp.where(r < 128, one(w[0]), jnp.where(c < wide, one(w[1]), 0.0))
    return jnp.where((r & 7) == ((c % wide) // hid), value, 0.0).astype(BF16)


def limiter_forward(first, weights, hid):
    first_ref, first_bias_ref, mid_ref, mid_bias_ref, out_ref, out_bias_ref = weights
    width = first[0].shape[1]
    if first_bias_ref is None:
        h1 = jnp.tanh(dot(first_ref[...], stack(stacked(first) + [jnp.ones((ONES, width), BF16)])))
    else:
        h1 = jnp.tanh(dot(first_ref[...], stack(stacked(first))) + first_bias_ref[...])
    h1_parts = split3(h1)
    block = 2 * hid
    parts = []
    for at in range(0, FACES * hid, block):
        high, middle, low = (p[at : at + block] for p in h1_parts)
        both = dot(mid_ref[...], stack([high, middle, low, high]))
        parts.append(jnp.tanh(both[:block] + both[block:] + mid_bias_ref[...]))
    h2 = stack(parts)
    h2_parts = split3(h2)
    rows = 8 * FACES
    a = dot(out_ref[...], h2_parts[0])
    b = dot(out_ref[: 2 * rows, :], h2_parts[1])
    c = dot(out_ref[:rows, :], h2_parts[2])
    gates = jnp.tanh(
        ((a[2 * rows :] + b[rows:] + c) + (a[rows : 2 * rows] + b[:rows])) + a[:rows] + out_bias_ref[...]
    )
    return h1, h1_parts[:2], h2, h2_parts[:2], gates


def limiter_backward(d3, h1, h2, out_back_ref, mid_back_ref, hid):
    d3_hi, d3_lo = split(d3)
    d2 = dot(out_back_ref[...], stack([d3_hi, d3_hi, d3_lo])) * (1.0 - h2 * h2)
    d2_hi, d2_lo = split(d2)
    block = 2 * hid
    parts = []
    for at in range(0, FACES * hid, block):
        hi, lo = d2_hi[at : at + block], d2_lo[at : at + block]
        parts.append(dot(mid_back_ref[...], stack([hi, hi, lo])))
    d1 = stack(parts) * (1.0 - h1 * h1)
    return (d3_hi, d3_lo), (d2_hi, d2_lo), split(d1)


def first_backward(d1, back_ref):
    both = dot(back_ref[...], stack([d1[0], d1[1]]))
    half = both.shape[0] // 2
    return both[:half] + both[half:]


def add_weight_grads(first, h1, h2, d1, d2, d3, d3_full, acc, hid):
    acc_in, acc_mid, acc_out, acc_out_bias = acc
    width = d3_full.shape[1]
    ones = jnp.ones((ONES, width), BF16)
    nothing = jnp.zeros((ONES, width), BF16)
    acc_in[...] += dot_nt(
        side([stack([first[0], ones]), stack([first[0], ones]), stack([first[1], nothing])]),
        side([d1[0], d1[1], d1[0]]),
    )
    lefts, rights = [], []
    for at in range(0, FACES * hid, hid):
        lefts.append(stack([h1[0][at : at + hid], h1[1][at : at + hid], ones]))
        rights.append(stack([d2[0][at : at + hid], d2[1][at : at + hid]]))
    acc_mid[...] += dot_nt(side(lefts), side(rights))
    acc_out[...] += dot_nt(side([d3[0], d3[0], d3[1]]), side([h2[0], h2[1], h2[0]]))
    acc_out_bias[...] += d3_full


def edge_states(cells, gates):
    left, right = [], []
    for c in range(4):
        low = gates[FACES * c : FACES * (c + 1)]
        high = gates[FACES * (c + 4) : FACES * (c + 5)]
        left.append(cells[1][c] + slope_gain * low * (cells[2][c] - cells[0][c]))
        right.append(cells[2][c] - slope_gain * high * (cells[3][c] - cells[1][c]))
    return left, right


def face_flux(left, right):
    ul = left[1] / left[0]
    ur = right[1] / right[0]
    half_speed = 0.5 * (jnp.maximum(jnp.abs(ul), jnp.abs(ur)) + 1.0)
    fl = [left[1], left[1] * ul + left[0], left[2] * ul, left[3] * ul]
    fr = [right[1], right[1] * ur + right[0], right[2] * ur, right[3] * ur]
    return [0.5 * (fl[c] + fr[c]) - half_speed * (right[c] - left[c]) for c in range(4)]


def sign_of(values):
    return jnp.where(values > 0.0, 1.0, jnp.where(values < 0.0, -1.0, 0.0))


def face_flux_backward(left, right, d_flux):
    inv_l, inv_r = 1.0 / left[0], 1.0 / right[0]
    ul, ur = left[1] / left[0], right[1] / right[0]
    al, ar = jnp.abs(ul), jnp.abs(ur)
    half_speed = 0.5 * (jnp.maximum(al, ar) + 1.0)
    d_speed = -0.5 * sum(d_flux[c] * (right[c] - left[c]) for c in range(4))
    share = jnp.where(al > ar, 1.0, jnp.where(al < ar, 0.0, 0.5))
    half = [0.5 * d for d in d_flux]
    spread = [half_speed * d for d in d_flux]

    def one(state, u, inv, speed_part, sign):
        du = half[1] * state[1] + half[2] * state[2] + half[3] * state[3] + speed_part * sign_of(u)
        over = du * inv
        return [
            half[1] - over * u + sign * spread[0],
            half[0] + half[1] * u + over + sign * spread[1],
            half[2] * u + sign * spread[2],
            half[3] * u + sign * spread[3],
        ]

    return (
        one(left, ul, inv_l, d_speed * share, 1.0),
        one(right, ur, inv_r, d_speed * (1.0 - share), -1.0),
    )


def edge_backward(cells, gates, d_left, d_right):
    lows, highs = [], []
    direct = [[None] * 4 for _ in range(4)]
    for c in range(4):
        low = gates[FACES * c : FACES * (c + 1)]
        high = gates[FACES * (c + 4) : FACES * (c + 5)]
        lows.append(slope_gain * (cells[2][c] - cells[0][c]) * d_left[c])
        highs.append(-slope_gain * (cells[3][c] - cells[1][c]) * d_right[c])
        low_part = slope_gain * low * d_left[c]
        high_part = slope_gain * high * d_right[c]
        direct[0][c] = -low_part
        direct[1][c] = d_left[c] + high_part
        direct[2][c] = d_right[c] + low_part
        direct[3][c] = -high_part
    return stack(lows + highs) * (1.0 - gates * gates), direct


def turn(values, shift, axis):
    size = values.shape[axis]
    return values if shift % size == 0 else pltpu.roll(values, shift % size, axis)


def x_cells(tiles):
    return [[turn(t, -s, 0)[:FACES] for t in tiles] for s in range(4)]


def pack_kernel(den, mom, tra, cot, w_in, b_in, w_mid, b_mid, w_out, b_out,
                rim, state, cots, first_x, first_y, first_bias, mid, mid_bias, out, out_bias,
                out_back, mid_back, first_x_back, first_y_back, *scratch):
    *small, sems = scratch
    nx, ny = den.shape[1:]
    segs = ny // SEG
    rows = nx // segs
    hid = w_in.shape[1]
    copies = [
        pltpu.make_async_copy(source, target, sems.at[k])
        for k, (source, target) in enumerate(
            list(zip([w_in, b_in, w_mid, b_mid, w_out, b_out], small))
            + [
                (den.at[0], state.at[0]),
                (mom.at[0], state.at[pl.ds(1, 2)]),
                (tra.at[0], state.at[3]),
                (cot.at[0], cots),
            ]
        )
    ]
    for one in copies:
        one.start()
    for one in copies[:6]:
        one.wait()
    w_in, b_in, w_mid, b_mid, w_out, b_out = small
    eye = pick((hid, hid), lambda q, n: q == n)
    wi = [dot_nt(eye, level).astype(BF16) for level in split3(w_in[...])]
    wm, wo = split3(w_mid[...]), split3(w_out[...])
    lanes = out_bias.shape[1]
    first_x[...] = build_first_x(wi, b_in[...], hid)
    first_y[...] = build_first_y(wi, hid)
    first_bias[...] = spread_bias(b_in[...], FACES * hid, lanes, lambda q: q % hid)
    mid[...] = build_mid(wm, hid)
    mid_bias[...] = spread_bias(b_mid[...], 2 * hid, lanes, lambda q: q % hid)
    out[...] = build_out(wo, hid)
    out_bias[...] = spread_bias(b_out[...], 64, lanes, lambda q: q >> 3)
    out_back[...] = build_out_back(wo, hid)
    mid_back[...] = build_mid_back(wm, hid)
    first_x_back[...] = build_first_x_back(wi, hid)
    first_y_back[...] = build_first_y_back(wi, hid)

    for one in copies[6:]:
        one.wait()
    lane = lane_index(ny)
    for v in range(8):
        plane = state.at[v] if v < 4 else cots.at[v - 4]
        for at in range(0, rows, FACES):
            total = jnp.zeros((FACES, ny), F32)
            for s in range(segs):
                first = s * SEG + RIM
                moved = turn(plane[pl.ds(s * rows + at, FACES), :], first + RIM, 1)
                total = jnp.where((lane >= first) & (lane < first + 2 * RIM), moved, total)
            rim[v, pl.ds(at, FACES), :] = total


def row_block(at):
    return pl.ds(pl.multiple_of(at * FACES, FACES), FACES)


def x_tiles(planes, group, groups):
    after = jnp.where(group + 1 == groups, 0, group + 1)
    return [stack([plane[row_block(group), :], plane[row_block(after), :]]) for plane in planes]


def pair_tiles(planes, step, half):
    sets = [x_tiles(planes, step + k * half, PAIR * half) for k in range(PAIR)]
    return [side([one[c] for one in sets]) for c in range(len(planes))]


def x_forward(tiles, weights, hid):
    h1, h1_pair, h2, h2_pair, gates = limiter_forward(split3(stack(tiles)), weights, hid)
    cells = x_cells(tiles)
    return h1_pair, h2_pair, gates, face_flux(*edge_states(cells, gates))


def update_cells(plane_rows, flux_rows):
    upper = turn(flux_rows, -7, 0)[:FACES]
    lower = turn(flux_rows, -6, 0)[:FACES]
    return plane_rows - courant * (upper - lower)


def x_forward_kernel(state, first_x, mid, mid_bias, out, out_bias,
                     middle, h1_hi, h1_lo, h2_hi, h2_lo, gates_out, flux):
    nx, ny = state.shape[1:]
    groups = nx // FACES
    half = groups // PAIR
    hid = mid.shape[0] // 4
    x_weights = (first_x, None, mid, mid_bias, out, out_bias)
    planes = [state.at[c] for c in range(4)]

    def step_of(step, _):
        tiles = pair_tiles(planes, step, half)
        h1_pair, h2_pair, gates, fluxes = x_forward(tiles, x_weights, hid)
        for target, value in zip((h1_hi, h1_lo, h2_hi, h2_lo, gates_out), h1_pair + h2_pair + (gates,)):
            target[step] = value
        for c in range(4):
            for k in range(PAIR):
                flux[c, row_block(step + k * half + 1), :] = fluxes[c][:, k * ny : (k + 1) * ny]
        return 0

    lax.fori_loop(0, half, step_of, 0)
    for c in range(4):
        flux[c, :FACES, :] = flux[c, nx : nx + FACES, :]

    def update(group, _):
        for c in range(4):
            both = stack([flux[c, row_block(group), :], flux[c, row_block(group + 1), :]])
            middle[c, row_block(group), :] = update_cells(planes[c][row_block(group), :], both)
        return 0

    lax.fori_loop(0, groups, update, 0)


def y_order(planes):
    return [planes[0], planes[2], planes[1], planes[3]]


def lane_index(width):
    return lax.broadcasted_iota(jnp.int32, (FACES, width), 1)


def y_step(cells, cots, halo_mask, refs, hid):
    weights, out_back, mid_back, first_y_back = refs
    window = split3(stack([cells[s][c] for s in range(4) for c in range(4)]))
    h1, h1_pair, h2, h2_pair, gates = limiter_forward(window, weights, hid)
    left, right = edge_states(cells, gates)
    d_flux = [courant * (cots[1][c] - cots[0][c]) for c in range(4)]
    d_left, d_right = face_flux_backward(left, right, d_flux)
    if halo_mask is not None:
        d_left = [jnp.where(halo_mask, d, 0.0) for d in d_left]
        d_right = [jnp.where(halo_mask, d, 0.0) for d in d_right]
    d3_full, direct = edge_backward(cells, gates, d_left, d_right)
    d3, d2, d1 = limiter_backward(d3_full, h1, h2, out_back, mid_back, hid)
    d_window = first_backward(d1, first_y_back)
    parts = [
        [d_window[FACES * (4 * s + c) : FACES * (4 * s + c + 1)] + direct[s][c] for c in range(4)]
        for s in range(4)
    ]
    return parts, (window, h1_pair, h2_pair, d1, d2, d3, d3_full)


def y_gather(parts, ny):
    lane = lane_index(ny)
    out = []
    for c in range(4):
        a = turn(jnp.where(lane >= 1, parts[0][c], 0.0), -1, 1)
        b = turn(jnp.where(lane < ny - 1, parts[2][c], 0.0), 1, 1)
        d = turn(jnp.where(lane < ny - 2, parts[3][c], 0.0), 2, 1)
        out.append(parts[1][c] + a + b + d)
    return out


def fold_first_x(acc, hid):
    shape = acc.shape
    r, c = rows_cols(shape)
    fold = pick((shape[1], hid), lambda q, n: (q % hid) == n, F32)
    total = jnp.zeros((24, hid), F32)
    for s in range(4):
        keep = ((r & 15) - (c // hid) == s) & (r < 64)
        sel = lambda q, n: (n < 64) & (q == 4 * s + (n >> 4))
        if s == 0:
            keep = keep | (r >= 64)
            sel = lambda q, n: ((n < 64) & (q == (n >> 4))) | ((n == 64) & (q == 16))
        total = total + exact(pick((24, shape[0]), sel, F32), exact(jnp.where(keep, acc, 0.0), fold))
    return total


def fold_first_y(acc, hid):
    shape = acc.shape
    r, c = rows_cols(shape)
    fold = pick((shape[1], hid), lambda q, n: (q % hid) == n, F32)
    keep = ((r & 7) == (c // hid)) | (r >= 128)
    sel = lambda q, n: ((n < 128) & (q == (n >> 3))) | ((n == 128) & (q == 16))
    return exact(pick((24, shape[0]), sel, F32), exact(jnp.where(keep, acc, 0.0), fold))


def back_kernel(state, cot, middle, own, from_left, from_right,
                first_x, first_y, first_bias, mid, mid_bias, out, out_bias,
                out_back, mid_back, first_x_back, first_y_back,
                h1_hi, h1_lo, h2_hi, h2_lo, gates_in,
                g_den, g_mom, g_tra, g_weights,
                rim_state, rim_cot, rim_flux, rim_middle, rim_grad, d_middle,
                acc_x, acc_y, acc_mid, acc_out, acc_out_bias):
    nx, ny = state.shape[1:]
    groups = nx // FACES
    half = groups // PAIR
    hid = mid.shape[0] // 4
    x_weights = (first_x, None, mid, mid_bias, out, out_bias)
    segs = ny // SEG
    rim_rows = nx // segs
    rim_groups = rim_rows // FACES
    rim_half = rim_groups // PAIR

    for acc in (acc_x, acc_y, acc_mid, acc_out, acc_out_bias):
        acc[...] = jnp.zeros(acc.shape, F32)

    lane = lane_index(ny)
    spot = lane & (SEG - 1)
    for v in range(8):
        for g in range(rim_groups):
            rows = pl.ds(g * FACES, FACES)
            mine = own[v, rows, :]
            value = jnp.where(
                spot < RIM,
                turn(from_left[v, rows, :], -RIM, 1),
                jnp.where(
                    spot < 2 * RIM,
                    turn(mine, -RIM, 1),
                    jnp.where(spot < 3 * RIM, turn(mine, RIM, 1), turn(from_right[v, rows, :], RIM, 1)),
                ),
            )
            if v < 4:
                rim_state[v, rows, :] = value
                if g == 0:
                    rim_state[v, pl.ds(rim_rows, FACES), :] = turn(value, -SEG, 1)
            else:
                rim_cot[v - 4, rows, :] = value

    def rim_forward(step, _):
        sets = [
            [
                stack([
                    rim_state[c, row_block(step + k * rim_half), :],
                    rim_state[c, row_block(step + k * rim_half + 1), :],
                ])
                for c in range(4)
            ]
            for k in range(PAIR)
        ]
        tiles = [side([one[c] for one in sets]) for c in range(4)]
        fluxes = x_forward(tiles, x_weights, hid)[3]
        for c in range(4):
            for k in range(PAIR):
                rim_flux[c, row_block(step + k * rim_half + 1), :] = fluxes[c][:, k * ny : (k + 1) * ny]
        return 0

    lax.fori_loop(0, rim_half, rim_forward, 0)
    for c in range(4):
        rim_flux[c, :FACES, :] = turn(rim_flux[c, rim_rows : rim_rows + FACES, :], SEG, 1)
        for g in range(rim_groups):
            rows = pl.ds(g * FACES, FACES)
            both = stack([rim_flux[c, rows, :], rim_flux[c, pl.ds((g + 1) * FACES, FACES), :]])
            rim_middle[c, rows, :] = update_cells(rim_state[c, rows, :], both)

    refs = ((first_y, first_bias, mid, mid_bias, out, out_bias), out_back, mid_back, first_y_back)
    spot_wide = lane_index(PAIR * ny) & (SEG - 1)
    rim_faces = (spot_wide == RIM - 2) | (spot_wide == RIM - 1) | (spot_wide == 3 * RIM)

    def rim_back(step, _):
        cells = [[[] for _ in range(4)] for _ in range(4)]
        cots = [[[] for _ in range(4)] for _ in range(2)]
        for k in range(PAIR):
            rows = row_block(step + k * rim_half)
            for c in range(4):
                value = rim_middle[c, rows, :]
                for s in range(4):
                    cells[s][c].append(turn(value, 1 - s, 1))
                value = rim_cot[c, rows, :]
                for s in range(2):
                    cots[s][c].append(turn(value, -s, 1))
        cells = [y_order([side(one) for one in row]) for row in cells]
        cots = [y_order([side(one) for one in row]) for row in cots]
        parts, _ = y_step(cells, cots, rim_faces, refs, hid)
        for k in range(PAIR):
            own_parts = [[one[:, k * ny : (k + 1) * ny] for one in row] for row in parts]
            gathered = y_order(y_gather(own_parts, ny))
            for c in range(4):
                rim_grad[c, row_block(step + k * rim_half), :] = gathered[c]
        return 0

    lax.fori_loop(0, rim_half, rim_back, 0)

    def main_y(step, _):
        cells = [[[] for _ in range(4)] for _ in range(4)]
        cots = [[[] for _ in range(4)] for _ in range(2)]
        for k in range(PAIR):
            group = step + k * half
            rows = row_block(group)
            seg = group // rim_groups
            rim_at = row_block(group - seg * rim_groups)
            to_low = ny - (seg * SEG + 3 * RIM)
            to_high = lax.rem(ny - 1 - (seg * SEG + RIM - 1) + ny, ny)
            for c in range(4):
                value = middle[c, rows, :]
                rim_value = rim_middle[c, rim_at, :]
                low = jnp.where(lane < 2, pltpu.roll(rim_value, to_low, 1), value)
                high = jnp.where(lane == ny - 1, pltpu.roll(rim_value, to_high, 1), value)
                cells[0][c].append(turn(high, 1, 1))
                cells[1][c].append(value)
                cells[2][c].append(turn(jnp.where(lane < 1, low, value), -1, 1))
                cells[3][c].append(turn(low, -2, 1))
                value = cot[c, rows, :]
                rim_value = rim_cot[c, rim_at, :]
                low = jnp.where(lane < 1, pltpu.roll(rim_value, to_low, 1), value)
                cots[0][c].append(value)
                cots[1][c].append(turn(low, -1, 1))
        cells = [y_order([side(one) for one in row]) for row in cells]
        cots = [y_order([side(one) for one in row]) for row in cots]
        parts, (window, h1_pair, h2_pair, d1, d2, d3, d3_full) = y_step(cells, cots, None, refs, hid)
        add_weight_grads(
            window, h1_pair, h2_pair, d1, d2, d3, d3_full, (acc_y, acc_mid, acc_out, acc_out_bias), hid
        )
        for k in range(PAIR):
            group = step + k * half
            rows = row_block(group)
            seg = group // rim_groups
            rim_at = row_block(group - seg * rim_groups)
            own_parts = [[one[:, k * ny : (k + 1) * ny] for one in row] for row in parts]
            gathered = y_order(y_gather(own_parts, ny))
            to_low = ny - (seg * SEG + RIM)
            to_high = lax.rem(ny - 1 - (seg * SEG + 3 * RIM - 1) + ny, ny)
            for c in range(4):
                rim_value = rim_grad[c, rim_at, :]
                from_rim = jnp.where(
                    lane < 2,
                    pltpu.roll(rim_value, to_low, 1),
                    jnp.where(lane == ny - 1, pltpu.roll(rim_value, to_high, 1), 0.0),
                )
                d_middle[c, rows, :] = cot[c, rows, :] + gathered[c] + from_rim
        return 0

    lax.fori_loop(0, half, main_y, 0)

    planes = [state.at[c] for c in range(4)]
    grads = [g_den.at[0], g_mom.at[0, 0], g_mom.at[0, 1], g_tra.at[0]]
    d_planes = [d_middle.at[c] for c in range(4)]

    def main_x(step, carry):
        tiles = pair_tiles(planes, step, half)
        d_tiles = pair_tiles(d_planes, step, half)
        gates = gates_in[step]
        h1_pair = (h1_hi[step], h1_lo[step])
        h2_pair = (h2_hi[step], h2_lo[step])
        h1 = h1_pair[0].astype(F32) + h1_pair[1].astype(F32)
        h2 = h2_pair[0].astype(F32) + h2_pair[1].astype(F32)
        cells = x_cells(tiles)
        left, right = edge_states(cells, gates)
        d_flux = [courant * (turn(d, -2, 0)[:FACES] - turn(d, -1, 0)[:FACES]) for d in d_tiles]
        d_left, d_right = face_flux_backward(left, right, d_flux)
        d3_full, direct = edge_backward(cells, gates, d_left, d_right)
        d3, d2, d1 = limiter_backward(d3_full, h1, h2, out_back, mid_back, hid)
        d_window = first_backward(d1, first_x_back)
        add_weight_grads(
            split(stack(tiles)), h1_pair, h2_pair, d1, d2, d3, d3_full,
            (acc_x, acc_mid, acc_out, acc_out_bias), hid,
        )
        later = []
        for c in range(4):
            total = d_window[2 * FACES * c : 2 * FACES * (c + 1)]
            for s in range(4):
                total = total + turn(stack([direct[s][c], jnp.zeros_like(direct[s][c])]), s, 0)
            now = total[:FACES] + d_tiles[c][:FACES] + carry[c]
            for k in range(PAIR):
                grads[c][row_block(step + k * half), :] = now[:, k * ny : (k + 1) * ny]
            later.append(total[FACES:])
        return tuple(later)

    start = tuple(jnp.zeros((FACES, PAIR * ny), F32) for _ in range(4))
    last = lax.fori_loop(0, half, main_x, start)
    for c in range(4):
        for k in range(PAIR):
            at = (k + 1) % PAIR * half * FACES
            grads[c][pl.ds(at, FACES), :] += last[c][:, k * ny : (k + 1) * ny]

    eye = pick((hid, hid), lambda q, n: q == n, F32)
    grad_first = fold_first_x(acc_x[...], hid) + fold_first_y(acc_y[...], hid)
    both = acc_mid[...]
    grad_mid = both[:hid, :hid] + both[:hid, hid:] + both[hid : 2 * hid, :hid]
    grad_mid_bias = both[2 * hid :, :hid] + both[2 * hid :, hid:]
    r, c = rows_cols(acc_out.shape)
    fold = pick((acc_out.shape[1], hid), lambda q, n: (q % hid) == n, F32)
    rows = pick((8, 64), lambda q, n: (n >> 3) == q, F32)
    grad_out = exact(rows, exact(jnp.where((r & 7) == (c // hid), acc_out[...], 0.0), fold))
    out_bias_rows = exact_nt(jnp.ones((8, acc_out_bias.shape[1]), F32), acc_out_bias[...])
    grad_out_bias = exact_nt(out_bias_rows, pick((hid, 64), lambda q, n: (n >> 3) == q, F32))
    r, c = rows_cols((8, hid))
    biases = jnp.where(
        r == 0,
        grad_first[16:24],
        jnp.where(r == 1, jnp.broadcast_to(grad_mid_bias[:1], (8, hid)), jnp.where(r == 2, grad_out_bias, 0.0)),
    )
    width = g_weights.shape[1]
    beside = stack([grad_first[:16], grad_out, biases])
    g_weights[...] = exact(
        exact_nt(eye, grad_mid), pick((hid, width), lambda q, n: n == q, F32)
    ) + exact(beside, pick((hid, width), lambda q, n: n == q + hid, F32))


def finish_kernel(one, other, g_w_in, g_b_in, g_w_mid, g_b_mid, g_w_out, g_b_out):
    hid = g_w_mid.shape[0]
    total = one[...] + other[...]
    g_w_mid[...] = total[:, :hid]
    beside = total[:, hid : 2 * hid]
    g_w_in[...] = beside[:16]
    g_w_out[...] = beside[16:24]
    g_b_in[...] = beside[24:25]
    g_b_mid[...] = beside[25:26]
    g_b_out[...] = beside[26:27, :8]


def whole(count, space=pltpu.VMEM):
    return [pl.BlockSpec(memory_space=space)] * count


def call(kernel, outs, operands, out_spaces=None, in_spaces=None, scratch=(), flops=0, moved=0):
    return pl.pallas_call(
        kernel,
        out_shape=outs,
        in_specs=in_spaces or whole(len(operands)),
        out_specs=out_spaces or whole(len(outs)),
        scratch_shapes=list(scratch),
        compiler_params=pltpu.CompilerParams(vmem_limit_bytes=VMEM_BYTES),
        cost_estimate=pl.CostEstimate(flops=flops, bytes_accessed=moved, transcendentals=0),
    )(*operands)


def others(values, axis, size):
    return [lax.ppermute(values, axis, [(i, i ^ k) for i in range(size)]) for k in range(1, size)]


def tree_sum(parts):
    while len(parts) > 1:
        parts = [parts[k] + parts[k + 1] for k in range(0, len(parts), 2)]
    return parts[0]


def body(sizes, density, momentum, tracer, cotangent, w_in, b_in, w_mid, b_mid, w_out, b_out):
    nx, ny = density.shape[1:]
    hid = w_in.shape[0]
    wide = FACES * hid
    groups = nx // FACES
    half = groups // PAIR
    lanes = PAIR * ny
    segs = ny // SEG
    rim_rows = nx // segs
    ring = sizes["tx"] * sizes["ty"]
    shape = jax.ShapeDtypeStruct

    operands = [
        density, momentum, tracer, cotangent, w_in.T, b_in[None], w_mid, b_mid[None], w_out, b_out[None]
    ]
    rim, state, cots, *matrices = call(
        pack_kernel,
        [
            shape((8, rim_rows, ny), F32),
            shape((4, nx, ny), F32),
            shape((4, nx, ny), F32),
            shape((wide, 6 * 64 + ONES), BF16),
            shape((wide, 6 * 128), BF16),
            shape((wide, lanes), F32),
            shape((4 * hid, 8 * hid), BF16),
            shape((2 * hid, lanes), F32),
            shape((192, wide), BF16),
            shape((64, lanes), F32),
            shape((wide, 192), BF16),
            shape((2 * hid, 6 * hid), BF16),
            shape((128, 2 * wide), BF16),
            shape((256, 2 * wide), BF16),
        ],
        operands,
        in_spaces=whole(10, pltpu.HBM),
        scratch=[pltpu.VMEM(one.shape, F32) for one in operands[4:]] + [pltpu.SemaphoreType.DMA((10,))],
    )
    axes = ("tx", "ty")
    from_left = lax.ppermute(rim, axes, [(i, (i + 1) % ring) for i in range(ring)])
    from_right = lax.ppermute(rim, axes, [((i + 1) % ring, i) for i in range(ring)])

    middle, *kept = call(
        x_forward_kernel,
        [shape((4, nx, ny), F32)]
        + [shape((half, wide, lanes), BF16)] * 4
        + [shape((half, 64, lanes), F32)],
        [state, matrices[0]] + matrices[3:7],
        scratch=[pltpu.VMEM((4, nx + FACES, ny), F32)],
        flops=10**10,
        moved=10**7,
    )
    g_den, g_mom, g_tra, g_weights = call(
        back_kernel,
        [
            shape(density.shape, F32),
            shape(momentum.shape, F32),
            shape(tracer.shape, F32),
            shape((hid, 128), F32),
        ],
        [state, cots, middle, rim, from_left, from_right] + matrices + kept,
        scratch=[
            pltpu.VMEM((4, rim_rows + FACES, ny), F32),
            pltpu.VMEM((4, rim_rows, ny), F32),
            pltpu.VMEM((4, rim_rows + FACES, ny), F32),
            pltpu.VMEM((4, rim_rows, ny), F32),
            pltpu.VMEM((4, rim_rows, ny), F32),
            pltpu.VMEM((4, nx, ny), F32),
            pltpu.VMEM((64 + ONES, wide), F32),
            pltpu.VMEM((128 + ONES, wide), F32),
            pltpu.VMEM((2 * hid + ONES, 2 * hid), F32),
            pltpu.VMEM((64, wide), F32),
            pltpu.VMEM((64, lanes), F32),
        ],
        flops=4 * 10**10,
        moved=2 * 10**7,
    )
    totals = tree_sum([g_weights] + others(g_weights, "traj", sizes["traj"]))
    totals = tree_sum([totals] + others(totals, "ty", sizes["ty"]))
    parts = [totals] + others(totals, "tx", sizes["tx"])
    g_w_in, g_b_in, g_w_mid, g_b_mid, g_w_out, g_b_out = call(
        finish_kernel,
        [
            shape((w_in.shape[1], hid), F32),
            shape((1, hid), F32),
            shape(w_mid.shape, F32),
            shape((1, hid), F32),
            shape(w_out.shape, F32),
            shape((1, b_out.shape[0]), F32),
        ],
        [tree_sum(parts[: len(parts) // 2]), tree_sum(parts[len(parts) // 2 :])],
    )
    return (g_den, g_mom, g_tra, g_w_in.T, g_b_in[0], g_w_mid, g_b_mid[0], g_w_out, g_b_out[0])


def solution(mesh):
    flow = P("traj", None, ("tx", "ty"))
    deep = P("traj", None, None, ("tx", "ty"))
    return jax.shard_map(
        functools.partial(body, dict(mesh.shape)),
        mesh=mesh,
        in_specs=(flow, deep, flow, deep) + (P(),) * 6,
        out_specs=(flow, deep, flow) + (P(),) * 6,
        check_vma=False,
    )
```

```python
import functools

import jax
import jax.numpy as jnp
from jax import lax
from jax.experimental import pallas as pl
from jax.experimental.pallas import tpu as pltpu
from jax.sharding import PartitionSpec as P

courant = 0.1
slope_gain = 0.25
F32 = jnp.float32
BF16 = jnp.bfloat16
FACES = 8
SEG = 16
RIM = 4
PAIR = 8
RIM_PAIR = 4
ONES = 16
VMEM_BYTES = 32 * 2**20


def dot(a, b):
    return lax.dot_general(a, b, (((1,), (0,)), ((), ())), preferred_element_type=F32)


def dot_nt(a, b):
    return lax.dot_general(a, b, (((1,), (1,)), ((), ())), preferred_element_type=F32)


def exact(a, b):
    return lax.dot_general(
        a, b, (((1,), (0,)), ((), ())), precision=lax.Precision.HIGHEST, preferred_element_type=F32
    )


def exact_nt(a, b):
    return lax.dot_general(
        a, b, (((1,), (1,)), ((), ())), precision=lax.Precision.HIGHEST, preferred_element_type=F32
    )


def split(values):
    high = values.astype(BF16)
    return high, (values - high.astype(F32)).astype(BF16)


def split3(values):
    high = values.astype(BF16)
    rest = values - high.astype(F32)
    middle = rest.astype(BF16)
    return high, middle, (rest - middle.astype(F32)).astype(BF16)


def rows_cols(shape):
    return lax.broadcasted_iota(jnp.int32, shape, 0), lax.broadcasted_iota(jnp.int32, shape, 1)


def pick(shape, test, dtype=BF16):
    r, c = rows_cols(shape)
    return jnp.where(test(r, c), 1.0, 0.0).astype(dtype)


def stack(parts):
    return jnp.concatenate(parts, 0)


def side(parts):
    return jnp.concatenate(parts, 1)


def place(left, levels, rights):
    total = None
    for values, right in zip(levels, rights):
        values = values if left is None else left(values).astype(BF16)
        part = dot(values, right)
        total = part if total is None else total + part
    return total


STACKED = (0, 0, 0, 1, 1, 2)


def stacked(parts):
    return [parts[0], parts[1], parts[2], parts[0], parts[1], parts[0]]


def level_of(block):
    return jnp.where(block < 3, 0, jnp.where(block < 5, 1, 2))


def build_first_x(w, b, hid):
    wide, cols = FACES * hid, 6 * 64 + ONES
    shape = (wide, cols)
    r, c = rows_cols(shape)
    total = jnp.zeros(shape, F32)
    for s in range(4):
        rights = [
            pick((16, cols), lambda q, n: (n < 384) & (level_of(n >> 6) == lev) & (q == 4 * s + ((n >> 4) & 3)))
            for lev in range(3)
        ]
        part = place(None, w, rights)
        total = total + jnp.where((c & 15) - (r // hid) == s, stack([part] * FACES), 0.0)
    levels = split3(b)
    at, _ = rows_cols((cols, hid))
    rows = jnp.zeros((cols, hid), F32)
    for lev in range(3):
        rows = jnp.where(at == 384 + lev, jnp.broadcast_to(levels[lev].astype(F32), (cols, hid)), rows)
    bias = dot_nt(pick((wide, hid), lambda q, n: (q % hid) == n), rows.astype(BF16))
    return (jnp.where(c < 384, total, 0.0) + bias).astype(BF16)


def build_first_y(w, hid):
    wide, cols = FACES * hid, 6 * 128
    shape = (wide, cols)
    r, c = rows_cols(shape)
    rights = [
        pick((16, cols), lambda q, n: (level_of(n >> 7) == lev) & (q == ((n & 127) >> 3))) for lev in range(3)
    ]
    part = place(None, w, rights)
    return jnp.where((c & 7) == (r // hid), stack([part] * FACES), 0.0).astype(BF16)


def build_mid(w, hid):
    block = 2 * hid
    shape = (2 * block, 4 * block)
    r, c = rows_cols(shape)

    def rights(levels):
        def test(lev):
            def inner(q, n):
                at = jnp.full(n.shape, -1, jnp.int32)
                for k, level in enumerate(levels):
                    at = jnp.where(n // block == k, level, at)
                return (at == lev) & ((n % hid) == q)

            return inner

        return [pick((hid, 4 * block), test(lev)) for lev in range(3)]

    upper = place(None, w, rights((0, 0, 0, 2)))
    lower = place(None, w, rights((1, 1, -1, -1)))
    keep = ((r % block) // hid) == ((c % block) // hid)
    return jnp.where(keep, stack([upper, upper, lower, lower]), 0.0).astype(BF16)


def build_mid_back(w, hid):
    block = 2 * hid
    shape = (block, 3 * block)
    r, c = rows_cols(shape)
    eye = pick((hid, hid), lambda q, n: q == n)
    rights = [
        pick((hid, 3 * block), lambda q, n: ((n // block == 1) == (lev == 1)) & ((n % hid) == q))
        for lev in range(2)
    ]
    part = place(lambda v: dot_nt(eye, v), w[:2], rights)
    return jnp.where((r // hid) == ((c % block) // hid), stack([part] * 2), 0.0).astype(BF16)


def build_out(w, hid):
    wide = FACES * hid
    shape = (64, wide)
    r, c = rows_cols(shape)
    right = pick((hid, wide), lambda q, n: (n % hid) == q)
    left = pick((64, 8), lambda q, n: (q >> 3) == n)
    keep = (r & 7) == (c // hid)
    return stack([jnp.where(keep, dot(dot(left, v).astype(BF16), right), 0.0) for v in w]).astype(BF16)


def spread_bias(b, rows, lanes, unit):
    n = b.shape[1]
    return exact_nt(pick((rows, n), lambda q, m: unit(q) == m, F32), jnp.broadcast_to(b, (lanes, n)))


def build_out_back(w, hid):
    wide = FACES * hid
    shape = (wide, 192)
    r, c = rows_cols(shape)
    left = pick((wide, hid), lambda q, n: (q % hid) == n)

    rights = [
        pick((8, 192), lambda q, n: (((n >> 6) == 1) == (lev == 1)) & (((n & 63) >> 3) == q)) for lev in range(2)
    ]
    part = place(lambda v: dot_nt(left, v), w[:2], rights)
    return jnp.where((r // hid) == (c & 7), part, 0.0).astype(BF16)


def build_first_x_back(w, hid):
    wide = FACES * hid
    shape = (128, 2 * wide)
    r, c = rows_cols(shape)
    right = pick((hid, 2 * wide), lambda q, n: (n % hid) == q)
    total = jnp.zeros(shape, F32)
    for s in range(4):
        left = pick((128, 16), lambda q, n: n == 4 * s + ((q & 63) >> 4))

        def one(values):
            return dot(dot_nt(left, values).astype(BF16), right)

        value = jnp.where(r < 64, one(w[0]), jnp.where(c < wide, one(w[1]), 0.0))
        total = total + jnp.where((r & 15) - ((c % wide) // hid) == s, value, 0.0)
    return total.astype(BF16)


def build_first_y_back(w, hid):
    wide = FACES * hid
    shape = (256, 2 * wide)
    r, c = rows_cols(shape)
    right = pick((hid, 2 * wide), lambda q, n: (n % hid) == q)
    left = pick((256, 16), lambda q, n: n == ((q & 127) >> 3))

    def one(values):
        return dot(dot_nt(left, values).astype(BF16), right)

    value = jnp.where(r < 128, one(w[0]), jnp.where(c < wide, one(w[1]), 0.0))
    return jnp.where((r & 7) == ((c % wide) // hid), value, 0.0).astype(BF16)


def limiter_forward(first, weights, hid):
    first_ref, first_bias_ref, mid_ref, mid_bias_ref, out_ref, out_bias_ref = weights
    width = first[0].shape[1]
    if first_bias_ref is None:
        h1 = jnp.tanh(dot(first_ref[...], stack(stacked(first) + [jnp.ones((ONES, width), BF16)])))
    else:
        h1 = jnp.tanh(dot(first_ref[...], stack(stacked(first))) + first_bias_ref[:, :width])
    h1_parts = split3(h1)
    block = 2 * hid
    parts = []
    for at in range(0, FACES * hid, block):
        high, middle, low = (p[at : at + block] for p in h1_parts)
        both = dot(mid_ref[...], stack([high, middle, low, high]))
        parts.append(jnp.tanh(both[:block] + both[block:] + mid_bias_ref[:, :width]))
    h2 = stack(parts)
    h2_parts = split3(h2)
    rows = 8 * FACES
    a = dot(out_ref[...], h2_parts[0])
    b = dot(out_ref[: 2 * rows, :], h2_parts[1])
    c = dot(out_ref[:rows, :], h2_parts[2])
    gates = jnp.tanh(
        ((a[2 * rows :] + b[rows:] + c) + (a[rows : 2 * rows] + b[:rows])) + a[:rows] + out_bias_ref[:, :width]
    )
    return h1, h1_parts[:2], h2, h2_parts[:2], gates


def limiter_backward(d3, h1, h2, out_back_ref, mid_back_ref, hid):
    d3_hi, d3_lo = split(d3)
    d2 = dot(out_back_ref[...], stack([d3_hi, d3_hi, d3_lo])) * (1.0 - h2 * h2)
    d2_hi, d2_lo = split(d2)
    block = 2 * hid
    parts = []
    for at in range(0, FACES * hid, block):
        hi, lo = d2_hi[at : at + block], d2_lo[at : at + block]
        parts.append(dot(mid_back_ref[...], stack([hi, hi, lo])))
    d1 = stack(parts) * (1.0 - h1 * h1)
    return (d3_hi, d3_lo), (d2_hi, d2_lo), split(d1)


def first_backward(d1, back_ref):
    both = dot(back_ref[...], stack([d1[0], d1[1]]))
    half = both.shape[0] // 2
    return both[:half] + both[half:]


def add_weight_grads(first, h1, h2, d1, d2, d3, d3_full, acc, hid):
    acc_in, acc_mid, acc_out, acc_out_bias = acc
    width = d3_full.shape[1]
    ones = jnp.ones((ONES, width), BF16)
    rows = first[0].shape[0]
    high = dot_nt(stack([first[0], ones, first[1]]), d1[0])
    low = dot_nt(stack([first[0], ones]), d1[1])
    acc_in[...] += high[: rows + ONES] + low
    acc_in[:rows, :] += high[rows + ONES :]
    lefts, rights = [], []
    for at in range(0, FACES * hid, hid):
        lefts.append(stack([h1[0][at : at + hid], h1[1][at : at + hid], ones]))
        rights.append(stack([d2[0][at : at + hid], d2[1][at : at + hid]]))
    acc_mid[...] += dot_nt(side(lefts), side(rights))
    rows = d3[0].shape[0]
    high = dot_nt(stack([d3[0], d3[1]]), h2[0])
    acc_out[...] += high[:rows] + high[rows:] + dot_nt(d3[0], h2[1])
    acc_out_bias[...] += d3_full


def edge_states(cells, gates):
    left, right = [], []
    for c in range(4):
        low = gates[FACES * c : FACES * (c + 1)]
        high = gates[FACES * (c + 4) : FACES * (c + 5)]
        left.append(cells[1][c] + slope_gain * low * (cells[2][c] - cells[0][c]))
        right.append(cells[2][c] - slope_gain * high * (cells[3][c] - cells[1][c]))
    return left, right


def face_flux(left, right):
    ul = left[1] / left[0]
    ur = right[1] / right[0]
    half_speed = 0.5 * (jnp.maximum(jnp.abs(ul), jnp.abs(ur)) + 1.0)
    fl = [left[1], left[1] * ul + left[0], left[2] * ul, left[3] * ul]
    fr = [right[1], right[1] * ur + right[0], right[2] * ur, right[3] * ur]
    return [0.5 * (fl[c] + fr[c]) - half_speed * (right[c] - left[c]) for c in range(4)]


def sign_of(values):
    return jnp.where(values > 0.0, 1.0, jnp.where(values < 0.0, -1.0, 0.0))


def face_flux_backward(left, right, d_flux):
    inv_l, inv_r = 1.0 / left[0], 1.0 / right[0]
    ul, ur = left[1] / left[0], right[1] / right[0]
    al, ar = jnp.abs(ul), jnp.abs(ur)
    half_speed = 0.5 * (jnp.maximum(al, ar) + 1.0)
    d_speed = -0.5 * sum(d_flux[c] * (right[c] - left[c]) for c in range(4))
    share = jnp.where(al > ar, 1.0, jnp.where(al < ar, 0.0, 0.5))
    half = [0.5 * d for d in d_flux]
    spread = [half_speed * d for d in d_flux]

    def one(state, u, inv, speed_part, sign):
        du = half[1] * state[1] + half[2] * state[2] + half[3] * state[3] + speed_part * sign_of(u)
        over = du * inv
        return [
            half[1] - over * u + sign * spread[0],
            half[0] + half[1] * u + over + sign * spread[1],
            half[2] * u + sign * spread[2],
            half[3] * u + sign * spread[3],
        ]

    return (
        one(left, ul, inv_l, d_speed * share, 1.0),
        one(right, ur, inv_r, d_speed * (1.0 - share), -1.0),
    )


def edge_backward(cells, gates, d_left, d_right):
    lows, highs = [], []
    direct = [[None] * 4 for _ in range(4)]
    for c in range(4):
        low = gates[FACES * c : FACES * (c + 1)]
        high = gates[FACES * (c + 4) : FACES * (c + 5)]
        lows.append(slope_gain * (cells[2][c] - cells[0][c]) * d_left[c])
        highs.append(-slope_gain * (cells[3][c] - cells[1][c]) * d_right[c])
        low_part = slope_gain * low * d_left[c]
        high_part = slope_gain * high * d_right[c]
        direct[0][c] = -low_part
        direct[1][c] = d_left[c] + high_part
        direct[2][c] = d_right[c] + low_part
        direct[3][c] = -high_part
    return stack(lows + highs) * (1.0 - gates * gates), direct


def turn(values, shift, axis):
    size = values.shape[axis]
    return values if shift % size == 0 else pltpu.roll(values, shift % size, axis)


def x_cells(tiles):
    return [[turn(t, -s, 0)[:FACES] for t in tiles] for s in range(4)]


def pack_kernel(den, mom, tra, cot, w_in, b_in, w_mid, b_mid, w_out, b_out,
                rim, state, cots, first_x, first_y, first_bias, mid, mid_bias, out, out_bias,
                out_back, mid_back, first_x_back, first_y_back, *scratch):
    *small, sems = scratch
    nx, ny = den.shape[1:]
    segs = ny // SEG
    rows = nx // segs
    hid = w_in.shape[1]
    copies = [
        pltpu.make_async_copy(source, target, sems.at[k])
        for k, (source, target) in enumerate(
            list(zip([w_in, b_in, w_mid, b_mid, w_out, b_out], small))
            + [
                (den.at[0], state.at[0]),
                (mom.at[0], state.at[pl.ds(1, 2)]),
                (tra.at[0], state.at[3]),
                (cot.at[0], cots),
            ]
        )
    ]
    for one in copies:
        one.start()
    for one in copies[:6]:
        one.wait()
    w_in, b_in, w_mid, b_mid, w_out, b_out = small
    eye = pick((hid, hid), lambda q, n: q == n)
    wi = [dot_nt(eye, level).astype(BF16) for level in split3(w_in[...])]
    wm, wo = split3(w_mid[...]), split3(w_out[...])
    lanes = out_bias.shape[1]
    first_x[...] = build_first_x(wi, b_in[...], hid)
    first_y[...] = build_first_y(wi, hid)
    first_bias[...] = spread_bias(b_in[...], FACES * hid, lanes, lambda q: q % hid)
    mid[...] = build_mid(wm, hid)
    mid_bias[...] = spread_bias(b_mid[...], 2 * hid, lanes, lambda q: q % hid)
    out[...] = build_out(wo, hid)
    out_bias[...] = spread_bias(b_out[...], 64, lanes, lambda q: q >> 3)
    out_back[...] = build_out_back(wo, hid)
    mid_back[...] = build_mid_back(wm, hid)
    first_x_back[...] = build_first_x_back(wi, hid)
    first_y_back[...] = build_first_y_back(wi, hid)

    for one in copies[6:]:
        one.wait()
    lane = lane_index(ny)
    for v in range(8):
        plane = state.at[v] if v < 4 else cots.at[v - 4]
        for at in range(0, rows, FACES):
            total = jnp.zeros((FACES, ny), F32)
            for s in range(segs):
                first = s * SEG + RIM
                moved = turn(plane[pl.ds(s * rows + at, FACES), :], first + RIM, 1)
                total = jnp.where((lane >= first) & (lane < first + 2 * RIM), moved, total)
            rim[v, pl.ds(at, FACES), :] = total


def row_block(at):
    return pl.ds(pl.multiple_of(at * FACES, FACES), FACES)


def x_tiles(planes, group, groups):
    after = jnp.where(group + 1 == groups, 0, group + 1)
    return [stack([plane[row_block(group), :], plane[row_block(after), :]]) for plane in planes]


def pair_tiles(planes, step, half):
    sets = [x_tiles(planes, step + k * half, PAIR * half) for k in range(PAIR)]
    return [side([one[c] for one in sets]) for c in range(len(planes))]


def x_forward(tiles, weights, hid):
    h1, h1_pair, h2, h2_pair, gates = limiter_forward(split3(stack(tiles)), weights, hid)
    cells = x_cells(tiles)
    return h1_pair, h2_pair, gates, face_flux(*edge_states(cells, gates))


def update_cells(plane_rows, flux_rows):
    upper = turn(flux_rows, -7, 0)[:FACES]
    lower = turn(flux_rows, -6, 0)[:FACES]
    return plane_rows - courant * (upper - lower)


def x_forward_kernel(state, first_x, mid, mid_bias, out, out_bias,
                     middle, h1_hi, h1_lo, h2_hi, h2_lo, gates_out, flux):
    nx, ny = state.shape[1:]
    groups = nx // FACES
    half = groups // PAIR
    hid = mid.shape[0] // 4
    x_weights = (first_x, None, mid, mid_bias, out, out_bias)
    planes = [state.at[c] for c in range(4)]

    def step_of(step, _):
        tiles = pair_tiles(planes, step, half)
        h1_pair, h2_pair, gates, fluxes = x_forward(tiles, x_weights, hid)
        for target, value in zip((h1_hi, h1_lo, h2_hi, h2_lo, gates_out), h1_pair + h2_pair + (gates,)):
            target[step] = value
        for c in range(4):
            for k in range(PAIR):
                flux[c, row_block(step + k * half + 1), :] = fluxes[c][:, k * ny : (k + 1) * ny]
        return 0

    lax.fori_loop(0, half, step_of, 0)
    for c in range(4):
        flux[c, :FACES, :] = flux[c, nx : nx + FACES, :]

    def update(group, _):
        for c in range(4):
            both = stack([flux[c, row_block(group), :], flux[c, row_block(group + 1), :]])
            middle[c, row_block(group), :] = update_cells(planes[c][row_block(group), :], both)
        return 0

    lax.fori_loop(0, groups, update, 0)


def y_order(planes):
    return [planes[0], planes[2], planes[1], planes[3]]


def lane_index(width):
    return lax.broadcasted_iota(jnp.int32, (FACES, width), 1)


def y_step(cells, cots, halo_mask, refs, hid):
    weights, out_back, mid_back, first_y_back = refs
    window = split3(stack([cells[s][c] for s in range(4) for c in range(4)]))
    h1, h1_pair, h2, h2_pair, gates = limiter_forward(window, weights, hid)
    left, right = edge_states(cells, gates)
    d_flux = [courant * (cots[1][c] - cots[0][c]) for c in range(4)]
    d_left, d_right = face_flux_backward(left, right, d_flux)
    if halo_mask is not None:
        d_left = [jnp.where(halo_mask, d, 0.0) for d in d_left]
        d_right = [jnp.where(halo_mask, d, 0.0) for d in d_right]
    d3_full, direct = edge_backward(cells, gates, d_left, d_right)
    d3, d2, d1 = limiter_backward(d3_full, h1, h2, out_back, mid_back, hid)
    d_window = first_backward(d1, first_y_back)
    parts = [
        [d_window[FACES * (4 * s + c) : FACES * (4 * s + c + 1)] + direct[s][c] for c in range(4)]
        for s in range(4)
    ]
    return parts, (window, h1_pair, h2_pair, d1, d2, d3, d3_full)


def y_gather(parts, ny):
    lane = lane_index(ny)
    out = []
    for c in range(4):
        a = turn(jnp.where(lane >= 1, parts[0][c], 0.0), -1, 1)
        b = turn(jnp.where(lane < ny - 1, parts[2][c], 0.0), 1, 1)
        d = turn(jnp.where(lane < ny - 2, parts[3][c], 0.0), 2, 1)
        out.append(parts[1][c] + a + b + d)
    return out


def fold_first_x(acc, hid):
    shape = acc.shape
    r, c = rows_cols(shape)
    fold = pick((shape[1], hid), lambda q, n: (q % hid) == n, F32)
    total = jnp.zeros((24, hid), F32)
    for s in range(4):
        keep = ((r & 15) - (c // hid) == s) & (r < 64)
        sel = lambda q, n: (n < 64) & (q == 4 * s + (n >> 4))
        if s == 0:
            keep = keep | (r >= 64)
            sel = lambda q, n: ((n < 64) & (q == (n >> 4))) | ((n == 64) & (q == 16))
        total = total + exact(pick((24, shape[0]), sel, F32), exact(jnp.where(keep, acc, 0.0), fold))
    return total


def fold_first_y(acc, hid):
    shape = acc.shape
    r, c = rows_cols(shape)
    fold = pick((shape[1], hid), lambda q, n: (q % hid) == n, F32)
    keep = ((r & 7) == (c // hid)) | (r >= 128)
    sel = lambda q, n: ((n < 128) & (q == (n >> 3))) | ((n == 128) & (q == 16))
    return exact(pick((24, shape[0]), sel, F32), exact(jnp.where(keep, acc, 0.0), fold))


def back_kernel(state, cot, middle, own, from_left, from_right,
                first_x, first_y, first_bias, mid, mid_bias, out, out_bias,
                out_back, mid_back, first_x_back, first_y_back,
                h1_hi, h1_lo, h2_hi, h2_lo, gates_in,
                g_den, g_mom, g_tra, g_weights,
                rim_state, rim_cot, rim_flux, rim_middle, rim_grad, d_middle,
                acc_x, acc_y, acc_mid, acc_out, acc_out_bias):
    nx, ny = state.shape[1:]
    groups = nx // FACES
    half = groups // PAIR
    hid = mid.shape[0] // 4
    x_weights = (first_x, None, mid, mid_bias, out, out_bias)
    segs = ny // SEG
    rim_rows = nx // segs
    rim_groups = rim_rows // FACES
    rim_half = rim_groups // RIM_PAIR

    for acc in (acc_x, acc_y, acc_mid, acc_out, acc_out_bias):
        acc[...] = jnp.zeros(acc.shape, F32)

    lane = lane_index(ny)
    spot = lane & (SEG - 1)
    for v in range(8):
        for g in range(rim_groups):
            rows = pl.ds(g * FACES, FACES)
            mine = own[v, rows, :]
            value = jnp.where(
                spot < RIM,
                turn(from_left[v, rows, :], -RIM, 1),
                jnp.where(
                    spot < 2 * RIM,
                    turn(mine, -RIM, 1),
                    jnp.where(spot < 3 * RIM, turn(mine, RIM, 1), turn(from_right[v, rows, :], RIM, 1)),
                ),
            )
            if v < 4:
                rim_state[v, rows, :] = value
                if g == 0:
                    rim_state[v, pl.ds(rim_rows, FACES), :] = turn(value, -SEG, 1)
            else:
                rim_cot[v - 4, rows, :] = value

    def rim_forward(step, _):
        sets = [
            [
                stack([
                    rim_state[c, row_block(step + k * rim_half), :],
                    rim_state[c, row_block(step + k * rim_half + 1), :],
                ])
                for c in range(4)
            ]
            for k in range(RIM_PAIR)
        ]
        tiles = [side([one[c] for one in sets]) for c in range(4)]
        fluxes = x_forward(tiles, x_weights, hid)[3]
        for c in range(4):
            for k in range(RIM_PAIR):
                rim_flux[c, row_block(step + k * rim_half + 1), :] = fluxes[c][:, k * ny : (k + 1) * ny]
        return 0

    lax.fori_loop(0, rim_half, rim_forward, 0)
    for c in range(4):
        rim_flux[c, :FACES, :] = turn(rim_flux[c, rim_rows : rim_rows + FACES, :], SEG, 1)
        for g in range(rim_groups):
            rows = pl.ds(g * FACES, FACES)
            both = stack([rim_flux[c, rows, :], rim_flux[c, pl.ds((g + 1) * FACES, FACES), :]])
            rim_middle[c, rows, :] = update_cells(rim_state[c, rows, :], both)

    refs = ((first_y, first_bias, mid, mid_bias, out, out_bias), out_back, mid_back, first_y_back)
    spot_wide = lane_index(RIM_PAIR * ny) & (SEG - 1)
    rim_faces = (spot_wide == RIM - 2) | (spot_wide == RIM - 1) | (spot_wide == 3 * RIM)

    def rim_back(step, _):
        cells = [[[] for _ in range(4)] for _ in range(4)]
        cots = [[[] for _ in range(4)] for _ in range(2)]
        for k in range(RIM_PAIR):
            rows = row_block(step + k * rim_half)
            for c in range(4):
                value = rim_middle[c, rows, :]
                for s in range(4):
                    cells[s][c].append(turn(value, 1 - s, 1))
                value = rim_cot[c, rows, :]
                for s in range(2):
                    cots[s][c].append(turn(value, -s, 1))
        cells = [y_order([side(one) for one in row]) for row in cells]
        cots = [y_order([side(one) for one in row]) for row in cots]
        parts, _ = y_step(cells, cots, rim_faces, refs, hid)
        for k in range(RIM_PAIR):
            own_parts = [[one[:, k * ny : (k + 1) * ny] for one in row] for row in parts]
            gathered = y_order(y_gather(own_parts, ny))
            for c in range(4):
                rim_grad[c, row_block(step + k * rim_half), :] = gathered[c]
        return 0

    lax.fori_loop(0, rim_half, rim_back, 0)

    def main_y(step, _):
        cells = [[[] for _ in range(4)] for _ in range(4)]
        cots = [[[] for _ in range(4)] for _ in range(2)]
        for k in range(PAIR):
            group = step + k * half
            rows = row_block(group)
            seg = group // rim_groups
            rim_at = row_block(group - seg * rim_groups)
            to_low = ny - (seg * SEG + 3 * RIM)
            to_high = lax.rem(ny - 1 - (seg * SEG + RIM - 1) + ny, ny)
            for c in range(4):
                value = middle[c, rows, :]
                rim_value = rim_middle[c, rim_at, :]
                low = jnp.where(lane < 2, pltpu.roll(rim_value, to_low, 1), value)
                high = jnp.where(lane == ny - 1, pltpu.roll(rim_value, to_high, 1), value)
                cells[0][c].append(turn(high, 1, 1))
                cells[1][c].append(value)
                cells[2][c].append(turn(jnp.where(lane < 1, low, value), -1, 1))
                cells[3][c].append(turn(low, -2, 1))
                value = cot[c, rows, :]
                rim_value = rim_cot[c, rim_at, :]
                low = jnp.where(lane < 1, pltpu.roll(rim_value, to_low, 1), value)
                cots[0][c].append(value)
                cots[1][c].append(turn(low, -1, 1))
        cells = [y_order([side(one) for one in row]) for row in cells]
        cots = [y_order([side(one) for one in row]) for row in cots]
        parts, (window, h1_pair, h2_pair, d1, d2, d3, d3_full) = y_step(cells, cots, None, refs, hid)
        add_weight_grads(
            window, h1_pair, h2_pair, d1, d2, d3, d3_full, (acc_y, acc_mid, acc_out, acc_out_bias), hid
        )
        for k in range(PAIR):
            group = step + k * half
            rows = row_block(group)
            seg = group // rim_groups
            rim_at = row_block(group - seg * rim_groups)
            own_parts = [[one[:, k * ny : (k + 1) * ny] for one in row] for row in parts]
            gathered = y_order(y_gather(own_parts, ny))
            to_low = ny - (seg * SEG + RIM)
            to_high = lax.rem(ny - 1 - (seg * SEG + 3 * RIM - 1) + ny, ny)
            for c in range(4):
                rim_value = rim_grad[c, rim_at, :]
                from_rim = jnp.where(
                    lane < 2,
                    pltpu.roll(rim_value, to_low, 1),
                    jnp.where(lane == ny - 1, pltpu.roll(rim_value, to_high, 1), 0.0),
                )
                d_middle[c, rows, :] = cot[c, rows, :] + gathered[c] + from_rim
        return 0

    lax.fori_loop(0, half, main_y, 0)

    planes = [state.at[c] for c in range(4)]
    grads = [g_den.at[0], g_mom.at[0, 0], g_mom.at[0, 1], g_tra.at[0]]
    d_planes = [d_middle.at[c] for c in range(4)]

    def main_x(step, carry):
        tiles = pair_tiles(planes, step, half)
        d_tiles = pair_tiles(d_planes, step, half)
        gates = gates_in[step]
        h1_pair = (h1_hi[step], h1_lo[step])
        h2_pair = (h2_hi[step], h2_lo[step])
        h1 = h1_pair[0].astype(F32) + h1_pair[1].astype(F32)
        h2 = h2_pair[0].astype(F32) + h2_pair[1].astype(F32)
        cells = x_cells(tiles)
        left, right = edge_states(cells, gates)
        d_flux = [courant * (turn(d, -2, 0)[:FACES] - turn(d, -1, 0)[:FACES]) for d in d_tiles]
        d_left, d_right = face_flux_backward(left, right, d_flux)
        d3_full, direct = edge_backward(cells, gates, d_left, d_right)
        d3, d2, d1 = limiter_backward(d3_full, h1, h2, out_back, mid_back, hid)
        d_window = first_backward(d1, first_x_back)
        add_weight_grads(
            split(stack(tiles)), h1_pair, h2_pair, d1, d2, d3, d3_full,
            (acc_x, acc_mid, acc_out, acc_out_bias), hid,
        )
        later = []
        for c in range(4):
            total = d_window[2 * FACES * c : 2 * FACES * (c + 1)]
            for s in range(4):
                total = total + turn(stack([direct[s][c], jnp.zeros_like(direct[s][c])]), s, 0)
            now = total[:FACES] + d_tiles[c][:FACES] + carry[c]
            for k in range(PAIR):
                grads[c][row_block(step + k * half), :] = now[:, k * ny : (k + 1) * ny]
            later.append(total[FACES:])
        return tuple(later)

    start = tuple(jnp.zeros((FACES, PAIR * ny), F32) for _ in range(4))
    last = lax.fori_loop(0, half, main_x, start)
    for c in range(4):
        for k in range(PAIR):
            at = (k + 1) % PAIR * half * FACES
            grads[c][pl.ds(at, FACES), :] += last[c][:, k * ny : (k + 1) * ny]

    eye = pick((hid, hid), lambda q, n: q == n, F32)
    grad_first = fold_first_x(acc_x[...], hid) + fold_first_y(acc_y[...], hid)
    both = acc_mid[...]
    grad_mid = both[:hid, :hid] + both[:hid, hid:] + both[hid : 2 * hid, :hid]
    grad_mid_bias = both[2 * hid :, :hid] + both[2 * hid :, hid:]
    r, c = rows_cols(acc_out.shape)
    fold = pick((acc_out.shape[1], hid), lambda q, n: (q % hid) == n, F32)
    rows = pick((8, 64), lambda q, n: (n >> 3) == q, F32)
    grad_out = exact(rows, exact(jnp.where((r & 7) == (c // hid), acc_out[...], 0.0), fold))
    out_bias_rows = exact_nt(jnp.ones((8, acc_out_bias.shape[1]), F32), acc_out_bias[...])
    grad_out_bias = exact_nt(out_bias_rows, pick((hid, 64), lambda q, n: (n >> 3) == q, F32))
    r, c = rows_cols((8, hid))
    biases = jnp.where(
        r == 0,
        grad_first[16:24],
        jnp.where(r == 1, jnp.broadcast_to(grad_mid_bias[:1], (8, hid)), jnp.where(r == 2, grad_out_bias, 0.0)),
    )
    width = g_weights.shape[1]
    beside = stack([grad_first[:16], grad_out, biases])
    g_weights[...] = exact(
        exact_nt(eye, grad_mid), pick((hid, width), lambda q, n: n == q, F32)
    ) + exact(beside, pick((hid, width), lambda q, n: n == q + hid, F32))


def finish_kernel(one, other, g_w_in, g_b_in, g_w_mid, g_b_mid, g_w_out, g_b_out):
    hid = g_w_mid.shape[0]
    total = one[...] + other[...]
    g_w_mid[...] = total[:, :hid]
    beside = total[:, hid : 2 * hid]
    g_w_in[...] = beside[:16]
    g_w_out[...] = beside[16:24]
    g_b_in[...] = beside[24:25]
    g_b_mid[...] = beside[25:26]
    g_b_out[...] = beside[26:27, :8]


def whole(count, space=pltpu.VMEM):
    return [pl.BlockSpec(memory_space=space)] * count


def call(kernel, outs, operands, out_spaces=None, in_spaces=None, scratch=(), flops=0, moved=0):
    return pl.pallas_call(
        kernel,
        out_shape=outs,
        in_specs=in_spaces or whole(len(operands)),
        out_specs=out_spaces or whole(len(outs)),
        scratch_shapes=list(scratch),
        compiler_params=pltpu.CompilerParams(vmem_limit_bytes=VMEM_BYTES),
        cost_estimate=pl.CostEstimate(flops=flops, bytes_accessed=moved, transcendentals=0),
    )(*operands)


def others(values, axis, size):
    return [lax.ppermute(values, axis, [(i, i ^ k) for i in range(size)]) for k in range(1, size)]


def tree_sum(parts):
    while len(parts) > 1:
        parts = [parts[k] + parts[k + 1] for k in range(0, len(parts), 2)]
    return parts[0]


def body(sizes, density, momentum, tracer, cotangent, w_in, b_in, w_mid, b_mid, w_out, b_out):
    nx, ny = density.shape[1:]
    hid = w_in.shape[0]
    wide = FACES * hid
    groups = nx // FACES
    half = groups // PAIR
    lanes = PAIR * ny
    segs = ny // SEG
    rim_rows = nx // segs
    ring = sizes["tx"] * sizes["ty"]
    shape = jax.ShapeDtypeStruct

    operands = [
        density, momentum, tracer, cotangent, w_in.T, b_in[None], w_mid, b_mid[None], w_out, b_out[None]
    ]
    rim, state, cots, *matrices = call(
        pack_kernel,
        [
            shape((8, rim_rows, ny), F32),
            shape((4, nx, ny), F32),
            shape((4, nx, ny), F32),
            shape((wide, 6 * 64 + ONES), BF16),
            shape((wide, 6 * 128), BF16),
            shape((wide, lanes), F32),
            shape((4 * hid, 8 * hid), BF16),
            shape((2 * hid, lanes), F32),
            shape((192, wide), BF16),
            shape((64, lanes), F32),
            shape((wide, 192), BF16),
            shape((2 * hid, 6 * hid), BF16),
            shape((128, 2 * wide), BF16),
            shape((256, 2 * wide), BF16),
        ],
        [pltpu.with_memory_space_constraint(one, pltpu.HBM) for one in operands],
        in_spaces=whole(10, pltpu.HBM),
        scratch=[pltpu.VMEM(one.shape, F32) for one in operands[4:]] + [pltpu.SemaphoreType.DMA((10,))],
    )
    axes = ("tx", "ty")
    from_left = lax.ppermute(rim, axes, [(i, (i + 1) % ring) for i in range(ring)])
    from_right = lax.ppermute(rim, axes, [((i + 1) % ring, i) for i in range(ring)])

    middle, *kept = call(
        x_forward_kernel,
        [shape((4, nx, ny), F32)]
        + [shape((half, wide, lanes), BF16)] * 4
        + [shape((half, 64, lanes), F32)],
        [state, matrices[0]] + matrices[3:7],
        scratch=[pltpu.VMEM((4, nx + FACES, ny), F32)],
        flops=10**10,
        moved=10**7,
    )
    g_den, g_mom, g_tra, g_weights = call(
        back_kernel,
        [
            shape(density.shape, F32),
            shape(momentum.shape, F32),
            shape(tracer.shape, F32),
            shape((hid, 128), F32),
        ],
        [state, cots, middle, rim, from_left, from_right] + matrices + kept,
        scratch=[
            pltpu.VMEM((4, rim_rows + FACES, ny), F32),
            pltpu.VMEM((4, rim_rows, ny), F32),
            pltpu.VMEM((4, rim_rows + FACES, ny), F32),
            pltpu.VMEM((4, rim_rows, ny), F32),
            pltpu.VMEM((4, rim_rows, ny), F32),
            pltpu.VMEM((4, nx, ny), F32),
            pltpu.VMEM((64 + ONES, wide), F32),
            pltpu.VMEM((128 + ONES, wide), F32),
            pltpu.VMEM((2 * hid + ONES, 2 * hid), F32),
            pltpu.VMEM((64, wide), F32),
            pltpu.VMEM((64, lanes), F32),
        ],
        flops=4 * 10**10,
        moved=2 * 10**7,
    )
    totals = tree_sum([g_weights] + others(g_weights, "traj", sizes["traj"]))
    totals = tree_sum([totals] + others(totals, "ty", sizes["ty"]))
    parts = [totals] + others(totals, "tx", sizes["tx"])
    g_w_in, g_b_in, g_w_mid, g_b_mid, g_w_out, g_b_out = call(
        finish_kernel,
        [
            shape((w_in.shape[1], hid), F32),
            shape((1, hid), F32),
            shape(w_mid.shape, F32),
            shape((1, hid), F32),
            shape(w_out.shape, F32),
            shape((1, b_out.shape[0]), F32),
        ],
        [tree_sum(parts[: len(parts) // 2]), tree_sum(parts[len(parts) // 2 :])],
    )
    return (g_den, g_mom, g_tra, g_w_in.T, g_b_in[0], g_w_mid, g_b_mid[0], g_w_out, g_b_out[0])


def solution(mesh):
    flow = P("traj", None, ("tx", "ty"))
    deep = P("traj", None, None, ("tx", "ty"))
    return jax.shard_map(
        functools.partial(body, dict(mesh.shape)),
        mesh=mesh,
        in_specs=(flow, deep, flow, deep) + (P(),) * 6,
        out_specs=(flow, deep, flow) + (P(),) * 6,
        check_vma=False,
    )
```

```python
import functools

import jax
import jax.numpy as jnp
from jax import lax
from jax.experimental import pallas as pl
from jax.experimental.pallas import tpu as pltpu
from jax.sharding import PartitionSpec as P

courant = 0.1
slope_gain = 0.25
F32 = jnp.float32
BF16 = jnp.bfloat16
FACES = 8
SEG = 16
RIM = 4
PAIR = 8
RIM_PAIR = 4
ONES = 16
VMEM_BYTES = 32 * 2**20


def dot(a, b):
    return lax.dot_general(a, b, (((1,), (0,)), ((), ())), preferred_element_type=F32)


def dot_nt(a, b):
    return lax.dot_general(a, b, (((1,), (1,)), ((), ())), preferred_element_type=F32)


def exact(a, b):
    return lax.dot_general(
        a, b, (((1,), (0,)), ((), ())), precision=lax.Precision.HIGHEST, preferred_element_type=F32
    )


def exact_nt(a, b):
    return lax.dot_general(
        a, b, (((1,), (1,)), ((), ())), precision=lax.Precision.HIGHEST, preferred_element_type=F32
    )


def split(values):
    high = values.astype(BF16)
    return high, (values - high.astype(F32)).astype(BF16)


def split3(values):
    high = values.astype(BF16)
    rest = values - high.astype(F32)
    middle = rest.astype(BF16)
    return high, middle, (rest - middle.astype(F32)).astype(BF16)


def rows_cols(shape):
    return lax.broadcasted_iota(jnp.int32, shape, 0), lax.broadcasted_iota(jnp.int32, shape, 1)


def quot(values, n):
    return values >> (n.bit_length() - 1) if n & (n - 1) == 0 else values // n


def rest(values, n):
    return values & (n - 1) if n & (n - 1) == 0 else values % n


def pick(shape, test, dtype=BF16):
    r, c = rows_cols(shape)
    return jnp.where(test(r, c), 1.0, 0.0).astype(dtype)


def stack(parts):
    return jnp.concatenate(parts, 0)


def side(parts):
    return jnp.concatenate(parts, 1)


def place(left, levels, rights):
    total = None
    for values, right in zip(levels, rights):
        values = values if left is None else left(values).astype(BF16)
        part = dot(values, right)
        total = part if total is None else total + part
    return total


STACKED = (0, 0, 0, 1, 1, 2)


def stacked(parts):
    return [parts[0], parts[1], parts[2], parts[0], parts[1], parts[0]]


def level_of(block):
    return jnp.where(block < 3, 0, jnp.where(block < 5, 1, 2))


def build_first_x(w, b, hid):
    wide, cols = FACES * hid, 6 * 64 + ONES
    shape = (wide, cols)
    r, c = rows_cols(shape)
    total = jnp.zeros(shape, F32)
    for s in range(4):
        rights = [
            pick((16, cols), lambda q, n: (n < 384) & (level_of(n >> 6) == lev) & (q == 4 * s + ((n >> 4) & 3)))
            for lev in range(3)
        ]
        part = place(None, w, rights)
        total = total + jnp.where((c & 15) - (quot(r, hid)) == s, stack([part] * FACES), 0.0)
    levels = split3(b)
    at, _ = rows_cols((cols, hid))
    rows = jnp.zeros((cols, hid), F32)
    for lev in range(3):
        rows = jnp.where(at == 384 + lev, jnp.broadcast_to(levels[lev].astype(F32), (cols, hid)), rows)
    bias = dot_nt(pick((wide, hid), lambda q, n: (rest(q, hid)) == n), rows.astype(BF16))
    return (jnp.where(c < 384, total, 0.0) + bias).astype(BF16)


def build_first_y(w, hid):
    wide, cols = FACES * hid, 6 * 128
    shape = (wide, cols)
    r, c = rows_cols(shape)
    rights = [
        pick((16, cols), lambda q, n: (level_of(n >> 7) == lev) & (q == ((n & 127) >> 3))) for lev in range(3)
    ]
    part = place(None, w, rights)
    return jnp.where((c & 7) == (quot(r, hid)), stack([part] * FACES), 0.0).astype(BF16)


def build_mid(w, hid):
    block = 2 * hid
    shape = (2 * block, 4 * block)
    r, c = rows_cols(shape)

    def rights(levels):
        def test(lev):
            def inner(q, n):
                at = jnp.full(n.shape, -1, jnp.int32)
                for k, level in enumerate(levels):
                    at = jnp.where(quot(n, block) == k, level, at)
                return (at == lev) & ((rest(n, hid)) == q)

            return inner

        return [pick((hid, 4 * block), test(lev)) for lev in range(3)]

    upper = place(None, w, rights((0, 0, 0, 2)))
    lower = place(None, w, rights((1, 1, -1, -1)))
    keep = (quot(rest(r, block), hid)) == (quot(rest(c, block), hid))
    return jnp.where(keep, stack([upper, upper, lower, lower]), 0.0).astype(BF16)


def build_mid_back(w, hid):
    block = 2 * hid
    shape = (block, 3 * block)
    r, c = rows_cols(shape)
    eye = pick((hid, hid), lambda q, n: q == n)
    rights = [
        pick((hid, 3 * block), lambda q, n: ((quot(n, block) == 1) == (lev == 1)) & ((rest(n, hid)) == q))
        for lev in range(2)
    ]
    part = place(lambda v: dot_nt(eye, v), w[:2], rights)
    return jnp.where((quot(r, hid)) == (quot(rest(c, block), hid)), stack([part] * 2), 0.0).astype(BF16)


def build_out(w, hid):
    wide = FACES * hid
    shape = (64, wide)
    r, c = rows_cols(shape)
    right = pick((hid, wide), lambda q, n: (rest(n, hid)) == q)
    left = pick((64, 8), lambda q, n: (q >> 3) == n)
    keep = (r & 7) == (quot(c, hid))
    return stack([jnp.where(keep, dot(dot(left, v).astype(BF16), right), 0.0) for v in w]).astype(BF16)


def spread_bias(b, rows, lanes, unit):
    n = b.shape[1]
    return exact_nt(pick((rows, n), lambda q, m: unit(q) == m, F32), jnp.broadcast_to(b, (lanes, n)))


def build_out_back(w, hid):
    wide = FACES * hid
    shape = (wide, 192)
    r, c = rows_cols(shape)
    left = pick((wide, hid), lambda q, n: (rest(q, hid)) == n)

    rights = [
        pick((8, 192), lambda q, n: (((n >> 6) == 1) == (lev == 1)) & (((n & 63) >> 3) == q)) for lev in range(2)
    ]
    part = place(lambda v: dot_nt(left, v), w[:2], rights)
    return jnp.where((quot(r, hid)) == (c & 7), part, 0.0).astype(BF16)


def build_first_x_back(w, hid):
    wide = FACES * hid
    shape = (128, 2 * wide)
    r, c = rows_cols(shape)
    right = pick((hid, 2 * wide), lambda q, n: (rest(n, hid)) == q)
    total = jnp.zeros(shape, F32)
    for s in range(4):
        left = pick((128, 16), lambda q, n: n == 4 * s + ((q & 63) >> 4))

        def one(values):
            return dot(dot_nt(left, values).astype(BF16), right)

        value = jnp.where(r < 64, one(w[0]), jnp.where(c < wide, one(w[1]), 0.0))
        total = total + jnp.where((r & 15) - (quot(rest(c, wide), hid)) == s, value, 0.0)
    return total.astype(BF16)


def build_first_y_back(w, hid):
    wide = FACES * hid
    shape = (256, 2 * wide)
    r, c = rows_cols(shape)
    right = pick((hid, 2 * wide), lambda q, n: (rest(n, hid)) == q)
    left = pick((256, 16), lambda q, n: n == ((q & 127) >> 3))

    def one(values):
        return dot(dot_nt(left, values).astype(BF16), right)

    value = jnp.where(r < 128, one(w[0]), jnp.where(c < wide, one(w[1]), 0.0))
    return jnp.where((r & 7) == (quot(rest(c, wide), hid)), value, 0.0).astype(BF16)


def spread(bias_ref, width):
    return side([bias_ref[...]] * (width // bias_ref.shape[1]))


def limiter_forward(first, weights, hid):
    first_ref, first_bias_ref, mid_ref, mid_bias_ref, out_ref, out_bias_ref = weights
    width = first[0].shape[1]
    if first_bias_ref is None:
        h1 = jnp.tanh(dot(first_ref[...], stack(stacked(first) + [jnp.ones((ONES, width), BF16)])))
    else:
        h1 = jnp.tanh(dot(first_ref[...], stack(stacked(first))) + spread(first_bias_ref, width))
    h1_parts = split3(h1)
    block = 2 * hid
    parts = []
    for at in range(0, FACES * hid, block):
        high, middle, low = (p[at : at + block] for p in h1_parts)
        both = dot(mid_ref[...], stack([high, middle, low, high]))
        parts.append(jnp.tanh(both[:block] + both[block:] + spread(mid_bias_ref, width)))
    h2 = stack(parts)
    h2_parts = split3(h2)
    rows = 8 * FACES
    a = dot(out_ref[...], h2_parts[0])
    b = dot(out_ref[: 2 * rows, :], h2_parts[1])
    c = dot(out_ref[:rows, :], h2_parts[2])
    gates = jnp.tanh(
        ((a[2 * rows :] + b[rows:] + c) + (a[rows : 2 * rows] + b[:rows])) + a[:rows] + spread(out_bias_ref, width)
    )
    return h1, h1_parts[:2], h2, h2_parts[:2], gates


def limiter_backward(d3, h1, h2, h1_pair, h2_pair, out_back_ref, mid_back_ref, acc, hid):
    d3_hi, d3_lo = split(d3)
    dh2 = dot(out_back_ref[...], stack([d3_hi, d3_hi, d3_lo]))
    if acc is not None:
        rows = d3.shape[0]
        high = dot_nt(stack([d3_hi, d3_lo]), h2_pair[0])
        acc[2][...] += high[:rows] + high[rows:] + dot_nt(d3_hi, h2_pair[1])
        acc[3][...] += d3
    d2_hi, d2_lo = split(dh2 * (1.0 - h2 * h2))
    block = 2 * hid
    parts = []
    for at in range(0, FACES * hid, block):
        hi, lo = d2_hi[at : at + block], d2_lo[at : at + block]
        parts.append(dot(mid_back_ref[...], stack([hi, hi, lo])))
    if acc is not None:
        ones = jnp.ones((ONES, d3.shape[1]), BF16)
        lefts, rights = [], []
        for at in range(0, FACES * hid, hid):
            lefts.append(stack([h1_pair[0][at : at + hid], h1_pair[1][at : at + hid], ones]))
            rights.append(stack([d2_hi[at : at + hid], d2_lo[at : at + hid]]))
        acc[1][...] += dot_nt(side(lefts), side(rights))
    return split(stack(parts) * (1.0 - h1 * h1))


def first_backward(d1, back_ref):
    both = dot(back_ref[...], stack([d1[0], d1[1]]))
    half = both.shape[0] // 2
    return both[:half] + both[half:]


def add_first_grads(first, d1, acc_in):
    ones = jnp.ones((ONES, d1[0].shape[1]), BF16)
    rows = first[0].shape[0]
    high = dot_nt(stack([first[0], ones, first[1]]), d1[0])
    low = dot_nt(stack([first[0], ones]), d1[1])
    acc_in[...] += high[: rows + ONES] + low
    acc_in[:rows, :] += high[rows + ONES :]


def edge_states(cells, gates):
    left, right = [], []
    for c in range(4):
        low = gates[FACES * c : FACES * (c + 1)]
        high = gates[FACES * (c + 4) : FACES * (c + 5)]
        left.append(cells[1][c] + slope_gain * low * (cells[2][c] - cells[0][c]))
        right.append(cells[2][c] - slope_gain * high * (cells[3][c] - cells[1][c]))
    return left, right


def face_flux(left, right):
    ul = left[1] / left[0]
    ur = right[1] / right[0]
    half_speed = 0.5 * (jnp.maximum(jnp.abs(ul), jnp.abs(ur)) + 1.0)
    fl = [left[1], left[1] * ul + left[0], left[2] * ul, left[3] * ul]
    fr = [right[1], right[1] * ur + right[0], right[2] * ur, right[3] * ur]
    return [0.5 * (fl[c] + fr[c]) - half_speed * (right[c] - left[c]) for c in range(4)]


def sign_of(values):
    return jnp.where(values > 0.0, 1.0, jnp.where(values < 0.0, -1.0, 0.0))


def face_flux_backward(left, right, d_flux):
    inv_l, inv_r = 1.0 / left[0], 1.0 / right[0]
    ul, ur = left[1] / left[0], right[1] / right[0]
    al, ar = jnp.abs(ul), jnp.abs(ur)
    half_speed = 0.5 * (jnp.maximum(al, ar) + 1.0)
    d_speed = -0.5 * sum(d_flux[c] * (right[c] - left[c]) for c in range(4))
    share = jnp.where(al > ar, 1.0, jnp.where(al < ar, 0.0, 0.5))
    half = [0.5 * d for d in d_flux]
    spread = [half_speed * d for d in d_flux]

    def one(state, u, inv, speed_part, sign):
        du = half[1] * state[1] + half[2] * state[2] + half[3] * state[3] + speed_part * sign_of(u)
        over = du * inv
        return [
            half[1] - over * u + sign * spread[0],
            half[0] + half[1] * u + over + sign * spread[1],
            half[2] * u + sign * spread[2],
            half[3] * u + sign * spread[3],
        ]

    return (
        one(left, ul, inv_l, d_speed * share, 1.0),
        one(right, ur, inv_r, d_speed * (1.0 - share), -1.0),
    )


def edge_backward(cells, gates, d_left, d_right):
    lows, highs = [], []
    direct = [[None] * 4 for _ in range(4)]
    for c in range(4):
        low = gates[FACES * c : FACES * (c + 1)]
        high = gates[FACES * (c + 4) : FACES * (c + 5)]
        lows.append(slope_gain * (cells[2][c] - cells[0][c]) * d_left[c])
        highs.append(-slope_gain * (cells[3][c] - cells[1][c]) * d_right[c])
        low_part = slope_gain * low * d_left[c]
        high_part = slope_gain * high * d_right[c]
        direct[0][c] = -low_part
        direct[1][c] = d_left[c] + high_part
        direct[2][c] = d_right[c] + low_part
        direct[3][c] = -high_part
    return stack(lows + highs) * (1.0 - gates * gates), direct


def turn(values, shift, axis):
    size = values.shape[axis]
    return values if shift % size == 0 else pltpu.roll(values, shift % size, axis)


def x_cells(tiles):
    return [[turn(t, -s, 0)[:FACES] for t in tiles] for s in range(4)]


def pack_kernel(den, mom, tra, cot, w_in, b_in, w_mid, b_mid, w_out, b_out,
                rim, state, cots, first_x, first_y, first_bias, mid, mid_bias, out, out_bias,
                out_back, mid_back, first_x_back, first_y_back, *scratch):
    *small, sems = scratch
    nx, ny = den.shape[1:]
    segs = ny // SEG
    rows = nx // segs
    hid = w_in.shape[1]
    copies = [
        pltpu.make_async_copy(source, target, sems.at[k])
        for k, (source, target) in enumerate(
            list(zip([w_in, b_in, w_mid, b_mid, w_out, b_out], small))
            + [
                (den.at[0], state.at[0]),
                (mom.at[0], state.at[pl.ds(1, 2)]),
                (tra.at[0], state.at[3]),
                (cot.at[0], cots),
            ]
        )
    ]
    for one in copies:
        one.start()
    for one in copies[:6]:
        one.wait()
    w_in, b_in, w_mid, b_mid, w_out, b_out = small
    eye = pick((hid, hid), lambda q, n: q == n)
    wi = [dot_nt(eye, level).astype(BF16) for level in split3(w_in[...])]
    wm, wo = split3(w_mid[...]), split3(w_out[...])
    lanes = out_bias.shape[1]
    first_x[...] = build_first_x(wi, b_in[...], hid)
    first_y[...] = build_first_y(wi, hid)
    first_bias[...] = spread_bias(b_in[...], FACES * hid, lanes, lambda q: rest(q, hid))
    mid[...] = build_mid(wm, hid)
    mid_bias[...] = spread_bias(b_mid[...], 2 * hid, lanes, lambda q: rest(q, hid))
    out[...] = build_out(wo, hid)
    out_bias[...] = spread_bias(b_out[...], 64, lanes, lambda q: q >> 3)
    out_back[...] = build_out_back(wo, hid)
    mid_back[...] = build_mid_back(wm, hid)
    first_x_back[...] = build_first_x_back(wi, hid)
    first_y_back[...] = build_first_y_back(wi, hid)

    for one in copies[6:]:
        one.wait()
    lane = lane_index(ny)
    for v in range(8):
        plane = state.at[v] if v < 4 else cots.at[v - 4]
        for at in range(0, rows, FACES):
            total = jnp.zeros((FACES, ny), F32)
            for s in range(segs):
                first = s * SEG + RIM
                moved = turn(plane[pl.ds(s * rows + at, FACES), :], first + RIM, 1)
                total = jnp.where((lane >= first) & (lane < first + 2 * RIM), moved, total)
            rim[v, pl.ds(at, FACES), :] = total


def row_block(at):
    return pl.ds(pl.multiple_of(at * FACES, FACES), FACES)


def x_tiles(planes, group, groups):
    after = jnp.where(group + 1 == groups, 0, group + 1)
    return [stack([plane[row_block(group), :], plane[row_block(after), :]]) for plane in planes]


def pair_tiles(planes, step, half):
    sets = [x_tiles(planes, step + k * half, PAIR * half) for k in range(PAIR)]
    return [side([one[c] for one in sets]) for c in range(len(planes))]


def x_forward(tiles, weights, hid):
    h1, h1_pair, h2, h2_pair, gates = limiter_forward(split3(stack(tiles)), weights, hid)
    cells = x_cells(tiles)
    return h1_pair, h2_pair, gates, face_flux(*edge_states(cells, gates))


def update_cells(plane_rows, flux_rows):
    upper = turn(flux_rows, -7, 0)[:FACES]
    lower = turn(flux_rows, -6, 0)[:FACES]
    return plane_rows - courant * (upper - lower)


def x_forward_kernel(state, first_x, mid, mid_bias, out, out_bias,
                     middle, h1_hi, h1_lo, h2_hi, h2_lo, gates_out, flux):
    nx, ny = state.shape[1:]
    groups = nx // FACES
    half = groups // PAIR
    hid = mid.shape[0] // 4
    x_weights = (first_x, None, mid, mid_bias, out, out_bias)
    planes = [state.at[c] for c in range(4)]

    def step_of(step, _):
        tiles = pair_tiles(planes, step, half)
        h1_pair, h2_pair, gates, fluxes = x_forward(tiles, x_weights, hid)
        for target, value in zip((h1_hi, h1_lo, h2_hi, h2_lo, gates_out), h1_pair + h2_pair + (gates,)):
            target[step] = value
        for c in range(4):
            for k in range(PAIR):
                flux[c, row_block(step + k * half + 1), :] = fluxes[c][:, k * ny : (k + 1) * ny]
        return 0

    lax.fori_loop(0, half, step_of, 0)
    for c in range(4):
        flux[c, :FACES, :] = flux[c, nx : nx + FACES, :]

    def update(group, _):
        for c in range(4):
            both = stack([flux[c, row_block(group), :], flux[c, row_block(group + 1), :]])
            middle[c, row_block(group), :] = update_cells(planes[c][row_block(group), :], both)
        return 0

    lax.fori_loop(0, groups, update, 0)


def y_order(planes):
    return [planes[0], planes[2], planes[1], planes[3]]


def lane_index(width):
    return lax.broadcasted_iota(jnp.int32, (FACES, width), 1)


def y_step(cells, cots, halo_mask, refs, acc, hid):
    weights, out_back, mid_back, first_y_back = refs
    window = split3(stack([cells[s][c] for s in range(4) for c in range(4)]))
    h1, h1_pair, h2, h2_pair, gates = limiter_forward(window, weights, hid)
    left, right = edge_states(cells, gates)
    d_flux = [courant * (cots[1][c] - cots[0][c]) for c in range(4)]
    d_left, d_right = face_flux_backward(left, right, d_flux)
    if halo_mask is not None:
        d_left = [jnp.where(halo_mask, d, 0.0) for d in d_left]
        d_right = [jnp.where(halo_mask, d, 0.0) for d in d_right]
    d3_full, direct = edge_backward(cells, gates, d_left, d_right)
    d1 = limiter_backward(d3_full, h1, h2, h1_pair, h2_pair, out_back, mid_back, acc, hid)
    d_window = first_backward(d1, first_y_back)
    if acc is not None:
        add_first_grads(window, d1, acc[0])
    return [
        [d_window[FACES * (4 * s + c) : FACES * (4 * s + c + 1)] + direct[s][c] for c in range(4)]
        for s in range(4)
    ]


def y_gather(parts, ny):
    lane = lane_index(ny)
    out = []
    for c in range(4):
        a = turn(jnp.where(lane >= 1, parts[0][c], 0.0), -1, 1)
        b = turn(jnp.where(lane < ny - 1, parts[2][c], 0.0), 1, 1)
        d = turn(jnp.where(lane < ny - 2, parts[3][c], 0.0), 2, 1)
        out.append(parts[1][c] + a + b + d)
    return out


def fold_first_x(acc, hid):
    shape = acc.shape
    r, c = rows_cols(shape)
    fold = pick((shape[1], hid), lambda q, n: rest(n - q, hid) == 0, F32)
    face = quot(c, hid)
    parts = [
        jnp.where((((r & 15) - face) == s) & (r < 64) | (r >= 64) & (s == 0), acc, 0.0)[: 80 if s == 0 else 64]
        for s in range(4)
    ]
    folded = exact(stack(parts), fold)
    def test(q, n):
        at = jnp.where(n < 64, n, n - ONES)
        return ((n < 64) | (n >= 64 + ONES)) & (q == (at >> 4)) | (n == 64) & (q == 16)

    return exact(pick((24, folded.shape[0]), test, F32), folded)


def fold_first_y(acc, hid):
    shape = acc.shape
    r, c = rows_cols(shape)
    fold = pick((shape[1], hid), lambda q, n: (rest(q, hid)) == n, F32)
    keep = ((r & 7) == (quot(c, hid))) | (r >= 128)
    sel = lambda q, n: ((n < 128) & (q == (n >> 3))) | ((n == 128) & (q == 16))
    return exact(pick((24, shape[0]), sel, F32), exact(jnp.where(keep, acc, 0.0), fold))


def back_kernel(state, cot, middle, own, from_left, from_right,
                first_x, first_y, first_bias, mid, mid_bias, out, out_bias,
                out_back, mid_back, first_x_back, first_y_back,
                h1_hi, h1_lo, h2_hi, h2_lo, gates_in,
                g_den, g_mom, g_tra, g_weights,
                rim_state, rim_cot, rim_flux, rim_middle, rim_grad, d_middle,
                acc_x, acc_y, acc_mid, acc_out, acc_out_bias):
    nx, ny = state.shape[1:]
    groups = nx // FACES
    half = groups // PAIR
    hid = mid.shape[0] // 4
    x_weights = (first_x, None, mid, mid_bias, out, out_bias)
    segs = ny // SEG
    rim_rows = nx // segs
    rim_groups = rim_rows // FACES
    rim_half = rim_groups // RIM_PAIR

    for acc in (acc_x, acc_y, acc_mid, acc_out, acc_out_bias):
        acc[...] = jnp.zeros(acc.shape, F32)

    lane = lane_index(ny)
    spot = lane & (SEG - 1)
    for v in range(8):
        for g in range(rim_groups):
            rows = pl.ds(g * FACES, FACES)
            mine = own[v, rows, :]
            value = jnp.where(
                spot < RIM,
                turn(from_left[v, rows, :], -RIM, 1),
                jnp.where(
                    spot < 2 * RIM,
                    turn(mine, -RIM, 1),
                    jnp.where(spot < 3 * RIM, turn(mine, RIM, 1), turn(from_right[v, rows, :], RIM, 1)),
                ),
            )
            if v < 4:
                rim_state[v, rows, :] = value
                if g == 0:
                    rim_state[v, pl.ds(rim_rows, FACES), :] = turn(value, -SEG, 1)
            else:
                rim_cot[v - 4, rows, :] = value

    def rim_forward(step, _):
        sets = [
            [
                stack([
                    rim_state[c, row_block(step + k * rim_half), :],
                    rim_state[c, row_block(step + k * rim_half + 1), :],
                ])
                for c in range(4)
            ]
            for k in range(RIM_PAIR)
        ]
        tiles = [side([one[c] for one in sets]) for c in range(4)]
        fluxes = x_forward(tiles, x_weights, hid)[3]
        for c in range(4):
            for k in range(RIM_PAIR):
                rim_flux[c, row_block(step + k * rim_half + 1), :] = fluxes[c][:, k * ny : (k + 1) * ny]
        return 0

    lax.fori_loop(0, rim_half, rim_forward, 0)
    for c in range(4):
        rim_flux[c, :FACES, :] = turn(rim_flux[c, rim_rows : rim_rows + FACES, :], SEG, 1)
        for g in range(rim_groups):
            rows = pl.ds(g * FACES, FACES)
            both = stack([rim_flux[c, rows, :], rim_flux[c, pl.ds((g + 1) * FACES, FACES), :]])
            rim_middle[c, rows, :] = update_cells(rim_state[c, rows, :], both)

    refs = ((first_y, first_bias, mid, mid_bias, out, out_bias), out_back, mid_back, first_y_back)
    spot_wide = lane_index(RIM_PAIR * ny) & (SEG - 1)
    rim_faces = (spot_wide == RIM - 2) | (spot_wide == RIM - 1) | (spot_wide == 3 * RIM)

    def rim_back(step, _):
        cells = [[[] for _ in range(4)] for _ in range(4)]
        cots = [[[] for _ in range(4)] for _ in range(2)]
        for k in range(RIM_PAIR):
            rows = row_block(step + k * rim_half)
            for c in range(4):
                value = rim_middle[c, rows, :]
                for s in range(4):
                    cells[s][c].append(turn(value, 1 - s, 1))
                value = rim_cot[c, rows, :]
                for s in range(2):
                    cots[s][c].append(turn(value, -s, 1))
        cells = [y_order([side(one) for one in row]) for row in cells]
        cots = [y_order([side(one) for one in row]) for row in cots]
        parts = y_step(cells, cots, rim_faces, refs, None, hid)
        for k in range(RIM_PAIR):
            own_parts = [[one[:, k * ny : (k + 1) * ny] for one in row] for row in parts]
            gathered = y_order(y_gather(own_parts, ny))
            for c in range(4):
                rim_grad[c, row_block(step + k * rim_half), :] = gathered[c]
        return 0

    lax.fori_loop(0, rim_half, rim_back, 0)

    def main_y(step, _):
        cells = [[[] for _ in range(4)] for _ in range(4)]
        cots = [[[] for _ in range(4)] for _ in range(2)]
        for k in range(PAIR):
            group = step + k * half
            rows = row_block(group)
            seg = group // rim_groups
            rim_at = row_block(group - seg * rim_groups)
            to_low = ny - (seg * SEG + 3 * RIM)
            to_high = lax.rem(ny - 1 - (seg * SEG + RIM - 1) + ny, ny)
            for c in range(4):
                value = middle[c, rows, :]
                rim_value = rim_middle[c, rim_at, :]
                low = jnp.where(lane < 2, pltpu.roll(rim_value, to_low, 1), value)
                high = jnp.where(lane == ny - 1, pltpu.roll(rim_value, to_high, 1), value)
                cells[0][c].append(turn(high, 1, 1))
                cells[1][c].append(value)
                cells[2][c].append(turn(jnp.where(lane < 1, low, value), -1, 1))
                cells[3][c].append(turn(low, -2, 1))
                value = cot[c, rows, :]
                rim_value = rim_cot[c, rim_at, :]
                low = jnp.where(lane < 1, pltpu.roll(rim_value, to_low, 1), value)
                cots[0][c].append(value)
                cots[1][c].append(turn(low, -1, 1))
        cells = [y_order([side(one) for one in row]) for row in cells]
        cots = [y_order([side(one) for one in row]) for row in cots]
        parts = y_step(cells, cots, None, refs, (acc_y, acc_mid, acc_out, acc_out_bias), hid)
        for k in range(PAIR):
            group = step + k * half
            rows = row_block(group)
            seg = group // rim_groups
            rim_at = row_block(group - seg * rim_groups)
            own_parts = [[one[:, k * ny : (k + 1) * ny] for one in row] for row in parts]
            gathered = y_order(y_gather(own_parts, ny))
            to_low = ny - (seg * SEG + RIM)
            to_high = lax.rem(ny - 1 - (seg * SEG + 3 * RIM - 1) + ny, ny)
            for c in range(4):
                rim_value = rim_grad[c, rim_at, :]
                from_rim = jnp.where(
                    lane < 2,
                    pltpu.roll(rim_value, to_low, 1),
                    jnp.where(lane == ny - 1, pltpu.roll(rim_value, to_high, 1), 0.0),
                )
                d_middle[c, rows, :] = cot[c, rows, :] + gathered[c] + from_rim
        return 0

    lax.fori_loop(0, half, main_y, 0)

    planes = [state.at[c] for c in range(4)]
    grads = [g_den.at[0], g_mom.at[0, 0], g_mom.at[0, 1], g_tra.at[0]]
    d_planes = [d_middle.at[c] for c in range(4)]

    def main_x(step, carry):
        tiles = pair_tiles(planes, step, half)
        d_tiles = pair_tiles(d_planes, step, half)
        gates = gates_in[step]
        h1_pair = (h1_hi[step], h1_lo[step])
        h2_pair = (h2_hi[step], h2_lo[step])
        h1 = h1_pair[0].astype(F32) + h1_pair[1].astype(F32)
        h2 = h2_pair[0].astype(F32) + h2_pair[1].astype(F32)
        cells = x_cells(tiles)
        left, right = edge_states(cells, gates)
        d_flux = [courant * (turn(d, -2, 0)[:FACES] - turn(d, -1, 0)[:FACES]) for d in d_tiles]
        d_left, d_right = face_flux_backward(left, right, d_flux)
        d3_full, direct = edge_backward(cells, gates, d_left, d_right)
        d1 = limiter_backward(
            d3_full, h1, h2, h1_pair, h2_pair, out_back, mid_back, (acc_x, acc_mid, acc_out, acc_out_bias), hid
        )
        d_window = first_backward(d1, first_x_back)
        add_first_grads(split(stack(tiles)), d1, acc_x)
        later = []
        for c in range(4):
            total = d_window[2 * FACES * c : 2 * FACES * (c + 1)]
            for s in range(4):
                total = total + turn(stack([direct[s][c], jnp.zeros_like(direct[s][c])]), s, 0)
            now = total[:FACES] + d_tiles[c][:FACES] + carry[c]
            for k in range(PAIR):
                grads[c][row_block(step + k * half), :] = now[:, k * ny : (k + 1) * ny]
            later.append(total[FACES:])
        return tuple(later)

    start = tuple(jnp.zeros((FACES, PAIR * ny), F32) for _ in range(4))
    last = lax.fori_loop(0, half, main_x, start)
    for c in range(4):
        for k in range(PAIR):
            at = (k + 1) % PAIR * half * FACES
            grads[c][pl.ds(at, FACES), :] += last[c][:, k * ny : (k + 1) * ny]

    eye = pick((hid, hid), lambda q, n: q == n, F32)
    grad_first = fold_first_x(acc_x[...], hid) + fold_first_y(acc_y[...], hid)
    both = acc_mid[...]
    grad_mid = both[:hid, :hid] + both[:hid, hid:] + both[hid : 2 * hid, :hid]
    grad_mid_bias = both[2 * hid :, :hid] + both[2 * hid :, hid:]
    r, c = rows_cols(acc_out.shape)
    fold = pick((acc_out.shape[1], hid), lambda q, n: (rest(q, hid)) == n, F32)
    rows = pick((8, 64), lambda q, n: (n >> 3) == q, F32)
    grad_out = exact(rows, exact(jnp.where((r & 7) == (quot(c, hid)), acc_out[...], 0.0), fold))
    out_bias_rows = exact_nt(jnp.ones((8, acc_out_bias.shape[1]), F32), acc_out_bias[...])
    grad_out_bias = exact_nt(out_bias_rows, pick((hid, 64), lambda q, n: (n >> 3) == q, F32))
    r, c = rows_cols((8, hid))
    biases = jnp.where(
        r == 0,
        grad_first[16:24],
        jnp.where(r == 1, jnp.broadcast_to(grad_mid_bias[:1], (8, hid)), jnp.where(r == 2, grad_out_bias, 0.0)),
    )
    g_weights[...] = jnp.zeros(g_weights.shape, F32)
    g_weights[:, :hid] = stack([exact_nt(eye, grad_mid), grad_first[:16], grad_out, biases])


def finish_kernel(parts, g_w_in, g_b_in, g_w_mid, g_b_mid, g_w_out, g_b_out):
    hid = g_w_mid.shape[0]
    found = [parts[k] for k in range(parts.shape[0])]
    while len(found) > 1:
        found = [found[k] + found[k + 1] if k + 1 < len(found) else found[k] for k in range(0, len(found), 2)]
    total = found[0][:, :hid]
    g_w_mid[...] = total[:hid]
    g_w_in[...] = total[hid : hid + 16]
    g_w_out[...] = total[hid + 16 : hid + 24]
    g_b_in[...] = total[hid + 24 : hid + 25]
    g_b_mid[...] = total[hid + 25 : hid + 26]
    g_b_out[...] = total[hid + 26 : hid + 27, :8]


def whole(count, space=pltpu.VMEM):
    return [pl.BlockSpec(memory_space=space)] * count


def call(kernel, outs, operands, out_spaces=None, in_spaces=None, scratch=(), flops=0, moved=0):
    return pl.pallas_call(
        kernel,
        out_shape=outs,
        in_specs=in_spaces or whole(len(operands)),
        out_specs=out_spaces or whole(len(outs)),
        scratch_shapes=list(scratch),
        compiler_params=pltpu.CompilerParams(vmem_limit_bytes=VMEM_BYTES),
        cost_estimate=pl.CostEstimate(flops=flops, bytes_accessed=moved, transcendentals=0),
    )(*operands)


def others(values, axis, size):
    return [lax.ppermute(values, axis, [(i, i ^ k) for i in range(size)]) for k in range(1, size)]


def tree_sum(parts):
    while len(parts) > 1:
        parts = [parts[k] + parts[k + 1] for k in range(0, len(parts), 2)]
    return parts[0]


def body(sizes, density, momentum, tracer, cotangent, w_in, b_in, w_mid, b_mid, w_out, b_out):
    nx, ny = density.shape[1:]
    hid = w_in.shape[0]
    wide = FACES * hid
    groups = nx // FACES
    half = groups // PAIR
    lanes = PAIR * ny
    segs = ny // SEG
    rim_rows = nx // segs
    ring = sizes["tx"] * sizes["ty"]
    shape = jax.ShapeDtypeStruct

    operands = [
        density, momentum, tracer, cotangent, w_in.T, b_in[None], w_mid, b_mid[None], w_out, b_out[None]
    ]
    rim, state, cots, *matrices = call(
        pack_kernel,
        [
            shape((8, rim_rows, ny), F32),
            shape((4, nx, ny), F32),
            shape((4, nx, ny), F32),
            shape((wide, 6 * 64 + ONES), BF16),
            shape((wide, 6 * 128), BF16),
            shape((wide, ny), F32),
            shape((4 * hid, 8 * hid), BF16),
            shape((2 * hid, ny), F32),
            shape((192, wide), BF16),
            shape((64, ny), F32),
            shape((wide, 192), BF16),
            shape((2 * hid, 6 * hid), BF16),
            shape((128, 2 * wide), BF16),
            shape((256, 2 * wide), BF16),
        ],
        [pltpu.with_memory_space_constraint(one, pltpu.HBM) for one in operands],
        in_spaces=whole(10, pltpu.HBM),
        scratch=[pltpu.VMEM(one.shape, F32) for one in operands[4:]] + [pltpu.SemaphoreType.DMA((10,))],
    )
    axes = ("tx", "ty")
    from_left = lax.ppermute(rim, axes, [(i, (i + 1) % ring) for i in range(ring)])
    from_right = lax.ppermute(rim, axes, [((i + 1) % ring, i) for i in range(ring)])

    middle, *kept = call(
        x_forward_kernel,
        [shape((4, nx, ny), F32)]
        + [shape((half, wide, lanes), BF16)] * 4
        + [shape((half, 64, lanes), F32)],
        [state, matrices[0]] + matrices[3:7],
        scratch=[pltpu.VMEM((4, nx + FACES, ny), F32)],
        flops=10**10,
        moved=10**7,
    )
    g_den, g_mom, g_tra, g_weights = call(
        back_kernel,
        [
            shape(density.shape, F32),
            shape(momentum.shape, F32),
            shape(tracer.shape, F32),
            shape((2 * hid, 128), F32),
        ],
        [state, cots, middle, rim, from_left, from_right] + matrices + kept,
        scratch=[
            pltpu.VMEM((4, rim_rows + FACES, ny), F32),
            pltpu.VMEM((4, rim_rows, ny), F32),
            pltpu.VMEM((4, rim_rows + FACES, ny), F32),
            pltpu.VMEM((4, rim_rows, ny), F32),
            pltpu.VMEM((4, rim_rows, ny), F32),
            pltpu.VMEM((4, nx, ny), F32),
            pltpu.VMEM((64 + ONES, wide), F32),
            pltpu.VMEM((128 + ONES, wide), F32),
            pltpu.VMEM((2 * hid + ONES, 2 * hid), F32),
            pltpu.VMEM((64, wide), F32),
            pltpu.VMEM((64, lanes), F32),
        ],
        flops=4 * 10**10,
        moved=2 * 10**7,
    )
    everyone = lax.all_gather(g_weights, ("traj", "tx", "ty"))
    g_w_in, g_b_in, g_w_mid, g_b_mid, g_w_out, g_b_out = call(
        finish_kernel,
        [
            shape((w_in.shape[1], hid), F32),
            shape((1, hid), F32),
            shape(w_mid.shape, F32),
            shape((1, hid), F32),
            shape(w_out.shape, F32),
            shape((1, b_out.shape[0]), F32),
        ],
        [everyone],
    )
    return (g_den, g_mom, g_tra, g_w_in.T, g_b_in[0], g_w_mid, g_b_mid[0], g_w_out, g_b_out[0])


def solution(mesh):
    flow = P("traj", None, ("tx", "ty"))
    deep = P("traj", None, None, ("tx", "ty"))
    return jax.shard_map(
        functools.partial(body, dict(mesh.shape)),
        mesh=mesh,
        in_specs=(flow, deep, flow, deep) + (P(),) * 6,
        out_specs=(flow, deep, flow) + (P(),) * 6,
        check_vma=False,
    )
```

```python
import functools

import jax
import jax.numpy as jnp
from jax import lax
from jax.experimental import pallas as pl
from jax.experimental.pallas import tpu as pltpu
from jax.sharding import PartitionSpec as P

courant = 0.1
slope_gain = 0.25
F32 = jnp.float32
BF16 = jnp.bfloat16
FACES = 8
SEG = 16
RIM = 4
PAIR = 8
RIM_PAIR = 4
ONES = 16
VMEM_BYTES = 32 * 2**20


def dot(a, b):
    return lax.dot_general(a, b, (((1,), (0,)), ((), ())), preferred_element_type=F32)


def dot_nt(a, b):
    return lax.dot_general(a, b, (((1,), (1,)), ((), ())), preferred_element_type=F32)


def exact(a, b):
    return lax.dot_general(
        a, b, (((1,), (0,)), ((), ())), precision=lax.Precision.HIGHEST, preferred_element_type=F32
    )


def exact_nt(a, b):
    return lax.dot_general(
        a, b, (((1,), (1,)), ((), ())), precision=lax.Precision.HIGHEST, preferred_element_type=F32
    )


def split(values):
    high = values.astype(BF16)
    return high, (values - high.astype(F32)).astype(BF16)


def split3(values):
    high = values.astype(BF16)
    rest = values - high.astype(F32)
    middle = rest.astype(BF16)
    return high, middle, (rest - middle.astype(F32)).astype(BF16)


def rows_cols(shape):
    return lax.broadcasted_iota(jnp.int32, shape, 0), lax.broadcasted_iota(jnp.int32, shape, 1)


def quot(values, n):
    return values >> (n.bit_length() - 1) if n & (n - 1) == 0 else values // n


def rest(values, n):
    return values & (n - 1) if n & (n - 1) == 0 else values % n


def pick(shape, test, dtype=BF16):
    r, c = rows_cols(shape)
    return jnp.where(test(r, c), 1.0, 0.0).astype(dtype)


def stack(parts):
    return jnp.concatenate(parts, 0)


def side(parts):
    return jnp.concatenate(parts, 1)


STACKED = (0, 0, 0, 1, 1, 2)


def stacked(parts):
    return [parts[0], parts[1], parts[2], parts[0], parts[1], parts[0]]


def level_of(block):
    return jnp.where(block < 3, 0, jnp.where(block < 5, 1, 2))


def choose(values, levels):
    parts = [part.astype(F32) for part in split3(values)]
    total = jnp.zeros(values.shape, F32)
    for k, part in enumerate(parts):
        total = jnp.where(levels == k, part, total)
    return total


def build_first(w, b, hid):
    x_cols, y_cols, step = 6 * 64 + ONES, 6 * 128, 512

    def source(q, n):
        s = n >> 9
        m = n & (step - 1)
        in_x = (s < 4) & (m < 384) & (q == 4 * s + ((m >> 4) & 3))
        in_y = (n >= 4 * step) & (q == (((n - 4 * step) & 127) >> 3))
        return in_x | in_y

    spread_out = exact(w, pick((16, 4 * step + y_cols), source, F32))
    _, n = rows_cols(spread_out.shape)
    block = jnp.where(n < 4 * step, (n & (step - 1)) >> 6, (n - 4 * step) >> 7)
    spread_out = choose(spread_out, level_of(block))

    at, _ = rows_cols((x_cols, hid))
    rows = jnp.zeros((x_cols, hid), F32)
    for k, level in enumerate(split3(b)):
        rows = jnp.where(at == 384 + k, jnp.broadcast_to(level.astype(F32), (x_cols, hid)), rows)
    bias = dot_nt(pick((hid, hid), lambda q, n: q == n), rows.astype(BF16))

    r, c = rows_cols((FACES * hid, x_cols))
    shift = jnp.where(c < 384, (c & 15) - quot(r, hid), -1)
    first_x = stack([bias] * FACES)
    for s in range(4):
        part = spread_out[:, s * step : s * step + x_cols]
        first_x = jnp.where(shift == s, stack([part] * FACES), first_x)
    r, c = rows_cols((FACES * hid, y_cols))
    first_y = jnp.where((c & 7) == quot(r, hid), stack([spread_out[:, 4 * step :]] * FACES), 0.0)
    return first_x.astype(BF16), first_y.astype(BF16)


def build_first_back(w_t, hid):
    wide = FACES * hid

    def source(q, n):
        in_x = (q < 512) & (n == 4 * (q >> 7) + ((q & 63) >> 4))
        in_y = (q >= 512) & (n == (((q - 512) & 127) >> 3))
        return in_x | in_y

    rows = exact(pick((512 + 256, 16), source, F32), w_t)
    right = pick((hid, 2 * wide), lambda q, n: rest(n, hid) == q)
    high, low = (dot(part, right) for part in split(rows))
    r, c = rows_cols(high.shape)
    is_low = jnp.where(r < 512, r & 64, (r - 512) & 128) > 0
    value = jnp.where(is_low, jnp.where(c < wide, low, 0.0), high)
    face = quot(rest(c, wide), hid)
    r, c = r[:128], c[:128]
    shift = (r & 15) - face[:128]
    back_x = jnp.zeros((128, 2 * wide), F32)
    for s in range(4):
        back_x = jnp.where(shift == s, value[128 * s : 128 * (s + 1)], back_x)
    r, _ = rows_cols((256, 2 * wide))
    back_y = jnp.where((r & 7) == face[512:], value[512:], 0.0)
    return back_x.astype(BF16), back_y.astype(BF16)


def build_mid(w, hid):
    block = 2 * hid
    tiled = exact(w, pick((hid, 4 * block), lambda q, n: rest(n, hid) == q, F32))
    _, n = rows_cols(tiled.shape)
    upper = choose(tiled, jnp.where(n < 3 * block, 0, 2))
    lower = choose(tiled, jnp.where(n < 2 * block, 1, -1))
    r, c = rows_cols((2 * block, 4 * block))
    keep = quot(rest(r, block), hid) == quot(rest(c, block), hid)
    return jnp.where(keep, stack([upper, upper, lower, lower]), 0.0).astype(BF16)


def build_mid_back(w, hid):
    block = 2 * hid
    turned = exact_nt(pick((hid, hid), lambda q, n: q == n, F32), w)
    tiled = exact(turned, pick((hid, 3 * block), lambda q, n: rest(n, hid) == q, F32))
    _, n = rows_cols(tiled.shape)
    tiled = choose(tiled, jnp.where(quot(n, block) == 1, 1, 0))
    r, c = rows_cols((block, 3 * block))
    keep = quot(r, hid) == quot(rest(c, block), hid)
    return jnp.where(keep, stack([tiled] * 2), 0.0).astype(BF16)


def build_out(w, hid):
    wide = FACES * hid
    rows = exact(pick((64, 8), lambda q, n: (q >> 3) == n, F32), w)
    tiled = dot(stack(list(split3(rows))), pick((hid, wide), lambda q, n: rest(n, hid) == q))
    r, c = rows_cols(tiled.shape)
    return jnp.where((r & 7) == quot(c, hid), tiled, 0.0).astype(BF16)


def build_out_back(w, hid):
    wide = FACES * hid
    turned = exact_nt(pick((hid, hid), lambda q, n: q == n, F32), w)
    tiled = exact(turned, pick((8, 192), lambda q, n: ((n & 63) >> 3) == q, F32))
    _, n = rows_cols(tiled.shape)
    tiled = choose(tiled, jnp.where((n >> 6) == 1, 1, 0))
    r, c = rows_cols((wide, 192))
    return jnp.where(quot(r, hid) == (c & 7), stack([tiled] * FACES), 0.0).astype(BF16)


def spread_bias(b, lanes, copies):
    n = b.shape[1]
    rows = exact_nt(pick((n, n), lambda q, m: q == m, F32), jnp.broadcast_to(b, (lanes, n)))
    return stack([rows] * copies)


def spread(bias_ref, width):
    return side([bias_ref[...]] * (width // bias_ref.shape[1]))


def limiter_forward(first, weights, hid):
    first_ref, first_bias_ref, mid_ref, mid_bias_ref, out_ref, out_bias_ref = weights
    width = first[0].shape[1]
    if first_bias_ref is None:
        h1 = jnp.tanh(dot(first_ref[...], stack(stacked(first) + [jnp.ones((ONES, width), BF16)])))
    else:
        h1 = jnp.tanh(dot(first_ref[...], stack(stacked(first))) + spread(first_bias_ref, width))
    h1_parts = split3(h1)
    block = 2 * hid
    parts = []
    for at in range(0, FACES * hid, block):
        high, middle, low = (p[at : at + block] for p in h1_parts)
        both = dot(mid_ref[...], stack([high, middle, low, high]))
        parts.append(jnp.tanh(both[:block] + both[block:] + spread(mid_bias_ref, width)))
    h2 = stack(parts)
    h2_parts = split3(h2)
    rows = 8 * FACES
    a = dot(out_ref[...], h2_parts[0])
    b = dot(out_ref[: 2 * rows, :], h2_parts[1])
    c = dot(out_ref[:rows, :], h2_parts[2])
    gates = jnp.tanh(
        ((a[2 * rows :] + b[rows:] + c) + (a[rows : 2 * rows] + b[:rows])) + a[:rows] + spread(out_bias_ref, width)
    )
    return h1, h1_parts[:2], h2, h2_parts[:2], gates


def limiter_backward(d3, h1, h2, h1_pair, h2_pair, out_back_ref, mid_back_ref, acc, hid):
    d3_hi, d3_lo = split(d3)
    dh2 = dot(out_back_ref[...], stack([d3_hi, d3_hi, d3_lo]))
    if acc is not None:
        rows = d3.shape[0]
        high = dot_nt(stack([d3_hi, d3_lo]), h2_pair[0])
        acc[2][...] += high[:rows] + high[rows:] + dot_nt(d3_hi, h2_pair[1])
        acc[3][...] += d3
    d2_hi, d2_lo = split(dh2 * (1.0 - h2 * h2))
    block = 2 * hid
    parts = []
    for at in range(0, FACES * hid, block):
        hi, lo = d2_hi[at : at + block], d2_lo[at : at + block]
        parts.append(dot(mid_back_ref[...], stack([hi, hi, lo])))
    if acc is not None:
        ones = jnp.ones((ONES, d3.shape[1]), BF16)
        lefts, rights = [], []
        for at in range(0, FACES * hid, hid):
            lefts.append(stack([h1_pair[0][at : at + hid], h1_pair[1][at : at + hid], ones]))
            rights.append(stack([d2_hi[at : at + hid], d2_lo[at : at + hid]]))
        acc[1][...] += dot_nt(side(lefts), side(rights))
    return split(stack(parts) * (1.0 - h1 * h1))


def first_backward(d1, back_ref):
    both = dot(back_ref[...], stack([d1[0], d1[1]]))
    half = both.shape[0] // 2
    return both[:half] + both[half:]


def add_first_grads(first, d1, acc_in):
    ones = jnp.ones((ONES, d1[0].shape[1]), BF16)
    rows = first[0].shape[0]
    high = dot_nt(stack([first[0], ones, first[1]]), d1[0])
    low = dot_nt(stack([first[0], ones]), d1[1])
    acc_in[...] += high[: rows + ONES] + low
    acc_in[:rows, :] += high[rows + ONES :]


def edge_states(cells, gates):
    left, right = [], []
    for c in range(4):
        low = gates[FACES * c : FACES * (c + 1)]
        high = gates[FACES * (c + 4) : FACES * (c + 5)]
        left.append(cells[1][c] + slope_gain * low * (cells[2][c] - cells[0][c]))
        right.append(cells[2][c] - slope_gain * high * (cells[3][c] - cells[1][c]))
    return left, right


def face_flux(left, right):
    ul = left[1] / left[0]
    ur = right[1] / right[0]
    half_speed = 0.5 * (jnp.maximum(jnp.abs(ul), jnp.abs(ur)) + 1.0)
    fl = [left[1], left[1] * ul + left[0], left[2] * ul, left[3] * ul]
    fr = [right[1], right[1] * ur + right[0], right[2] * ur, right[3] * ur]
    return [0.5 * (fl[c] + fr[c]) - half_speed * (right[c] - left[c]) for c in range(4)]


def sign_of(values):
    return jnp.where(values > 0.0, 1.0, jnp.where(values < 0.0, -1.0, 0.0))


def face_flux_backward(left, right, d_flux):
    inv_l, inv_r = 1.0 / left[0], 1.0 / right[0]
    ul, ur = left[1] / left[0], right[1] / right[0]
    al, ar = jnp.abs(ul), jnp.abs(ur)
    half_speed = 0.5 * (jnp.maximum(al, ar) + 1.0)
    d_speed = -0.5 * sum(d_flux[c] * (right[c] - left[c]) for c in range(4))
    share = jnp.where(al > ar, 1.0, jnp.where(al < ar, 0.0, 0.5))
    half = [0.5 * d for d in d_flux]
    spread = [half_speed * d for d in d_flux]

    def one(state, u, inv, speed_part, sign):
        du = half[1] * state[1] + half[2] * state[2] + half[3] * state[3] + speed_part * sign_of(u)
        over = du * inv
        return [
            half[1] - over * u + sign * spread[0],
            half[0] + half[1] * u + over + sign * spread[1],
            half[2] * u + sign * spread[2],
            half[3] * u + sign * spread[3],
        ]

    return (
        one(left, ul, inv_l, d_speed * share, 1.0),
        one(right, ur, inv_r, d_speed * (1.0 - share), -1.0),
    )


def edge_backward(cells, gates, d_left, d_right):
    lows, highs = [], []
    direct = [[None] * 4 for _ in range(4)]
    for c in range(4):
        low = gates[FACES * c : FACES * (c + 1)]
        high = gates[FACES * (c + 4) : FACES * (c + 5)]
        lows.append(slope_gain * (cells[2][c] - cells[0][c]) * d_left[c])
        highs.append(-slope_gain * (cells[3][c] - cells[1][c]) * d_right[c])
        low_part = slope_gain * low * d_left[c]
        high_part = slope_gain * high * d_right[c]
        direct[0][c] = -low_part
        direct[1][c] = d_left[c] + high_part
        direct[2][c] = d_right[c] + low_part
        direct[3][c] = -high_part
    return stack(lows + highs) * (1.0 - gates * gates), direct


def turn(values, shift, axis):
    size = values.shape[axis]
    return values if shift % size == 0 else pltpu.roll(values, shift % size, axis)


def x_cells(tiles):
    return [[turn(t, -s, 0)[:FACES] for t in tiles] for s in range(4)]


def pack_kernel(den, mom, tra, cot, w_in, b_in, w_mid, b_mid, w_out, b_out,
                rim, state, cots, first_x, first_y, first_bias, mid, mid_bias, out, out_bias,
                out_back, mid_back, first_x_back, first_y_back, *scratch):
    *small, sems = scratch
    nx, ny = den.shape[1:]
    segs = ny // SEG
    rows = nx // segs
    hid = w_in.shape[1]
    copies = [
        pltpu.make_async_copy(source, target, sems.at[k])
        for k, (source, target) in enumerate(
            list(zip([w_in, b_in, w_mid, b_mid, w_out, b_out], small))
            + [
                (den.at[0], state.at[0]),
                (mom.at[0], state.at[pl.ds(1, 2)]),
                (tra.at[0], state.at[3]),
                (cot.at[0], cots),
            ]
        )
    ]
    for one in copies:
        one.start()
    for one in copies[:6]:
        one.wait()
    w_in, b_in, w_mid, b_mid, w_out, b_out = small
    lanes = out_bias.shape[1]
    w_in_rows = exact_nt(pick((hid, hid), lambda q, n: q == n, F32), w_in[...])
    first_x[...], first_y[...] = build_first(w_in_rows, b_in[...], hid)
    first_bias[...] = spread_bias(b_in[...], lanes, FACES)
    mid[...] = build_mid(w_mid[...], hid)
    mid_bias[...] = spread_bias(b_mid[...], lanes, 2)
    out[...] = build_out(w_out[...], hid)
    out_bias[...] = exact_nt(
        pick((64, 8), lambda q, n: (q >> 3) == n, F32), jnp.broadcast_to(b_out[...], (lanes, 8))
    )
    out_back[...] = build_out_back(w_out[...], hid)
    mid_back[...] = build_mid_back(w_mid[...], hid)
    first_x_back[...], first_y_back[...] = build_first_back(w_in[...], hid)

    for one in copies[6:]:
        one.wait()
    lane = lane_index(ny)
    for v in range(8):
        plane = state.at[v] if v < 4 else cots.at[v - 4]
        for at in range(0, rows, FACES):
            total = jnp.zeros((FACES, ny), F32)
            for s in range(segs):
                first = s * SEG + RIM
                moved = turn(plane[pl.ds(s * rows + at, FACES), :], first + RIM, 1)
                total = jnp.where((lane >= first) & (lane < first + 2 * RIM), moved, total)
            rim[v, pl.ds(at, FACES), :] = total


def row_block(at):
    return pl.ds(pl.multiple_of(at * FACES, FACES), FACES)


def x_tiles(planes, group, groups):
    after = jnp.where(group + 1 == groups, 0, group + 1)
    return [stack([plane[row_block(group), :], plane[row_block(after), :]]) for plane in planes]


def pair_tiles(planes, step, half):
    sets = [x_tiles(planes, step + k * half, PAIR * half) for k in range(PAIR)]
    return [side([one[c] for one in sets]) for c in range(len(planes))]


def x_forward(tiles, weights, hid):
    h1, h1_pair, h2, h2_pair, gates = limiter_forward(split3(stack(tiles)), weights, hid)
    cells = x_cells(tiles)
    return h1_pair, h2_pair, gates, face_flux(*edge_states(cells, gates))


def update_cells(plane_rows, flux_rows):
    upper = turn(flux_rows, -7, 0)[:FACES]
    lower = turn(flux_rows, -6, 0)[:FACES]
    return plane_rows - courant * (upper - lower)


def x_forward_kernel(state, first_x, mid, mid_bias, out, out_bias,
                     middle, h1_hi, h1_lo, h2_hi, h2_lo, gates_out, flux):
    nx, ny = state.shape[1:]
    groups = nx // FACES
    half = groups // PAIR
    hid = mid.shape[0] // 4
    x_weights = (first_x, None, mid, mid_bias, out, out_bias)
    planes = [state.at[c] for c in range(4)]

    def step_of(step, _):
        tiles = pair_tiles(planes, step, half)
        h1_pair, h2_pair, gates, fluxes = x_forward(tiles, x_weights, hid)
        for target, value in zip((h1_hi, h1_lo, h2_hi, h2_lo, gates_out), h1_pair + h2_pair + (gates,)):
            target[step] = value
        for c in range(4):
            for k in range(PAIR):
                flux[c, row_block(step + k * half + 1), :] = fluxes[c][:, k * ny : (k + 1) * ny]
        return 0

    lax.fori_loop(0, half, step_of, 0)
    for c in range(4):
        flux[c, :FACES, :] = flux[c, nx : nx + FACES, :]

    def update(group, _):
        for c in range(4):
            both = stack([flux[c, row_block(group), :], flux[c, row_block(group + 1), :]])
            middle[c, row_block(group), :] = update_cells(planes[c][row_block(group), :], both)
        return 0

    lax.fori_loop(0, groups, update, 0)


def y_order(planes):
    return [planes[0], planes[2], planes[1], planes[3]]


def lane_index(width):
    return lax.broadcasted_iota(jnp.int32, (FACES, width), 1)


def y_step(cells, cots, halo_mask, refs, acc, hid):
    weights, out_back, mid_back, first_y_back = refs
    window = split3(stack([cells[s][c] for s in range(4) for c in range(4)]))
    h1, h1_pair, h2, h2_pair, gates = limiter_forward(window, weights, hid)
    left, right = edge_states(cells, gates)
    d_flux = [courant * (cots[1][c] - cots[0][c]) for c in range(4)]
    d_left, d_right = face_flux_backward(left, right, d_flux)
    if halo_mask is not None:
        d_left = [jnp.where(halo_mask, d, 0.0) for d in d_left]
        d_right = [jnp.where(halo_mask, d, 0.0) for d in d_right]
    d3_full, direct = edge_backward(cells, gates, d_left, d_right)
    d1 = limiter_backward(d3_full, h1, h2, h1_pair, h2_pair, out_back, mid_back, acc, hid)
    d_window = first_backward(d1, first_y_back)
    if acc is not None:
        add_first_grads(window, d1, acc[0])
    return [
        [d_window[FACES * (4 * s + c) : FACES * (4 * s + c + 1)] + direct[s][c] for c in range(4)]
        for s in range(4)
    ]


def y_gather(parts, ny):
    lane = lane_index(ny)
    out = []
    for c in range(4):
        a = turn(jnp.where(lane >= 1, parts[0][c], 0.0), -1, 1)
        b = turn(jnp.where(lane < ny - 1, parts[2][c], 0.0), 1, 1)
        d = turn(jnp.where(lane < ny - 2, parts[3][c], 0.0), 2, 1)
        out.append(parts[1][c] + a + b + d)
    return out


def fold_faces(rows, hid, lanes):
    fold = pick((rows.shape[1], lanes), lambda q, n: (rest(n - q, hid) == 0) & (n >= hid) & (n < 2 * hid), F32)
    return exact(rows, fold)


def fold_first_x(acc, hid, lanes):
    r, c = rows_cols(acc.shape)
    shift = jnp.where(r < 64, (r & 15) - quot(c, hid), -1)
    parts = [
        jnp.where((shift == s) | (r >= 64) & (s == 0), acc, 0.0)[: 64 + ONES if s == 0 else 64] for s in range(4)
    ]
    folded = fold_faces(stack(parts), hid, lanes)

    def test(q, n):
        at = jnp.where(n < 64, n, n - ONES)
        return ((n < 64) | (n >= 64 + ONES)) & (q == (at >> 4)) | (n == 64) & (q == 16)

    return exact(pick((24, folded.shape[0]), test, F32), folded)


def fold_first_y(acc, hid, lanes):
    r, c = rows_cols(acc.shape)
    keep = ((r & 7) == quot(c, hid)) | (r >= 128)
    sel = lambda q, n: ((n < 128) & (q == (n >> 3))) | ((n == 128) & (q == 16))
    return exact(pick((24, acc.shape[0]), sel, F32), fold_faces(jnp.where(keep, acc, 0.0), hid, lanes))


def back_kernel(odd, state, cot, middle, own, from_first, from_second,
                first_x, first_y, first_bias, mid, mid_bias, out, out_bias,
                out_back, mid_back, first_x_back, first_y_back,
                h1_hi, h1_lo, h2_hi, h2_lo, gates_in,
                g_den, g_mom, g_tra, g_weights,
                rim_state, rim_cot, rim_flux, rim_middle, rim_grad, d_middle,
                acc_x, acc_y, acc_mid, acc_out, acc_out_bias):
    nx, ny = state.shape[1:]
    groups = nx // FACES
    half = groups // PAIR
    hid = mid.shape[0] // 4
    x_weights = (first_x, None, mid, mid_bias, out, out_bias)
    segs = ny // SEG
    rim_rows = nx // segs
    rim_groups = rim_rows // FACES
    rim_half = rim_groups // RIM_PAIR

    for acc in (acc_x, acc_y, acc_mid, acc_out, acc_out_bias):
        acc[...] = jnp.zeros(acc.shape, F32)

    lane = lane_index(ny)
    spot = lane & (SEG - 1)
    is_odd = jnp.full((FACES, ny), odd[0], jnp.int32) == 1
    for v in range(8):
        for g in range(rim_groups):
            rows = pl.ds(g * FACES, FACES)
            mine, first, second = own[v, rows, :], from_first[v, rows, :], from_second[v, rows, :]
            left, right = jnp.where(is_odd, first, second), jnp.where(is_odd, second, first)
            value = jnp.where(
                spot < RIM,
                turn(left, -RIM, 1),
                jnp.where(
                    spot < 2 * RIM,
                    turn(mine, -RIM, 1),
                    jnp.where(spot < 3 * RIM, turn(mine, RIM, 1), turn(right, RIM, 1)),
                ),
            )
            if v < 4:
                rim_state[v, rows, :] = value
                if g == 0:
                    rim_state[v, pl.ds(rim_rows, FACES), :] = turn(value, -SEG, 1)
            else:
                rim_cot[v - 4, rows, :] = value

    def rim_forward(step, _):
        sets = [
            [
                stack([
                    rim_state[c, row_block(step + k * rim_half), :],
                    rim_state[c, row_block(step + k * rim_half + 1), :],
                ])
                for c in range(4)
            ]
            for k in range(RIM_PAIR)
        ]
        tiles = [side([one[c] for one in sets]) for c in range(4)]
        fluxes = x_forward(tiles, x_weights, hid)[3]
        for c in range(4):
            for k in range(RIM_PAIR):
                rim_flux[c, row_block(step + k * rim_half + 1), :] = fluxes[c][:, k * ny : (k + 1) * ny]
        return 0

    lax.fori_loop(0, rim_half, rim_forward, 0)
    for c in range(4):
        rim_flux[c, :FACES, :] = turn(rim_flux[c, rim_rows : rim_rows + FACES, :], SEG, 1)
        for g in range(rim_groups):
            rows = pl.ds(g * FACES, FACES)
            both = stack([rim_flux[c, rows, :], rim_flux[c, pl.ds((g + 1) * FACES, FACES), :]])
            rim_middle[c, rows, :] = update_cells(rim_state[c, rows, :], both)

    refs = ((first_y, first_bias, mid, mid_bias, out, out_bias), out_back, mid_back, first_y_back)
    spot_wide = lane_index(RIM_PAIR * ny) & (SEG - 1)
    rim_faces = (spot_wide == RIM - 2) | (spot_wide == RIM - 1) | (spot_wide == 3 * RIM)

    def rim_back(step, _):
        cells = [[[] for _ in range(4)] for _ in range(4)]
        cots = [[[] for _ in range(4)] for _ in range(2)]
        for k in range(RIM_PAIR):
            rows = row_block(step + k * rim_half)
            for c in range(4):
                value = rim_middle[c, rows, :]
                for s in range(4):
                    cells[s][c].append(turn(value, 1 - s, 1))
                value = rim_cot[c, rows, :]
                for s in range(2):
                    cots[s][c].append(turn(value, -s, 1))
        cells = [y_order([side(one) for one in row]) for row in cells]
        cots = [y_order([side(one) for one in row]) for row in cots]
        parts = y_step(cells, cots, rim_faces, refs, None, hid)
        for k in range(RIM_PAIR):
            own_parts = [[one[:, k * ny : (k + 1) * ny] for one in row] for row in parts]
            gathered = y_order(y_gather(own_parts, ny))
            for c in range(4):
                rim_grad[c, row_block(step + k * rim_half), :] = gathered[c]
        return 0

    lax.fori_loop(0, rim_half, rim_back, 0)

    def main_y(step, _):
        cells = [[[] for _ in range(4)] for _ in range(4)]
        cots = [[[] for _ in range(4)] for _ in range(2)]
        for k in range(PAIR):
            group = step + k * half
            rows = row_block(group)
            seg = group // rim_groups
            rim_at = row_block(group - seg * rim_groups)
            to_low = ny - (seg * SEG + 3 * RIM)
            to_high = lax.rem(ny - 1 - (seg * SEG + RIM - 1) + ny, ny)
            for c in range(4):
                value = middle[c, rows, :]
                rim_value = rim_middle[c, rim_at, :]
                low = jnp.where(lane < 2, pltpu.roll(rim_value, to_low, 1), value)
                high = jnp.where(lane == ny - 1, pltpu.roll(rim_value, to_high, 1), value)
                cells[0][c].append(turn(high, 1, 1))
                cells[1][c].append(value)
                cells[2][c].append(turn(jnp.where(lane < 1, low, value), -1, 1))
                cells[3][c].append(turn(low, -2, 1))
                value = cot[c, rows, :]
                rim_value = rim_cot[c, rim_at, :]
                low = jnp.where(lane < 1, pltpu.roll(rim_value, to_low, 1), value)
                cots[0][c].append(value)
                cots[1][c].append(turn(low, -1, 1))
        cells = [y_order([side(one) for one in row]) for row in cells]
        cots = [y_order([side(one) for one in row]) for row in cots]
        parts = y_step(cells, cots, None, refs, (acc_y, acc_mid, acc_out, acc_out_bias), hid)
        for k in range(PAIR):
            group = step + k * half
            rows = row_block(group)
            seg = group // rim_groups
            rim_at = row_block(group - seg * rim_groups)
            own_parts = [[one[:, k * ny : (k + 1) * ny] for one in row] for row in parts]
            gathered = y_order(y_gather(own_parts, ny))
            to_low = ny - (seg * SEG + RIM)
            to_high = lax.rem(ny - 1 - (seg * SEG + 3 * RIM - 1) + ny, ny)
            for c in range(4):
                rim_value = rim_grad[c, rim_at, :]
                from_rim = jnp.where(
                    lane < 2,
                    pltpu.roll(rim_value, to_low, 1),
                    jnp.where(lane == ny - 1, pltpu.roll(rim_value, to_high, 1), 0.0),
                )
                d_middle[c, rows, :] = cot[c, rows, :] + gathered[c] + from_rim
        return 0

    lax.fori_loop(0, half, main_y, 0)

    planes = [state.at[c] for c in range(4)]
    grads = [g_den.at[0], g_mom.at[0, 0], g_mom.at[0, 1], g_tra.at[0]]
    d_planes = [d_middle.at[c] for c in range(4)]

    def main_x(step, carry):
        tiles = pair_tiles(planes, step, half)
        d_tiles = pair_tiles(d_planes, step, half)
        gates = gates_in[step]
        h1_pair = (h1_hi[step], h1_lo[step])
        h2_pair = (h2_hi[step], h2_lo[step])
        h1 = h1_pair[0].astype(F32) + h1_pair[1].astype(F32)
        h2 = h2_pair[0].astype(F32) + h2_pair[1].astype(F32)
        cells = x_cells(tiles)
        left, right = edge_states(cells, gates)
        d_flux = [courant * (turn(d, -2, 0)[:FACES] - turn(d, -1, 0)[:FACES]) for d in d_tiles]
        d_left, d_right = face_flux_backward(left, right, d_flux)
        d3_full, direct = edge_backward(cells, gates, d_left, d_right)
        d1 = limiter_backward(
            d3_full, h1, h2, h1_pair, h2_pair, out_back, mid_back, (acc_x, acc_mid, acc_out, acc_out_bias), hid
        )
        d_window = first_backward(d1, first_x_back)
        add_first_grads(split(stack(tiles)), d1, acc_x)
        later = []
        for c in range(4):
            total = d_window[2 * FACES * c : 2 * FACES * (c + 1)]
            for s in range(4):
                total = total + turn(stack([direct[s][c], jnp.zeros_like(direct[s][c])]), s, 0)
            now = total[:FACES] + d_tiles[c][:FACES] + carry[c]
            for k in range(PAIR):
                grads[c][row_block(step + k * half), :] = now[:, k * ny : (k + 1) * ny]
            later.append(total[FACES:])
        return tuple(later)

    start = tuple(jnp.zeros((FACES, PAIR * ny), F32) for _ in range(4))
    last = lax.fori_loop(0, half, main_x, start)
    for c in range(4):
        for k in range(PAIR):
            at = (k + 1) % PAIR * half * FACES
            grads[c][pl.ds(at, FACES), :] += last[c][:, k * ny : (k + 1) * ny]

    lanes = g_weights.shape[1]
    grad_first = fold_first_x(acc_x[...], hid, lanes) + fold_first_y(acc_y[...], hid, lanes)
    both = acc_mid[...]
    grad_mid = both[:hid, :hid] + both[:hid, hid:] + both[hid : 2 * hid, :hid]
    grad_mid = exact_nt(
        pick((hid, hid), lambda q, n: q == n, F32), stack([grad_mid, jnp.zeros((lanes - hid, hid), F32)])
    )
    grad_mid_bias = both[2 * hid :, :hid] + both[2 * hid :, hid:]
    r, c = rows_cols(acc_out.shape)
    grad_out = exact(
        pick((8, 64), lambda q, n: (n >> 3) == q, F32),
        fold_faces(jnp.where((r & 7) == quot(c, hid), acc_out[...], 0.0), hid, lanes),
    )
    out_bias_rows = exact_nt(jnp.ones((8, acc_out_bias.shape[1]), F32), acc_out_bias[...])
    grad_out_bias = exact_nt(out_bias_rows, pick((lanes, 64), lambda q, n: (n >> 3) == q - hid, F32))
    r, c = rows_cols((8, lanes))
    biases = jnp.where(r == 0, grad_first[16:24], jnp.where(r == 1, grad_out_bias, 0.0))
    g_weights[:hid, :] = grad_mid + stack([grad_first[:16], grad_out, biases])
    g_weights[hid:, :] = jnp.zeros((8, lanes), F32)
    g_weights[hid:, :hid] = grad_mid_bias[:8]


def finish_kernel(total, g_w_in, g_b_in, g_w_mid, g_b_mid, g_w_out, g_b_out):
    hid = g_w_mid.shape[0]
    g_w_mid[...] = total[:hid, :hid]
    beside = total[:hid, hid : 2 * hid]
    g_w_in[...] = beside[:16]
    g_w_out[...] = beside[16:24]
    g_b_in[...] = beside[24:25]
    g_b_out[...] = beside[25:26, :8]
    g_b_mid[...] = total[hid : hid + 1, :hid]


def whole(count, space=pltpu.VMEM):
    return [pl.BlockSpec(memory_space=space)] * count


def call(kernel, outs, operands, out_spaces=None, in_spaces=None, scratch=(), flops=0, moved=0):
    return pl.pallas_call(
        kernel,
        out_shape=outs,
        in_specs=in_spaces or whole(len(operands)),
        out_specs=out_spaces or whole(len(outs)),
        scratch_shapes=list(scratch),
        compiler_params=pltpu.CompilerParams(vmem_limit_bytes=VMEM_BYTES),
        cost_estimate=pl.CostEstimate(flops=flops, bytes_accessed=moved, transcendentals=0),
    )(*operands)


def sum_all(values, sizes):
    for axis, size in sizes.items():
        if size & (size - 1):
            values = lax.psum(values, axis)
            continue
        for k in range(size.bit_length() - 1):
            values = values + lax.ppermute(values, axis, [(i, i ^ (1 << k)) for i in range(size)])
    return values


def body(sizes, density, momentum, tracer, cotangent, w_in, b_in, w_mid, b_mid, w_out, b_out):
    nx, ny = density.shape[1:]
    hid = w_in.shape[0]
    wide = FACES * hid
    groups = nx // FACES
    half = groups // PAIR
    lanes = PAIR * ny
    segs = ny // SEG
    rim_rows = nx // segs
    ring = sizes["tx"] * sizes["ty"]
    shape = jax.ShapeDtypeStruct

    operands = [
        density, momentum, tracer, cotangent, w_in.T, b_in[None], w_mid, b_mid[None], w_out, b_out[None]
    ]
    rim, state, cots, *matrices = call(
        pack_kernel,
        [
            shape((8, rim_rows, ny), F32),
            shape((4, nx, ny), F32),
            shape((4, nx, ny), F32),
            shape((wide, 6 * 64 + ONES), BF16),
            shape((wide, 6 * 128), BF16),
            shape((wide, ny), F32),
            shape((4 * hid, 8 * hid), BF16),
            shape((2 * hid, ny), F32),
            shape((192, wide), BF16),
            shape((64, ny), F32),
            shape((wide, 192), BF16),
            shape((2 * hid, 6 * hid), BF16),
            shape((128, 2 * wide), BF16),
            shape((256, 2 * wide), BF16),
        ],
        [pltpu.with_memory_space_constraint(one, pltpu.HBM) for one in operands],
        in_spaces=whole(10, pltpu.HBM),
        scratch=[pltpu.VMEM(one.shape, F32) for one in operands[4:]] + [pltpu.SemaphoreType.DMA((10,))],
    )
    axes = ("tx", "ty")
    swaps = [[(i, (i + 1 if (i + first) % 2 == 0 else i - 1) % ring) for i in range(ring)] for first in range(2)]
    from_first, from_second = (lax.ppermute(rim, axes, swap) for swap in swaps)
    odd = (lax.axis_index(axes) % 2).astype(jnp.int32).reshape(1)

    middle, *kept = call(
        x_forward_kernel,
        [shape((4, nx, ny), F32)]
        + [shape((half, wide, lanes), BF16)] * 4
        + [shape((half, 64, lanes), F32)],
        [state, matrices[0]] + matrices[3:7],
        scratch=[pltpu.VMEM((4, nx + FACES, ny), F32)],
        flops=10**10,
        moved=10**7,
    )
    g_den, g_mom, g_tra, g_weights = call(
        back_kernel,
        [
            shape(density.shape, F32),
            shape(momentum.shape, F32),
            shape(tracer.shape, F32),
            shape((hid + 8, 128), F32),
        ],
        [odd, state, cots, middle, rim, from_first, from_second] + matrices + kept,
        in_spaces=whole(1, pltpu.SMEM) + whole(6 + len(matrices) + len(kept)),
        scratch=[
            pltpu.VMEM((4, rim_rows + FACES, ny), F32),
            pltpu.VMEM((4, rim_rows, ny), F32),
            pltpu.VMEM((4, rim_rows + FACES, ny), F32),
            pltpu.VMEM((4, rim_rows, ny), F32),
            pltpu.VMEM((4, rim_rows, ny), F32),
            pltpu.VMEM((4, nx, ny), F32),
            pltpu.VMEM((64 + ONES, wide), F32),
            pltpu.VMEM((128 + ONES, wide), F32),
            pltpu.VMEM((2 * hid + ONES, 2 * hid), F32),
            pltpu.VMEM((64, wide), F32),
            pltpu.VMEM((64, lanes), F32),
        ],
        flops=4 * 10**10,
        moved=2 * 10**7,
    )
    total = sum_all(g_weights, sizes)
    g_w_in, g_b_in, g_w_mid, g_b_mid, g_w_out, g_b_out = call(
        finish_kernel,
        [
            shape((w_in.shape[1], hid), F32),
            shape((1, hid), F32),
            shape(w_mid.shape, F32),
            shape((1, hid), F32),
            shape(w_out.shape, F32),
            shape((1, b_out.shape[0]), F32),
        ],
        [total],
    )
    return (g_den, g_mom, g_tra, g_w_in.T, g_b_in[0], g_w_mid, g_b_mid[0], g_w_out, g_b_out[0])


def solution(mesh):
    flow = P("traj", None, ("tx", "ty"))
    deep = P("traj", None, None, ("tx", "ty"))
    return jax.shard_map(
        functools.partial(body, dict(mesh.shape)),
        mesh=mesh,
        in_specs=(flow, deep, flow, deep) + (P(),) * 6,
        out_specs=(flow, deep, flow) + (P(),) * 6,
        check_vma=False,
    )
```

```python
import functools

import jax
import jax.numpy as jnp
from jax import lax
from jax.experimental import pallas as pl
from jax.experimental.pallas import tpu as pltpu
from jax.sharding import PartitionSpec as P

courant = 0.1
slope_gain = 0.25
F32 = jnp.float32
BF16 = jnp.bfloat16
FACES = 8
SEG = 16
RIM = 4
PAIR = 8
RIM_PAIR = 4
ONES = 16
VMEM_BYTES = 32 * 2**20


def dot(a, b):
    return lax.dot_general(a, b, (((1,), (0,)), ((), ())), preferred_element_type=F32)


def dot_nt(a, b):
    return lax.dot_general(a, b, (((1,), (1,)), ((), ())), preferred_element_type=F32)


def exact(a, b):
    return lax.dot_general(
        a, b, (((1,), (0,)), ((), ())), precision=lax.Precision.HIGHEST, preferred_element_type=F32
    )


def exact_nt(a, b):
    return lax.dot_general(
        a, b, (((1,), (1,)), ((), ())), precision=lax.Precision.HIGHEST, preferred_element_type=F32
    )


def split(values):
    high = values.astype(BF16)
    return high, (values - high.astype(F32)).astype(BF16)


def split3(values):
    high = values.astype(BF16)
    rest = values - high.astype(F32)
    middle = rest.astype(BF16)
    return high, middle, (rest - middle.astype(F32)).astype(BF16)


def rows_cols(shape):
    return lax.broadcasted_iota(jnp.int32, shape, 0), lax.broadcasted_iota(jnp.int32, shape, 1)


def quot(values, n):
    return values >> (n.bit_length() - 1) if n & (n - 1) == 0 else values // n


def rest(values, n):
    return values & (n - 1) if n & (n - 1) == 0 else values % n


def pick(shape, test, dtype=BF16):
    r, c = rows_cols(shape)
    return jnp.where(test(r, c), 1.0, 0.0).astype(dtype)


def stack(parts):
    return jnp.concatenate(parts, 0)


def side(parts):
    return jnp.concatenate(parts, 1)


STACKED = (0, 0, 0, 1, 1, 2)


def stacked(parts):
    return [parts[0], parts[1], parts[2], parts[0], parts[1], parts[0]]


def level_of(block):
    return jnp.where(block < 3, 0, jnp.where(block < 5, 1, 2))


def choose(values, levels):
    parts = [part.astype(F32) for part in split3(values)]
    total = jnp.zeros(values.shape, F32)
    for k, part in enumerate(parts):
        total = jnp.where(levels == k, part, total)
    return total


def build_first(w, b, hid):
    x_cols, y_cols, step = 6 * 64 + ONES, 6 * 128, 512

    def source(q, n):
        s = n >> 9
        m = n & (step - 1)
        in_x = (s < 4) & (m < 384) & (q == 4 * s + ((m >> 4) & 3))
        in_y = (n >= 4 * step) & (q == (((n - 4 * step) & 127) >> 3))
        return in_x | in_y

    spread_out = exact(w, pick((16, 4 * step + y_cols), source, F32))
    _, n = rows_cols(spread_out.shape)
    block = jnp.where(n < 4 * step, (n & (step - 1)) >> 6, (n - 4 * step) >> 7)
    spread_out = choose(spread_out, level_of(block))

    at, _ = rows_cols((x_cols, hid))
    rows = jnp.zeros((x_cols, hid), F32)
    for k, level in enumerate(split3(b)):
        rows = jnp.where(at == 384 + k, jnp.broadcast_to(level.astype(F32), (x_cols, hid)), rows)
    bias = dot_nt(pick((hid, hid), lambda q, n: q == n), rows.astype(BF16))

    r, c = rows_cols((FACES * hid, x_cols))
    shift = jnp.where(c < 384, (c & 15) - quot(r, hid), -1)
    first_x = stack([bias] * FACES)
    for s in range(4):
        part = spread_out[:, s * step : s * step + x_cols]
        first_x = jnp.where(shift == s, stack([part] * FACES), first_x)
    r, c = rows_cols((FACES * hid, y_cols))
    first_y = jnp.where((c & 7) == quot(r, hid), stack([spread_out[:, 4 * step :]] * FACES), 0.0)
    return first_x.astype(BF16), first_y.astype(BF16)


def build_first_back(w_t, hid):
    wide = FACES * hid

    def source(q, n):
        in_x = (q < 512) & (n == 4 * (q >> 7) + ((q & 63) >> 4))
        in_y = (q >= 512) & (n == (((q - 512) & 127) >> 3))
        return in_x | in_y

    rows = exact(pick((512 + 256, 16), source, F32), w_t)
    right = pick((hid, 2 * wide), lambda q, n: rest(n, hid) == q)
    high, low = (dot(part, right) for part in split(rows))
    r, c = rows_cols(high.shape)
    is_low = jnp.where(r < 512, r & 64, (r - 512) & 128) > 0
    value = jnp.where(is_low, jnp.where(c < wide, low, 0.0), high)
    face = quot(rest(c, wide), hid)
    r, c = r[:128], c[:128]
    shift = (r & 15) - face[:128]
    back_x = jnp.zeros((128, 2 * wide), F32)
    for s in range(4):
        back_x = jnp.where(shift == s, value[128 * s : 128 * (s + 1)], back_x)
    r, _ = rows_cols((256, 2 * wide))
    back_y = jnp.where((r & 7) == face[512:], value[512:], 0.0)
    return back_x.astype(BF16), back_y.astype(BF16)


def build_mid(w, hid):
    block = 2 * hid
    tiled = exact(w, pick((hid, 4 * block), lambda q, n: rest(n, hid) == q, F32))
    _, n = rows_cols(tiled.shape)
    upper = choose(tiled, jnp.where(n < 3 * block, 0, 2))
    lower = choose(tiled, jnp.where(n < 2 * block, 1, -1))
    r, c = rows_cols((2 * block, 4 * block))
    keep = quot(rest(r, block), hid) == quot(rest(c, block), hid)
    return jnp.where(keep, stack([upper, upper, lower, lower]), 0.0).astype(BF16)


def build_mid_back(w, hid):
    block = 2 * hid
    turned = exact_nt(pick((hid, hid), lambda q, n: q == n, F32), w)
    tiled = exact(turned, pick((hid, 3 * block), lambda q, n: rest(n, hid) == q, F32))
    _, n = rows_cols(tiled.shape)
    tiled = choose(tiled, jnp.where(quot(n, block) == 1, 1, 0))
    r, c = rows_cols((block, 3 * block))
    keep = quot(r, hid) == quot(rest(c, block), hid)
    return jnp.where(keep, stack([tiled] * 2), 0.0).astype(BF16)


def build_out(w, hid):
    wide = FACES * hid
    rows = exact(pick((64, 8), lambda q, n: (q >> 3) == n, F32), w)
    tiled = dot(stack(list(split3(rows))), pick((hid, wide), lambda q, n: rest(n, hid) == q))
    r, c = rows_cols(tiled.shape)
    return jnp.where((r & 7) == quot(c, hid), tiled, 0.0).astype(BF16)


def build_out_back(w, hid):
    wide = FACES * hid
    turned = exact_nt(pick((hid, hid), lambda q, n: q == n, F32), w)
    tiled = exact(turned, pick((8, 192), lambda q, n: ((n & 63) >> 3) == q, F32))
    _, n = rows_cols(tiled.shape)
    tiled = choose(tiled, jnp.where((n >> 6) == 1, 1, 0))
    r, c = rows_cols((wide, 192))
    return jnp.where(quot(r, hid) == (c & 7), stack([tiled] * FACES), 0.0).astype(BF16)


def spread_bias(b, lanes, copies):
    n = b.shape[1]
    rows = exact_nt(pick((n, n), lambda q, m: q == m, F32), jnp.broadcast_to(b, (lanes, n)))
    return stack([rows] * copies)


def spread(bias_ref, width):
    return side([bias_ref[...]] * (width // bias_ref.shape[1]))


def limiter_forward(first, weights, hid):
    first_ref, first_bias_ref, mid_ref, mid_bias_ref, out_ref, out_bias_ref = weights
    width = first[0].shape[1]
    if first_bias_ref is None:
        h1 = jnp.tanh(dot(first_ref[...], stack(stacked(first) + [jnp.ones((ONES, width), BF16)])))
    else:
        h1 = jnp.tanh(dot(first_ref[...], stack(stacked(first))) + spread(first_bias_ref, width))
    h1_parts = split3(h1)
    block = 2 * hid
    parts = []
    for at in range(0, FACES * hid, block):
        high, middle, low = (p[at : at + block] for p in h1_parts)
        both = dot(mid_ref[...], stack([high, middle, low, high]))
        parts.append(jnp.tanh(both[:block] + both[block:] + spread(mid_bias_ref, width)))
    h2 = stack(parts)
    h2_parts = split3(h2)
    rows = 8 * FACES
    a = dot(out_ref[...], h2_parts[0])
    b = dot(out_ref[: 2 * rows, :], h2_parts[1])
    c = dot(out_ref[:rows, :], h2_parts[2])
    gates = jnp.tanh(
        ((a[2 * rows :] + b[rows:] + c) + (a[rows : 2 * rows] + b[:rows])) + a[:rows] + spread(out_bias_ref, width)
    )
    return h1, h1_parts[:2], h2, h2_parts[:2], gates


def limiter_backward(d3, h1, h2, h1_pair, h2_pair, out_back_ref, mid_back_ref, acc, hid):
    d3_hi, d3_lo = split(d3)
    dh2 = dot(out_back_ref[...], stack([d3_hi, d3_hi, d3_lo]))
    if acc is not None:
        acc[2][...] += dot_nt(stack(list(h2_pair)), stack([d3_hi, d3_lo]))
        acc[3][...] += d3
    d2_hi, d2_lo = split(dh2 * (1.0 - h2 * h2))
    block = 2 * hid
    parts = []
    for at in range(0, FACES * hid, block):
        hi, lo = d2_hi[at : at + block], d2_lo[at : at + block]
        parts.append(dot(mid_back_ref[...], stack([hi, hi, lo])))
    if acc is not None:
        ones = jnp.ones((ONES, d3.shape[1]), BF16)
        lefts, rights = [], []
        for at in range(0, FACES * hid, hid):
            lefts.append(stack([h1_pair[0][at : at + hid], h1_pair[1][at : at + hid], ones]))
            rights.append(stack([d2_hi[at : at + hid], d2_lo[at : at + hid]]))
        acc[1][...] += dot_nt(side(lefts), side(rights))
    return stack(parts) * (1.0 - h1 * h1)


def first_backward(d1, back_ref):
    both = dot(back_ref[...], stack([d1[0], d1[1]]))
    half = both.shape[0] // 2
    return both[:half] + both[half:]


def add_first_grads(first, d1, acc_in):
    high, low = first[:2]
    both = stack(list(d1))
    if 2 * high.shape[0] + ONES <= acc_in.shape[1]:
        ones = jnp.ones((ONES, high.shape[1]), BF16)
        acc_in[:, : 2 * high.shape[0] + ONES] += dot_nt(both, stack([high, low, ones]))
    else:
        acc_in[...] += dot_nt(both, stack([high, low]))


def edge_states(cells, gates):
    left, right = [], []
    for c in range(4):
        low = gates[FACES * c : FACES * (c + 1)]
        high = gates[FACES * (c + 4) : FACES * (c + 5)]
        left.append(cells[1][c] + slope_gain * low * (cells[2][c] - cells[0][c]))
        right.append(cells[2][c] - slope_gain * high * (cells[3][c] - cells[1][c]))
    return left, right


def face_flux(left, right):
    ul = left[1] / left[0]
    ur = right[1] / right[0]
    half_speed = 0.5 * (jnp.maximum(jnp.abs(ul), jnp.abs(ur)) + 1.0)
    fl = [left[1], left[1] * ul + left[0], left[2] * ul, left[3] * ul]
    fr = [right[1], right[1] * ur + right[0], right[2] * ur, right[3] * ur]
    return [0.5 * (fl[c] + fr[c]) - half_speed * (right[c] - left[c]) for c in range(4)]


def sign_of(values):
    return jnp.where(values > 0.0, 1.0, jnp.where(values < 0.0, -1.0, 0.0))


def face_flux_backward(left, right, d_flux):
    inv_l, inv_r = 1.0 / left[0], 1.0 / right[0]
    ul, ur = left[1] / left[0], right[1] / right[0]
    al, ar = jnp.abs(ul), jnp.abs(ur)
    half_speed = 0.5 * (jnp.maximum(al, ar) + 1.0)
    d_speed = -0.5 * sum(d_flux[c] * (right[c] - left[c]) for c in range(4))
    share = jnp.where(al > ar, 1.0, jnp.where(al < ar, 0.0, 0.5))
    half = [0.5 * d for d in d_flux]
    spread = [half_speed * d for d in d_flux]

    def one(state, u, inv, speed_part, sign):
        du = half[1] * state[1] + half[2] * state[2] + half[3] * state[3] + speed_part * sign_of(u)
        over = du * inv
        return [
            half[1] - over * u + sign * spread[0],
            half[0] + half[1] * u + over + sign * spread[1],
            half[2] * u + sign * spread[2],
            half[3] * u + sign * spread[3],
        ]

    return (
        one(left, ul, inv_l, d_speed * share, 1.0),
        one(right, ur, inv_r, d_speed * (1.0 - share), -1.0),
    )


def edge_backward(cells, gates, d_left, d_right):
    lows, highs = [], []
    direct = [[None] * 4 for _ in range(4)]
    for c in range(4):
        low = gates[FACES * c : FACES * (c + 1)]
        high = gates[FACES * (c + 4) : FACES * (c + 5)]
        lows.append(slope_gain * (cells[2][c] - cells[0][c]) * d_left[c])
        highs.append(-slope_gain * (cells[3][c] - cells[1][c]) * d_right[c])
        low_part = slope_gain * low * d_left[c]
        high_part = slope_gain * high * d_right[c]
        direct[0][c] = -low_part
        direct[1][c] = d_left[c] + high_part
        direct[2][c] = d_right[c] + low_part
        direct[3][c] = -high_part
    return stack(lows + highs) * (1.0 - gates * gates), direct


def turn(values, shift, axis):
    size = values.shape[axis]
    return values if shift % size == 0 else pltpu.roll(values, shift % size, axis)


def x_cells(tiles):
    return [[turn(t, -s, 0)[:FACES] for t in tiles] for s in range(4)]


def pack_kernel(den, mom, tra, cot, w_in, b_in, w_mid, b_mid, w_out, b_out,
                rim, state, cots, first_x, first_y, first_bias, mid, mid_bias, out, out_bias,
                out_back, mid_back, first_x_back, first_y_back, *scratch):
    *small, sems = scratch
    nx, ny = den.shape[1:]
    segs = ny // SEG
    rows = nx // segs
    hid = w_in.shape[1]
    copies = [
        pltpu.make_async_copy(source, target, sems.at[k])
        for k, (source, target) in enumerate(
            list(zip([w_in, b_in, w_mid, b_mid, w_out, b_out], small))
            + [
                (den.at[0], state.at[0]),
                (mom.at[0], state.at[pl.ds(1, 2)]),
                (tra.at[0], state.at[3]),
                (cot.at[0], cots),
            ]
        )
    ]
    for one in copies:
        one.start()
    for one in copies[:6]:
        one.wait()
    w_in, b_in, w_mid, b_mid, w_out, b_out = small
    lanes = out_bias.shape[1]
    w_in_rows = exact_nt(pick((hid, hid), lambda q, n: q == n, F32), w_in[...])
    first_x[...], first_y[...] = build_first(w_in_rows, b_in[...], hid)
    first_bias[...] = spread_bias(b_in[...], lanes, FACES)
    mid[...] = build_mid(w_mid[...], hid)
    mid_bias[...] = spread_bias(b_mid[...], lanes, 2)
    out[...] = build_out(w_out[...], hid)
    out_bias[...] = exact_nt(
        pick((64, 8), lambda q, n: (q >> 3) == n, F32), jnp.broadcast_to(b_out[...], (lanes, 8))
    )
    out_back[...] = build_out_back(w_out[...], hid)
    mid_back[...] = build_mid_back(w_mid[...], hid)
    first_x_back[...], first_y_back[...] = build_first_back(w_in[...], hid)

    for one in copies[6:]:
        one.wait()
    lane = lane_index(ny)
    for v in range(8):
        plane = state.at[v] if v < 4 else cots.at[v - 4]
        for at in range(0, rows, FACES):
            total = jnp.zeros((FACES, ny), F32)
            for s in range(segs):
                first = s * SEG + RIM
                moved = turn(plane[pl.ds(s * rows + at, FACES), :], first + RIM, 1)
                total = jnp.where((lane >= first) & (lane < first + 2 * RIM), moved, total)
            rim[v, pl.ds(at, FACES), :] = total


def row_block(at):
    return pl.ds(pl.multiple_of(at * FACES, FACES), FACES)


def x_tiles(planes, group, groups):
    after = jnp.where(group + 1 == groups, 0, group + 1)
    return [stack([plane[row_block(group), :], plane[row_block(after), :]]) for plane in planes]


def pair_tiles(planes, step, half):
    sets = [x_tiles(planes, step + k * half, PAIR * half) for k in range(PAIR)]
    return [side([one[c] for one in sets]) for c in range(len(planes))]


def x_forward(tiles, weights, hid):
    h1, h1_pair, h2, h2_pair, gates = limiter_forward(split3(stack(tiles)), weights, hid)
    cells = x_cells(tiles)
    return h1_pair, h2_pair, gates, face_flux(*edge_states(cells, gates))


def update_cells(plane_rows, flux_rows):
    upper = turn(flux_rows, -7, 0)[:FACES]
    lower = turn(flux_rows, -6, 0)[:FACES]
    return plane_rows - courant * (upper - lower)


def x_forward_kernel(state, first_x, mid, mid_bias, out, out_bias,
                     middle, h1_hi, h1_lo, h2_hi, h2_lo, gates_out, flux):
    nx, ny = state.shape[1:]
    groups = nx // FACES
    half = groups // PAIR
    hid = mid.shape[0] // 4
    x_weights = (first_x, None, mid, mid_bias, out, out_bias)
    planes = [state.at[c] for c in range(4)]

    def step_of(step, _):
        tiles = pair_tiles(planes, step, half)
        h1_pair, h2_pair, gates, fluxes = x_forward(tiles, x_weights, hid)
        for target, value in zip((h1_hi, h1_lo, h2_hi, h2_lo, gates_out), h1_pair + h2_pair + (gates,)):
            target[step] = value
        for c in range(4):
            for k in range(PAIR):
                flux[c, row_block(step + k * half + 1), :] = fluxes[c][:, k * ny : (k + 1) * ny]
        return 0

    lax.fori_loop(0, half, step_of, 0)
    for c in range(4):
        flux[c, :FACES, :] = flux[c, nx : nx + FACES, :]

    def update(group, _):
        for c in range(4):
            both = stack([flux[c, row_block(group), :], flux[c, row_block(group + 1), :]])
            middle[c, row_block(group), :] = update_cells(planes[c][row_block(group), :], both)
        return 0

    lax.fori_loop(0, groups, update, 0)


def y_order(planes):
    return [planes[0], planes[2], planes[1], planes[3]]


def lane_index(width):
    return lax.broadcasted_iota(jnp.int32, (FACES, width), 1)


def y_step(cells, cots, halo_mask, refs, acc, hid):
    weights, out_back, mid_back, first_y_back = refs
    window = split3(stack([cells[s][c] for s in range(4) for c in range(4)]))
    h1, h1_pair, h2, h2_pair, gates = limiter_forward(window, weights, hid)
    left, right = edge_states(cells, gates)
    d_flux = [courant * (cots[1][c] - cots[0][c]) for c in range(4)]
    d_left, d_right = face_flux_backward(left, right, d_flux)
    if halo_mask is not None:
        d_left = [jnp.where(halo_mask, d, 0.0) for d in d_left]
        d_right = [jnp.where(halo_mask, d, 0.0) for d in d_right]
    d3_full, direct = edge_backward(cells, gates, d_left, d_right)
    d1_full = limiter_backward(d3_full, h1, h2, h1_pair, h2_pair, out_back, mid_back, acc, hid)
    d1 = split(d1_full)
    d_window = first_backward(d1, first_y_back)
    if acc is not None:
        add_first_grads(window, d1, acc[0])
        ny = acc[4].shape[1]
        acc[4][...] += sum(d1_full[:, at : at + ny] for at in range(0, d1_full.shape[1], ny))
    return [
        [d_window[FACES * (4 * s + c) : FACES * (4 * s + c + 1)] + direct[s][c] for c in range(4)]
        for s in range(4)
    ]


def y_gather(parts, ny):
    lane = lane_index(ny)
    out = []
    for c in range(4):
        a = turn(jnp.where(lane >= 1, parts[0][c], 0.0), -1, 1)
        b = turn(jnp.where(lane < ny - 1, parts[2][c], 0.0), 1, 1)
        d = turn(jnp.where(lane < ny - 2, parts[3][c], 0.0), 2, 1)
        out.append(parts[1][c] + a + b + d)
    return out


def fold_rows(values, hid):
    return sum(values[at : at + hid] for at in range(0, values.shape[0], hid))


def back_kernel(state, cot, middle, own, from_first, from_second,
                first_x, first_y, first_bias, mid, mid_bias, out, out_bias,
                out_back, mid_back, first_x_back, first_y_back,
                h1_hi, h1_lo, h2_hi, h2_lo, gates_in,
                g_den, g_mom, g_tra, g_weights,
                rim_state, rim_cot, rim_flux, rim_middle, rim_grad, d_middle,
                acc_x, acc_y, acc_y_bias, acc_mid, acc_out, acc_out_bias):
    nx, ny = state.shape[1:]
    groups = nx // FACES
    half = groups // PAIR
    hid = mid.shape[0] // 4
    x_weights = (first_x, None, mid, mid_bias, out, out_bias)
    segs = ny // SEG
    rim_rows = nx // segs
    rim_groups = rim_rows // FACES
    rim_half = rim_groups // RIM_PAIR

    for acc in (acc_x, acc_y, acc_y_bias, acc_mid, acc_out, acc_out_bias):
        acc[...] = jnp.zeros(acc.shape, F32)

    lane = lane_index(ny)
    spot = lane & (SEG - 1)
    is_odd = jnp.full((FACES, ny), lax.rem(lax.axis_index(("tx", "ty")), 2), jnp.int32) == 1
    for v in range(8):
        for g in range(rim_groups):
            rows = pl.ds(g * FACES, FACES)
            mine, first, second = own[v, rows, :], from_first[v, rows, :], from_second[v, rows, :]
            left, right = jnp.where(is_odd, first, second), jnp.where(is_odd, second, first)
            value = jnp.where(
                spot < RIM,
                turn(left, -RIM, 1),
                jnp.where(
                    spot < 2 * RIM,
                    turn(mine, -RIM, 1),
                    jnp.where(spot < 3 * RIM, turn(mine, RIM, 1), turn(right, RIM, 1)),
                ),
            )
            if v < 4:
                rim_state[v, rows, :] = value
                if g == 0:
                    rim_state[v, pl.ds(rim_rows, FACES), :] = turn(value, -SEG, 1)
            else:
                rim_cot[v - 4, rows, :] = value

    def rim_forward(step, _):
        sets = [
            [
                stack([
                    rim_state[c, row_block(step + k * rim_half), :],
                    rim_state[c, row_block(step + k * rim_half + 1), :],
                ])
                for c in range(4)
            ]
            for k in range(RIM_PAIR)
        ]
        tiles = [side([one[c] for one in sets]) for c in range(4)]
        fluxes = x_forward(tiles, x_weights, hid)[3]
        for c in range(4):
            for k in range(RIM_PAIR):
                rim_flux[c, row_block(step + k * rim_half + 1), :] = fluxes[c][:, k * ny : (k + 1) * ny]
        return 0

    lax.fori_loop(0, rim_half, rim_forward, 0)
    for c in range(4):
        rim_flux[c, :FACES, :] = turn(rim_flux[c, rim_rows : rim_rows + FACES, :], SEG, 1)
        for g in range(rim_groups):
            rows = pl.ds(g * FACES, FACES)
            both = stack([rim_flux[c, rows, :], rim_flux[c, pl.ds((g + 1) * FACES, FACES), :]])
            rim_middle[c, rows, :] = update_cells(rim_state[c, rows, :], both)

    refs = ((first_y, first_bias, mid, mid_bias, out, out_bias), out_back, mid_back, first_y_back)
    spot_wide = lane_index(RIM_PAIR * ny) & (SEG - 1)
    rim_faces = (spot_wide == RIM - 2) | (spot_wide == RIM - 1) | (spot_wide == 3 * RIM)

    def rim_back(step, _):
        cells = [[[] for _ in range(4)] for _ in range(4)]
        cots = [[[] for _ in range(4)] for _ in range(2)]
        for k in range(RIM_PAIR):
            rows = row_block(step + k * rim_half)
            for c in range(4):
                value = rim_middle[c, rows, :]
                for s in range(4):
                    cells[s][c].append(turn(value, 1 - s, 1))
                value = rim_cot[c, rows, :]
                for s in range(2):
                    cots[s][c].append(turn(value, -s, 1))
        cells = [y_order([side(one) for one in row]) for row in cells]
        cots = [y_order([side(one) for one in row]) for row in cots]
        parts = y_step(cells, cots, rim_faces, refs, None, hid)
        for k in range(RIM_PAIR):
            own_parts = [[one[:, k * ny : (k + 1) * ny] for one in row] for row in parts]
            gathered = y_order(y_gather(own_parts, ny))
            for c in range(4):
                rim_grad[c, row_block(step + k * rim_half), :] = gathered[c]
        return 0

    lax.fori_loop(0, rim_half, rim_back, 0)

    def main_y(step, _):
        cells = [[[] for _ in range(4)] for _ in range(4)]
        cots = [[[] for _ in range(4)] for _ in range(2)]
        for k in range(PAIR):
            group = step + k * half
            rows = row_block(group)
            seg = group // rim_groups
            rim_at = row_block(group - seg * rim_groups)
            to_low = ny - (seg * SEG + 3 * RIM)
            to_high = lax.rem(ny - 1 - (seg * SEG + RIM - 1) + ny, ny)
            for c in range(4):
                value = middle[c, rows, :]
                rim_value = rim_middle[c, rim_at, :]
                low = jnp.where(lane < 2, pltpu.roll(rim_value, to_low, 1), value)
                high = jnp.where(lane == ny - 1, pltpu.roll(rim_value, to_high, 1), value)
                cells[0][c].append(turn(high, 1, 1))
                cells[1][c].append(value)
                cells[2][c].append(turn(jnp.where(lane < 1, low, value), -1, 1))
                cells[3][c].append(turn(low, -2, 1))
                value = cot[c, rows, :]
                rim_value = rim_cot[c, rim_at, :]
                low = jnp.where(lane < 1, pltpu.roll(rim_value, to_low, 1), value)
                cots[0][c].append(value)
                cots[1][c].append(turn(low, -1, 1))
        cells = [y_order([side(one) for one in row]) for row in cells]
        cots = [y_order([side(one) for one in row]) for row in cots]
        parts = y_step(cells, cots, None, refs, (acc_y, acc_mid, acc_out, acc_out_bias, acc_y_bias), hid)
        for k in range(PAIR):
            group = step + k * half
            rows = row_block(group)
            seg = group // rim_groups
            rim_at = row_block(group - seg * rim_groups)
            own_parts = [[one[:, k * ny : (k + 1) * ny] for one in row] for row in parts]
            gathered = y_order(y_gather(own_parts, ny))
            to_low = ny - (seg * SEG + RIM)
            to_high = lax.rem(ny - 1 - (seg * SEG + 3 * RIM - 1) + ny, ny)
            for c in range(4):
                rim_value = rim_grad[c, rim_at, :]
                from_rim = jnp.where(
                    lane < 2,
                    pltpu.roll(rim_value, to_low, 1),
                    jnp.where(lane == ny - 1, pltpu.roll(rim_value, to_high, 1), 0.0),
                )
                d_middle[c, rows, :] = cot[c, rows, :] + gathered[c] + from_rim
        return 0

    lax.fori_loop(0, half, main_y, 0)

    planes = [state.at[c] for c in range(4)]
    grads = [g_den.at[0], g_mom.at[0, 0], g_mom.at[0, 1], g_tra.at[0]]
    d_planes = [d_middle.at[c] for c in range(4)]

    def main_x(step, carry):
        tiles = pair_tiles(planes, step, half)
        d_tiles = pair_tiles(d_planes, step, half)
        gates = gates_in[step]
        h1_pair = (h1_hi[step], h1_lo[step])
        h2_pair = (h2_hi[step], h2_lo[step])
        h1 = h1_pair[0].astype(F32) + h1_pair[1].astype(F32)
        h2 = h2_pair[0].astype(F32) + h2_pair[1].astype(F32)
        cells = x_cells(tiles)
        left, right = edge_states(cells, gates)
        d_flux = [courant * (turn(d, -2, 0)[:FACES] - turn(d, -1, 0)[:FACES]) for d in d_tiles]
        d_left, d_right = face_flux_backward(left, right, d_flux)
        d3_full, direct = edge_backward(cells, gates, d_left, d_right)
        d1_full = limiter_backward(
            d3_full, h1, h2, h1_pair, h2_pair, out_back, mid_back, (acc_x, acc_mid, acc_out, acc_out_bias), hid
        )
        d1 = split(d1_full)
        d_window = first_backward(d1, first_x_back)
        add_first_grads(split(stack(tiles)), d1, acc_x)
        later = []
        for c in range(4):
            total = d_window[2 * FACES * c : 2 * FACES * (c + 1)]
            for s in range(4):
                total = total + turn(stack([direct[s][c], jnp.zeros_like(direct[s][c])]), s, 0)
            now = total[:FACES] + d_tiles[c][:FACES] + carry[c]
            for k in range(PAIR):
                grads[c][row_block(step + k * half), :] = now[:, k * ny : (k + 1) * ny]
            later.append(total[FACES:])
        return tuple(later)

    start = tuple(jnp.zeros((FACES, PAIR * ny), F32) for _ in range(4))
    last = lax.fori_loop(0, half, main_x, start)
    for c in range(4):
        for k in range(PAIR):
            at = (k + 1) % PAIR * half * FACES
            grads[c][pl.ds(at, FACES), :] += last[c][:, k * ny : (k + 1) * ny]

    lanes = g_weights.shape[1]
    both = acc_mid[...]
    grad_mid = both[:hid, :hid] + both[:hid, hid:] + both[hid : 2 * hid, :hid]
    grad_mid = exact_nt(
        pick((hid, hid), lambda q, n: q == n, F32), stack([grad_mid, jnp.zeros((lanes - hid, hid), F32)])
    )
    grad_mid_bias = both[2 * hid :, :hid] + both[2 * hid :, hid:]
    r, c = rows_cols(acc_x.shape)
    face = rest(quot(r, hid), FACES)
    values = acc_x[...]
    found = [fold_rows(jnp.where((c & 15) - face == s, values, 0.0)[:, :128], hid) for s in range(4)]
    found.append(fold_rows(values[:, 128:], hid))
    found.append(fold_rows(jnp.where((c & 7) == face, acc_y[...], 0.0), hid))
    found.append(fold_rows(acc_y_bias[...], hid))
    found.append(fold_rows(jnp.where((c[:, :128] & 7) == face[:, :128], acc_out[...], 0.0), hid))
    found = side(found)

    def source(q, n):
        block = n >> 7
        in_x = (block < 4) & (q == 4 * block + ((n & 63) >> 4))
        in_y = (block >= 5) & (block < 7) & (q == ((n & 127) >> 3))
        in_bias = ((n == 512) | (block == 7)) & (q == 24)
        in_out = (block == 8) & (q == 16 + ((n & 63) >> 3))
        return in_x | in_y | in_bias | in_out

    beside = exact_nt(
        pick((32, found.shape[1]), source, F32),
        stack([jnp.zeros((hid, found.shape[1]), F32), found, jnp.zeros((lanes - 2 * hid, found.shape[1]), F32)]),
    )
    out_bias_rows = exact_nt(jnp.ones((8, acc_out_bias.shape[1]), F32), acc_out_bias[...])
    grad_out_bias = exact_nt(out_bias_rows, pick((lanes, 64), lambda q, n: (n >> 3) == q - hid, F32))
    r, c = rows_cols((8, lanes))
    g_weights[:hid, :] = grad_mid + beside
    g_weights[25:26, :] += grad_out_bias[:1]
    g_weights[hid:, :] = jnp.zeros((8, lanes), F32)
    g_weights[hid:, :hid] = grad_mid_bias[:8]


def finish_kernel(total, g_w_in, g_b_in, g_w_mid, g_b_mid, g_w_out, g_b_out):
    hid = g_w_mid.shape[0]
    g_w_mid[...] = total[:hid, :hid]
    beside = total[:hid, hid : 2 * hid]
    g_w_in[...] = beside[:16]
    g_w_out[...] = beside[16:24]
    g_b_in[...] = beside[24:25]
    g_b_out[...] = beside[25:26, :8]
    g_b_mid[...] = total[hid : hid + 1, :hid]


def whole(count, space=pltpu.VMEM):
    return [pl.BlockSpec(memory_space=space)] * count


def call(kernel, outs, operands, out_spaces=None, in_spaces=None, scratch=(), flops=0, moved=0):
    return pl.pallas_call(
        kernel,
        out_shape=outs,
        in_specs=in_spaces or whole(len(operands)),
        out_specs=out_spaces or whole(len(outs)),
        scratch_shapes=list(scratch),
        compiler_params=pltpu.CompilerParams(vmem_limit_bytes=VMEM_BYTES),
        cost_estimate=pl.CostEstimate(flops=flops, bytes_accessed=moved, transcendentals=0),
    )(*operands)


def sum_all(values, sizes):
    for axis, size in sizes.items():
        if size & (size - 1):
            values = lax.psum(values, axis)
            continue
        parts = [values] + [lax.ppermute(values, axis, [(i, i ^ k) for i in range(size)]) for k in range(1, size)]
        while len(parts) > 1:
            parts = [parts[k] + parts[k + 1] for k in range(0, len(parts), 2)]
        values = parts[0]
    return values


def body(sizes, density, momentum, tracer, cotangent, w_in, b_in, w_mid, b_mid, w_out, b_out):
    nx, ny = density.shape[1:]
    hid = w_in.shape[0]
    wide = FACES * hid
    groups = nx // FACES
    half = groups // PAIR
    lanes = PAIR * ny
    segs = ny // SEG
    rim_rows = nx // segs
    ring = sizes["tx"] * sizes["ty"]
    shape = jax.ShapeDtypeStruct

    operands = [
        density, momentum, tracer, cotangent, w_in.T, b_in[None], w_mid, b_mid[None], w_out, b_out[None]
    ]
    rim, state, cots, *matrices = call(
        pack_kernel,
        [
            shape((8, rim_rows, ny), F32),
            shape((4, nx, ny), F32),
            shape((4, nx, ny), F32),
            shape((wide, 6 * 64 + ONES), BF16),
            shape((wide, 6 * 128), BF16),
            shape((wide, ny), F32),
            shape((4 * hid, 8 * hid), BF16),
            shape((2 * hid, ny), F32),
            shape((192, wide), BF16),
            shape((64, ny), F32),
            shape((wide, 192), BF16),
            shape((2 * hid, 6 * hid), BF16),
            shape((128, 2 * wide), BF16),
            shape((256, 2 * wide), BF16),
        ],
        [pltpu.with_memory_space_constraint(one, pltpu.HBM) for one in operands],
        in_spaces=whole(10, pltpu.HBM),
        scratch=[pltpu.VMEM(one.shape, F32) for one in operands[4:]] + [pltpu.SemaphoreType.DMA((10,))],
    )
    axes = ("tx", "ty")
    swaps = [[(i, (i + 1 if (i + first) % 2 == 0 else i - 1) % ring) for i in range(ring)] for first in range(2)]
    from_first, from_second = (lax.ppermute(rim, axes, swap) for swap in swaps)

    middle, *kept = call(
        x_forward_kernel,
        [shape((4, nx, ny), F32)]
        + [shape((half, wide, lanes), BF16)] * 4
        + [shape((half, 64, lanes), F32)],
        [state, matrices[0]] + matrices[3:7],
        scratch=[pltpu.VMEM((4, nx + FACES, ny), F32)],
        flops=10**10,
        moved=10**7,
    )
    g_den, g_mom, g_tra, g_weights = call(
        back_kernel,
        [
            shape(density.shape, F32),
            shape(momentum.shape, F32),
            shape(tracer.shape, F32),
            shape((hid + 8, 128), F32),
        ],
        [state, cots, middle, rim, from_first, from_second] + matrices + kept,
        scratch=[
            pltpu.VMEM((4, rim_rows + FACES, ny), F32),
            pltpu.VMEM((4, rim_rows, ny), F32),
            pltpu.VMEM((4, rim_rows + FACES, ny), F32),
            pltpu.VMEM((4, rim_rows, ny), F32),
            pltpu.VMEM((4, rim_rows, ny), F32),
            pltpu.VMEM((4, nx, ny), F32),
            pltpu.VMEM((2 * wide, 256), F32),
            pltpu.VMEM((2 * wide, 256), F32),
            pltpu.VMEM((wide, ny), F32),
            pltpu.VMEM((2 * hid + ONES, 2 * hid), F32),
            pltpu.VMEM((2 * wide, 128), F32),
            pltpu.VMEM((64, lanes), F32),
        ],
        flops=4 * 10**10,
        moved=2 * 10**7,
    )
    total = sum_all(g_weights, sizes)
    g_w_in, g_b_in, g_w_mid, g_b_mid, g_w_out, g_b_out = call(
        finish_kernel,
        [
            shape((w_in.shape[1], hid), F32),
            shape((1, hid), F32),
            shape(w_mid.shape, F32),
            shape((1, hid), F32),
            shape(w_out.shape, F32),
            shape((1, b_out.shape[0]), F32),
        ],
        [total],
    )
    return (g_den, g_mom, g_tra, g_w_in.T, g_b_in[0], g_w_mid, g_b_mid[0], g_w_out, g_b_out[0])


def solution(mesh):
    flow = P("traj", None, ("tx", "ty"))
    deep = P("traj", None, None, ("tx", "ty"))
    return jax.shard_map(
        functools.partial(body, dict(mesh.shape)),
        mesh=mesh,
        in_specs=(flow, deep, flow, deep) + (P(),) * 6,
        out_specs=(flow, deep, flow) + (P(),) * 6,
        check_vma=False,
    )
```

```python
import functools

import jax
import jax.numpy as jnp
from jax import lax
from jax.experimental import pallas as pl
from jax.experimental.pallas import tpu as pltpu
from jax.sharding import PartitionSpec as P

courant = 0.1
slope_gain = 0.25
F32 = jnp.float32
BF16 = jnp.bfloat16
FACES = 8
SEG = 16
RIM = 4
PAIR = 8
RIM_PAIR = 4
ONES = 16
VMEM_BYTES = 32 * 2**20


def dot(a, b):
    return lax.dot_general(a, b, (((1,), (0,)), ((), ())), preferred_element_type=F32)


def dot_nt(a, b):
    return lax.dot_general(a, b, (((1,), (1,)), ((), ())), preferred_element_type=F32)


def exact(a, b):
    return lax.dot_general(
        a, b, (((1,), (0,)), ((), ())), precision=lax.Precision.HIGHEST, preferred_element_type=F32
    )


def exact_nt(a, b):
    return lax.dot_general(
        a, b, (((1,), (1,)), ((), ())), precision=lax.Precision.HIGHEST, preferred_element_type=F32
    )


def split(values):
    high = values.astype(BF16)
    return high, (values - high.astype(F32)).astype(BF16)


def split3(values):
    high = values.astype(BF16)
    rest = values - high.astype(F32)
    middle = rest.astype(BF16)
    return high, middle, (rest - middle.astype(F32)).astype(BF16)


def rows_cols(shape):
    return lax.broadcasted_iota(jnp.int32, shape, 0), lax.broadcasted_iota(jnp.int32, shape, 1)


def quot(values, n):
    return values >> (n.bit_length() - 1) if n & (n - 1) == 0 else values // n


def rest(values, n):
    return values & (n - 1) if n & (n - 1) == 0 else values % n


def pick(shape, test, dtype=BF16):
    r, c = rows_cols(shape)
    return jnp.where(test(r, c), 1.0, 0.0).astype(dtype)


def stack(parts):
    return jnp.concatenate(parts, 0)


def side(parts):
    return jnp.concatenate(parts, 1)


STACKED = (0, 0, 0, 1, 1, 2)


def stacked(parts):
    return [parts[0], parts[1], parts[2], parts[0], parts[1], parts[0]]


def level_of(block):
    return jnp.where(block < 3, 0, jnp.where(block < 5, 1, 2))


def choose(values, levels):
    parts = [part.astype(F32) for part in split3(values)]
    total = jnp.zeros(values.shape, F32)
    for k, part in enumerate(parts):
        total = jnp.where(levels == k, part, total)
    return total


def build_first(w, b, hid):
    x_cols, y_cols, step = 6 * 32 + ONES, 6 * 128, 256

    def source(q, n):
        s = n >> 8
        m = n & (step - 1)
        in_x = (s < 4) & (m < 192) & (q == 4 * s + ((m & 31) >> 3))
        in_y = (n >= 4 * step) & (q == (((n - 4 * step) & 127) >> 3))
        return in_x | in_y

    spread_out = exact(w, pick((16, 4 * step + y_cols), source, F32))
    _, n = rows_cols(spread_out.shape)
    block = jnp.where(n < 4 * step, (n & (step - 1)) >> 5, (n - 4 * step) >> 7)
    spread_out = choose(spread_out, level_of(block))

    at, _ = rows_cols((x_cols, hid))
    rows = jnp.zeros((x_cols, hid), F32)
    for k, level in enumerate(split3(b)):
        rows = jnp.where(at == 192 + k, jnp.broadcast_to(level.astype(F32), (x_cols, hid)), rows)
    bias = dot_nt(pick((hid, hid), lambda q, n: q == n), rows.astype(BF16))

    r, c = rows_cols((FACES // 2 * hid, x_cols))
    shift = jnp.where(c < 192, (c & 7) - quot(r, hid), -1)
    first_x = stack([bias] * (FACES // 2))
    for s in range(4):
        part = spread_out[:, s * step : s * step + x_cols]
        first_x = jnp.where(shift == s, stack([part] * (FACES // 2)), first_x)
    r, c = rows_cols((FACES * hid, y_cols))
    first_y = jnp.where((c & 7) == quot(r, hid), stack([spread_out[:, 4 * step :]] * FACES), 0.0)
    return first_x.astype(BF16), first_y.astype(BF16)


def build_first_back(w_t, hid):
    wide = FACES * hid

    def source(q, n):
        in_x = (q < 256) & (n == 4 * (q >> 6) + ((q & 63) >> 4))
        in_y = (q >= 256) & (n == ((q - 256) >> 3))
        return in_x | in_y

    rows = exact(pick((256 + 128, 16), source, F32), w_t).astype(BF16)
    value = dot(rows, pick((hid, wide), lambda q, n: rest(n, hid) == q))
    r, c = rows_cols((64, wide))
    shift = (r & 15) - quot(c, hid)
    back_x = jnp.zeros((64, wide), F32)
    for s in range(4):
        back_x = jnp.where(shift == s, value[64 * s : 64 * (s + 1)], back_x)
    r, c = rows_cols((128, wide))
    back_y = jnp.where((r & 7) == quot(c, hid), value[256:], 0.0)
    return back_x.astype(BF16), back_y.astype(BF16)


def build_mid(w, hid):
    block = 2 * hid
    tiled = exact(w, pick((hid, 4 * block), lambda q, n: rest(n, hid) == q, F32))
    _, n = rows_cols(tiled.shape)
    upper = choose(tiled, jnp.where(n < 3 * block, 0, 2))
    lower = choose(tiled, jnp.where(n < 2 * block, 1, -1))
    r, c = rows_cols((2 * block, 4 * block))
    keep = quot(rest(r, block), hid) == quot(rest(c, block), hid)
    return jnp.where(keep, stack([upper, upper, lower, lower]), 0.0).astype(BF16)


def build_mid_back(w, hid):
    block = 2 * hid
    turned = exact_nt(pick((hid, hid), lambda q, n: q == n, F32), w)
    tiled = exact(turned, pick((hid, 3 * block), lambda q, n: rest(n, hid) == q, F32))
    _, n = rows_cols(tiled.shape)
    tiled = choose(tiled, jnp.where(quot(n, block) == 1, 1, 0))
    r, c = rows_cols((block, 3 * block))
    keep = quot(r, hid) == quot(rest(c, block), hid)
    return jnp.where(keep, stack([tiled] * 2), 0.0).astype(BF16)


def build_out(w, hid):
    wide = FACES * hid
    rows = exact(pick((64, 8), lambda q, n: (q >> 3) == n, F32), w)
    tiled = dot(stack(list(split3(rows))), pick((hid, wide), lambda q, n: rest(n, hid) == q))
    r, c = rows_cols(tiled.shape)
    return jnp.where((r & 7) == quot(c, hid), tiled, 0.0).astype(BF16)


def build_out_back(w, hid):
    wide = FACES * hid
    turned = exact_nt(pick((hid, hid), lambda q, n: q == n, F32), w)
    tiled = exact(turned, pick((8, 192), lambda q, n: ((n & 63) >> 3) == q, F32))
    _, n = rows_cols(tiled.shape)
    tiled = choose(tiled, jnp.where((n >> 6) == 1, 1, 0))
    r, c = rows_cols((wide, 192))
    return jnp.where(quot(r, hid) == (c & 7), stack([tiled] * FACES), 0.0).astype(BF16)


def spread_bias(b, lanes, copies):
    n = b.shape[1]
    rows = exact_nt(pick((n, n), lambda q, m: q == m, F32), jnp.broadcast_to(b, (lanes, n)))
    return stack([rows] * copies)


def spread(bias_ref, width):
    return side([bias_ref[...]] * (width // bias_ref.shape[1]))


def limiter_forward(first, weights, hid):
    first_ref, first_bias_ref, mid_ref, mid_bias_ref, out_ref, out_bias_ref = weights
    width = first[0][0].shape[1]
    if first_bias_ref is None:
        ones = [jnp.ones((ONES, width), BF16)]
        h1 = stack([jnp.tanh(dot(first_ref[...], stack(stacked(one) + ones))) for one in first])
    else:
        h1 = jnp.tanh(dot(first_ref[...], stack(stacked(first[0]))) + spread(first_bias_ref, width))
    h1_parts = split3(h1)
    block = 2 * hid
    parts = []
    for at in range(0, FACES * hid, block):
        high, middle, low = (p[at : at + block] for p in h1_parts)
        both = dot(mid_ref[...], stack([high, middle, low, high]))
        parts.append(jnp.tanh(both[:block] + both[block:] + spread(mid_bias_ref, width)))
    h2 = stack(parts)
    h2_parts = split3(h2)
    rows = 8 * FACES
    a = dot(out_ref[...], h2_parts[0])
    b = dot(out_ref[: 2 * rows, :], h2_parts[1])
    c = dot(out_ref[:rows, :], h2_parts[2])
    gates = jnp.tanh(
        ((a[2 * rows :] + b[rows:] + c) + (a[rows : 2 * rows] + b[:rows])) + a[:rows] + spread(out_bias_ref, width)
    )
    return h1, h1_parts[:2], h2, h2_parts[:2], gates


def limiter_backward(d3, h1, h2, h1_pair, h2_pair, out_back_ref, mid_back_ref, acc, hid):
    d3_hi, d3_lo = split(d3)
    dh2 = dot(out_back_ref[...], stack([d3_hi, d3_hi, d3_lo]))
    if acc is not None:
        acc[2][...] += dot_nt(stack(list(h2_pair)), stack([d3_hi, d3_lo]))
        acc[3][...] += d3
    d2_hi, d2_lo = split(dh2 * (1.0 - h2 * h2))
    block = 2 * hid
    parts = []
    for at in range(0, FACES * hid, block):
        hi, lo = d2_hi[at : at + block], d2_lo[at : at + block]
        parts.append(dot(mid_back_ref[...], stack([hi, hi, lo])))
    if acc is not None:
        ones = jnp.ones((ONES, d3.shape[1]), BF16)
        lefts, rights = [], []
        for at in range(0, FACES * hid, 2 * block):
            lefts.append(stack([part[at : at + 2 * block] for part in h1_pair] + [ones]))
            rights.append(stack([part[at : at + 2 * block] for part in (d2_hi, d2_lo)]))
        acc[1][...] += dot_nt(side(lefts), side(rights))
    return stack(parts) * (1.0 - h1 * h1)


def add_first_grads(first, d1, acc_in):
    high, low = first[:2]
    both = stack(list(d1))
    if 2 * high.shape[0] + ONES <= acc_in.shape[1]:
        ones = jnp.ones((ONES, high.shape[1]), BF16)
        acc_in[:, : 2 * high.shape[0] + ONES] += dot_nt(both, stack([high, low, ones]))
    else:
        acc_in[...] += dot_nt(both, stack([high, low]))


def edge_states(cells, gates):
    left, right = [], []
    for c in range(4):
        low = gates[FACES * c : FACES * (c + 1)]
        high = gates[FACES * (c + 4) : FACES * (c + 5)]
        left.append(cells[1][c] + slope_gain * low * (cells[2][c] - cells[0][c]))
        right.append(cells[2][c] - slope_gain * high * (cells[3][c] - cells[1][c]))
    return left, right


def face_flux(left, right):
    ul = left[1] / left[0]
    ur = right[1] / right[0]
    half_speed = 0.5 * (jnp.maximum(jnp.abs(ul), jnp.abs(ur)) + 1.0)
    fl = [left[1], left[1] * ul + left[0], left[2] * ul, left[3] * ul]
    fr = [right[1], right[1] * ur + right[0], right[2] * ur, right[3] * ur]
    return [0.5 * (fl[c] + fr[c]) - half_speed * (right[c] - left[c]) for c in range(4)]


def sign_of(values):
    return jnp.where(values > 0.0, 1.0, jnp.where(values < 0.0, -1.0, 0.0))


def face_flux_backward(left, right, d_flux):
    inv_l, inv_r = 1.0 / left[0], 1.0 / right[0]
    ul, ur = left[1] / left[0], right[1] / right[0]
    al, ar = jnp.abs(ul), jnp.abs(ur)
    half_speed = 0.5 * (jnp.maximum(al, ar) + 1.0)
    d_speed = -0.5 * sum(d_flux[c] * (right[c] - left[c]) for c in range(4))
    share = jnp.where(al > ar, 1.0, jnp.where(al < ar, 0.0, 0.5))
    half = [0.5 * d for d in d_flux]
    spread = [half_speed * d for d in d_flux]

    def one(state, u, inv, speed_part, sign):
        du = half[1] * state[1] + half[2] * state[2] + half[3] * state[3] + speed_part * sign_of(u)
        over = du * inv
        return [
            half[1] - over * u + sign * spread[0],
            half[0] + half[1] * u + over + sign * spread[1],
            half[2] * u + sign * spread[2],
            half[3] * u + sign * spread[3],
        ]

    return (
        one(left, ul, inv_l, d_speed * share, 1.0),
        one(right, ur, inv_r, d_speed * (1.0 - share), -1.0),
    )


def edge_backward(cells, gates, d_left, d_right):
    lows, highs = [], []
    direct = [[None] * 4 for _ in range(4)]
    for c in range(4):
        low = gates[FACES * c : FACES * (c + 1)]
        high = gates[FACES * (c + 4) : FACES * (c + 5)]
        lows.append(slope_gain * (cells[2][c] - cells[0][c]) * d_left[c])
        highs.append(-slope_gain * (cells[3][c] - cells[1][c]) * d_right[c])
        low_part = slope_gain * low * d_left[c]
        high_part = slope_gain * high * d_right[c]
        direct[0][c] = -low_part
        direct[1][c] = d_left[c] + high_part
        direct[2][c] = d_right[c] + low_part
        direct[3][c] = -high_part
    return stack(lows + highs) * (1.0 - gates * gates), direct


def turn(values, shift, axis):
    size = values.shape[axis]
    return values if shift % size == 0 else pltpu.roll(values, shift % size, axis)


def x_cells(tiles):
    return [[turn(t, -s, 0)[:FACES] for t in tiles] for s in range(4)]


def pack_kernel(den, mom, tra, cot, w_in, b_in, w_mid, b_mid, w_out, b_out,
                rim, to_first, to_second, state, cots, first_x, first_y, first_bias, mid, mid_bias, out, out_bias,
                out_back, mid_back, first_x_back, first_y_back, *scratch):
    *small, sems = scratch
    nx, ny = den.shape[1:]
    segs = ny // SEG
    rows = nx // segs
    hid = w_in.shape[1]
    copies = [
        pltpu.make_async_copy(source, target, sems.at[k])
        for k, (source, target) in enumerate(
            list(zip([w_in, b_in, w_mid, b_mid, w_out, b_out], small))
            + [
                (den.at[0], state.at[0]),
                (mom.at[0], state.at[pl.ds(1, 2)]),
                (tra.at[0], state.at[3]),
                (cot.at[0], cots),
            ]
        )
    ]
    for one in copies:
        one.start()
    for one in copies[:6]:
        one.wait()
    w_in, b_in, w_mid, b_mid, w_out, b_out = small
    lanes = out_bias.shape[1]
    w_in_rows = exact_nt(pick((hid, hid), lambda q, n: q == n, F32), w_in[...])
    first_x[...], first_y[...] = build_first(w_in_rows, b_in[...], hid)
    first_bias[...] = spread_bias(b_in[...], lanes, FACES)
    mid[...] = build_mid(w_mid[...], hid)
    mid_bias[...] = spread_bias(b_mid[...], lanes, 2)
    out[...] = build_out(w_out[...], hid)
    out_bias[...] = exact_nt(
        pick((64, 8), lambda q, n: (q >> 3) == n, F32), jnp.broadcast_to(b_out[...], (lanes, 8))
    )
    out_back[...] = build_out_back(w_out[...], hid)
    mid_back[...] = build_mid_back(w_mid[...], hid)
    first_x_back[...], first_y_back[...] = build_first_back(w_in[...], hid)

    for one in copies[6:]:
        one.wait()
    lane = lane_index(ny)
    for v in range(8):
        plane = state.at[v] if v < 4 else cots.at[v - 4]
        for at in range(0, rows, FACES):
            total = jnp.zeros((FACES, ny), F32)
            for s in range(segs):
                first = s * SEG + RIM
                moved = turn(plane[pl.ds(s * rows + at, FACES), :], first + RIM, 1)
                total = jnp.where((lane >= first) & (lane < first + 2 * RIM), moved, total)
            rim[v, pl.ds(at, FACES), :] = total
    is_odd = odd_mask(ny)
    spot = lane & (SEG - 1)
    for v in range(8):
        sides = []
        for first in (2 * RIM, RIM):
            total = jnp.zeros((FACES, ny), F32)
            for g in range(rows // FACES):
                moved = turn(rim[v, pl.ds(g * FACES, FACES), :], g * RIM - first, 1)
                total = jnp.where((spot >= g * RIM) & (spot < (g + 1) * RIM), moved, total)
            sides.append(total)
        to_first[v] = jnp.where(is_odd, sides[0], sides[1])
        to_second[v] = jnp.where(is_odd, sides[1], sides[0])


def odd_mask(ny):
    return jnp.full((FACES, ny), lax.rem(lax.axis_index(("tx", "ty")), 2), jnp.int32) == 1


def row_block(at):
    return pl.ds(pl.multiple_of(at * FACES, FACES), FACES)


def x_tiles(planes, group, groups):
    after = jnp.where(group + 1 == groups, 0, group + 1)
    return [stack([plane[row_block(group), :], plane[row_block(after), :]]) for plane in planes]


def pair_tiles(planes, step, half):
    sets = [x_tiles(planes, step + k * half, PAIR * half) for k in range(PAIR)]
    return [side([one[c] for one in sets]) for c in range(len(planes))]


def x_windows(tiles):
    half = FACES // 2
    return [split3(stack([turn(tile, -at, 0)[:FACES] for tile in tiles])) for at in (0, half)]


def x_forward(tiles, weights, hid):
    h1, h1_pair, h2, h2_pair, gates = limiter_forward(x_windows(tiles), weights, hid)
    cells = x_cells(tiles)
    return h1_pair, h2_pair, gates, face_flux(*edge_states(cells, gates))


def update_cells(plane_rows, flux_rows):
    upper = turn(flux_rows, -7, 0)[:FACES]
    lower = turn(flux_rows, -6, 0)[:FACES]
    return plane_rows - courant * (upper - lower)


def x_forward_kernel(state, first_x, mid, mid_bias, out, out_bias,
                     middle, h1_hi, h1_lo, h2_hi, h2_lo, gates_out, flux):
    nx, ny = state.shape[1:]
    groups = nx // FACES
    half = groups // PAIR
    hid = mid.shape[0] // 4
    x_weights = (first_x, None, mid, mid_bias, out, out_bias)
    planes = [state.at[c] for c in range(4)]

    def step_of(step, _):
        tiles = pair_tiles(planes, step, half)
        h1_pair, h2_pair, gates, fluxes = x_forward(tiles, x_weights, hid)
        for target, value in zip((h1_hi, h1_lo, h2_hi, h2_lo, gates_out), h1_pair + h2_pair + (gates,)):
            target[step] = value
        for c in range(4):
            for k in range(PAIR):
                flux[c, row_block(step + k * half + 1), :] = fluxes[c][:, k * ny : (k + 1) * ny]
        return 0

    lax.fori_loop(0, half, step_of, 0)
    for c in range(4):
        flux[c, :FACES, :] = flux[c, nx : nx + FACES, :]

    def update(group, _):
        for c in range(4):
            both = stack([flux[c, row_block(group), :], flux[c, row_block(group + 1), :]])
            middle[c, row_block(group), :] = update_cells(planes[c][row_block(group), :], both)
        return 0

    lax.fori_loop(0, groups, update, 0)


def y_order(planes):
    return [planes[0], planes[2], planes[1], planes[3]]


def lane_index(width):
    return lax.broadcasted_iota(jnp.int32, (FACES, width), 1)


def y_step(cells, cots, halo_mask, refs, acc, hid):
    weights, out_back, mid_back, first_y_back = refs
    window = split3(stack([cells[s][c] for s in range(4) for c in range(4)]))
    h1, h1_pair, h2, h2_pair, gates = limiter_forward([window], weights, hid)
    left, right = edge_states(cells, gates)
    d_flux = [courant * (cots[1][c] - cots[0][c]) for c in range(4)]
    d_left, d_right = face_flux_backward(left, right, d_flux)
    if halo_mask is not None:
        d_left = [jnp.where(halo_mask, d, 0.0) for d in d_left]
        d_right = [jnp.where(halo_mask, d, 0.0) for d in d_right]
    d3_full, direct = edge_backward(cells, gates, d_left, d_right)
    d1_full = limiter_backward(d3_full, h1, h2, h1_pair, h2_pair, out_back, mid_back, acc, hid)
    d1 = split(d1_full)
    d_window = dot(first_y_back[...], d1[0])
    if acc is not None:
        add_first_grads(window, d1, acc[0])
        ny = acc[4].shape[1]
        acc[4][...] += sum(d1_full[:, at : at + ny] for at in range(0, d1_full.shape[1], ny))
    return [
        [d_window[FACES * (4 * s + c) : FACES * (4 * s + c + 1)] + direct[s][c] for c in range(4)]
        for s in range(4)
    ]


def y_gather(parts, ny):
    lane = lane_index(ny)
    out = []
    for c in range(4):
        a = turn(jnp.where(lane >= 1, parts[0][c], 0.0), -1, 1)
        b = turn(jnp.where(lane < ny - 1, parts[2][c], 0.0), 1, 1)
        d = turn(jnp.where(lane < ny - 2, parts[3][c], 0.0), 2, 1)
        out.append(parts[1][c] + a + b + d)
    return out


def fold_rows(values, hid):
    return sum(values[at : at + hid] for at in range(0, values.shape[0], hid))


def back_kernel(state, cot, middle, own, from_first, from_second,
                first_x, first_y, first_bias, mid, mid_bias, out, out_bias,
                out_back, mid_back, first_x_back, first_y_back,
                h1_hi, h1_lo, h2_hi, h2_lo, gates_in,
                g_den, g_mom, g_tra, g_weights,
                rim_state, rim_cot, rim_flux, rim_middle, rim_grad, d_middle,
                acc_x, acc_y, acc_y_bias, acc_mid, acc_out, acc_out_bias):
    nx, ny = state.shape[1:]
    groups = nx // FACES
    half = groups // PAIR
    hid = mid.shape[0] // 4
    x_weights = (first_x, None, mid, mid_bias, out, out_bias)
    segs = ny // SEG
    rim_rows = nx // segs
    rim_groups = rim_rows // FACES
    rim_half = rim_groups // RIM_PAIR

    for acc in (acc_x, acc_y, acc_y_bias, acc_mid, acc_out, acc_out_bias):
        acc[...] = jnp.zeros(acc.shape, F32)

    lane = lane_index(ny)
    spot = lane & (SEG - 1)
    is_odd = odd_mask(ny)
    for v in range(8):
        for g in range(rim_groups):
            rows = pl.ds(g * FACES, FACES)
            mine, first, second = own[v, rows, :], from_first[v], from_second[v]
            left, right = jnp.where(is_odd, first, second), jnp.where(is_odd, second, first)
            value = jnp.where(
                spot < RIM,
                turn(left, -g * RIM, 1),
                jnp.where(
                    spot < 2 * RIM,
                    turn(mine, -RIM, 1),
                    jnp.where(spot < 3 * RIM, turn(mine, RIM, 1), turn(right, (3 - g) * RIM, 1)),
                ),
            )
            if v < 4:
                rim_state[v, rows, :] = value
                if g == 0:
                    rim_state[v, pl.ds(rim_rows, FACES), :] = turn(value, -SEG, 1)
            else:
                rim_cot[v - 4, rows, :] = value

    def rim_forward(step, _):
        sets = [
            [
                stack([
                    rim_state[c, row_block(step + k * rim_half), :],
                    rim_state[c, row_block(step + k * rim_half + 1), :],
                ])
                for c in range(4)
            ]
            for k in range(RIM_PAIR)
        ]
        tiles = [side([one[c] for one in sets]) for c in range(4)]
        fluxes = x_forward(tiles, x_weights, hid)[3]
        for c in range(4):
            for k in range(RIM_PAIR):
                rim_flux[c, row_block(step + k * rim_half + 1), :] = fluxes[c][:, k * ny : (k + 1) * ny]
        return 0

    lax.fori_loop(0, rim_half, rim_forward, 0)
    for c in range(4):
        rim_flux[c, :FACES, :] = turn(rim_flux[c, rim_rows : rim_rows + FACES, :], SEG, 1)
        for g in range(rim_groups):
            rows = pl.ds(g * FACES, FACES)
            both = stack([rim_flux[c, rows, :], rim_flux[c, pl.ds((g + 1) * FACES, FACES), :]])
            rim_middle[c, rows, :] = update_cells(rim_state[c, rows, :], both)

    refs = ((first_y, first_bias, mid, mid_bias, out, out_bias), out_back, mid_back, first_y_back)
    spot_wide = lane_index(RIM_PAIR * ny) & (SEG - 1)
    rim_faces = (spot_wide == RIM - 2) | (spot_wide == RIM - 1) | (spot_wide == 3 * RIM)

    def rim_back(step, _):
        cells = [[[] for _ in range(4)] for _ in range(4)]
        cots = [[[] for _ in range(4)] for _ in range(2)]
        for k in range(RIM_PAIR):
            rows = row_block(step + k * rim_half)
            for c in range(4):
                value = rim_middle[c, rows, :]
                for s in range(4):
                    cells[s][c].append(turn(value, 1 - s, 1))
                value = rim_cot[c, rows, :]
                for s in range(2):
                    cots[s][c].append(turn(value, -s, 1))
        cells = [y_order([side(one) for one in row]) for row in cells]
        cots = [y_order([side(one) for one in row]) for row in cots]
        parts = y_step(cells, cots, rim_faces, refs, None, hid)
        for k in range(RIM_PAIR):
            own_parts = [[one[:, k * ny : (k + 1) * ny] for one in row] for row in parts]
            gathered = y_order(y_gather(own_parts, ny))
            for c in range(4):
                rim_grad[c, row_block(step + k * rim_half), :] = gathered[c]
        return 0

    lax.fori_loop(0, rim_half, rim_back, 0)

    def main_y(step, _):
        cells = [[[] for _ in range(4)] for _ in range(4)]
        cots = [[[] for _ in range(4)] for _ in range(2)]
        for k in range(PAIR):
            group = step + k * half
            rows = row_block(group)
            seg = group // rim_groups
            rim_at = row_block(group - seg * rim_groups)
            to_low = ny - (seg * SEG + 3 * RIM)
            to_high = lax.rem(ny - 1 - (seg * SEG + RIM - 1) + ny, ny)
            for c in range(4):
                value = middle[c, rows, :]
                rim_value = rim_middle[c, rim_at, :]
                low = jnp.where(lane < 2, pltpu.roll(rim_value, to_low, 1), value)
                high = jnp.where(lane == ny - 1, pltpu.roll(rim_value, to_high, 1), value)
                cells[0][c].append(turn(high, 1, 1))
                cells[1][c].append(value)
                cells[2][c].append(turn(jnp.where(lane < 1, low, value), -1, 1))
                cells[3][c].append(turn(low, -2, 1))
                value = cot[c, rows, :]
                rim_value = rim_cot[c, rim_at, :]
                low = jnp.where(lane < 1, pltpu.roll(rim_value, to_low, 1), value)
                cots[0][c].append(value)
                cots[1][c].append(turn(low, -1, 1))
        cells = [y_order([side(one) for one in row]) for row in cells]
        cots = [y_order([side(one) for one in row]) for row in cots]
        parts = y_step(cells, cots, None, refs, (acc_y, acc_mid, acc_out, acc_out_bias, acc_y_bias), hid)
        for k in range(PAIR):
            group = step + k * half
            rows = row_block(group)
            seg = group // rim_groups
            rim_at = row_block(group - seg * rim_groups)
            own_parts = [[one[:, k * ny : (k + 1) * ny] for one in row] for row in parts]
            gathered = y_order(y_gather(own_parts, ny))
            to_low = ny - (seg * SEG + RIM)
            to_high = lax.rem(ny - 1 - (seg * SEG + 3 * RIM - 1) + ny, ny)
            for c in range(4):
                rim_value = rim_grad[c, rim_at, :]
                from_rim = jnp.where(
                    lane < 2,
                    pltpu.roll(rim_value, to_low, 1),
                    jnp.where(lane == ny - 1, pltpu.roll(rim_value, to_high, 1), 0.0),
                )
                d_middle[c, rows, :] = cot[c, rows, :] + gathered[c] + from_rim
        return 0

    lax.fori_loop(0, half, main_y, 0)

    planes = [state.at[c] for c in range(4)]
    grads = [g_den.at[0], g_mom.at[0, 0], g_mom.at[0, 1], g_tra.at[0]]
    d_planes = [d_middle.at[c] for c in range(4)]

    def main_x(step, carry):
        tiles = pair_tiles(planes, step, half)
        d_tiles = pair_tiles(d_planes, step, half)
        gates = gates_in[step]
        h1_pair = (h1_hi[step], h1_lo[step])
        h2_pair = (h2_hi[step], h2_lo[step])
        h1 = h1_pair[0].astype(F32) + h1_pair[1].astype(F32)
        h2 = h2_pair[0].astype(F32) + h2_pair[1].astype(F32)
        cells = x_cells(tiles)
        left, right = edge_states(cells, gates)
        d_flux = [courant * (turn(d, -2, 0)[:FACES] - turn(d, -1, 0)[:FACES]) for d in d_tiles]
        d_left, d_right = face_flux_backward(left, right, d_flux)
        d3_full, direct = edge_backward(cells, gates, d_left, d_right)
        d1_full = limiter_backward(
            d3_full, h1, h2, h1_pair, h2_pair, out_back, mid_back, (acc_x, acc_mid, acc_out, acc_out_bias), hid
        )
        d1 = split(d1_full)
        d_window = dot(first_x_back[...], d1[0])
        add_first_grads(split(stack(tiles)), d1, acc_x)
        later = []
        for c in range(4):
            total = d_window[2 * FACES * c : 2 * FACES * (c + 1)]
            for s in range(4):
                total = total + turn(stack([direct[s][c], jnp.zeros_like(direct[s][c])]), s, 0)
            now = total[:FACES] + d_tiles[c][:FACES] + carry[c]
            for k in range(PAIR):
                grads[c][row_block(step + k * half), :] = now[:, k * ny : (k + 1) * ny]
            later.append(total[FACES:])
        return tuple(later)

    start = tuple(jnp.zeros((FACES, PAIR * ny), F32) for _ in range(4))
    last = lax.fori_loop(0, half, main_x, start)
    for c in range(4):
        for k in range(PAIR):
            at = (k + 1) % PAIR * half * FACES
            grads[c][pl.ds(at, FACES), :] += last[c][:, k * ny : (k + 1) * ny]

    lanes = g_weights.shape[1]
    values = acc_mid[: 8 * hid, :]
    r, c = rows_cols(values.shape)
    same = rest(quot(r, hid), 4) == rest(quot(c, hid), 4)
    values = fold_rows(jnp.where(same, values, 0.0), hid)
    grad_mid = exact_nt(
        pick((hid, 8 * hid), lambda q, n: rest(n, hid) == q, F32),
        stack([values, jnp.zeros((lanes - hid, 8 * hid), F32)]),
    )
    grad_mid_bias = exact(
        acc_mid[8 * hid : 8 * hid + 8, :], pick((8 * hid, lanes), lambda q, n: rest(q, hid) == n, F32)
    )
    r, c = rows_cols(acc_x.shape)
    face = rest(quot(r, hid), FACES)
    values = acc_x[...]
    found = [fold_rows(jnp.where((c & 15) - face == s, values, 0.0)[:, :128], hid) for s in range(4)]
    found.append(fold_rows(values[:, 128:], hid))
    found.append(fold_rows(jnp.where((c & 7) == face, acc_y[...], 0.0), hid))
    found.append(fold_rows(acc_y_bias[...], hid))
    found.append(fold_rows(jnp.where((c[:, :128] & 7) == face[:, :128], acc_out[...], 0.0), hid))
    found = side(found)

    def source(q, n):
        block = n >> 7
        in_x = (block < 4) & (q == 4 * block + ((n & 63) >> 4))
        in_y = (block >= 5) & (block < 7) & (q == ((n & 127) >> 3))
        in_bias = ((n == 512) | (block == 7)) & (q == 24)
        in_out = (block == 8) & (q == 16 + ((n & 63) >> 3))
        return in_x | in_y | in_bias | in_out

    beside = exact_nt(
        pick((32, found.shape[1]), source, F32),
        stack([jnp.zeros((hid, found.shape[1]), F32), found, jnp.zeros((lanes - 2 * hid, found.shape[1]), F32)]),
    )
    out_bias_rows = exact_nt(jnp.ones((8, acc_out_bias.shape[1]), F32), acc_out_bias[...])
    grad_out_bias = exact_nt(out_bias_rows, pick((lanes, 64), lambda q, n: (n >> 3) == q - hid, F32))
    r, c = rows_cols((8, lanes))
    g_weights[:hid, :] = grad_mid + beside
    g_weights[25:26, :] += grad_out_bias[:1]
    g_weights[hid:, :] = grad_mid_bias


def finish_kernel(total, g_w_in, g_b_in, g_w_mid, g_b_mid, g_w_out, g_b_out):
    hid = g_w_mid.shape[0]
    g_w_mid[...] = total[:hid, :hid]
    beside = total[:hid, hid : 2 * hid]
    g_w_in[...] = beside[:16]
    g_w_out[...] = beside[16:24]
    g_b_in[...] = beside[24:25]
    g_b_out[...] = beside[25:26, :8]
    g_b_mid[...] = total[hid : hid + 1, :hid]


def whole(count, space=pltpu.VMEM):
    return [pl.BlockSpec(memory_space=space)] * count


def call(kernel, outs, operands, out_spaces=None, in_spaces=None, scratch=(), flops=0, moved=0):
    return pl.pallas_call(
        kernel,
        out_shape=outs,
        in_specs=in_spaces or whole(len(operands)),
        out_specs=out_spaces or whole(len(outs)),
        scratch_shapes=list(scratch),
        compiler_params=pltpu.CompilerParams(vmem_limit_bytes=VMEM_BYTES),
        cost_estimate=pl.CostEstimate(flops=flops, bytes_accessed=moved, transcendentals=0),
    )(*operands)


def sum_all(values, sizes):
    axes, size = tuple(sizes), 1
    for one in sizes.values():
        size *= one
    if size & (size - 1):
        return lax.psum(values, axes)
    bits = [1 << k for k in range(size.bit_length() - 1)]
    core = size // sizes["traj"]
    others = [bit for bit in reversed(bits) if bit != core]
    rounds = [[core]] * (core in bits) + [others[k : k + 2] for k in range(0, len(others), 2)]
    for masks in rounds:
        partners = [0]
        for mask in masks:
            partners = partners + [one ^ mask for one in partners]
        parts = [
            lax.ppermute(values, axes, [(i, i ^ one) for i in range(size)]) if one else values for one in partners
        ]
        while len(parts) > 1:
            parts = [parts[k] + parts[k + 1] for k in range(0, len(parts), 2)]
        values = parts[0]
    return values


def body(sizes, density, momentum, tracer, cotangent, w_in, b_in, w_mid, b_mid, w_out, b_out):
    nx, ny = density.shape[1:]
    hid = w_in.shape[0]
    wide = FACES * hid
    groups = nx // FACES
    half = groups // PAIR
    lanes = PAIR * ny
    segs = ny // SEG
    rim_rows = nx // segs
    ring = sizes["tx"] * sizes["ty"]
    shape = jax.ShapeDtypeStruct

    operands = [
        density, momentum, tracer, cotangent, w_in.T, b_in[None], w_mid, b_mid[None], w_out, b_out[None]
    ]
    rim, to_first, to_second, state, cots, *matrices = call(
        pack_kernel,
        [
            shape((8, rim_rows, ny), F32),
            shape((8, FACES, ny), F32),
            shape((8, FACES, ny), F32),
            shape((4, nx, ny), F32),
            shape((4, nx, ny), F32),
            shape((wide // 2, 6 * 32 + ONES), BF16),
            shape((wide, 6 * 128), BF16),
            shape((wide, ny), F32),
            shape((4 * hid, 8 * hid), BF16),
            shape((2 * hid, ny), F32),
            shape((192, wide), BF16),
            shape((64, ny), F32),
            shape((wide, 192), BF16),
            shape((2 * hid, 6 * hid), BF16),
            shape((64, wide), BF16),
            shape((128, wide), BF16),
        ],
        [pltpu.with_memory_space_constraint(one, pltpu.HBM) for one in operands],
        in_spaces=whole(10, pltpu.HBM),
        scratch=[pltpu.VMEM(one.shape, F32) for one in operands[4:]] + [pltpu.SemaphoreType.DMA((10,))],
    )
    axes = ("tx", "ty")
    swaps = [[(i, (i + 1 if (i + first) % 2 == 0 else i - 1) % ring) for i in range(ring)] for first in range(2)]
    from_first, from_second = (
        lax.ppermute(one, axes, swap) for one, swap in zip((to_first, to_second), swaps)
    )

    middle, *kept = call(
        x_forward_kernel,
        [shape((4, nx, ny), F32)]
        + [shape((half, wide, lanes), BF16)] * 4
        + [shape((half, 64, lanes), F32)],
        [state, matrices[0]] + matrices[3:7],
        scratch=[pltpu.VMEM((4, nx + FACES, ny), F32)],
        flops=10**10,
        moved=10**7,
    )
    g_den, g_mom, g_tra, g_weights = call(
        back_kernel,
        [
            shape(density.shape, F32),
            shape(momentum.shape, F32),
            shape(tracer.shape, F32),
            shape((hid + 8, 128), F32),
        ],
        [state, cots, middle, rim, from_first, from_second] + matrices + kept,
        scratch=[
            pltpu.VMEM((4, rim_rows + FACES, ny), F32),
            pltpu.VMEM((4, rim_rows, ny), F32),
            pltpu.VMEM((4, rim_rows + FACES, ny), F32),
            pltpu.VMEM((4, rim_rows, ny), F32),
            pltpu.VMEM((4, rim_rows, ny), F32),
            pltpu.VMEM((4, nx, ny), F32),
            pltpu.VMEM((2 * wide, 256), F32),
            pltpu.VMEM((2 * wide, 256), F32),
            pltpu.VMEM((wide, ny), F32),
            pltpu.VMEM((8 * hid + ONES, 8 * hid), F32),
            pltpu.VMEM((2 * wide, 128), F32),
            pltpu.VMEM((64, lanes), F32),
        ],
        flops=4 * 10**10,
        moved=2 * 10**7,
    )
    total = sum_all(g_weights, sizes)
    g_w_in, g_b_in, g_w_mid, g_b_mid, g_w_out, g_b_out = call(
        finish_kernel,
        [
            shape((w_in.shape[1], hid), F32),
            shape((1, hid), F32),
            shape(w_mid.shape, F32),
            shape((1, hid), F32),
            shape(w_out.shape, F32),
            shape((1, b_out.shape[0]), F32),
        ],
        [total],
    )
    return (g_den, g_mom, g_tra, g_w_in.T, g_b_in[0], g_w_mid, g_b_mid[0], g_w_out, g_b_out[0])


def solution(mesh):
    flow = P("traj", None, ("tx", "ty"))
    deep = P("traj", None, None, ("tx", "ty"))
    return jax.shard_map(
        functools.partial(body, dict(mesh.shape)),
        mesh=mesh,
        in_specs=(flow, deep, flow, deep) + (P(),) * 6,
        out_specs=(flow, deep, flow) + (P(),) * 6,
        check_vma=False,
    )
```

```python
import functools

import jax
import jax.numpy as jnp
from jax import lax
from jax.experimental import pallas as pl
from jax.experimental.pallas import tpu as pltpu
from jax.sharding import PartitionSpec as P

courant = 0.1
slope_gain = 0.25
F32 = jnp.float32
BF16 = jnp.bfloat16
FACES = 8
SEG = 16
RIM = 4
PAIR = 16
RIM_PAIR = 4
ONES = 16
VMEM_BYTES = 28 * 2**20


def dot(a, b):
    return lax.dot_general(a, b, (((1,), (0,)), ((), ())), preferred_element_type=F32)


def dot_nt(a, b):
    return lax.dot_general(a, b, (((1,), (1,)), ((), ())), preferred_element_type=F32)


def exact(a, b):
    return lax.dot_general(
        a, b, (((1,), (0,)), ((), ())), precision=lax.Precision.HIGHEST, preferred_element_type=F32
    )


def exact_nt(a, b):
    return lax.dot_general(
        a, b, (((1,), (1,)), ((), ())), precision=lax.Precision.HIGHEST, preferred_element_type=F32
    )


def split(values):
    high = values.astype(BF16)
    return high, (values - high.astype(F32)).astype(BF16)


def split3(values):
    high = values.astype(BF16)
    rest = values - high.astype(F32)
    middle = rest.astype(BF16)
    return high, middle, (rest - middle.astype(F32)).astype(BF16)


def rows_cols(shape):
    return lax.broadcasted_iota(jnp.int32, shape, 0), lax.broadcasted_iota(jnp.int32, shape, 1)


def quot(values, n):
    return values >> (n.bit_length() - 1) if n & (n - 1) == 0 else values // n


def rest(values, n):
    return values & (n - 1) if n & (n - 1) == 0 else values % n


def pick(shape, test, dtype=BF16):
    r, c = rows_cols(shape)
    return jnp.where(test(r, c), 1.0, 0.0).astype(dtype)


def stack(parts):
    return jnp.concatenate(parts, 0)


def side(parts):
    return jnp.concatenate(parts, 1)


STACKED = (0, 0, 0, 1, 1, 2)


def stacked(parts):
    return [parts[0], parts[1], parts[2], parts[0], parts[1], parts[0]]


def level_of(block):
    return jnp.where(block < 3, 0, jnp.where(block < 5, 1, 2))


def choose(values, levels):
    parts = [part.astype(F32) for part in split3(values)]
    total = jnp.zeros(values.shape, F32)
    for k, part in enumerate(parts):
        total = jnp.where(levels == k, part, total)
    return total


def build_first(w, b, hid):
    x_cols, y_cols, step = 6 * 32 + ONES, 6 * 128, 256

    def source(q, n):
        s = n >> 8
        m = n & (step - 1)
        in_x = (s < 4) & (m < 192) & (q == 4 * s + ((m & 31) >> 3))
        in_y = (n >= 4 * step) & (q == (((n - 4 * step) & 127) >> 3))
        return in_x | in_y

    spread_out = exact(w, pick((16, 4 * step + y_cols), source, F32))
    _, n = rows_cols(spread_out.shape)
    block = jnp.where(n < 4 * step, (n & (step - 1)) >> 5, (n - 4 * step) >> 7)
    spread_out = choose(spread_out, level_of(block))

    at, _ = rows_cols((x_cols, hid))
    rows = jnp.zeros((x_cols, hid), F32)
    for k, level in enumerate(split3(b)):
        rows = jnp.where(at == 192 + k, jnp.broadcast_to(level.astype(F32), (x_cols, hid)), rows)
    bias = dot_nt(pick((hid, hid), lambda q, n: q == n), rows.astype(BF16))

    r, c = rows_cols((FACES // 2 * hid, x_cols))
    shift = jnp.where(c < 192, (c & 7) - quot(r, hid), -1)
    first_x = stack([bias] * (FACES // 2))
    for s in range(4):
        part = spread_out[:, s * step : s * step + x_cols]
        first_x = jnp.where(shift == s, stack([part] * (FACES // 2)), first_x)
    r, c = rows_cols((FACES * hid, y_cols))
    first_y = jnp.where((c & 7) == quot(r, hid), stack([spread_out[:, 4 * step :]] * FACES), 0.0)
    return first_x.astype(BF16), first_y.astype(BF16)


def build_first_back(w_t, hid):
    wide = FACES * hid

    def source(q, n):
        in_x = (q < 512) & (n == 4 * (q >> 7) + ((q & 63) >> 4))
        in_y = (q >= 512) & (n == (((q - 512) & 127) >> 3))
        return in_x | in_y

    rows = exact(pick((512 + 256, 16), source, F32), w_t)
    right = pick((hid, 2 * wide), lambda q, n: rest(n, hid) == q)
    high, low = (dot(part, right) for part in split(rows))
    r, c = rows_cols(high.shape)
    is_low = jnp.where(r < 512, r & 64, (r - 512) & 128) > 0
    value = jnp.where(is_low, jnp.where(c < wide, low, 0.0), high)
    face = quot(rest(c, wide), hid)
    r, c = r[:128], c[:128]
    shift = (r & 15) - face[:128]
    back_x = jnp.zeros((128, 2 * wide), F32)
    for s in range(4):
        back_x = jnp.where(shift == s, value[128 * s : 128 * (s + 1)], back_x)
    r, _ = rows_cols((256, 2 * wide))
    back_y = jnp.where((r & 7) == face[512:], value[512:], 0.0)
    return back_x.astype(BF16), back_y.astype(BF16)


def build_mid(w, hid):
    block = 2 * hid
    tiled = exact(w, pick((hid, 4 * block), lambda q, n: rest(n, hid) == q, F32))
    _, n = rows_cols(tiled.shape)
    upper = choose(tiled, jnp.where(n < 3 * block, 0, 2))
    lower = choose(tiled, jnp.where(n < 2 * block, 1, -1))
    r, c = rows_cols((2 * block, 4 * block))
    keep = quot(rest(r, block), hid) == quot(rest(c, block), hid)
    return jnp.where(keep, stack([upper, upper, lower, lower]), 0.0).astype(BF16)


def build_mid_back(w, hid):
    block = 2 * hid
    turned = exact_nt(pick((hid, hid), lambda q, n: q == n, F32), w)
    tiled = exact(turned, pick((hid, 3 * block), lambda q, n: rest(n, hid) == q, F32))
    _, n = rows_cols(tiled.shape)
    tiled = choose(tiled, jnp.where(quot(n, block) == 1, 1, 0))
    r, c = rows_cols((block, 3 * block))
    keep = quot(r, hid) == quot(rest(c, block), hid)
    return jnp.where(keep, stack([tiled] * 2), 0.0).astype(BF16)


def build_out(w, hid):
    wide = FACES * hid
    rows = exact(pick((64, 8), lambda q, n: (q >> 3) == n, F32), w)
    tiled = dot(stack(list(split3(rows))), pick((hid, wide), lambda q, n: rest(n, hid) == q))
    r, c = rows_cols(tiled.shape)
    return jnp.where((r & 7) == quot(c, hid), tiled, 0.0).astype(BF16)


def build_out_back(w, hid):
    wide = FACES * hid
    turned = exact_nt(pick((hid, hid), lambda q, n: q == n, F32), w)
    tiled = exact(turned, pick((8, 192), lambda q, n: ((n & 63) >> 3) == q, F32))
    _, n = rows_cols(tiled.shape)
    tiled = choose(tiled, jnp.where((n >> 6) == 1, 1, 0))
    r, c = rows_cols((wide, 192))
    return jnp.where(quot(r, hid) == (c & 7), stack([tiled] * FACES), 0.0).astype(BF16)


def spread_bias(b, lanes, copies):
    n = b.shape[1]
    rows = exact_nt(pick((n, n), lambda q, m: q == m, F32), jnp.broadcast_to(b, (lanes, n)))
    return stack([rows] * copies)


def spread(bias_ref, width):
    return side([bias_ref[...]] * (width // bias_ref.shape[1]))


def limiter_forward(first, weights, hid):
    first_ref, first_bias_ref, mid_ref, mid_bias_ref, out_ref, out_bias_ref = weights
    width = first[0][0].shape[1]
    if first_bias_ref is None:
        ones = [jnp.ones((ONES, width), BF16)]
        h1 = stack([jnp.tanh(dot(first_ref[...], stack(stacked(one) + ones))) for one in first])
    else:
        h1 = jnp.tanh(dot(first_ref[...], stack(stacked(first[0]))) + spread(first_bias_ref, width))
    h1_parts = split3(h1)
    block = 2 * hid
    parts = []
    for at in range(0, FACES * hid, block):
        high, middle, low = (p[at : at + block] for p in h1_parts)
        both = dot(mid_ref[...], stack([high, middle, low, high]))
        parts.append(jnp.tanh(both[:block] + both[block:] + spread(mid_bias_ref, width)))
    h2 = stack(parts)
    h2_parts = split3(h2)
    rows = 8 * FACES
    a = dot(out_ref[...], h2_parts[0])
    b = dot(out_ref[: 2 * rows, :], h2_parts[1])
    c = dot(out_ref[:rows, :], h2_parts[2])
    gates = jnp.tanh(
        ((a[2 * rows :] + b[rows:] + c) + (a[rows : 2 * rows] + b[:rows])) + a[:rows] + spread(out_bias_ref, width)
    )
    return h1, h1_parts[:2], h2, h2_parts[:2], gates


def limiter_backward(d3, slope1, slope2, h1_pair, h2_pair, out_back_ref, mid_back_ref, acc, hid):
    d3_hi, d3_lo = split(d3)
    dh2 = dot(out_back_ref[...], stack([d3_hi, d3_hi, d3_lo]))
    if acc is not None:
        acc[2][...] += dot_nt(stack(list(h2_pair)), stack([d3_hi, d3_lo]))
        acc[3][...] += d3
    d2_hi, d2_lo = split(dh2 * slope2)
    block = 2 * hid
    parts = []
    for at in range(0, FACES * hid, block):
        hi, lo = d2_hi[at : at + block], d2_lo[at : at + block]
        parts.append(dot(mid_back_ref[...], stack([hi, hi, lo])))
    if acc is not None:
        ones = jnp.ones((ONES, d3.shape[1]), BF16)
        lefts, rights = [], []
        for at in range(0, FACES * hid, 2 * block):
            lefts.append(stack([part[at : at + 2 * block] for part in h1_pair] + [ones]))
            rights.append(stack([part[at : at + 2 * block] for part in (d2_hi, d2_lo)]))
        acc[1][...] += dot_nt(side(lefts), side(rights))
    return stack(parts) * slope1


def first_backward(d1, back_ref):
    both = dot(back_ref[...], stack([d1[0], d1[1]]))
    half = both.shape[0] // 2
    return both[:half] + both[half:]


def add_first_grads(first, d1, acc_in):
    high, low = first[:2]
    both = stack(list(d1))
    if 2 * high.shape[0] + ONES <= acc_in.shape[1]:
        ones = jnp.ones((ONES, high.shape[1]), BF16)
        acc_in[:, : 2 * high.shape[0] + ONES] += dot_nt(both, stack([high, low, ones]))
    else:
        acc_in[...] += dot_nt(both, stack([high, low]))


def edge_states(cells, gates):
    left, right = [], []
    for c in range(4):
        low = gates[FACES * c : FACES * (c + 1)]
        high = gates[FACES * (c + 4) : FACES * (c + 5)]
        left.append(cells[1][c] + slope_gain * low * (cells[2][c] - cells[0][c]))
        right.append(cells[2][c] - slope_gain * high * (cells[3][c] - cells[1][c]))
    return left, right


def face_flux(left, right):
    ul = left[1] / left[0]
    ur = right[1] / right[0]
    half_speed = 0.5 * (jnp.maximum(jnp.abs(ul), jnp.abs(ur)) + 1.0)
    fl = [left[1], left[1] * ul + left[0], left[2] * ul, left[3] * ul]
    fr = [right[1], right[1] * ur + right[0], right[2] * ur, right[3] * ur]
    return [0.5 * (fl[c] + fr[c]) - half_speed * (right[c] - left[c]) for c in range(4)]


def sign_of(values):
    return jnp.where(values > 0.0, 1.0, jnp.where(values < 0.0, -1.0, 0.0))


def face_flux_backward(left, right, d_flux):
    inv_l, inv_r = 1.0 / left[0], 1.0 / right[0]
    ul, ur = left[1] / left[0], right[1] / right[0]
    al, ar = jnp.abs(ul), jnp.abs(ur)
    half_speed = 0.5 * (jnp.maximum(al, ar) + 1.0)
    d_speed = -0.5 * sum(d_flux[c] * (right[c] - left[c]) for c in range(4))
    share = jnp.where(al > ar, 1.0, jnp.where(al < ar, 0.0, 0.5))
    half = [0.5 * d for d in d_flux]
    spread = [half_speed * d for d in d_flux]

    def one(state, u, inv, speed_part, sign):
        du = half[1] * state[1] + half[2] * state[2] + half[3] * state[3] + speed_part * sign_of(u)
        over = du * inv
        return [
            half[1] - over * u + sign * spread[0],
            half[0] + half[1] * u + over + sign * spread[1],
            half[2] * u + sign * spread[2],
            half[3] * u + sign * spread[3],
        ]

    return (
        one(left, ul, inv_l, d_speed * share, 1.0),
        one(right, ur, inv_r, d_speed * (1.0 - share), -1.0),
    )


def edge_backward(cells, gates, d_left, d_right):
    lows, highs = [], []
    direct = [[None] * 4 for _ in range(4)]
    for c in range(4):
        low = gates[FACES * c : FACES * (c + 1)]
        high = gates[FACES * (c + 4) : FACES * (c + 5)]
        lows.append(slope_gain * (cells[2][c] - cells[0][c]) * d_left[c])
        highs.append(-slope_gain * (cells[3][c] - cells[1][c]) * d_right[c])
        low_part = slope_gain * low * d_left[c]
        high_part = slope_gain * high * d_right[c]
        direct[0][c] = -low_part
        direct[1][c] = d_left[c] + high_part
        direct[2][c] = d_right[c] + low_part
        direct[3][c] = -high_part
    return stack(lows + highs) * (1.0 - gates * gates), direct


def turn(values, shift, axis):
    size = values.shape[axis]
    return values if shift % size == 0 else pltpu.roll(values, shift % size, axis)


def x_cells(tiles):
    return [[turn(t, -s, 0)[:FACES] for t in tiles] for s in range(4)]


def pack_kernel(den, mom, tra, cot, w_in, b_in, w_mid, b_mid, w_out, b_out,
                rim, to_first, to_second, state, cots, first_x, first_y, first_bias, mid, mid_bias, out, out_bias,
                out_back, mid_back, first_x_back, first_y_back, *scratch):
    *small, sems = scratch
    nx, ny = den.shape[1:]
    segs = ny // SEG
    rows = nx // segs
    hid = w_in.shape[1]
    copies = [
        pltpu.make_async_copy(source, target, sems.at[k])
        for k, (source, target) in enumerate(
            list(zip([w_in, b_in, w_mid, b_mid, w_out, b_out], small))
            + [
                (den.at[0], state.at[0]),
                (mom.at[0], state.at[pl.ds(1, 2)]),
                (tra.at[0], state.at[3]),
                (cot.at[0], cots),
            ]
        )
    ]
    for one in copies:
        one.start()
    for one in copies[:6]:
        one.wait()
    w_in, b_in, w_mid, b_mid, w_out, b_out = small
    lanes = out_bias.shape[1]
    w_in_rows = exact_nt(pick((hid, hid), lambda q, n: q == n, F32), w_in[...])
    first_x[...], first_y[...] = build_first(w_in_rows, b_in[...], hid)
    first_bias[...] = spread_bias(b_in[...], lanes, FACES)
    mid[...] = build_mid(w_mid[...], hid)
    mid_bias[...] = spread_bias(b_mid[...], lanes, 2)
    out[...] = build_out(w_out[...], hid)
    out_bias[...] = exact_nt(
        pick((64, 8), lambda q, n: (q >> 3) == n, F32), jnp.broadcast_to(b_out[...], (lanes, 8))
    )
    out_back[...] = build_out_back(w_out[...], hid)
    mid_back[...] = build_mid_back(w_mid[...], hid)
    first_x_back[...], first_y_back[...] = build_first_back(w_in[...], hid)

    for one in copies[6:]:
        one.wait()
    lane = lane_index(ny)
    for v in range(8):
        plane = state.at[v] if v < 4 else cots.at[v - 4]
        for at in range(0, rows, FACES):
            total = jnp.zeros((FACES, ny), F32)
            for s in range(segs):
                first = s * SEG + RIM
                moved = turn(plane[pl.ds(s * rows + at, FACES), :], first + RIM, 1)
                total = jnp.where((lane >= first) & (lane < first + 2 * RIM), moved, total)
            rim[v, pl.ds(at, FACES), :] = total
    is_odd = odd_mask(ny)
    spot = lane & (SEG - 1)
    for v in range(8):
        sides = []
        for first in (2 * RIM, RIM):
            total = jnp.zeros((FACES, ny), F32)
            for g in range(rows // FACES):
                moved = turn(rim[v, pl.ds(g * FACES, FACES), :], g * RIM - first, 1)
                total = jnp.where((spot >= g * RIM) & (spot < (g + 1) * RIM), moved, total)
            sides.append(total)
        to_first[v] = jnp.where(is_odd, sides[0], sides[1])
        to_second[v] = jnp.where(is_odd, sides[1], sides[0])


def odd_mask(ny):
    return jnp.full((FACES, ny), lax.rem(lax.axis_index(("tx", "ty")), 2), jnp.int32) == 1


def row_block(at):
    return pl.ds(pl.multiple_of(at * FACES, FACES), FACES)


def x_tiles(planes, group, groups):
    after = jnp.where(group + 1 == groups, 0, group + 1)
    return [stack([plane[row_block(group), :], plane[row_block(after), :]]) for plane in planes]


def pair_tiles(planes, step, half):
    sets = [x_tiles(planes, step + k * half, PAIR * half) for k in range(PAIR)]
    return [side([one[c] for one in sets]) for c in range(len(planes))]


def x_windows(tiles):
    half = FACES // 2
    return [split3(stack([turn(tile, -at, 0)[:FACES] for tile in tiles])) for at in (0, half)]


def x_forward(tiles, weights, hid):
    h1, h1_pair, h2, h2_pair, gates = limiter_forward(x_windows(tiles), weights, hid)
    cells = x_cells(tiles)
    return h1, h2, h1_pair, h2_pair, gates, face_flux(*edge_states(cells, gates))


def update_cells(plane_rows, flux_rows):
    upper = turn(flux_rows, -7, 0)[:FACES]
    lower = turn(flux_rows, -6, 0)[:FACES]
    return plane_rows - courant * (upper - lower)


def x_forward_kernel(state, first_x, mid, mid_bias, out, out_bias,
                     middle, h1_hi, h1_lo, h2_hi, h2_lo, slope1, slope2, gates_out, flux):
    nx, ny = state.shape[1:]
    groups = nx // FACES
    half = groups // PAIR
    hid = mid.shape[0] // 4
    x_weights = (first_x, None, mid, mid_bias, out, out_bias)
    planes = [state.at[c] for c in range(4)]

    def step_of(step, _):
        tiles = pair_tiles(planes, step, half)
        h1, h2, h1_pair, h2_pair, gates, fluxes = x_forward(tiles, x_weights, hid)
        for target, value in zip((h1_hi, h1_lo, h2_hi, h2_lo, gates_out), h1_pair + h2_pair + (gates,)):
            target[step] = value
        slope1[step] = 1.0 - h1 * h1
        slope2[step] = 1.0 - h2 * h2
        for c in range(4):
            for k in range(PAIR):
                flux[c, row_block(step + k * half + 1), :] = fluxes[c][:, k * ny : (k + 1) * ny]
        return 0

    lax.fori_loop(0, half, step_of, 0)
    for c in range(4):
        flux[c, :FACES, :] = flux[c, nx : nx + FACES, :]

    def update(group, _):
        for c in range(4):
            both = stack([flux[c, row_block(group), :], flux[c, row_block(group + 1), :]])
            middle[c, row_block(group), :] = update_cells(planes[c][row_block(group), :], both)
        return 0

    lax.fori_loop(0, groups, update, 0)


def y_order(planes):
    return [planes[0], planes[2], planes[1], planes[3]]


def lane_index(width):
    return lax.broadcasted_iota(jnp.int32, (FACES, width), 1)


def y_step(cells, cots, halo_mask, refs, acc, hid):
    weights, out_back, mid_back, first_y_back = refs
    window = split3(stack([cells[s][c] for s in range(4) for c in range(4)]))
    h1, h1_pair, h2, h2_pair, gates = limiter_forward([window], weights, hid)
    left, right = edge_states(cells, gates)
    d_flux = [courant * (cots[1][c] - cots[0][c]) for c in range(4)]
    d_left, d_right = face_flux_backward(left, right, d_flux)
    if halo_mask is not None:
        d_left = [jnp.where(halo_mask, d, 0.0) for d in d_left]
        d_right = [jnp.where(halo_mask, d, 0.0) for d in d_right]
    d3_full, direct = edge_backward(cells, gates, d_left, d_right)
    d1_full = limiter_backward(
        d3_full, 1.0 - h1 * h1, 1.0 - h2 * h2, h1_pair, h2_pair, out_back, mid_back, acc, hid
    )
    d1 = split(d1_full)
    d_window = first_backward(d1, first_y_back)
    if acc is not None:
        add_first_grads(window, d1, acc[0])
        ny = acc[4].shape[1]
        acc[4][...] += sum(d1_full[:, at : at + ny] for at in range(0, d1_full.shape[1], ny))
    return [
        [d_window[FACES * (4 * s + c) : FACES * (4 * s + c + 1)] + direct[s][c] for c in range(4)]
        for s in range(4)
    ]


def y_gather(parts, ny):
    lane = lane_index(ny)
    out = []
    for c in range(4):
        a = turn(jnp.where(lane >= 1, parts[0][c], 0.0), -1, 1)
        b = turn(jnp.where(lane < ny - 1, parts[2][c], 0.0), 1, 1)
        d = turn(jnp.where(lane < ny - 2, parts[3][c], 0.0), 2, 1)
        out.append(parts[1][c] + a + b + d)
    return out


def fold_rows(values, hid):
    return sum(values[at : at + hid] for at in range(0, values.shape[0], hid))


def back_kernel(state, cot, middle, own, from_first, from_second,
                first_x, first_y, first_bias, mid, mid_bias, out, out_bias,
                out_back, mid_back, first_x_back, first_y_back,
                h1_hi, h1_lo, h2_hi, h2_lo, slope1, slope2, gates_in,
                g_den, g_mom, g_tra, g_weights,
                rim_state, rim_cot, rim_flux, rim_middle, rim_grad, d_middle,
                acc_x, acc_y, acc_y_bias, acc_mid, acc_out, acc_out_bias):
    nx, ny = state.shape[1:]
    groups = nx // FACES
    half = groups // PAIR
    hid = mid.shape[0] // 4
    x_weights = (first_x, None, mid, mid_bias, out, out_bias)
    segs = ny // SEG
    rim_rows = nx // segs
    rim_groups = rim_rows // FACES
    rim_half = rim_groups // RIM_PAIR

    for acc in (acc_x, acc_y, acc_y_bias, acc_mid, acc_out, acc_out_bias):
        acc[...] = jnp.zeros(acc.shape, F32)

    lane = lane_index(ny)
    spot = lane & (SEG - 1)
    is_odd = odd_mask(ny)
    for v in range(8):
        for g in range(rim_groups):
            rows = pl.ds(g * FACES, FACES)
            mine, first, second = own[v, rows, :], from_first[v], from_second[v]
            left, right = jnp.where(is_odd, first, second), jnp.where(is_odd, second, first)
            value = jnp.where(
                spot < RIM,
                turn(left, -g * RIM, 1),
                jnp.where(
                    spot < 2 * RIM,
                    turn(mine, -RIM, 1),
                    jnp.where(spot < 3 * RIM, turn(mine, RIM, 1), turn(right, (3 - g) * RIM, 1)),
                ),
            )
            if v < 4:
                rim_state[v, rows, :] = value
                if g == 0:
                    rim_state[v, pl.ds(rim_rows, FACES), :] = turn(value, -SEG, 1)
            else:
                rim_cot[v - 4, rows, :] = value

    def rim_forward(step, _):
        sets = [
            [
                stack([
                    rim_state[c, row_block(step + k * rim_half), :],
                    rim_state[c, row_block(step + k * rim_half + 1), :],
                ])
                for c in range(4)
            ]
            for k in range(RIM_PAIR)
        ]
        tiles = [side([one[c] for one in sets]) for c in range(4)]
        fluxes = x_forward(tiles, x_weights, hid)[-1]
        for c in range(4):
            for k in range(RIM_PAIR):
                rim_flux[c, row_block(step + k * rim_half + 1), :] = fluxes[c][:, k * ny : (k + 1) * ny]
        return 0

    lax.fori_loop(0, rim_half, rim_forward, 0)
    for c in range(4):
        rim_flux[c, :FACES, :] = turn(rim_flux[c, rim_rows : rim_rows + FACES, :], SEG, 1)
        for g in range(rim_groups):
            rows = pl.ds(g * FACES, FACES)
            both = stack([rim_flux[c, rows, :], rim_flux[c, pl.ds((g + 1) * FACES, FACES), :]])
            rim_middle[c, rows, :] = update_cells(rim_state[c, rows, :], both)

    refs = ((first_y, first_bias, mid, mid_bias, out, out_bias), out_back, mid_back, first_y_back)
    spot_wide = lane_index(RIM_PAIR * ny) & (SEG - 1)
    rim_faces = (spot_wide == RIM - 2) | (spot_wide == RIM - 1) | (spot_wide == 3 * RIM)

    def rim_back(step, _):
        cells = [[[] for _ in range(4)] for _ in range(4)]
        cots = [[[] for _ in range(4)] for _ in range(2)]
        for k in range(RIM_PAIR):
            rows = row_block(step + k * rim_half)
            for c in range(4):
                value = rim_middle[c, rows, :]
                for s in range(4):
                    cells[s][c].append(turn(value, 1 - s, 1))
                value = rim_cot[c, rows, :]
                for s in range(2):
                    cots[s][c].append(turn(value, -s, 1))
        cells = [y_order([side(one) for one in row]) for row in cells]
        cots = [y_order([side(one) for one in row]) for row in cots]
        parts = y_step(cells, cots, rim_faces, refs, None, hid)
        for k in range(RIM_PAIR):
            own_parts = [[one[:, k * ny : (k + 1) * ny] for one in row] for row in parts]
            gathered = y_order(y_gather(own_parts, ny))
            for c in range(4):
                rim_grad[c, row_block(step + k * rim_half), :] = gathered[c]
        return 0

    lax.fori_loop(0, rim_half, rim_back, 0)

    def main_y(step, _):
        cells = [[[] for _ in range(4)] for _ in range(4)]
        cots = [[[] for _ in range(4)] for _ in range(2)]
        for k in range(PAIR):
            group = step + k * half
            rows = row_block(group)
            seg = group // rim_groups
            rim_at = row_block(group - seg * rim_groups)
            to_low = ny - (seg * SEG + 3 * RIM)
            to_high = lax.rem(ny - 1 - (seg * SEG + RIM - 1) + ny, ny)
            for c in range(4):
                value = middle[c, rows, :]
                rim_value = rim_middle[c, rim_at, :]
                low = jnp.where(lane < 2, pltpu.roll(rim_value, to_low, 1), value)
                high = jnp.where(lane == ny - 1, pltpu.roll(rim_value, to_high, 1), value)
                cells[0][c].append(turn(high, 1, 1))
                cells[1][c].append(value)
                cells[2][c].append(turn(jnp.where(lane < 1, low, value), -1, 1))
                cells[3][c].append(turn(low, -2, 1))
                value = cot[c, rows, :]
                rim_value = rim_cot[c, rim_at, :]
                low = jnp.where(lane < 1, pltpu.roll(rim_value, to_low, 1), value)
                cots[0][c].append(value)
                cots[1][c].append(turn(low, -1, 1))
        cells = [y_order([side(one) for one in row]) for row in cells]
        cots = [y_order([side(one) for one in row]) for row in cots]
        parts = y_step(cells, cots, None, refs, (acc_y, acc_mid, acc_out, acc_out_bias, acc_y_bias), hid)
        for k in range(PAIR):
            group = step + k * half
            rows = row_block(group)
            seg = group // rim_groups
            rim_at = row_block(group - seg * rim_groups)
            own_parts = [[one[:, k * ny : (k + 1) * ny] for one in row] for row in parts]
            gathered = y_order(y_gather(own_parts, ny))
            to_low = ny - (seg * SEG + RIM)
            to_high = lax.rem(ny - 1 - (seg * SEG + 3 * RIM - 1) + ny, ny)
            for c in range(4):
                rim_value = rim_grad[c, rim_at, :]
                from_rim = jnp.where(
                    lane < 2,
                    pltpu.roll(rim_value, to_low, 1),
                    jnp.where(lane == ny - 1, pltpu.roll(rim_value, to_high, 1), 0.0),
                )
                d_middle[c, rows, :] = cot[c, rows, :] + gathered[c] + from_rim
        return 0

    lax.fori_loop(0, half, main_y, 0)

    planes = [state.at[c] for c in range(4)]
    grads = [g_den.at[0], g_mom.at[0, 0], g_mom.at[0, 1], g_tra.at[0]]
    d_planes = [d_middle.at[c] for c in range(4)]

    def main_x(step, carry):
        tiles = pair_tiles(planes, step, half)
        d_tiles = pair_tiles(d_planes, step, half)
        gates = gates_in[step]
        h1_pair = (h1_hi[step], h1_lo[step])
        h2_pair = (h2_hi[step], h2_lo[step])
        cells = x_cells(tiles)
        left, right = edge_states(cells, gates)
        d_flux = [courant * (turn(d, -2, 0)[:FACES] - turn(d, -1, 0)[:FACES]) for d in d_tiles]
        d_left, d_right = face_flux_backward(left, right, d_flux)
        d3_full, direct = edge_backward(cells, gates, d_left, d_right)
        d1_full = limiter_backward(
            d3_full, slope1[step], slope2[step], h1_pair, h2_pair, out_back, mid_back, (acc_x, acc_mid, acc_out, acc_out_bias), hid
        )
        d1 = split(d1_full)
        d_window = first_backward(d1, first_x_back)
        add_first_grads(split(stack(tiles)), d1, acc_x)
        later = []
        for c in range(4):
            total = d_window[2 * FACES * c : 2 * FACES * (c + 1)]
            for s in range(4):
                total = total + turn(stack([direct[s][c], jnp.zeros_like(direct[s][c])]), s, 0)
            now = total[:FACES] + d_tiles[c][:FACES] + carry[c]
            for k in range(PAIR):
                grads[c][row_block(step + k * half), :] = now[:, k * ny : (k + 1) * ny]
            later.append(total[FACES:])
        return tuple(later)

    start = tuple(jnp.zeros((FACES, PAIR * ny), F32) for _ in range(4))
    last = lax.fori_loop(0, half, main_x, start)
    for c in range(4):
        for k in range(PAIR):
            at = (k + 1) % PAIR * half * FACES
            grads[c][pl.ds(at, FACES), :] += last[c][:, k * ny : (k + 1) * ny]

    lanes = g_weights.shape[1]
    values = acc_mid[: 8 * hid, :]
    r, c = rows_cols(values.shape)
    same = rest(quot(r, hid), 4) == rest(quot(c, hid), 4)
    values = fold_rows(jnp.where(same, values, 0.0), hid)
    grad_mid = exact_nt(
        pick((hid, 8 * hid), lambda q, n: rest(n, hid) == q, F32),
        stack([values, jnp.zeros((lanes - hid, 8 * hid), F32)]),
    )
    grad_mid_bias = exact(
        acc_mid[8 * hid : 8 * hid + 8, :], pick((8 * hid, lanes), lambda q, n: rest(q, hid) == n, F32)
    )
    r, c = rows_cols(acc_x.shape)
    face = rest(quot(r, hid), FACES)
    values = acc_x[...]
    found = [fold_rows(jnp.where((c & 15) - face == s, values, 0.0)[:, :128], hid) for s in range(4)]
    found.append(fold_rows(values[:, 128:], hid))
    found.append(fold_rows(jnp.where((c & 7) == face, acc_y[...], 0.0), hid))
    found.append(fold_rows(acc_y_bias[...], hid))
    found.append(fold_rows(jnp.where((c[:, :128] & 7) == face[:, :128], acc_out[...], 0.0), hid))
    found = side(found)

    def source(q, n):
        block = n >> 7
        in_x = (block < 4) & (q == 4 * block + ((n & 63) >> 4))
        in_y = (block >= 5) & (block < 7) & (q == ((n & 127) >> 3))
        in_bias = ((n == 512) | (block == 7)) & (q == 24)
        in_out = (block == 8) & (q == 16 + ((n & 63) >> 3))
        return in_x | in_y | in_bias | in_out

    beside = exact_nt(
        pick((32, found.shape[1]), source, F32),
        stack([jnp.zeros((hid, found.shape[1]), F32), found, jnp.zeros((lanes - 2 * hid, found.shape[1]), F32)]),
    )
    out_bias_rows = exact_nt(jnp.ones((8, acc_out_bias.shape[1]), F32), acc_out_bias[...])
    grad_out_bias = exact_nt(out_bias_rows, pick((lanes, 64), lambda q, n: (n >> 3) == q - hid, F32))
    r, c = rows_cols((8, lanes))
    g_weights[:hid, :] = grad_mid + beside
    g_weights[25:26, :] += grad_out_bias[:1]
    g_weights[hid:, :] = grad_mid_bias


def finish_kernel(total, g_w_in, g_b_in, g_w_mid, g_b_mid, g_w_out, g_b_out):
    hid = g_w_mid.shape[0]
    g_w_mid[...] = total[:hid, :hid]
    beside = total[:hid, hid : 2 * hid]
    g_w_in[...] = beside[:16]
    g_w_out[...] = beside[16:24]
    g_b_in[...] = beside[24:25]
    g_b_out[...] = beside[25:26, :8]
    g_b_mid[...] = total[hid : hid + 1, :hid]


def whole(count, space=pltpu.VMEM):
    return [pl.BlockSpec(memory_space=space)] * count


def call(kernel, outs, operands, out_spaces=None, in_spaces=None, scratch=(), flops=0, moved=0):
    return pl.pallas_call(
        kernel,
        out_shape=outs,
        in_specs=in_spaces or whole(len(operands)),
        out_specs=out_spaces or whole(len(outs)),
        scratch_shapes=list(scratch),
        compiler_params=pltpu.CompilerParams(vmem_limit_bytes=VMEM_BYTES),
        cost_estimate=pl.CostEstimate(flops=flops, bytes_accessed=moved, transcendentals=0),
    )(*operands)


def sum_all(values, sizes):
    axes, size = tuple(sizes), 1
    for one in sizes.values():
        size *= one
    if size & (size - 1):
        return lax.psum(values, axes)
    bits = [1 << k for k in range(size.bit_length() - 1)]
    core = size // sizes["traj"]
    others = [bit for bit in reversed(bits) if bit != core]
    rounds = [[core]] * (core in bits) + [others[k : k + 2] for k in range(0, len(others), 2)]
    for masks in rounds:
        partners = [0]
        for mask in masks:
            partners = partners + [one ^ mask for one in partners]
        parts = [
            lax.ppermute(values, axes, [(i, i ^ one) for i in range(size)]) if one else values for one in partners
        ]
        while len(parts) > 1:
            parts = [parts[k] + parts[k + 1] for k in range(0, len(parts), 2)]
        values = parts[0]
    return values


def body(sizes, density, momentum, tracer, cotangent, w_in, b_in, w_mid, b_mid, w_out, b_out):
    nx, ny = density.shape[1:]
    hid = w_in.shape[0]
    wide = FACES * hid
    groups = nx // FACES
    half = groups // PAIR
    lanes = PAIR * ny
    segs = ny // SEG
    rim_rows = nx // segs
    ring = sizes["tx"] * sizes["ty"]
    shape = jax.ShapeDtypeStruct

    operands = [
        density, momentum, tracer, cotangent, w_in.T, b_in[None], w_mid, b_mid[None], w_out, b_out[None]
    ]
    rim, to_first, to_second, state, cots, *matrices = call(
        pack_kernel,
        [
            shape((8, rim_rows, ny), F32),
            shape((8, FACES, ny), F32),
            shape((8, FACES, ny), F32),
            shape((4, nx, ny), F32),
            shape((4, nx, ny), F32),
            shape((wide // 2, 6 * 32 + ONES), BF16),
            shape((wide, 6 * 128), BF16),
            shape((wide, ny), F32),
            shape((4 * hid, 8 * hid), BF16),
            shape((2 * hid, ny), F32),
            shape((192, wide), BF16),
            shape((64, ny), F32),
            shape((wide, 192), BF16),
            shape((2 * hid, 6 * hid), BF16),
            shape((128, 2 * wide), BF16),
            shape((256, 2 * wide), BF16),
        ],
        [pltpu.with_memory_space_constraint(one, pltpu.HBM) for one in operands],
        in_spaces=whole(10, pltpu.HBM),
        scratch=[pltpu.VMEM(one.shape, F32) for one in operands[4:]] + [pltpu.SemaphoreType.DMA((10,))],
    )
    axes = ("tx", "ty")
    swaps = [[(i, (i + 1 if (i + first) % 2 == 0 else i - 1) % ring) for i in range(ring)] for first in range(2)]
    from_first, from_second = (
        lax.ppermute(one, axes, swap) for one, swap in zip((to_first, to_second), swaps)
    )

    middle, *kept = call(
        x_forward_kernel,
        [shape((4, nx, ny), F32)]
        + [shape((half, wide, lanes), BF16)] * 4
        + [shape((half, wide, lanes), F32)] * 2
        + [shape((half, 64, lanes), F32)],
        [state, matrices[0]] + matrices[3:7],
        scratch=[pltpu.VMEM((4, nx + FACES, ny), F32)],
        flops=10**10,
        moved=10**7,
    )
    g_den, g_mom, g_tra, g_weights = call(
        back_kernel,
        [
            shape(density.shape, F32),
            shape(momentum.shape, F32),
            shape(tracer.shape, F32),
            shape((hid + 8, 128), F32),
        ],
        [state, cots, middle, rim, from_first, from_second] + matrices + kept,
        scratch=[
            pltpu.VMEM((4, rim_rows + FACES, ny), F32),
            pltpu.VMEM((4, rim_rows, ny), F32),
            pltpu.VMEM((4, rim_rows + FACES, ny), F32),
            pltpu.VMEM((4, rim_rows, ny), F32),
            pltpu.VMEM((4, rim_rows, ny), F32),
            pltpu.VMEM((4, nx, ny), F32),
            pltpu.VMEM((2 * wide, 256), F32),
            pltpu.VMEM((2 * wide, 256), F32),
            pltpu.VMEM((wide, ny), F32),
            pltpu.VMEM((8 * hid + ONES, 8 * hid), F32),
            pltpu.VMEM((2 * wide, 128), F32),
            pltpu.VMEM((64, lanes), F32),
        ],
        flops=4 * 10**10,
        moved=2 * 10**7,
    )
    total = sum_all(g_weights, sizes)
    g_w_in, g_b_in, g_w_mid, g_b_mid, g_w_out, g_b_out = call(
        finish_kernel,
        [
            shape((w_in.shape[1], hid), F32),
            shape((1, hid), F32),
            shape(w_mid.shape, F32),
            shape((1, hid), F32),
            shape(w_out.shape, F32),
            shape((1, b_out.shape[0]), F32),
        ],
        [total],
    )
    return (g_den, g_mom, g_tra, g_w_in.T, g_b_in[0], g_w_mid, g_b_mid[0], g_w_out, g_b_out[0])


def solution(mesh):
    flow = P("traj", None, ("tx", "ty"))
    deep = P("traj", None, None, ("tx", "ty"))
    return jax.shard_map(
        functools.partial(body, dict(mesh.shape)),
        mesh=mesh,
        in_specs=(flow, deep, flow, deep) + (P(),) * 6,
        out_specs=(flow, deep, flow) + (P(),) * 6,
        check_vma=False,
    )
```

```python
import functools

import jax
import jax.numpy as jnp
from jax import lax
from jax.experimental import pallas as pl
from jax.experimental.pallas import tpu as pltpu
from jax.sharding import PartitionSpec as P

courant = 0.1
slope_gain = 0.25
F32 = jnp.float32
BF16 = jnp.bfloat16
FACES = 8
SEG = 16
RIM = 4
PAIR = 8
RIM_PAIR = 4
ONES = 16
VMEM_BYTES = 32 * 2**20


def dot(a, b):
    return lax.dot_general(a, b, (((1,), (0,)), ((), ())), preferred_element_type=F32)


def dot_nt(a, b):
    return lax.dot_general(a, b, (((1,), (1,)), ((), ())), preferred_element_type=F32)


def exact(a, b):
    return lax.dot_general(
        a, b, (((1,), (0,)), ((), ())), precision=lax.Precision.HIGHEST, preferred_element_type=F32
    )


def exact_nt(a, b):
    return lax.dot_general(
        a, b, (((1,), (1,)), ((), ())), precision=lax.Precision.HIGHEST, preferred_element_type=F32
    )


def split(values):
    high = values.astype(BF16)
    return high, (values - high.astype(F32)).astype(BF16)


def split3(values):
    high = values.astype(BF16)
    rest = values - high.astype(F32)
    middle = rest.astype(BF16)
    return high, middle, (rest - middle.astype(F32)).astype(BF16)


def rows_cols(shape):
    return lax.broadcasted_iota(jnp.int32, shape, 0), lax.broadcasted_iota(jnp.int32, shape, 1)


def quot(values, n):
    return values >> (n.bit_length() - 1) if n & (n - 1) == 0 else values // n


def rest(values, n):
    return values & (n - 1) if n & (n - 1) == 0 else values % n


def pick(shape, test, dtype=BF16):
    r, c = rows_cols(shape)
    return jnp.where(test(r, c), 1.0, 0.0).astype(dtype)


def stack(parts):
    return jnp.concatenate(parts, 0)


def side(parts):
    return jnp.concatenate(parts, 1)


STACKED = (0, 0, 0, 1, 1, 2)


def stacked(parts):
    return [parts[0], parts[1], parts[2], parts[0], parts[1], parts[0]]


def level_of(block):
    return jnp.where(block < 3, 0, jnp.where(block < 5, 1, 2))


def choose(values, levels):
    parts = [part.astype(F32) for part in split3(values)]
    total = jnp.zeros(values.shape, F32)
    for k, part in enumerate(parts):
        total = jnp.where(levels == k, part, total)
    return total


def y_column(m):
    return 4 * (2 * (m >> 5) + ((m & 7) >> 2)) + ((m & 31) >> 3)


def build_first(w, b, hid):
    x_cols, y_cols, step = 6 * 32 + ONES, 4 * 64, 256

    def source(q, n):
        s = n >> 8
        m = n & (step - 1)
        in_x = (s < 4) & (m < 192) & (q == 4 * s + ((m & 31) >> 3))
        in_y = (s == 4) & (q == y_column(m & 63))
        return in_x | in_y

    values = exact(w, pick((16, 4 * step + y_cols), source, F32))
    _, n = rows_cols(values.shape)
    for_x = choose(values, level_of((n & (step - 1)) >> 5))
    for_y = values[:, 4 * step :]
    block = n[:, :y_cols] >> 6
    upper = choose(for_y, jnp.where(block < 3, 0, 2))
    lower = choose(for_y, jnp.where(block < 2, 1, -1))

    at, _ = rows_cols((x_cols, hid))
    rows = jnp.zeros((x_cols, hid), F32)
    for k, level in enumerate(split3(b)):
        rows = jnp.where(at == 192 + k, jnp.broadcast_to(level.astype(F32), (x_cols, hid)), rows)
    bias = dot_nt(pick((hid, hid), lambda q, n: q == n), rows.astype(BF16))

    half = FACES // 2
    r, c = rows_cols((half * hid, x_cols))
    shift = jnp.where(c < 192, (c & 7) - quot(r, hid), -1)
    first_x = stack([bias] * half)
    for s in range(4):
        part = for_x[:, s * step : s * step + x_cols]
        first_x = jnp.where(shift == s, stack([part] * half), first_x)
    r, c = rows_cols((2 * half * hid, y_cols))
    keep = (c & 3) == rest(quot(r, hid), half)
    first_y = jnp.where(keep, stack([upper] * half + [lower] * half), 0.0)
    return first_x.astype(BF16), first_y.astype(BF16)


def build_first_back(w_t, hid):
    wide = FACES // 2 * hid

    def source(q, n):
        in_x = (q < 128) & (n == 4 * (q >> 5) + ((q & 31) >> 3))
        in_y = (q >= 128) & (n == y_column(q - 128))
        return in_x | in_y

    rows = exact(pick((128 + 64, 16), source, F32), w_t)
    right = pick((hid, 2 * wide), lambda q, n: rest(n, hid) == q)
    high, low = (dot(part, right) for part in split(rows))
    r, c = rows_cols(high.shape)
    low = jnp.where(c < wide, low, 0.0)
    face = quot(rest(c, wide), hid)
    shift = (r & 7) - face
    upper = lower = jnp.zeros((32, 2 * wide), F32)
    for s in range(4):
        keep = shift[:32] == s
        upper = jnp.where(keep, high[32 * s : 32 * (s + 1)], upper)
        lower = jnp.where(keep, low[32 * s : 32 * (s + 1)], lower)
    keep = ((r & 3) == face)[128:]
    back_y = stack([jnp.where(keep, high[128:], 0.0), jnp.where(keep, low[128:], 0.0)])
    return stack([upper, lower]).astype(BF16), back_y.astype(BF16)


def build_mid(w, hid):
    block = 2 * hid
    tiled = exact(w, pick((hid, 4 * block), lambda q, n: rest(n, hid) == q, F32))
    _, n = rows_cols(tiled.shape)
    upper = choose(tiled, jnp.where(n < 3 * block, 0, 2))
    lower = choose(tiled, jnp.where(n < 2 * block, 1, -1))
    r, c = rows_cols((2 * block, 4 * block))
    keep = quot(rest(r, block), hid) == quot(rest(c, block), hid)
    return jnp.where(keep, stack([upper, upper, lower, lower]), 0.0).astype(BF16)


def build_mid_back(w, hid):
    block = 2 * hid
    turned = exact_nt(pick((hid, hid), lambda q, n: q == n, F32), w)
    tiled = exact(turned, pick((hid, 3 * block), lambda q, n: rest(n, hid) == q, F32))
    _, n = rows_cols(tiled.shape)
    tiled = choose(tiled, jnp.where(quot(n, block) == 1, 1, 0))
    r, c = rows_cols((block, 3 * block))
    keep = quot(r, hid) == quot(rest(c, block), hid)
    return jnp.where(keep, stack([tiled] * 2), 0.0).astype(BF16)


def build_out(w, hid):
    wide = FACES * hid
    rows = exact(pick((64, 8), lambda q, n: (q >> 3) == n, F32), w)
    tiled = dot(stack(list(split3(rows))), pick((hid, wide), lambda q, n: rest(n, hid) == q))
    r, c = rows_cols(tiled.shape)
    return jnp.where((r & 7) == quot(c, hid), tiled, 0.0).astype(BF16)


def build_out_back(w, hid):
    wide = FACES * hid
    turned = exact_nt(pick((hid, hid), lambda q, n: q == n, F32), w)
    tiled = exact(turned, pick((8, 192), lambda q, n: ((n & 63) >> 3) == q, F32))
    _, n = rows_cols(tiled.shape)
    tiled = choose(tiled, jnp.where((n >> 6) == 1, 1, 0))
    r, c = rows_cols((wide, 192))
    return jnp.where(quot(r, hid) == (c & 7), stack([tiled] * FACES), 0.0).astype(BF16)


def spread_bias(b, lanes, copies):
    n = b.shape[1]
    rows = exact_nt(pick((n, n), lambda q, m: q == m, F32), jnp.broadcast_to(b, (lanes, n)))
    return stack([rows] * copies)


def spread(bias_ref, width):
    return side([bias_ref[...]] * (width // bias_ref.shape[1]))


def limiter_forward(first, weights, hid):
    first_ref, first_bias_ref, mid_ref, mid_bias_ref, out_ref, out_bias_ref = weights
    width = first[0][0].shape[1]
    if first_bias_ref is None:
        ones = [jnp.ones((ONES, width), BF16)]
        h1 = stack([jnp.tanh(dot(first_ref[...], stack(stacked(one) + ones))) for one in first])
    else:
        parts = []
        for high, middle, low in first:
            both = dot(first_ref[...], stack([high, middle, low, high]))
            half = both.shape[0] // 2
            parts.append(jnp.tanh(both[:half] + both[half:] + spread(first_bias_ref, width)))
        h1 = stack(parts)
    h1_parts = split3(h1)
    block = 2 * hid
    parts = []
    for at in range(0, FACES * hid, block):
        high, middle, low = (p[at : at + block] for p in h1_parts)
        both = dot(mid_ref[...], stack([high, middle, low, high]))
        parts.append(jnp.tanh(both[:block] + both[block:] + spread(mid_bias_ref, width)))
    h2 = stack(parts)
    h2_parts = split3(h2)
    rows = 8 * FACES
    a = dot(out_ref[...], h2_parts[0])
    b = dot(out_ref[: 2 * rows, :], h2_parts[1])
    c = dot(out_ref[:rows, :], h2_parts[2])
    gates = jnp.tanh(
        ((a[2 * rows :] + b[rows:] + c) + (a[rows : 2 * rows] + b[:rows])) + a[:rows] + spread(out_bias_ref, width)
    )
    return h1, h1_parts[:2], h2, h2_parts[:2], gates


def limiter_backward(d3, h1, h2, h1_pair, h2_pair, out_back_ref, mid_back_ref, acc, hid):
    d3_hi, d3_lo = split(d3)
    dh2 = dot(out_back_ref[...], stack([d3_hi, d3_hi, d3_lo]))
    if acc is not None:
        acc[2][...] += dot_nt(stack(list(h2_pair)), stack([d3_hi, d3_lo]))
        acc[3][...] += d3
    d2_hi, d2_lo = split(dh2 * (1.0 - h2 * h2))
    block = 2 * hid
    parts = []
    for at in range(0, FACES * hid, block):
        hi, lo = d2_hi[at : at + block], d2_lo[at : at + block]
        parts.append(dot(mid_back_ref[...], stack([hi, hi, lo])))
    if acc is not None:
        ones = jnp.ones((ONES, d3.shape[1]), BF16)
        lefts, rights = [], []
        for at in range(0, FACES * hid, 2 * block):
            lefts.append(stack([part[at : at + 2 * block] for part in h1_pair] + [ones]))
            rights.append(stack([part[at : at + 2 * block] for part in (d2_hi, d2_lo)]))
        acc[1][...] += dot_nt(side(lefts), side(rights))
    return stack(parts) * (1.0 - h1 * h1)


def first_backward(d1, back_ref):
    wide = d1[0].shape[0] // 2
    found = []
    for at in (0, wide):
        both = dot(back_ref[...], stack([part[at : at + wide] for part in d1]))
        half = both.shape[0] // 2
        found.append(both[:half] + both[half:])
    return found


def add_first_grads(first, d1, acc_in):
    ones = jnp.ones((ONES, d1[0].shape[1]), BF16)
    wide = d1[0].shape[0] // 2
    lefts = [stack([one[0], one[1], ones]) for one in first]
    rights = [stack([part[at : at + wide] for part in d1]) for at in (0, wide)]
    acc_in[...] += dot_nt(side(lefts), side(rights))


def edge_states(cells, gates):
    left, right = [], []
    for c in range(4):
        low = gates[FACES * c : FACES * (c + 1)]
        high = gates[FACES * (c + 4) : FACES * (c + 5)]
        left.append(cells[1][c] + slope_gain * low * (cells[2][c] - cells[0][c]))
        right.append(cells[2][c] - slope_gain * high * (cells[3][c] - cells[1][c]))
    return left, right


def face_flux(left, right):
    ul = left[1] / left[0]
    ur = right[1] / right[0]
    half_speed = 0.5 * (jnp.maximum(jnp.abs(ul), jnp.abs(ur)) + 1.0)
    fl = [left[1], left[1] * ul + left[0], left[2] * ul, left[3] * ul]
    fr = [right[1], right[1] * ur + right[0], right[2] * ur, right[3] * ur]
    return [0.5 * (fl[c] + fr[c]) - half_speed * (right[c] - left[c]) for c in range(4)]


def sign_of(values):
    return jnp.where(values > 0.0, 1.0, jnp.where(values < 0.0, -1.0, 0.0))


def face_flux_backward(left, right, d_flux):
    inv_l, inv_r = 1.0 / left[0], 1.0 / right[0]
    ul, ur = left[1] / left[0], right[1] / right[0]
    al, ar = jnp.abs(ul), jnp.abs(ur)
    half_speed = 0.5 * (jnp.maximum(al, ar) + 1.0)
    d_speed = -0.5 * sum(d_flux[c] * (right[c] - left[c]) for c in range(4))
    share = jnp.where(al > ar, 1.0, jnp.where(al < ar, 0.0, 0.5))
    half = [0.5 * d for d in d_flux]
    spread = [half_speed * d for d in d_flux]

    def one(state, u, inv, speed_part, sign):
        du = half[1] * state[1] + half[2] * state[2] + half[3] * state[3] + speed_part * sign_of(u)
        over = du * inv
        return [
            half[1] - over * u + sign * spread[0],
            half[0] + half[1] * u + over + sign * spread[1],
            half[2] * u + sign * spread[2],
            half[3] * u + sign * spread[3],
        ]

    return (
        one(left, ul, inv_l, d_speed * share, 1.0),
        one(right, ur, inv_r, d_speed * (1.0 - share), -1.0),
    )


def edge_backward(cells, gates, d_left, d_right):
    lows, highs = [], []
    direct = [[None] * 4 for _ in range(4)]
    for c in range(4):
        low = gates[FACES * c : FACES * (c + 1)]
        high = gates[FACES * (c + 4) : FACES * (c + 5)]
        lows.append(slope_gain * (cells[2][c] - cells[0][c]) * d_left[c])
        highs.append(-slope_gain * (cells[3][c] - cells[1][c]) * d_right[c])
        low_part = slope_gain * low * d_left[c]
        high_part = slope_gain * high * d_right[c]
        direct[0][c] = -low_part
        direct[1][c] = d_left[c] + high_part
        direct[2][c] = d_right[c] + low_part
        direct[3][c] = -high_part
    return stack(lows + highs) * (1.0 - gates * gates), direct


def turn(values, shift, axis):
    size = values.shape[axis]
    return values if shift % size == 0 else pltpu.roll(values, shift % size, axis)


def x_cells(tiles):
    return [[turn(t, -s, 0)[:FACES] for t in tiles] for s in range(4)]


def pack_kernel(den, mom, tra, cot, w_in, b_in, w_mid, b_mid, w_out, b_out,
                rim, to_first, to_second, state, cots, first_x, first_y, first_bias, mid, mid_bias, out, out_bias,
                out_back, mid_back, first_x_back, first_y_back, *scratch):
    *small, sems = scratch
    nx, ny = den.shape[1:]
    segs = ny // SEG
    rows = nx // segs
    hid = w_in.shape[1]
    copies = [
        pltpu.make_async_copy(source, target, sems.at[k])
        for k, (source, target) in enumerate(
            list(zip([w_in, b_in, w_mid, b_mid, w_out, b_out], small))
            + [
                (den.at[0], state.at[0]),
                (mom.at[0], state.at[pl.ds(1, 2)]),
                (tra.at[0], state.at[3]),
                (cot.at[0], cots),
            ]
        )
    ]
    for one in copies:
        one.start()
    for one in copies[:6]:
        one.wait()
    w_in, b_in, w_mid, b_mid, w_out, b_out = small
    lanes = out_bias.shape[1]
    w_in_rows = exact_nt(pick((hid, hid), lambda q, n: q == n, F32), w_in[...])
    first_x[...], first_y[...] = build_first(w_in_rows, b_in[...], hid)
    first_bias[...] = spread_bias(b_in[...], lanes, FACES // 2)
    mid[...] = build_mid(w_mid[...], hid)
    mid_bias[...] = spread_bias(b_mid[...], lanes, 2)
    out[...] = build_out(w_out[...], hid)
    out_bias[...] = exact_nt(
        pick((64, 8), lambda q, n: (q >> 3) == n, F32), jnp.broadcast_to(b_out[...], (lanes, 8))
    )
    out_back[...] = build_out_back(w_out[...], hid)
    mid_back[...] = build_mid_back(w_mid[...], hid)
    first_x_back[...], first_y_back[...] = build_first_back(w_in[...], hid)

    for one in copies[6:]:
        one.wait()
    lane = lane_index(ny)
    for v in range(8):
        plane = state.at[v] if v < 4 else cots.at[v - 4]
        for at in range(0, rows, FACES):
            total = jnp.zeros((FACES, ny), F32)
            for s in range(segs):
                first = s * SEG + RIM
                moved = turn(plane[pl.ds(s * rows + at, FACES), :], first + RIM, 1)
                total = jnp.where((lane >= first) & (lane < first + 2 * RIM), moved, total)
            rim[v, pl.ds(at, FACES), :] = total
    is_odd = odd_mask(ny)
    spot = lane & (SEG - 1)
    for v in range(8):
        sides = []
        for first in (2 * RIM, RIM):
            total = jnp.zeros((FACES, ny), F32)
            for g in range(rows // FACES):
                moved = turn(rim[v, pl.ds(g * FACES, FACES), :], g * RIM - first, 1)
                total = jnp.where((spot >= g * RIM) & (spot < (g + 1) * RIM), moved, total)
            sides.append(total)
        to_first[v] = jnp.where(is_odd, sides[0], sides[1])
        to_second[v] = jnp.where(is_odd, sides[1], sides[0])


def odd_mask(ny):
    return jnp.full((FACES, ny), lax.rem(lax.axis_index(("tx", "ty")), 2), jnp.int32) == 1


def row_block(at):
    return pl.ds(pl.multiple_of(at * FACES, FACES), FACES)


def x_tiles(planes, group, groups):
    after = jnp.where(group + 1 == groups, 0, group + 1)
    return [stack([plane[row_block(group), :], plane[row_block(after), :]]) for plane in planes]


def pair_tiles(planes, step, half):
    sets = [x_tiles(planes, step + k * half, PAIR * half) for k in range(PAIR)]
    return [side([one[c] for one in sets]) for c in range(len(planes))]


def x_windows(tiles):
    half = FACES // 2
    return [stack([turn(tile, -at, 0)[:FACES] for tile in tiles]) for at in (0, half)]


def swap_halves(first, second):
    half = FACES // 2
    upper = rows_cols(first.shape)[0] < half
    return jnp.where(upper, first, turn(second, half, 0)), jnp.where(upper, turn(first, half, 0), second)


def y_windows(cells):
    pairs = [swap_halves(cells[s][c], cells[s + 1][c]) for s in (0, 2) for c in range(4)]
    return [stack([one[k] for one in pairs]) for k in range(2)]


def y_unwindow(parts):
    found = [[None] * 4 for _ in range(4)]
    for s in (0, 2):
        for c in range(4):
            at = FACES * (2 * s + c)
            found[s][c], found[s + 1][c] = swap_halves(parts[0][at : at + FACES], parts[1][at : at + FACES])
    return found


def x_forward(tiles, weights, hid):
    h1, h1_pair, h2, h2_pair, gates = limiter_forward([split3(one) for one in x_windows(tiles)], weights, hid)
    cells = x_cells(tiles)
    return h1_pair, h2_pair, gates, face_flux(*edge_states(cells, gates))


def update_cells(plane_rows, flux_rows):
    upper = turn(flux_rows, -7, 0)[:FACES]
    lower = turn(flux_rows, -6, 0)[:FACES]
    return plane_rows - courant * (upper - lower)


def x_forward_kernel(state, first_x, mid, mid_bias, out, out_bias,
                     middle, h1_hi, h1_lo, h2_hi, h2_lo, gates_out, flux):
    nx, ny = state.shape[1:]
    groups = nx // FACES
    half = groups // PAIR
    hid = mid.shape[0] // 4
    x_weights = (first_x, None, mid, mid_bias, out, out_bias)
    planes = [state.at[c] for c in range(4)]

    def step_of(step, _):
        tiles = pair_tiles(planes, step, half)
        h1_pair, h2_pair, gates, fluxes = x_forward(tiles, x_weights, hid)
        for target, value in zip((h1_hi, h1_lo, h2_hi, h2_lo, gates_out), h1_pair + h2_pair + (gates,)):
            target[step] = value
        for c in range(4):
            for k in range(PAIR):
                flux[c, row_block(step + k * half + 1), :] = fluxes[c][:, k * ny : (k + 1) * ny]
        return 0

    lax.fori_loop(0, half, step_of, 0)
    for c in range(4):
        flux[c, :FACES, :] = flux[c, nx : nx + FACES, :]

    def update(group, _):
        for c in range(4):
            both = stack([flux[c, row_block(group), :], flux[c, row_block(group + 1), :]])
            middle[c, row_block(group), :] = update_cells(planes[c][row_block(group), :], both)
        return 0

    lax.fori_loop(0, groups, update, 0)


def y_order(planes):
    return [planes[0], planes[2], planes[1], planes[3]]


def lane_index(width):
    return lax.broadcasted_iota(jnp.int32, (FACES, width), 1)


def y_step(cells, cots, halo_mask, refs, acc, hid):
    weights, out_back, mid_back, first_y_back = refs
    window = [split3(one) for one in y_windows(cells)]
    h1, h1_pair, h2, h2_pair, gates = limiter_forward(window, weights, hid)
    left, right = edge_states(cells, gates)
    d_flux = [courant * (cots[1][c] - cots[0][c]) for c in range(4)]
    d_left, d_right = face_flux_backward(left, right, d_flux)
    if halo_mask is not None:
        d_left = [jnp.where(halo_mask, d, 0.0) for d in d_left]
        d_right = [jnp.where(halo_mask, d, 0.0) for d in d_right]
    d3_full, direct = edge_backward(cells, gates, d_left, d_right)
    d1_full = limiter_backward(d3_full, h1, h2, h1_pair, h2_pair, out_back, mid_back, acc, hid)
    d1 = split(d1_full)
    d_window = y_unwindow(first_backward(d1, first_y_back))
    if acc is not None:
        add_first_grads(window, d1, acc[0])
    return [
        [d_window[s][c] + direct[s][c] for c in range(4)]
        for s in range(4)
    ]


def y_gather(parts, ny):
    lane = lane_index(ny)
    out = []
    for c in range(4):
        a = turn(jnp.where(lane >= 1, parts[0][c], 0.0), -1, 1)
        b = turn(jnp.where(lane < ny - 1, parts[2][c], 0.0), 1, 1)
        d = turn(jnp.where(lane < ny - 2, parts[3][c], 0.0), 2, 1)
        out.append(parts[1][c] + a + b + d)
    return out


def fold_rows(values, hid):
    return sum(values[at : at + hid] for at in range(0, values.shape[0], hid))


def back_kernel(state, cot, middle, own, from_first, from_second,
                first_x, first_y, first_bias, mid, mid_bias, out, out_bias,
                out_back, mid_back, first_x_back, first_y_back,
                h1_hi, h1_lo, h2_hi, h2_lo, gates_in,
                g_den, g_mom, g_tra, g_weights,
                rim_state, rim_cot, rim_flux, rim_middle, rim_grad, d_middle,
                acc_x, acc_y, acc_mid, acc_out, acc_out_bias):
    nx, ny = state.shape[1:]
    groups = nx // FACES
    half = groups // PAIR
    hid = mid.shape[0] // 4
    x_weights = (first_x, None, mid, mid_bias, out, out_bias)
    segs = ny // SEG
    rim_rows = nx // segs
    rim_groups = rim_rows // FACES
    rim_half = rim_groups // RIM_PAIR

    for acc in (acc_x, acc_y, acc_mid, acc_out, acc_out_bias):
        acc[...] = jnp.zeros(acc.shape, F32)

    lane = lane_index(ny)
    spot = lane & (SEG - 1)
    is_odd = odd_mask(ny)
    for v in range(8):
        for g in range(rim_groups):
            rows = pl.ds(g * FACES, FACES)
            mine, first, second = own[v, rows, :], from_first[v], from_second[v]
            left, right = jnp.where(is_odd, first, second), jnp.where(is_odd, second, first)
            value = jnp.where(
                spot < RIM,
                turn(left, -g * RIM, 1),
                jnp.where(
                    spot < 2 * RIM,
                    turn(mine, -RIM, 1),
                    jnp.where(spot < 3 * RIM, turn(mine, RIM, 1), turn(right, (3 - g) * RIM, 1)),
                ),
            )
            if v < 4:
                rim_state[v, rows, :] = value
                if g == 0:
                    rim_state[v, pl.ds(rim_rows, FACES), :] = turn(value, -SEG, 1)
            else:
                rim_cot[v - 4, rows, :] = value

    def rim_forward(step, _):
        sets = [
            [
                stack([
                    rim_state[c, row_block(step + k * rim_half), :],
                    rim_state[c, row_block(step + k * rim_half + 1), :],
                ])
                for c in range(4)
            ]
            for k in range(RIM_PAIR)
        ]
        tiles = [side([one[c] for one in sets]) for c in range(4)]
        fluxes = x_forward(tiles, x_weights, hid)[3]
        for c in range(4):
            for k in range(RIM_PAIR):
                rim_flux[c, row_block(step + k * rim_half + 1), :] = fluxes[c][:, k * ny : (k + 1) * ny]
        return 0

    lax.fori_loop(0, rim_half, rim_forward, 0)
    for c in range(4):
        rim_flux[c, :FACES, :] = turn(rim_flux[c, rim_rows : rim_rows + FACES, :], SEG, 1)
        for g in range(rim_groups):
            rows = pl.ds(g * FACES, FACES)
            both = stack([rim_flux[c, rows, :], rim_flux[c, pl.ds((g + 1) * FACES, FACES), :]])
            rim_middle[c, rows, :] = update_cells(rim_state[c, rows, :], both)

    refs = ((first_y, first_bias, mid, mid_bias, out, out_bias), out_back, mid_back, first_y_back)
    spot_wide = lane_index(RIM_PAIR * ny) & (SEG - 1)
    rim_faces = (spot_wide == RIM - 2) | (spot_wide == RIM - 1) | (spot_wide == 3 * RIM)

    def rim_back(step, _):
        cells = [[[] for _ in range(4)] for _ in range(4)]
        cots = [[[] for _ in range(4)] for _ in range(2)]
        for k in range(RIM_PAIR):
            rows = row_block(step + k * rim_half)
            for c in range(4):
                value = rim_middle[c, rows, :]
                for s in range(4):
                    cells[s][c].append(turn(value, 1 - s, 1))
                value = rim_cot[c, rows, :]
                for s in range(2):
                    cots[s][c].append(turn(value, -s, 1))
        cells = [y_order([side(one) for one in row]) for row in cells]
        cots = [y_order([side(one) for one in row]) for row in cots]
        parts = y_step(cells, cots, rim_faces, refs, None, hid)
        for k in range(RIM_PAIR):
            own_parts = [[one[:, k * ny : (k + 1) * ny] for one in row] for row in parts]
            gathered = y_order(y_gather(own_parts, ny))
            for c in range(4):
                rim_grad[c, row_block(step + k * rim_half), :] = gathered[c]
        return 0

    lax.fori_loop(0, rim_half, rim_back, 0)

    def main_y(step, _):
        cells = [[[] for _ in range(4)] for _ in range(4)]
        cots = [[[] for _ in range(4)] for _ in range(2)]
        for k in range(PAIR):
            group = step + k * half
            rows = row_block(group)
            seg = group // rim_groups
            rim_at = row_block(group - seg * rim_groups)
            to_low = ny - (seg * SEG + 3 * RIM)
            to_high = lax.rem(ny - 1 - (seg * SEG + RIM - 1) + ny, ny)
            for c in range(4):
                value = middle[c, rows, :]
                rim_value = rim_middle[c, rim_at, :]
                low = jnp.where(lane < 2, pltpu.roll(rim_value, to_low, 1), value)
                high = jnp.where(lane == ny - 1, pltpu.roll(rim_value, to_high, 1), value)
                cells[0][c].append(turn(high, 1, 1))
                cells[1][c].append(value)
                cells[2][c].append(turn(jnp.where(lane < 1, low, value), -1, 1))
                cells[3][c].append(turn(low, -2, 1))
                value = cot[c, rows, :]
                rim_value = rim_cot[c, rim_at, :]
                low = jnp.where(lane < 1, pltpu.roll(rim_value, to_low, 1), value)
                cots[0][c].append(value)
                cots[1][c].append(turn(low, -1, 1))
        cells = [y_order([side(one) for one in row]) for row in cells]
        cots = [y_order([side(one) for one in row]) for row in cots]
        parts = y_step(cells, cots, None, refs, (acc_y, acc_mid, acc_out, acc_out_bias), hid)
        for k in range(PAIR):
            group = step + k * half
            rows = row_block(group)
            seg = group // rim_groups
            rim_at = row_block(group - seg * rim_groups)
            own_parts = [[one[:, k * ny : (k + 1) * ny] for one in row] for row in parts]
            gathered = y_order(y_gather(own_parts, ny))
            to_low = ny - (seg * SEG + RIM)
            to_high = lax.rem(ny - 1 - (seg * SEG + 3 * RIM - 1) + ny, ny)
            for c in range(4):
                rim_value = rim_grad[c, rim_at, :]
                from_rim = jnp.where(
                    lane < 2,
                    pltpu.roll(rim_value, to_low, 1),
                    jnp.where(lane == ny - 1, pltpu.roll(rim_value, to_high, 1), 0.0),
                )
                d_middle[c, rows, :] = cot[c, rows, :] + gathered[c] + from_rim
        return 0

    lax.fori_loop(0, half, main_y, 0)

    planes = [state.at[c] for c in range(4)]
    grads = [g_den.at[0], g_mom.at[0, 0], g_mom.at[0, 1], g_tra.at[0]]
    d_planes = [d_middle.at[c] for c in range(4)]

    def main_x(step, carry):
        tiles = pair_tiles(planes, step, half)
        d_tiles = pair_tiles(d_planes, step, half)
        gates = gates_in[step]
        h1_pair = (h1_hi[step], h1_lo[step])
        h2_pair = (h2_hi[step], h2_lo[step])
        h1 = h1_pair[0].astype(F32) + h1_pair[1].astype(F32)
        h2 = h2_pair[0].astype(F32) + h2_pair[1].astype(F32)
        cells = x_cells(tiles)
        left, right = edge_states(cells, gates)
        d_flux = [courant * (turn(d, -2, 0)[:FACES] - turn(d, -1, 0)[:FACES]) for d in d_tiles]
        d_left, d_right = face_flux_backward(left, right, d_flux)
        d3_full, direct = edge_backward(cells, gates, d_left, d_right)
        d1_full = limiter_backward(
            d3_full, h1, h2, h1_pair, h2_pair, out_back, mid_back, (acc_x, acc_mid, acc_out, acc_out_bias), hid
        )
        d1 = split(d1_full)
        d_window = first_backward(d1, first_x_back)
        add_first_grads([split(one) for one in x_windows(tiles)], d1, acc_x)
        later = []
        for c in range(4):
            rows = slice(FACES * c, FACES * (c + 1))
            nothing = jnp.zeros_like(direct[0][c])
            total = stack([direct[0][c] + d_window[0][rows], nothing])
            total = total + turn(stack([d_window[1][rows], nothing]), FACES // 2, 0)
            for s in range(1, 4):
                total = total + turn(stack([direct[s][c], nothing]), s, 0)
            now = total[:FACES] + d_tiles[c][:FACES] + carry[c]
            for k in range(PAIR):
                grads[c][row_block(step + k * half), :] = now[:, k * ny : (k + 1) * ny]
            later.append(total[FACES:])
        return tuple(later)

    start = tuple(jnp.zeros((FACES, PAIR * ny), F32) for _ in range(4))
    last = lax.fori_loop(0, half, main_x, start)
    for c in range(4):
        for k in range(PAIR):
            at = (k + 1) % PAIR * half * FACES
            grads[c][pl.ds(at, FACES), :] += last[c][:, k * ny : (k + 1) * ny]

    lanes = g_weights.shape[1]
    values = acc_mid[: 8 * hid, :]
    r, c = rows_cols(values.shape)
    same = rest(quot(r, hid), 4) == rest(quot(c, hid), 4)
    values = fold_rows(jnp.where(same, values, 0.0), hid)
    grad_mid = exact_nt(
        pick((hid, 8 * hid), lambda q, n: rest(n, hid) == q, F32),
        stack([values, jnp.zeros((lanes - hid, 8 * hid), F32)]),
    )
    grad_mid_bias = exact(
        acc_mid[8 * hid : 8 * hid + 8, :], pick((8 * hid, lanes), lambda q, n: rest(q, hid) == n, F32)
    )
    r, c = rows_cols(acc_x.shape)
    values, shift = acc_x[...], (r & 7) - rest(quot(c, hid), 4)
    found = [jnp.where((shift == s) & (r < 64), values, 0.0)[:64] for s in range(4)]
    found.append(values[64:])
    r, c = rows_cols(acc_y.shape)
    found.append(jnp.where(((r & 3) == rest(quot(c, hid), 4)) | (r >= 128), acc_y[...], 0.0))
    found = exact(
        stack(found),
        pick((8 * hid, lanes), lambda q, n: (rest(n - q, hid) == 0) & (n >= hid) & (n < 2 * hid), F32),
    )
    y_at = 4 * 64 + ONES

    def source(q, n):
        in_x = (n < 256) & (q == 4 * (n >> 6) + ((n & 31) >> 3))
        m = n - y_at
        in_y = (m >= 0) & (m < 128) & (q == y_column(m & 63))
        return in_x | in_y | ((n == 256) | (m == 128)) & (q == 24)

    beside = exact(pick((32, found.shape[0]), source, F32), found)
    r, c = rows_cols(acc_out.shape)
    found = fold_rows(jnp.where((c & 7) == rest(quot(r, hid), FACES), acc_out[...], 0.0), hid)
    beside = beside + exact_nt(
        pick((32, found.shape[1]), lambda q, n: q == 16 + ((n & 63) >> 3), F32),
        stack([jnp.zeros((hid, found.shape[1]), F32), found, jnp.zeros((lanes - 2 * hid, found.shape[1]), F32)]),
    )
    out_bias_rows = exact_nt(jnp.ones((8, acc_out_bias.shape[1]), F32), acc_out_bias[...])
    grad_out_bias = exact_nt(out_bias_rows, pick((lanes, 64), lambda q, n: (n >> 3) == q - hid, F32))
    r, c = rows_cols((8, lanes))
    g_weights[:hid, :] = grad_mid + beside
    g_weights[25:26, :] += grad_out_bias[:1]
    g_weights[hid:, :] = grad_mid_bias


def finish_kernel(total, g_w_in, g_b_in, g_w_mid, g_b_mid, g_w_out, g_b_out):
    hid = g_w_mid.shape[0]
    g_w_mid[...] = total[:hid, :hid]
    beside = total[:hid, hid : 2 * hid]
    g_w_in[...] = beside[:16]
    g_w_out[...] = beside[16:24]
    g_b_in[...] = beside[24:25]
    g_b_out[...] = beside[25:26, :8]
    g_b_mid[...] = total[hid : hid + 1, :hid]


def whole(count, space=pltpu.VMEM):
    return [pl.BlockSpec(memory_space=space)] * count


def call(kernel, outs, operands, out_spaces=None, in_spaces=None, scratch=(), flops=0, moved=0):
    return pl.pallas_call(
        kernel,
        out_shape=outs,
        in_specs=in_spaces or whole(len(operands)),
        out_specs=out_spaces or whole(len(outs)),
        scratch_shapes=list(scratch),
        compiler_params=pltpu.CompilerParams(vmem_limit_bytes=VMEM_BYTES),
        cost_estimate=pl.CostEstimate(flops=flops, bytes_accessed=moved, transcendentals=0),
    )(*operands)


def sum_all(values, sizes):
    axes, size = tuple(sizes), 1
    for one in sizes.values():
        size *= one
    if size & (size - 1):
        return lax.psum(values, axes)
    bits = [1 << k for k in range(size.bit_length() - 1)]
    core = size // sizes["traj"]
    others = [bit for bit in reversed(bits) if bit != core]
    rounds = [[core]] * (core in bits) + [others[k : k + 2] for k in range(0, len(others), 2)]
    for masks in rounds:
        partners = [0]
        for mask in masks:
            partners = partners + [one ^ mask for one in partners]
        parts = [
            lax.ppermute(values, axes, [(i, i ^ one) for i in range(size)]) if one else values for one in partners
        ]
        while len(parts) > 1:
            parts = [parts[k] + parts[k + 1] for k in range(0, len(parts), 2)]
        values = parts[0]
    return values


def body(sizes, density, momentum, tracer, cotangent, w_in, b_in, w_mid, b_mid, w_out, b_out):
    nx, ny = density.shape[1:]
    hid = w_in.shape[0]
    wide = FACES * hid
    groups = nx // FACES
    half = groups // PAIR
    lanes = PAIR * ny
    segs = ny // SEG
    rim_rows = nx // segs
    ring = sizes["tx"] * sizes["ty"]
    shape = jax.ShapeDtypeStruct

    operands = [
        density, momentum, tracer, cotangent, w_in.T, b_in[None], w_mid, b_mid[None], w_out, b_out[None]
    ]
    rim, to_first, to_second, state, cots, *matrices = call(
        pack_kernel,
        [
            shape((8, rim_rows, ny), F32),
            shape((8, FACES, ny), F32),
            shape((8, FACES, ny), F32),
            shape((4, nx, ny), F32),
            shape((4, nx, ny), F32),
            shape((wide // 2, 6 * 32 + ONES), BF16),
            shape((wide, 4 * 64), BF16),
            shape((wide // 2, ny), F32),
            shape((4 * hid, 8 * hid), BF16),
            shape((2 * hid, ny), F32),
            shape((192, wide), BF16),
            shape((64, ny), F32),
            shape((wide, 192), BF16),
            shape((2 * hid, 6 * hid), BF16),
            shape((64, wide), BF16),
            shape((128, wide), BF16),
        ],
        [pltpu.with_memory_space_constraint(one, pltpu.HBM) for one in operands],
        in_spaces=whole(10, pltpu.HBM),
        scratch=[pltpu.VMEM(one.shape, F32) for one in operands[4:]] + [pltpu.SemaphoreType.DMA((10,))],
    )
    axes = ("tx", "ty")
    swaps = [[(i, (i + 1 if (i + first) % 2 == 0 else i - 1) % ring) for i in range(ring)] for first in range(2)]
    from_first, from_second = (
        lax.ppermute(one, axes, swap) for one, swap in zip((to_first, to_second), swaps)
    )

    middle, *kept = call(
        x_forward_kernel,
        [shape((4, nx, ny), F32)]
        + [shape((half, wide, lanes), BF16)] * 4
        + [shape((half, 64, lanes), F32)],
        [state, matrices[0]] + matrices[3:7],
        scratch=[pltpu.VMEM((4, nx + FACES, ny), F32)],
        flops=10**10,
        moved=10**7,
    )
    g_den, g_mom, g_tra, g_weights = call(
        back_kernel,
        [
            shape(density.shape, F32),
            shape(momentum.shape, F32),
            shape(tracer.shape, F32),
            shape((hid + 8, 128), F32),
        ],
        [state, cots, middle, rim, from_first, from_second] + matrices + kept,
        scratch=[
            pltpu.VMEM((4, rim_rows + FACES, ny), F32),
            pltpu.VMEM((4, rim_rows, ny), F32),
            pltpu.VMEM((4, rim_rows + FACES, ny), F32),
            pltpu.VMEM((4, rim_rows, ny), F32),
            pltpu.VMEM((4, rim_rows, ny), F32),
            pltpu.VMEM((4, nx, ny), F32),
            pltpu.VMEM((2 * 32 + ONES, wide), F32),
            pltpu.VMEM((2 * 64 + ONES, wide), F32),
            pltpu.VMEM((8 * hid + ONES, 8 * hid), F32),
            pltpu.VMEM((2 * wide, 128), F32),
            pltpu.VMEM((64, lanes), F32),
        ],
        flops=4 * 10**10,
        moved=2 * 10**7,
    )
    total = sum_all(g_weights, sizes)
    g_w_in, g_b_in, g_w_mid, g_b_mid, g_w_out, g_b_out = call(
        finish_kernel,
        [
            shape((w_in.shape[1], hid), F32),
            shape((1, hid), F32),
            shape(w_mid.shape, F32),
            shape((1, hid), F32),
            shape(w_out.shape, F32),
            shape((1, b_out.shape[0]), F32),
        ],
        [total],
    )
    return (g_den, g_mom, g_tra, g_w_in.T, g_b_in[0], g_w_mid, g_b_mid[0], g_w_out, g_b_out[0])


def solution(mesh):
    flow = P("traj", None, ("tx", "ty"))
    deep = P("traj", None, None, ("tx", "ty"))
    return jax.shard_map(
        functools.partial(body, dict(mesh.shape)),
        mesh=mesh,
        in_specs=(flow, deep, flow, deep) + (P(),) * 6,
        out_specs=(flow, deep, flow) + (P(),) * 6,
        check_vma=False,
    )
```

```python
import functools

import jax
import jax.numpy as jnp
from jax import lax
from jax.experimental import pallas as pl
from jax.experimental.pallas import tpu as pltpu
from jax.sharding import PartitionSpec as P

courant = 0.1
slope_gain = 0.25
F32 = jnp.float32
BF16 = jnp.bfloat16
FACES = 8
SEG = 16
RIM = 4
PAIR = 8
RIM_PAIR = 4
ONES = 16
VMEM_BYTES = 32 * 2**20


def dot(a, b):
    return lax.dot_general(a, b, (((1,), (0,)), ((), ())), preferred_element_type=F32)


def dot_nt(a, b):
    return lax.dot_general(a, b, (((1,), (1,)), ((), ())), preferred_element_type=F32)


def exact(a, b):
    return lax.dot_general(
        a, b, (((1,), (0,)), ((), ())), precision=lax.Precision.HIGHEST, preferred_element_type=F32
    )


def exact_nt(a, b):
    return lax.dot_general(
        a, b, (((1,), (1,)), ((), ())), precision=lax.Precision.HIGHEST, preferred_element_type=F32
    )


def split(values):
    high = values.astype(BF16)
    return high, (values - high.astype(F32)).astype(BF16)


def split3(values):
    high = values.astype(BF16)
    rest = values - high.astype(F32)
    middle = rest.astype(BF16)
    return high, middle, (rest - middle.astype(F32)).astype(BF16)


def rows_cols(shape):
    return lax.broadcasted_iota(jnp.int32, shape, 0), lax.broadcasted_iota(jnp.int32, shape, 1)


def quot(values, n):
    return values >> (n.bit_length() - 1) if n & (n - 1) == 0 else values // n


def rest(values, n):
    return values & (n - 1) if n & (n - 1) == 0 else values % n


def pick(shape, test, dtype=BF16):
    r, c = rows_cols(shape)
    return jnp.where(test(r, c), 1.0, 0.0).astype(dtype)


def stack(parts):
    return jnp.concatenate(parts, 0)


def side(parts):
    return jnp.concatenate(parts, 1)


STACKED = (0, 0, 0, 1, 1, 2)


def stacked(parts):
    return [parts[0], parts[1], parts[2], parts[0], parts[1], parts[0]]


def level_of(block):
    return jnp.where(block < 3, 0, jnp.where(block < 5, 1, 2))


def choose(values, levels):
    parts = [part.astype(F32) for part in split3(values)]
    total = jnp.zeros(values.shape, F32)
    for k, part in enumerate(parts):
        total = jnp.where(levels == k, part, total)
    return total


def y_column(m):
    return 4 * (2 * (m >> 5) + ((m & 7) >> 2)) + ((m & 31) >> 3)


def build_first(w, b, hid):
    x_cols, y_cols, step = 6 * 32 + ONES, 4 * 64, 256

    def source(q, n):
        s = n >> 8
        m = n & (step - 1)
        in_x = (s < 4) & (m < 192) & (q == 4 * s + ((m & 31) >> 3))
        in_y = (s == 4) & (q == y_column(m & 63))
        return in_x | in_y

    values = exact(w, pick((16, 4 * step + y_cols), source, F32))
    _, n = rows_cols(values.shape)
    for_x = choose(values, level_of((n & (step - 1)) >> 5))
    for_y = values[:, 4 * step :]
    block = n[:, :y_cols] >> 6
    upper = choose(for_y, jnp.where(block < 3, 0, 2))
    lower = choose(for_y, jnp.where(block < 2, 1, -1))

    at, _ = rows_cols((x_cols, hid))
    rows = jnp.zeros((x_cols, hid), F32)
    for k, level in enumerate(split3(b)):
        rows = jnp.where(at == 192 + k, jnp.broadcast_to(level.astype(F32), (x_cols, hid)), rows)
    bias = dot_nt(pick((hid, hid), lambda q, n: q == n), rows.astype(BF16))

    half = FACES // 2
    r, c = rows_cols((half * hid, x_cols))
    shift = jnp.where(c < 192, (c & 7) - quot(r, hid), -1)
    first_x = stack([bias] * half)
    for s in range(4):
        part = for_x[:, s * step : s * step + x_cols]
        first_x = jnp.where(shift == s, stack([part] * half), first_x)
    r, c = rows_cols((2 * half * hid, y_cols))
    keep = (c & 3) == rest(quot(r, hid), half)
    first_y = jnp.where(keep, stack([upper] * half + [lower] * half), 0.0)
    return first_x.astype(BF16), first_y.astype(BF16)


def build_first_back(w_t, hid):
    wide = FACES // 2 * hid

    def source(q, n):
        in_x = (q < 128) & (n == 4 * (q >> 5) + ((q & 31) >> 3))
        in_y = (q >= 128) & (n == y_column(q - 128))
        return in_x | in_y

    rows = exact(pick((128 + 64, 16), source, F32), w_t)
    right = pick((hid, 2 * wide), lambda q, n: rest(n, hid) == q)
    high, low = (dot(part, right) for part in split(rows))
    r, c = rows_cols(high.shape)
    low = jnp.where(c < wide, low, 0.0)
    face = quot(rest(c, wide), hid)
    shift = (r & 7) - face
    upper = lower = jnp.zeros((32, 2 * wide), F32)
    for s in range(4):
        keep = shift[:32] == s
        upper = jnp.where(keep, high[32 * s : 32 * (s + 1)], upper)
        lower = jnp.where(keep, low[32 * s : 32 * (s + 1)], lower)
    keep = ((r & 3) == face)[128:]
    back_y = stack([jnp.where(keep, high[128:], 0.0), jnp.where(keep, low[128:], 0.0)])
    return stack([upper, lower]).astype(BF16), back_y.astype(BF16)


def build_mid(w, hid):
    block = 2 * hid
    tiled = exact(w, pick((hid, 4 * block), lambda q, n: rest(n, hid) == q, F32))
    _, n = rows_cols(tiled.shape)
    upper = choose(tiled, jnp.where(n < 3 * block, 0, 2))
    lower = choose(tiled, jnp.where(n < 2 * block, 1, -1))
    r, c = rows_cols((2 * block, 4 * block))
    keep = quot(rest(r, block), hid) == quot(rest(c, block), hid)
    return jnp.where(keep, stack([upper, upper, lower, lower]), 0.0).astype(BF16)


def build_mid_back(w, hid):
    block = 2 * hid
    turned = exact_nt(pick((hid, hid), lambda q, n: q == n, F32), w)
    tiled = exact(turned, pick((hid, 3 * block), lambda q, n: rest(n, hid) == q, F32))
    _, n = rows_cols(tiled.shape)
    tiled = choose(tiled, jnp.where(quot(n, block) == 1, 1, 0))
    r, c = rows_cols((block, 3 * block))
    keep = quot(r, hid) == quot(rest(c, block), hid)
    return jnp.where(keep, stack([tiled] * 2), 0.0).astype(BF16)


def build_out(w, hid):
    wide = FACES * hid
    rows = exact(pick((64, 8), lambda q, n: (q >> 3) == n, F32), w)
    tiled = dot(stack(list(split3(rows))), pick((hid, wide), lambda q, n: rest(n, hid) == q))
    r, c = rows_cols(tiled.shape)
    return jnp.where((r & 7) == quot(c, hid), tiled, 0.0).astype(BF16)


def build_out_back(w, hid):
    wide = FACES * hid
    turned = exact_nt(pick((hid, hid), lambda q, n: q == n, F32), w)
    tiled = exact(turned, pick((8, 192), lambda q, n: ((n & 63) >> 3) == q, F32))
    _, n = rows_cols(tiled.shape)
    tiled = choose(tiled, jnp.where((n >> 6) == 1, 1, 0))
    r, c = rows_cols((wide, 192))
    return jnp.where(quot(r, hid) == (c & 7), stack([tiled] * FACES), 0.0).astype(BF16)


def spread_bias(b, lanes, copies):
    n = b.shape[1]
    rows = exact_nt(pick((n, n), lambda q, m: q == m, F32), jnp.broadcast_to(b, (lanes, n)))
    return stack([rows] * copies)


def spread(bias_ref, width):
    return side([bias_ref[...]] * (width // bias_ref.shape[1]))


def limiter_forward(first, weights, hid):
    first_ref, first_bias_ref, mid_ref, mid_bias_ref, out_ref, out_bias_ref = weights
    width = first[0][0].shape[1]
    if first_bias_ref is None:
        ones = [jnp.ones((ONES, width), BF16)]
        h1 = stack([jnp.tanh(dot(first_ref[...], stack(stacked(one) + ones))) for one in first])
    else:
        parts = []
        for high, middle, low in first:
            both = dot(first_ref[...], stack([high, middle, low, high]))
            half = both.shape[0] // 2
            parts.append(jnp.tanh(both[:half] + both[half:] + spread(first_bias_ref, width)))
        h1 = stack(parts)
    h1_parts = split3(h1)
    block = 2 * hid
    parts = []
    for at in range(0, FACES * hid, block):
        high, middle, low = (p[at : at + block] for p in h1_parts)
        both = dot(mid_ref[...], stack([high, middle, low, high]))
        parts.append(jnp.tanh(both[:block] + both[block:] + spread(mid_bias_ref, width)))
    h2 = stack(parts)
    h2_parts = split3(h2)
    rows = 8 * FACES
    a = dot(out_ref[...], h2_parts[0])
    b = dot(out_ref[: 2 * rows, :], h2_parts[1])
    c = dot(out_ref[:rows, :], h2_parts[2])
    gates = jnp.tanh(
        ((a[2 * rows :] + b[rows:] + c) + (a[rows : 2 * rows] + b[:rows])) + a[:rows] + spread(out_bias_ref, width)
    )
    return h1, h1_parts[:2], h2, h2_parts[:2], gates


def limiter_backward(d3, h1, h2, h1_pair, h2_pair, out_back_ref, mid_back_ref, acc, hid):
    d3_hi, d3_lo = split(d3)
    dh2 = dot(out_back_ref[...], stack([d3_hi, d3_hi, d3_lo]))
    if acc is not None:
        acc[2][...] += dot_nt(stack(list(h2_pair)), stack([d3_hi, d3_lo]))
        acc[3][...] += d3
    d2_hi, d2_lo = split(dh2 * (1.0 - h2 * h2))
    block = 2 * hid
    parts = []
    for at in range(0, FACES * hid, block):
        hi, lo = d2_hi[at : at + block], d2_lo[at : at + block]
        parts.append(dot(mid_back_ref[...], stack([hi, hi, lo])))
    if acc is not None:
        ones = jnp.ones((ONES, d3.shape[1]), BF16)
        lefts, rights = [], []
        for at in range(0, FACES * hid, 2 * block):
            lefts.append(stack([part[at : at + 2 * block] for part in h1_pair] + [ones]))
            rights.append(stack([part[at : at + 2 * block] for part in (d2_hi, d2_lo)]))
        acc[1][...] += dot_nt(side(lefts), side(rights))
    return stack(parts) * (1.0 - h1 * h1)


def first_backward(d1, back_ref):
    wide = d1[0].shape[0] // 2
    found = []
    for at in (0, wide):
        both = dot(back_ref[...], stack([part[at : at + wide] for part in d1]))
        half = both.shape[0] // 2
        found.append(both[:half] + both[half:])
    return found


def add_first_grads(first, d1, acc_in):
    ones = jnp.ones((ONES, d1[0].shape[1]), BF16)
    wide = d1[0].shape[0] // 2
    lefts = [stack([one[0], one[1], ones]) for one in first]
    rights = [stack([part[at : at + wide] for part in d1]) for at in (0, wide)]
    acc_in[...] += dot_nt(side(lefts), side(rights))


def edge_states(cells, gates):
    left, right = [], []
    for c in range(4):
        low = gates[FACES * c : FACES * (c + 1)]
        high = gates[FACES * (c + 4) : FACES * (c + 5)]
        left.append(cells[1][c] + slope_gain * low * (cells[2][c] - cells[0][c]))
        right.append(cells[2][c] - slope_gain * high * (cells[3][c] - cells[1][c]))
    return left, right


def face_flux(left, right):
    ul = left[1] / left[0]
    ur = right[1] / right[0]
    half_speed = 0.5 * (jnp.maximum(jnp.abs(ul), jnp.abs(ur)) + 1.0)
    fl = [left[1], left[1] * ul + left[0], left[2] * ul, left[3] * ul]
    fr = [right[1], right[1] * ur + right[0], right[2] * ur, right[3] * ur]
    return [0.5 * (fl[c] + fr[c]) - half_speed * (right[c] - left[c]) for c in range(4)]


def sign_of(values):
    return jnp.where(values > 0.0, 1.0, jnp.where(values < 0.0, -1.0, 0.0))


def face_flux_backward(left, right, d_flux):
    inv_l, inv_r = 1.0 / left[0], 1.0 / right[0]
    ul, ur = left[1] / left[0], right[1] / right[0]
    al, ar = jnp.abs(ul), jnp.abs(ur)
    half_speed = 0.5 * (jnp.maximum(al, ar) + 1.0)
    d_speed = -0.5 * sum(d_flux[c] * (right[c] - left[c]) for c in range(4))
    share = jnp.where(al > ar, 1.0, jnp.where(al < ar, 0.0, 0.5))
    half = [0.5 * d for d in d_flux]
    spread = [half_speed * d for d in d_flux]

    def one(state, u, inv, speed_part, sign):
        du = half[1] * state[1] + half[2] * state[2] + half[3] * state[3] + speed_part * sign_of(u)
        over = du * inv
        return [
            half[1] - over * u + sign * spread[0],
            half[0] + half[1] * u + over + sign * spread[1],
            half[2] * u + sign * spread[2],
            half[3] * u + sign * spread[3],
        ]

    return (
        one(left, ul, inv_l, d_speed * share, 1.0),
        one(right, ur, inv_r, d_speed * (1.0 - share), -1.0),
    )


def edge_backward(cells, gates, d_left, d_right):
    lows, highs = [], []
    direct = [[None] * 4 for _ in range(4)]
    for c in range(4):
        low = gates[FACES * c : FACES * (c + 1)]
        high = gates[FACES * (c + 4) : FACES * (c + 5)]
        lows.append(slope_gain * (cells[2][c] - cells[0][c]) * d_left[c])
        highs.append(-slope_gain * (cells[3][c] - cells[1][c]) * d_right[c])
        low_part = slope_gain * low * d_left[c]
        high_part = slope_gain * high * d_right[c]
        direct[0][c] = -low_part
        direct[1][c] = d_left[c] + high_part
        direct[2][c] = d_right[c] + low_part
        direct[3][c] = -high_part
    return stack(lows + highs) * (1.0 - gates * gates), direct


def turn(values, shift, axis):
    size = values.shape[axis]
    return values if shift % size == 0 else pltpu.roll(values, shift % size, axis)


def x_cells(tiles):
    return [[turn(t, -s, 0)[:FACES] for t in tiles] for s in range(4)]


def pack_kernel(den, mom, tra, cot, w_in, b_in, w_mid, b_mid, w_out, b_out,
                rim, to_first, to_second, state, cots, first_x, first_y, first_bias, mid, mid_bias, out, out_bias,
                out_back, mid_back, first_x_back, first_y_back, *scratch):
    *small, sems = scratch
    nx, ny = den.shape[1:]
    segs = ny // SEG
    rows = nx // segs
    hid = w_in.shape[1]
    copies = [
        pltpu.make_async_copy(source, target, sems.at[k])
        for k, (source, target) in enumerate(
            list(zip([w_in, b_in, w_mid, b_mid, w_out, b_out], small))
            + [
                (den.at[0], state.at[0]),
                (mom.at[0], state.at[pl.ds(1, 2)]),
                (tra.at[0], state.at[3]),
                (cot.at[0], cots),
            ]
        )
    ]
    for one in copies:
        one.start()
    for one in copies[:6]:
        one.wait()
    w_in, b_in, w_mid, b_mid, w_out, b_out = small
    lanes = out_bias.shape[1]
    w_in_rows = exact_nt(pick((hid, hid), lambda q, n: q == n, F32), w_in[...])
    first_x[...], first_y[...] = build_first(w_in_rows, b_in[...], hid)
    first_bias[...] = spread_bias(b_in[...], lanes, FACES // 2)
    mid[...] = build_mid(w_mid[...], hid)
    mid_bias[...] = spread_bias(b_mid[...], lanes, 2)
    out[...] = build_out(w_out[...], hid)
    out_bias[...] = exact_nt(
        pick((64, 8), lambda q, n: (q >> 3) == n, F32), jnp.broadcast_to(b_out[...], (lanes, 8))
    )
    out_back[...] = build_out_back(w_out[...], hid)
    mid_back[...] = build_mid_back(w_mid[...], hid)
    first_x_back[...], first_y_back[...] = build_first_back(w_in[...], hid)

    for one in copies[6:]:
        one.wait()
    lane = lane_index(ny)
    for v in range(8):
        plane = state.at[v] if v < 4 else cots.at[v - 4]
        for at in range(0, rows, FACES):
            total = jnp.zeros((FACES, ny), F32)
            for s in range(segs):
                first = s * SEG + RIM
                moved = turn(plane[pl.ds(s * rows + at, FACES), :], first + RIM, 1)
                total = jnp.where((lane >= first) & (lane < first + 2 * RIM), moved, total)
            rim[v, pl.ds(at, FACES), :] = total
    is_odd = odd_mask(ny)
    spot = lane & (SEG - 1)
    for v in range(8):
        sides = []
        for first in (2 * RIM, RIM):
            total = jnp.zeros((FACES, ny), F32)
            for g in range(rows // FACES):
                moved = turn(rim[v, pl.ds(g * FACES, FACES), :], g * RIM - first, 1)
                total = jnp.where((spot >= g * RIM) & (spot < (g + 1) * RIM), moved, total)
            sides.append(total)
        to_first[v] = jnp.where(is_odd, sides[0], sides[1])
        to_second[v] = jnp.where(is_odd, sides[1], sides[0])


def odd_mask(ny):
    return jnp.full((FACES, ny), lax.rem(lax.axis_index(("tx", "ty")), 2), jnp.int32) == 1


def row_block(at):
    return pl.ds(pl.multiple_of(at * FACES, FACES), FACES)


def x_tiles(planes, group, groups):
    after = jnp.where(group + 1 == groups, 0, group + 1)
    return [stack([plane[row_block(group), :], plane[row_block(after), :]]) for plane in planes]


def pair_tiles(planes, step, half):
    sets = [x_tiles(planes, step + k * half, PAIR * half) for k in range(PAIR)]
    return [side([one[c] for one in sets]) for c in range(len(planes))]


def x_windows(tiles):
    half = FACES // 2
    return [stack([turn(tile, -at, 0)[:FACES] for tile in tiles]) for at in (0, half)]


def swap_halves(first, second):
    half = FACES // 2
    upper = rows_cols(first.shape)[0] < half
    return jnp.where(upper, first, turn(second, half, 0)), jnp.where(upper, turn(first, half, 0), second)


def y_windows(cells):
    pairs = [swap_halves(cells[s][c], cells[s + 1][c]) for s in (0, 2) for c in range(4)]
    return [stack([one[k] for one in pairs]) for k in range(2)]


def y_unwindow(parts):
    found = [[None] * 4 for _ in range(4)]
    for s in (0, 2):
        for c in range(4):
            at = FACES * (2 * s + c)
            found[s][c], found[s + 1][c] = swap_halves(parts[0][at : at + FACES], parts[1][at : at + FACES])
    return found


def x_forward(tiles, weights, hid):
    h1, h1_pair, h2, h2_pair, gates = limiter_forward([split3(one) for one in x_windows(tiles)], weights, hid)
    cells = x_cells(tiles)
    return h1_pair, h2_pair, gates, face_flux(*edge_states(cells, gates))


def update_cells(plane_rows, flux_rows):
    upper = turn(flux_rows, -7, 0)[:FACES]
    lower = turn(flux_rows, -6, 0)[:FACES]
    return plane_rows - courant * (upper - lower)


def x_forward_kernel(state, first_x, mid, mid_bias, out, out_bias,
                     middle, h1_hi, h1_lo, h2_hi, h2_lo, gates_out, flux):
    nx, ny = state.shape[1:]
    groups = nx // FACES
    half = groups // PAIR
    hid = mid.shape[0] // 4
    x_weights = (first_x, None, mid, mid_bias, out, out_bias)
    planes = [state.at[c] for c in range(4)]

    def step_of(step, _):
        tiles = pair_tiles(planes, step, half)
        h1_pair, h2_pair, gates, fluxes = x_forward(tiles, x_weights, hid)
        for target, value in zip((h1_hi, h1_lo, h2_hi, h2_lo, gates_out), h1_pair + h2_pair + (gates,)):
            target[step] = value
        for c in range(4):
            for k in range(PAIR):
                flux[c, row_block(step + k * half + 1), :] = fluxes[c][:, k * ny : (k + 1) * ny]
        return 0

    lax.fori_loop(0, half, step_of, 0)
    for c in range(4):
        flux[c, :FACES, :] = flux[c, nx : nx + FACES, :]

    def update(group, _):
        for c in range(4):
            both = stack([flux[c, row_block(group), :], flux[c, row_block(group + 1), :]])
            middle[c, row_block(group), :] = update_cells(planes[c][row_block(group), :], both)
        return 0

    lax.fori_loop(0, groups, update, 0)


def y_order(planes):
    return [planes[0], planes[2], planes[1], planes[3]]


def lane_index(width):
    return lax.broadcasted_iota(jnp.int32, (FACES, width), 1)


def y_step(cells, cots, halo_mask, refs, acc, hid):
    weights, out_back, mid_back, first_y_back = refs
    window = [split3(one) for one in y_windows(cells)]
    h1, h1_pair, h2, h2_pair, gates = limiter_forward(window, weights, hid)
    left, right = edge_states(cells, gates)
    d_flux = [courant * (cots[1][c] - cots[0][c]) for c in range(4)]
    d_left, d_right = face_flux_backward(left, right, d_flux)
    if halo_mask is not None:
        d_left = [jnp.where(halo_mask, d, 0.0) for d in d_left]
        d_right = [jnp.where(halo_mask, d, 0.0) for d in d_right]
    d3_full, direct = edge_backward(cells, gates, d_left, d_right)
    d1_full = limiter_backward(d3_full, h1, h2, h1_pair, h2_pair, out_back, mid_back, acc, hid)
    d1 = split(d1_full)
    d_window = y_unwindow(first_backward(d1, first_y_back))
    if acc is not None:
        add_first_grads(window, d1, acc[0])
    return [
        [d_window[s][c] + direct[s][c] for c in range(4)]
        for s in range(4)
    ]


def y_gather(parts, ny):
    lane = lane_index(ny)
    out = []
    for c in range(4):
        a = turn(jnp.where(lane >= 1, parts[0][c], 0.0), -1, 1)
        b = turn(jnp.where(lane < ny - 1, parts[2][c], 0.0), 1, 1)
        d = turn(jnp.where(lane < ny - 2, parts[3][c], 0.0), 2, 1)
        out.append(parts[1][c] + a + b + d)
    return out


def fold_rows(values, hid):
    return sum(values[at : at + hid] for at in range(0, values.shape[0], hid))


def back_kernel(state, cot, middle, own, from_first, from_second,
                first_x, first_y, first_bias, mid, mid_bias, out, out_bias,
                out_back, mid_back, first_y_back,
                h1_hi, h1_lo, h2_hi, h2_lo, gates_in,
                base, d1_hi, d1_lo, g_weights,
                rim_state, rim_cot, rim_flux, rim_middle, rim_grad, d_middle,
                acc_x, acc_y, acc_mid, acc_out, acc_out_bias):
    nx, ny = state.shape[1:]
    groups = nx // FACES
    half = groups // PAIR
    hid = mid.shape[0] // 4
    x_weights = (first_x, None, mid, mid_bias, out, out_bias)
    segs = ny // SEG
    rim_rows = nx // segs
    rim_groups = rim_rows // FACES
    rim_half = rim_groups // RIM_PAIR

    for acc in (acc_x, acc_y, acc_mid, acc_out, acc_out_bias):
        acc[...] = jnp.zeros(acc.shape, F32)

    lane = lane_index(ny)
    spot = lane & (SEG - 1)
    is_odd = odd_mask(ny)
    for v in range(8):
        for g in range(rim_groups):
            rows = pl.ds(g * FACES, FACES)
            mine, first, second = own[v, rows, :], from_first[v], from_second[v]
            left, right = jnp.where(is_odd, first, second), jnp.where(is_odd, second, first)
            value = jnp.where(
                spot < RIM,
                turn(left, -g * RIM, 1),
                jnp.where(
                    spot < 2 * RIM,
                    turn(mine, -RIM, 1),
                    jnp.where(spot < 3 * RIM, turn(mine, RIM, 1), turn(right, (3 - g) * RIM, 1)),
                ),
            )
            if v < 4:
                rim_state[v, rows, :] = value
                if g == 0:
                    rim_state[v, pl.ds(rim_rows, FACES), :] = turn(value, -SEG, 1)
            else:
                rim_cot[v - 4, rows, :] = value

    def rim_forward(step, _):
        sets = [
            [
                stack([
                    rim_state[c, row_block(step + k * rim_half), :],
                    rim_state[c, row_block(step + k * rim_half + 1), :],
                ])
                for c in range(4)
            ]
            for k in range(RIM_PAIR)
        ]
        tiles = [side([one[c] for one in sets]) for c in range(4)]
        fluxes = x_forward(tiles, x_weights, hid)[3]
        for c in range(4):
            for k in range(RIM_PAIR):
                rim_flux[c, row_block(step + k * rim_half + 1), :] = fluxes[c][:, k * ny : (k + 1) * ny]
        return 0

    lax.fori_loop(0, rim_half, rim_forward, 0)
    for c in range(4):
        rim_flux[c, :FACES, :] = turn(rim_flux[c, rim_rows : rim_rows + FACES, :], SEG, 1)
        for g in range(rim_groups):
            rows = pl.ds(g * FACES, FACES)
            both = stack([rim_flux[c, rows, :], rim_flux[c, pl.ds((g + 1) * FACES, FACES), :]])
            rim_middle[c, rows, :] = update_cells(rim_state[c, rows, :], both)

    refs = ((first_y, first_bias, mid, mid_bias, out, out_bias), out_back, mid_back, first_y_back)
    spot_wide = lane_index(RIM_PAIR * ny) & (SEG - 1)
    rim_faces = (spot_wide == RIM - 2) | (spot_wide == RIM - 1) | (spot_wide == 3 * RIM)

    def rim_back(step, _):
        cells = [[[] for _ in range(4)] for _ in range(4)]
        cots = [[[] for _ in range(4)] for _ in range(2)]
        for k in range(RIM_PAIR):
            rows = row_block(step + k * rim_half)
            for c in range(4):
                value = rim_middle[c, rows, :]
                for s in range(4):
                    cells[s][c].append(turn(value, 1 - s, 1))
                value = rim_cot[c, rows, :]
                for s in range(2):
                    cots[s][c].append(turn(value, -s, 1))
        cells = [y_order([side(one) for one in row]) for row in cells]
        cots = [y_order([side(one) for one in row]) for row in cots]
        parts = y_step(cells, cots, rim_faces, refs, None, hid)
        for k in range(RIM_PAIR):
            own_parts = [[one[:, k * ny : (k + 1) * ny] for one in row] for row in parts]
            gathered = y_order(y_gather(own_parts, ny))
            for c in range(4):
                rim_grad[c, row_block(step + k * rim_half), :] = gathered[c]
        return 0

    lax.fori_loop(0, rim_half, rim_back, 0)

    def main_y(step, _):
        cells = [[[] for _ in range(4)] for _ in range(4)]
        cots = [[[] for _ in range(4)] for _ in range(2)]
        for k in range(PAIR):
            group = step + k * half
            rows = row_block(group)
            seg = group // rim_groups
            rim_at = row_block(group - seg * rim_groups)
            to_low = ny - (seg * SEG + 3 * RIM)
            to_high = lax.rem(ny - 1 - (seg * SEG + RIM - 1) + ny, ny)
            for c in range(4):
                value = middle[c, rows, :]
                rim_value = rim_middle[c, rim_at, :]
                low = jnp.where(lane < 2, pltpu.roll(rim_value, to_low, 1), value)
                high = jnp.where(lane == ny - 1, pltpu.roll(rim_value, to_high, 1), value)
                cells[0][c].append(turn(high, 1, 1))
                cells[1][c].append(value)
                cells[2][c].append(turn(jnp.where(lane < 1, low, value), -1, 1))
                cells[3][c].append(turn(low, -2, 1))
                value = cot[c, rows, :]
                rim_value = rim_cot[c, rim_at, :]
                low = jnp.where(lane < 1, pltpu.roll(rim_value, to_low, 1), value)
                cots[0][c].append(value)
                cots[1][c].append(turn(low, -1, 1))
        cells = [y_order([side(one) for one in row]) for row in cells]
        cots = [y_order([side(one) for one in row]) for row in cots]
        parts = y_step(cells, cots, None, refs, (acc_y, acc_mid, acc_out, acc_out_bias), hid)
        for k in range(PAIR):
            group = step + k * half
            rows = row_block(group)
            seg = group // rim_groups
            rim_at = row_block(group - seg * rim_groups)
            own_parts = [[one[:, k * ny : (k + 1) * ny] for one in row] for row in parts]
            gathered = y_order(y_gather(own_parts, ny))
            to_low = ny - (seg * SEG + RIM)
            to_high = lax.rem(ny - 1 - (seg * SEG + 3 * RIM - 1) + ny, ny)
            for c in range(4):
                rim_value = rim_grad[c, rim_at, :]
                from_rim = jnp.where(
                    lane < 2,
                    pltpu.roll(rim_value, to_low, 1),
                    jnp.where(lane == ny - 1, pltpu.roll(rim_value, to_high, 1), 0.0),
                )
                d_middle[c, rows, :] = cot[c, rows, :] + gathered[c] + from_rim
        return 0

    lax.fori_loop(0, half, main_y, 0)

    planes = [state.at[c] for c in range(4)]
    d_planes = [d_middle.at[c] for c in range(4)]

    def main_x(step, carry):
        tiles = pair_tiles(planes, step, half)
        d_tiles = pair_tiles(d_planes, step, half)
        gates = gates_in[step]
        h1_pair = (h1_hi[step], h1_lo[step])
        h2_pair = (h2_hi[step], h2_lo[step])
        h1 = h1_pair[0].astype(F32) + h1_pair[1].astype(F32)
        h2 = h2_pair[0].astype(F32) + h2_pair[1].astype(F32)
        cells = x_cells(tiles)
        left, right = edge_states(cells, gates)
        d_flux = [courant * (turn(d, -2, 0)[:FACES] - turn(d, -1, 0)[:FACES]) for d in d_tiles]
        d_left, d_right = face_flux_backward(left, right, d_flux)
        d3_full, direct = edge_backward(cells, gates, d_left, d_right)
        d1_full = limiter_backward(
            d3_full, h1, h2, h1_pair, h2_pair, out_back, mid_back, (acc_x, acc_mid, acc_out, acc_out_bias), hid
        )
        d1 = split(d1_full)
        d1_hi[step], d1_lo[step] = d1
        add_first_grads([split(one) for one in x_windows(tiles)], d1, acc_x)
        later = []
        for c in range(4):
            nothing = jnp.zeros_like(direct[0][c])
            total = stack([direct[0][c], nothing])
            for s in range(1, 4):
                total = total + turn(stack([direct[s][c], nothing]), s, 0)
            now = total[:FACES] + d_tiles[c][:FACES] + carry[c]
            for k in range(PAIR):
                base[c, row_block(step + k * half), :] = now[:, k * ny : (k + 1) * ny]
            later.append(total[FACES:])
        return tuple(later)

    start = tuple(jnp.zeros((FACES, PAIR * ny), F32) for _ in range(4))
    last = lax.fori_loop(0, half, main_x, start)
    for c in range(4):
        for k in range(PAIR):
            at = (k + 1) % PAIR * half * FACES
            base[c, pl.ds(at, FACES), :] += last[c][:, k * ny : (k + 1) * ny]

    lanes = g_weights.shape[1]
    values = acc_mid[: 8 * hid, :]
    r, c = rows_cols(values.shape)
    same = rest(quot(r, hid), 4) == rest(quot(c, hid), 4)
    values = fold_rows(jnp.where(same, values, 0.0), hid)
    grad_mid = exact_nt(
        pick((hid, 8 * hid), lambda q, n: rest(n, hid) == q, F32),
        stack([values, jnp.zeros((lanes - hid, 8 * hid), F32)]),
    )
    grad_mid_bias = exact(
        acc_mid[8 * hid : 8 * hid + 8, :], pick((8 * hid, lanes), lambda q, n: rest(q, hid) == n, F32)
    )
    r, c = rows_cols(acc_x.shape)
    values, shift = acc_x[...], (r & 7) - rest(quot(c, hid), 4)
    found = [jnp.where((shift == s) & (r < 64), values, 0.0)[:64] for s in range(4)]
    found.append(values[64:])
    r, c = rows_cols(acc_y.shape)
    found.append(jnp.where(((r & 3) == rest(quot(c, hid), 4)) | (r >= 128), acc_y[...], 0.0))
    found = exact(
        stack(found),
        pick((8 * hid, lanes), lambda q, n: (rest(n - q, hid) == 0) & (n >= hid) & (n < 2 * hid), F32),
    )
    y_at = 4 * 64 + ONES

    def source(q, n):
        in_x = (n < 256) & (q == 4 * (n >> 6) + ((n & 31) >> 3))
        m = n - y_at
        in_y = (m >= 0) & (m < 128) & (q == y_column(m & 63))
        return in_x | in_y | ((n == 256) | (m == 128)) & (q == 24)

    beside = exact(pick((32, found.shape[0]), source, F32), found)
    r, c = rows_cols(acc_out.shape)
    found = fold_rows(jnp.where((c & 7) == rest(quot(r, hid), FACES), acc_out[...], 0.0), hid)
    beside = beside + exact_nt(
        pick((32, found.shape[1]), lambda q, n: q == 16 + ((n & 63) >> 3), F32),
        stack([jnp.zeros((hid, found.shape[1]), F32), found, jnp.zeros((lanes - 2 * hid, found.shape[1]), F32)]),
    )
    out_bias_rows = exact_nt(jnp.ones((8, acc_out_bias.shape[1]), F32), acc_out_bias[...])
    grad_out_bias = exact_nt(out_bias_rows, pick((lanes, 64), lambda q, n: (n >> 3) == q - hid, F32))
    r, c = rows_cols((8, lanes))
    g_weights[:hid, :] = grad_mid + beside
    g_weights[25:26, :] += grad_out_bias[:1]
    g_weights[hid:, :] = grad_mid_bias


def state_kernel(base, d1_hi, d1_lo, first_x_back, _, g_den, g_mom, g_tra):
    nx, ny = base.shape[1:]
    half = nx // FACES // PAIR
    grads = [g_den.at[0], g_mom.at[0, 0], g_mom.at[0, 1], g_tra.at[0]]
    upper = rows_cols((FACES, PAIR * ny))[0] < FACES // 2

    def step_of(step, carry):
        first, second = first_backward((d1_hi[step], d1_lo[step]), first_x_back)
        later = []
        for c in range(4):
            rows = slice(FACES * c, FACES * (c + 1))
            moved = turn(second[rows], FACES // 2, 0)
            now = first[rows] + jnp.where(upper, 0.0, moved) + carry[c]
            for k in range(PAIR):
                at = row_block(step + k * half)
                grads[c][at, :] = base[c, at, :] + now[:, k * ny : (k + 1) * ny]
            later.append(jnp.where(upper, moved, 0.0))
        return tuple(later)

    start = tuple(jnp.zeros((FACES, PAIR * ny), F32) for _ in range(4))
    last = lax.fori_loop(0, half, step_of, start)
    for c in range(4):
        for k in range(PAIR):
            at = (k + 1) % PAIR * half * FACES
            grads[c][pl.ds(at, FACES), :] += last[c][:, k * ny : (k + 1) * ny]


def finish_kernel(total, g_w_in, g_b_in, g_w_mid, g_b_mid, g_w_out, g_b_out):
    hid = g_w_mid.shape[0]
    g_w_mid[...] = total[:hid, :hid]
    beside = total[:hid, hid : 2 * hid]
    g_w_in[...] = beside[:16]
    g_w_out[...] = beside[16:24]
    g_b_in[...] = beside[24:25]
    g_b_out[...] = beside[25:26, :8]
    g_b_mid[...] = total[hid : hid + 1, :hid]


def whole(count, space=pltpu.VMEM):
    return [pl.BlockSpec(memory_space=space)] * count


def call(kernel, outs, operands, out_spaces=None, in_spaces=None, scratch=(), flops=0, moved=0):
    return pl.pallas_call(
        kernel,
        out_shape=outs,
        in_specs=in_spaces or whole(len(operands)),
        out_specs=out_spaces or whole(len(outs)),
        scratch_shapes=list(scratch),
        compiler_params=pltpu.CompilerParams(vmem_limit_bytes=VMEM_BYTES),
        cost_estimate=pl.CostEstimate(flops=flops, bytes_accessed=moved, transcendentals=0),
    )(*operands)


def sum_rounds(values, sizes):
    axes, size = tuple(sizes), 1
    for one in sizes.values():
        size *= one
    if size & (size - 1):
        return [values, lax.psum(values, axes)]
    bits = [1 << k for k in range(size.bit_length() - 1)]
    core = size // sizes["traj"]
    others = [bit for bit in reversed(bits) if bit != core]
    found = [values]
    for masks in [[core]] * (core in bits) + [others[k : k + 2] for k in range(0, len(others), 2)]:
        partners = [0]
        for mask in masks:
            partners = partners + [one ^ mask for one in partners]
        parts = [
            lax.ppermute(values, axes, [(i, i ^ one) for i in range(size)]) if one else values for one in partners
        ]
        while len(parts) > 1:
            parts = [parts[k] + parts[k + 1] for k in range(0, len(parts), 2)]
        values = parts[0]
        found.append(values)
    return found


def body(sizes, density, momentum, tracer, cotangent, w_in, b_in, w_mid, b_mid, w_out, b_out):
    nx, ny = density.shape[1:]
    hid = w_in.shape[0]
    wide = FACES * hid
    groups = nx // FACES
    half = groups // PAIR
    lanes = PAIR * ny
    segs = ny // SEG
    rim_rows = nx // segs
    ring = sizes["tx"] * sizes["ty"]
    shape = jax.ShapeDtypeStruct

    operands = [
        density, momentum, tracer, cotangent, w_in.T, b_in[None], w_mid, b_mid[None], w_out, b_out[None]
    ]
    rim, to_first, to_second, state, cots, *matrices = call(
        pack_kernel,
        [
            shape((8, rim_rows, ny), F32),
            shape((8, FACES, ny), F32),
            shape((8, FACES, ny), F32),
            shape((4, nx, ny), F32),
            shape((4, nx, ny), F32),
            shape((wide // 2, 6 * 32 + ONES), BF16),
            shape((wide, 4 * 64), BF16),
            shape((wide // 2, ny), F32),
            shape((4 * hid, 8 * hid), BF16),
            shape((2 * hid, ny), F32),
            shape((192, wide), BF16),
            shape((64, ny), F32),
            shape((wide, 192), BF16),
            shape((2 * hid, 6 * hid), BF16),
            shape((64, wide), BF16),
            shape((128, wide), BF16),
        ],
        [pltpu.with_memory_space_constraint(one, pltpu.HBM) for one in operands],
        in_spaces=whole(10, pltpu.HBM),
        scratch=[pltpu.VMEM(one.shape, F32) for one in operands[4:]] + [pltpu.SemaphoreType.DMA((10,))],
    )
    axes = ("tx", "ty")
    swaps = [[(i, (i + 1 if (i + first) % 2 == 0 else i - 1) % ring) for i in range(ring)] for first in range(2)]
    from_first, from_second = (
        lax.ppermute(one, axes, swap) for one, swap in zip((to_first, to_second), swaps)
    )

    middle, *kept = call(
        x_forward_kernel,
        [shape((4, nx, ny), F32)]
        + [shape((half, wide, lanes), BF16)] * 4
        + [shape((half, 64, lanes), F32)],
        [state, matrices[0]] + matrices[3:7],
        scratch=[pltpu.VMEM((4, nx + FACES, ny), F32)],
        flops=10**10,
        moved=10**7,
    )
    first_x_back = matrices.pop(-2)
    *found, g_weights = call(
        back_kernel,
        [
            shape((4, nx, ny), F32),
            shape((half, wide, lanes), BF16),
            shape((half, wide, lanes), BF16),
            shape((hid + 8, 128), F32),
        ],
        [state, cots, middle, rim, from_first, from_second] + matrices + kept,
        scratch=[
            pltpu.VMEM((4, rim_rows + FACES, ny), F32),
            pltpu.VMEM((4, rim_rows, ny), F32),
            pltpu.VMEM((4, rim_rows + FACES, ny), F32),
            pltpu.VMEM((4, rim_rows, ny), F32),
            pltpu.VMEM((4, rim_rows, ny), F32),
            pltpu.VMEM((4, nx, ny), F32),
            pltpu.VMEM((2 * 32 + ONES, wide), F32),
            pltpu.VMEM((2 * 64 + ONES, wide), F32),
            pltpu.VMEM((8 * hid + ONES, 8 * hid), F32),
            pltpu.VMEM((2 * wide, 128), F32),
            pltpu.VMEM((64, lanes), F32),
        ],
        flops=4 * 10**10,
        moved=2 * 10**7,
    )
    rounds = sum_rounds(g_weights, sizes)
    g_den, g_mom, g_tra = call(
        state_kernel,
        [shape(density.shape, F32), shape(momentum.shape, F32), shape(tracer.shape, F32)],
        found + [first_x_back, rounds[min(1, len(rounds) - 1)]],
        flops=2 * 10**9,
        moved=10**6,
    )
    total = rounds[-1]
    g_w_in, g_b_in, g_w_mid, g_b_mid, g_w_out, g_b_out = call(
        finish_kernel,
        [
            shape((w_in.shape[1], hid), F32),
            shape((1, hid), F32),
            shape(w_mid.shape, F32),
            shape((1, hid), F32),
            shape(w_out.shape, F32),
            shape((1, b_out.shape[0]), F32),
        ],
        [total],
    )
    return (g_den, g_mom, g_tra, g_w_in.T, g_b_in[0], g_w_mid, g_b_mid[0], g_w_out, g_b_out[0])


def solution(mesh):
    flow = P("traj", None, ("tx", "ty"))
    deep = P("traj", None, None, ("tx", "ty"))
    return jax.shard_map(
        functools.partial(body, dict(mesh.shape)),
        mesh=mesh,
        in_specs=(flow, deep, flow, deep) + (P(),) * 6,
        out_specs=(flow, deep, flow) + (P(),) * 6,
        check_vma=False,
    )
```

```python
import functools

import jax
import jax.numpy as jnp
from jax import lax
from jax.experimental import pallas as pl
from jax.experimental.pallas import tpu as pltpu
from jax.sharding import PartitionSpec as P

courant = 0.1
slope_gain = 0.25
F32 = jnp.float32
BF16 = jnp.bfloat16
FACES = 8
SEG = 16
RIM = 4
PAIR = 8
RIM_PAIR = 4
ONES = 16
VMEM_BYTES = 32 * 2**20


def dot(a, b):
    return lax.dot_general(a, b, (((1,), (0,)), ((), ())), preferred_element_type=F32)


def dot_nt(a, b):
    return lax.dot_general(a, b, (((1,), (1,)), ((), ())), preferred_element_type=F32)


def exact(a, b):
    return lax.dot_general(
        a, b, (((1,), (0,)), ((), ())), precision=lax.Precision.HIGHEST, preferred_element_type=F32
    )


def exact_nt(a, b):
    return lax.dot_general(
        a, b, (((1,), (1,)), ((), ())), precision=lax.Precision.HIGHEST, preferred_element_type=F32
    )


def split(values):
    high = values.astype(BF16)
    return high, (values - high.astype(F32)).astype(BF16)


def split3(values):
    high = values.astype(BF16)
    rest = values - high.astype(F32)
    middle = rest.astype(BF16)
    return high, middle, (rest - middle.astype(F32)).astype(BF16)


def rows_cols(shape):
    return lax.broadcasted_iota(jnp.int32, shape, 0), lax.broadcasted_iota(jnp.int32, shape, 1)


def quot(values, n):
    return values >> (n.bit_length() - 1) if n & (n - 1) == 0 else values // n


def rest(values, n):
    return values & (n - 1) if n & (n - 1) == 0 else values % n


def pick(shape, test, dtype=BF16):
    r, c = rows_cols(shape)
    return jnp.where(test(r, c), 1.0, 0.0).astype(dtype)


def stack(parts):
    return jnp.concatenate(parts, 0)


def side(parts):
    return jnp.concatenate(parts, 1)


STACKED = (0, 0, 0, 1, 1, 2)


def stacked(parts):
    return [parts[0], parts[1], parts[2], parts[0], parts[1], parts[0]]


def level_of(block):
    return jnp.where(block < 3, 0, jnp.where(block < 5, 1, 2))


def choose(values, levels):
    parts = [part.astype(F32) for part in split3(values)]
    total = jnp.zeros(values.shape, F32)
    for k, part in enumerate(parts):
        total = jnp.where(levels == k, part, total)
    return total


def y_column(m):
    return 4 * (2 * (m >> 5) + ((m & 7) >> 2)) + ((m & 31) >> 3)


def build_first(w, b, hid):
    x_cols, y_cols, step = 6 * 32 + ONES, 4 * 64, 256

    def source(q, n):
        s = n >> 8
        m = n & (step - 1)
        in_x = (s < 4) & (m < 192) & (q == 4 * s + ((m & 31) >> 3))
        in_y = (s == 4) & (q == y_column(m & 63))
        return in_x | in_y

    values = exact(w, pick((16, 4 * step + y_cols), source, F32))
    _, n = rows_cols(values.shape)
    for_x = choose(values, level_of((n & (step - 1)) >> 5))
    for_y = values[:, 4 * step :]
    block = n[:, :y_cols] >> 6
    upper = choose(for_y, jnp.where(block < 3, 0, 2))
    lower = choose(for_y, jnp.where(block < 2, 1, -1))

    at, _ = rows_cols((x_cols, hid))
    rows = jnp.zeros((x_cols, hid), F32)
    for k, level in enumerate(split3(b)):
        rows = jnp.where(at == 192 + k, jnp.broadcast_to(level.astype(F32), (x_cols, hid)), rows)
    bias = dot_nt(pick((hid, hid), lambda q, n: q == n), rows.astype(BF16))

    half = FACES // 2
    r, c = rows_cols((half * hid, x_cols))
    shift = jnp.where(c < 192, (c & 7) - quot(r, hid), -1)
    first_x = stack([bias] * half)
    for s in range(4):
        part = for_x[:, s * step : s * step + x_cols]
        first_x = jnp.where(shift == s, stack([part] * half), first_x)
    r, c = rows_cols((2 * half * hid, y_cols))
    keep = (c & 3) == rest(quot(r, hid), half)
    first_y = jnp.where(keep, stack([upper] * half + [lower] * half), 0.0)
    return first_x.astype(BF16), first_y.astype(BF16)


def build_first_back(w_t, hid):
    wide = FACES // 2 * hid

    def source(q, n):
        in_x = (q < 128) & (n == 4 * (q >> 5) + ((q & 31) >> 3))
        in_y = (q >= 128) & (n == y_column(q - 128))
        return in_x | in_y

    rows = exact(pick((128 + 64, 16), source, F32), w_t)
    right = pick((hid, 2 * wide), lambda q, n: rest(n, hid) == q)
    high, low = (dot(part, right) for part in split(rows))
    r, c = rows_cols(high.shape)
    low = jnp.where(c < wide, low, 0.0)
    face = quot(rest(c, wide), hid)
    shift = (r & 7) - face
    upper = lower = jnp.zeros((32, 2 * wide), F32)
    for s in range(4):
        keep = shift[:32] == s
        upper = jnp.where(keep, high[32 * s : 32 * (s + 1)], upper)
        lower = jnp.where(keep, low[32 * s : 32 * (s + 1)], lower)
    keep = ((r & 3) == face)[128:]
    back_y = stack([jnp.where(keep, high[128:], 0.0), jnp.where(keep, low[128:], 0.0)])
    return stack([upper, lower]).astype(BF16), back_y.astype(BF16)


def build_mid(w, hid):
    block = 2 * hid
    tiled = exact(w, pick((hid, 4 * block), lambda q, n: rest(n, hid) == q, F32))
    _, n = rows_cols(tiled.shape)
    upper = choose(tiled, jnp.where(n < 3 * block, 0, 2))
    lower = choose(tiled, jnp.where(n < 2 * block, 1, -1))
    r, c = rows_cols((2 * block, 4 * block))
    keep = quot(rest(r, block), hid) == quot(rest(c, block), hid)
    return jnp.where(keep, stack([upper, upper, lower, lower]), 0.0).astype(BF16)


def build_mid_back(w, hid):
    block = 2 * hid
    turned = exact_nt(pick((hid, hid), lambda q, n: q == n, F32), w)
    tiled = exact(turned, pick((hid, 3 * block), lambda q, n: rest(n, hid) == q, F32))
    _, n = rows_cols(tiled.shape)
    tiled = choose(tiled, jnp.where(quot(n, block) == 1, 1, 0))
    r, c = rows_cols((block, 3 * block))
    keep = quot(r, hid) == quot(rest(c, block), hid)
    return jnp.where(keep, stack([tiled] * 2), 0.0).astype(BF16)


def build_out(w, hid):
    wide = FACES * hid
    rows = exact(pick((64, 8), lambda q, n: (q >> 3) == n, F32), w)
    tiled = dot(stack(list(split3(rows))), pick((hid, wide), lambda q, n: rest(n, hid) == q))
    r, c = rows_cols(tiled.shape)
    return jnp.where((r & 7) == quot(c, hid), tiled, 0.0).astype(BF16)


def build_out_back(w, hid):
    wide = FACES * hid
    turned = exact_nt(pick((hid, hid), lambda q, n: q == n, F32), w)
    tiled = exact(turned, pick((8, 192), lambda q, n: ((n & 63) >> 3) == q, F32))
    _, n = rows_cols(tiled.shape)
    tiled = choose(tiled, jnp.where((n >> 6) == 1, 1, 0))
    r, c = rows_cols((wide, 192))
    return jnp.where(quot(r, hid) == (c & 7), stack([tiled] * FACES), 0.0).astype(BF16)


def spread_bias(b, lanes, copies):
    n = b.shape[1]
    rows = exact_nt(pick((n, n), lambda q, m: q == m, F32), jnp.broadcast_to(b, (lanes, n)))
    return stack([rows] * copies)


def spread(bias_ref, width):
    return side([bias_ref[...]] * (width // bias_ref.shape[1]))


def limiter_forward(first, weights, hid):
    first_ref, first_bias_ref, mid_ref, mid_bias_ref, out_ref, out_bias_ref = weights
    width = first[0][0].shape[1]
    if first_bias_ref is None:
        ones = [jnp.ones((ONES, width), BF16)]
        h1 = stack([jnp.tanh(dot(first_ref[...], stack(stacked(one) + ones))) for one in first])
    else:
        parts = []
        for high, middle, low in first:
            both = dot(first_ref[...], stack([high, middle, low, high]))
            half = both.shape[0] // 2
            parts.append(jnp.tanh(both[:half] + both[half:] + spread(first_bias_ref, width)))
        h1 = stack(parts)
    h1_parts = split3(h1)
    block = 2 * hid
    parts = []
    for at in range(0, FACES * hid, block):
        high, middle, low = (p[at : at + block] for p in h1_parts)
        both = dot(mid_ref[...], stack([high, middle, low, high]))
        parts.append(jnp.tanh(both[:block] + both[block:] + spread(mid_bias_ref, width)))
    h2 = stack(parts)
    h2_parts = split3(h2)
    rows = 8 * FACES
    a = dot(out_ref[...], h2_parts[0])
    b = dot(out_ref[: 2 * rows, :], h2_parts[1])
    c = dot(out_ref[:rows, :], h2_parts[2])
    gates = jnp.tanh(
        ((a[2 * rows :] + b[rows:] + c) + (a[rows : 2 * rows] + b[:rows])) + a[:rows] + spread(out_bias_ref, width)
    )
    return h1, h1_parts[:2], h2, h2_parts[:2], gates


def limiter_backward(d3, slope1, slope2, h1_pair, h2_pair, out_back_ref, mid_back_ref, acc, hid):
    d3_hi, d3_lo = split(d3)
    dh2 = dot(out_back_ref[...], stack([d3_hi, d3_hi, d3_lo]))
    if acc is not None:
        acc[2][...] += dot_nt(stack(list(h2_pair)), stack([d3_hi, d3_lo]))
        acc[3][...] += d3
    d2_hi, d2_lo = split(dh2 * slope2)
    block = 2 * hid
    parts = []
    for at in range(0, FACES * hid, block):
        hi, lo = d2_hi[at : at + block], d2_lo[at : at + block]
        parts.append(dot(mid_back_ref[...], stack([hi, hi, lo])))
    if acc is not None:
        ones = jnp.ones((ONES, d3.shape[1]), BF16)
        lefts, rights = [], []
        for at in range(0, FACES * hid, 2 * block):
            lefts.append(stack([part[at : at + 2 * block] for part in h1_pair] + [ones]))
            rights.append(stack([part[at : at + 2 * block] for part in (d2_hi, d2_lo)]))
        acc[1][...] += dot_nt(side(lefts), side(rights))
    return stack(parts) * slope1


def first_backward(d1, back_ref):
    wide = d1[0].shape[0] // 2
    found = []
    for at in (0, wide):
        both = dot(back_ref[...], stack([part[at : at + wide] for part in d1]))
        half = both.shape[0] // 2
        found.append(both[:half] + both[half:])
    return found


def add_first_grads(first, d1, acc_in):
    ones = jnp.ones((ONES, d1[0].shape[1]), BF16)
    wide = d1[0].shape[0] // 2
    lefts = [stack([one[0], one[1], ones]) for one in first]
    rights = [stack([part[at : at + wide] for part in d1]) for at in (0, wide)]
    acc_in[...] += dot_nt(side(lefts), side(rights))


def edge_states(cells, gates):
    left, right = [], []
    for c in range(4):
        low = gates[FACES * c : FACES * (c + 1)]
        high = gates[FACES * (c + 4) : FACES * (c + 5)]
        left.append(cells[1][c] + slope_gain * low * (cells[2][c] - cells[0][c]))
        right.append(cells[2][c] - slope_gain * high * (cells[3][c] - cells[1][c]))
    return left, right


def face_flux(left, right):
    ul = left[1] / left[0]
    ur = right[1] / right[0]
    half_speed = 0.5 * (jnp.maximum(jnp.abs(ul), jnp.abs(ur)) + 1.0)
    fl = [left[1], left[1] * ul + left[0], left[2] * ul, left[3] * ul]
    fr = [right[1], right[1] * ur + right[0], right[2] * ur, right[3] * ur]
    return [0.5 * (fl[c] + fr[c]) - half_speed * (right[c] - left[c]) for c in range(4)]


def sign_of(values):
    return jnp.where(values > 0.0, 1.0, jnp.where(values < 0.0, -1.0, 0.0))


def face_flux_backward(left, right, d_flux):
    inv_l, inv_r = 1.0 / left[0], 1.0 / right[0]
    ul, ur = left[1] / left[0], right[1] / right[0]
    al, ar = jnp.abs(ul), jnp.abs(ur)
    half_speed = 0.5 * (jnp.maximum(al, ar) + 1.0)
    d_speed = -0.5 * sum(d_flux[c] * (right[c] - left[c]) for c in range(4))
    share = jnp.where(al > ar, 1.0, jnp.where(al < ar, 0.0, 0.5))
    half = [0.5 * d for d in d_flux]
    spread = [half_speed * d for d in d_flux]

    def one(state, u, inv, speed_part, sign):
        du = half[1] * state[1] + half[2] * state[2] + half[3] * state[3] + speed_part * sign_of(u)
        over = du * inv
        return [
            half[1] - over * u + sign * spread[0],
            half[0] + half[1] * u + over + sign * spread[1],
            half[2] * u + sign * spread[2],
            half[3] * u + sign * spread[3],
        ]

    return (
        one(left, ul, inv_l, d_speed * share, 1.0),
        one(right, ur, inv_r, d_speed * (1.0 - share), -1.0),
    )


def edge_backward(cells, gates, d_left, d_right):
    lows, highs = [], []
    direct = [[None] * 4 for _ in range(4)]
    for c in range(4):
        low = gates[FACES * c : FACES * (c + 1)]
        high = gates[FACES * (c + 4) : FACES * (c + 5)]
        lows.append(slope_gain * (cells[2][c] - cells[0][c]) * d_left[c])
        highs.append(-slope_gain * (cells[3][c] - cells[1][c]) * d_right[c])
        low_part = slope_gain * low * d_left[c]
        high_part = slope_gain * high * d_right[c]
        direct[0][c] = -low_part
        direct[1][c] = d_left[c] + high_part
        direct[2][c] = d_right[c] + low_part
        direct[3][c] = -high_part
    return stack(lows + highs) * (1.0 - gates * gates), direct


def turn(values, shift, axis):
    size = values.shape[axis]
    return values if shift % size == 0 else pltpu.roll(values, shift % size, axis)


def x_cells(tiles):
    return [[turn(t, -s, 0)[:FACES] for t in tiles] for s in range(4)]


def pack_kernel(den, mom, tra, cot, w_in, b_in, w_mid, b_mid, w_out, b_out,
                rim, to_first, to_second, state, cots, first_x, first_y, first_bias, mid, mid_bias, out, out_bias,
                out_back, mid_back, first_x_back, first_y_back, *scratch):
    *small, sems = scratch
    nx, ny = den.shape[1:]
    segs = ny // SEG
    rows = nx // segs
    hid = w_in.shape[1]
    copies = [
        pltpu.make_async_copy(source, target, sems.at[k])
        for k, (source, target) in enumerate(
            list(zip([w_in, b_in, w_mid, b_mid, w_out, b_out], small))
            + [
                (den.at[0], state.at[0]),
                (mom.at[0], state.at[pl.ds(1, 2)]),
                (tra.at[0], state.at[3]),
                (cot.at[0], cots),
            ]
        )
    ]
    for one in copies:
        one.start()
    for one in copies[:6]:
        one.wait()
    w_in, b_in, w_mid, b_mid, w_out, b_out = small
    lanes = out_bias.shape[1]
    w_in_rows = exact_nt(pick((hid, hid), lambda q, n: q == n, F32), w_in[...])
    first_x[...], first_y[...] = build_first(w_in_rows, b_in[...], hid)
    first_bias[...] = spread_bias(b_in[...], lanes, FACES // 2)
    mid[...] = build_mid(w_mid[...], hid)
    mid_bias[...] = spread_bias(b_mid[...], lanes, 2)
    out[...] = build_out(w_out[...], hid)
    out_bias[...] = exact_nt(
        pick((64, 8), lambda q, n: (q >> 3) == n, F32), jnp.broadcast_to(b_out[...], (lanes, 8))
    )
    out_back[...] = build_out_back(w_out[...], hid)
    mid_back[...] = build_mid_back(w_mid[...], hid)
    first_x_back[...], first_y_back[...] = build_first_back(w_in[...], hid)

    for one in copies[6:]:
        one.wait()
    lane = lane_index(ny)
    for v in range(8):
        plane = state.at[v] if v < 4 else cots.at[v - 4]
        for at in range(0, rows, FACES):
            total = jnp.zeros((FACES, ny), F32)
            for s in range(segs):
                first = s * SEG + RIM
                moved = turn(plane[pl.ds(s * rows + at, FACES), :], first + RIM, 1)
                total = jnp.where((lane >= first) & (lane < first + 2 * RIM), moved, total)
            rim[v, pl.ds(at, FACES), :] = total
    is_odd = odd_mask(ny)
    spot = lane & (SEG - 1)
    for v in range(8):
        sides = []
        for first in (2 * RIM, RIM):
            total = jnp.zeros((FACES, ny), F32)
            for g in range(rows // FACES):
                moved = turn(rim[v, pl.ds(g * FACES, FACES), :], g * RIM - first, 1)
                total = jnp.where((spot >= g * RIM) & (spot < (g + 1) * RIM), moved, total)
            sides.append(total)
        to_first[v] = jnp.where(is_odd, sides[0], sides[1])
        to_second[v] = jnp.where(is_odd, sides[1], sides[0])


def odd_mask(ny):
    return jnp.full((FACES, ny), lax.rem(lax.axis_index(("tx", "ty")), 2), jnp.int32) == 1


def row_block(at):
    return pl.ds(pl.multiple_of(at * FACES, FACES), FACES)


def x_tiles(planes, group, groups):
    after = jnp.where(group + 1 == groups, 0, group + 1)
    return [stack([plane[row_block(group), :], plane[row_block(after), :]]) for plane in planes]


def pair_tiles(planes, step, half):
    sets = [x_tiles(planes, step + k * half, PAIR * half) for k in range(PAIR)]
    return [side([one[c] for one in sets]) for c in range(len(planes))]


def x_windows(tiles):
    half = FACES // 2
    return [stack([turn(tile, -at, 0)[:FACES] for tile in tiles]) for at in (0, half)]


def swap_halves(first, second):
    half = FACES // 2
    upper = rows_cols(first.shape)[0] < half
    return jnp.where(upper, first, turn(second, half, 0)), jnp.where(upper, turn(first, half, 0), second)


def y_windows(cells):
    pairs = [swap_halves(cells[s][c], cells[s + 1][c]) for s in (0, 2) for c in range(4)]
    return [stack([one[k] for one in pairs]) for k in range(2)]


def y_unwindow(parts):
    found = [[None] * 4 for _ in range(4)]
    for s in (0, 2):
        for c in range(4):
            at = FACES * (2 * s + c)
            found[s][c], found[s + 1][c] = swap_halves(parts[0][at : at + FACES], parts[1][at : at + FACES])
    return found


def x_forward(tiles, weights, hid):
    h1, h1_pair, h2, h2_pair, gates = limiter_forward([split3(one) for one in x_windows(tiles)], weights, hid)
    cells = x_cells(tiles)
    return h1, h2, h1_pair, h2_pair, gates, face_flux(*edge_states(cells, gates))


def update_cells(plane_rows, flux_rows):
    upper = turn(flux_rows, -7, 0)[:FACES]
    lower = turn(flux_rows, -6, 0)[:FACES]
    return plane_rows - courant * (upper - lower)


def x_forward_kernel(state, first_x, mid, mid_bias, out, out_bias,
                     middle, h1_hi, h1_lo, h2_hi, h2_lo, slope1, gates_out, flux):
    nx, ny = state.shape[1:]
    groups = nx // FACES
    half = groups // PAIR
    hid = mid.shape[0] // 4
    x_weights = (first_x, None, mid, mid_bias, out, out_bias)
    planes = [state.at[c] for c in range(4)]

    def step_of(step, _):
        tiles = pair_tiles(planes, step, half)
        h1, h2, h1_pair, h2_pair, gates, fluxes = x_forward(tiles, x_weights, hid)
        for target, value in zip((h1_hi, h1_lo, h2_hi, h2_lo, gates_out), h1_pair + h2_pair + (gates,)):
            target[step] = value
        slope1[step] = 1.0 - h1 * h1
        for c in range(4):
            for k in range(PAIR):
                flux[c, row_block(step + k * half + 1), :] = fluxes[c][:, k * ny : (k + 1) * ny]
        return 0

    lax.fori_loop(0, half, step_of, 0)
    for c in range(4):
        flux[c, :FACES, :] = flux[c, nx : nx + FACES, :]

    def update(group, _):
        for c in range(4):
            both = stack([flux[c, row_block(group), :], flux[c, row_block(group + 1), :]])
            middle[c, row_block(group), :] = update_cells(planes[c][row_block(group), :], both)
        return 0

    lax.fori_loop(0, groups, update, 0, unroll=4)


def y_order(planes):
    return [planes[0], planes[2], planes[1], planes[3]]


def lane_index(width):
    return lax.broadcasted_iota(jnp.int32, (FACES, width), 1)


def y_step(cells, cots, halo_mask, refs, acc, hid):
    weights, out_back, mid_back, first_y_back = refs
    window = [split3(one) for one in y_windows(cells)]
    h1, h1_pair, h2, h2_pair, gates = limiter_forward(window, weights, hid)
    left, right = edge_states(cells, gates)
    d_flux = [courant * (cots[1][c] - cots[0][c]) for c in range(4)]
    d_left, d_right = face_flux_backward(left, right, d_flux)
    if halo_mask is not None:
        d_left = [jnp.where(halo_mask, d, 0.0) for d in d_left]
        d_right = [jnp.where(halo_mask, d, 0.0) for d in d_right]
    d3_full, direct = edge_backward(cells, gates, d_left, d_right)
    d1_full = limiter_backward(
        d3_full, 1.0 - h1 * h1, 1.0 - h2 * h2, h1_pair, h2_pair, out_back, mid_back, acc, hid
    )
    d1 = split(d1_full)
    d_window = y_unwindow(first_backward(d1, first_y_back))
    if acc is not None:
        add_first_grads(window, d1, acc[0])
    return [
        [d_window[s][c] + direct[s][c] for c in range(4)]
        for s in range(4)
    ]


def y_gather(parts, ny):
    lane = lane_index(ny)
    out = []
    for c in range(4):
        a = turn(jnp.where(lane >= 1, parts[0][c], 0.0), -1, 1)
        b = turn(jnp.where(lane < ny - 1, parts[2][c], 0.0), 1, 1)
        d = turn(jnp.where(lane < ny - 2, parts[3][c], 0.0), 2, 1)
        out.append(parts[1][c] + a + b + d)
    return out


def fold_rows(values, hid):
    return sum(values[at : at + hid] for at in range(0, values.shape[0], hid))


def back_kernel(state, cot, middle, own, from_first, from_second,
                first_x, first_y, first_bias, mid, mid_bias, out, out_bias,
                out_back, mid_back, first_y_back,
                h1_hi, h1_lo, h2_hi, h2_lo, slope1, gates_in,
                base, d1_hi, d1_lo, g_weights,
                rim_state, rim_cot, rim_flux, rim_middle, rim_grad, d_middle,
                acc_x, acc_y, acc_mid, acc_out, acc_out_bias):
    nx, ny = state.shape[1:]
    groups = nx // FACES
    half = groups // PAIR
    hid = mid.shape[0] // 4
    x_weights = (first_x, None, mid, mid_bias, out, out_bias)
    segs = ny // SEG
    rim_rows = nx // segs
    rim_groups = rim_rows // FACES
    rim_half = rim_groups // RIM_PAIR

    for acc in (acc_x, acc_y, acc_mid, acc_out, acc_out_bias):
        acc[...] = jnp.zeros(acc.shape, F32)

    lane = lane_index(ny)
    spot = lane & (SEG - 1)
    is_odd = odd_mask(ny)
    for v in range(8):
        for g in range(rim_groups):
            rows = pl.ds(g * FACES, FACES)
            mine, first, second = own[v, rows, :], from_first[v], from_second[v]
            left, right = jnp.where(is_odd, first, second), jnp.where(is_odd, second, first)
            value = jnp.where(
                spot < RIM,
                turn(left, -g * RIM, 1),
                jnp.where(
                    spot < 2 * RIM,
                    turn(mine, -RIM, 1),
                    jnp.where(spot < 3 * RIM, turn(mine, RIM, 1), turn(right, (3 - g) * RIM, 1)),
                ),
            )
            if v < 4:
                rim_state[v, rows, :] = value
                if g == 0:
                    rim_state[v, pl.ds(rim_rows, FACES), :] = turn(value, -SEG, 1)
            else:
                rim_cot[v - 4, rows, :] = value

    def rim_forward(step, _):
        sets = [
            [
                stack([
                    rim_state[c, row_block(step + k * rim_half), :],
                    rim_state[c, row_block(step + k * rim_half + 1), :],
                ])
                for c in range(4)
            ]
            for k in range(RIM_PAIR)
        ]
        tiles = [side([one[c] for one in sets]) for c in range(4)]
        fluxes = x_forward(tiles, x_weights, hid)[-1]
        for c in range(4):
            for k in range(RIM_PAIR):
                rim_flux[c, row_block(step + k * rim_half + 1), :] = fluxes[c][:, k * ny : (k + 1) * ny]
        return 0

    lax.fori_loop(0, rim_half, rim_forward, 0)
    for c in range(4):
        rim_flux[c, :FACES, :] = turn(rim_flux[c, rim_rows : rim_rows + FACES, :], SEG, 1)
        for g in range(rim_groups):
            rows = pl.ds(g * FACES, FACES)
            both = stack([rim_flux[c, rows, :], rim_flux[c, pl.ds((g + 1) * FACES, FACES), :]])
            rim_middle[c, rows, :] = update_cells(rim_state[c, rows, :], both)

    refs = ((first_y, first_bias, mid, mid_bias, out, out_bias), out_back, mid_back, first_y_back)
    spot_wide = lane_index(RIM_PAIR * ny) & (SEG - 1)
    rim_faces = (spot_wide == RIM - 2) | (spot_wide == RIM - 1) | (spot_wide == 3 * RIM)

    def rim_back(step, _):
        cells = [[[] for _ in range(4)] for _ in range(4)]
        cots = [[[] for _ in range(4)] for _ in range(2)]
        for k in range(RIM_PAIR):
            rows = row_block(step + k * rim_half)
            for c in range(4):
                value = rim_middle[c, rows, :]
                for s in range(4):
                    cells[s][c].append(turn(value, 1 - s, 1))
                value = rim_cot[c, rows, :]
                for s in range(2):
                    cots[s][c].append(turn(value, -s, 1))
        cells = [y_order([side(one) for one in row]) for row in cells]
        cots = [y_order([side(one) for one in row]) for row in cots]
        parts = y_step(cells, cots, rim_faces, refs, None, hid)
        for k in range(RIM_PAIR):
            own_parts = [[one[:, k * ny : (k + 1) * ny] for one in row] for row in parts]
            gathered = y_order(y_gather(own_parts, ny))
            for c in range(4):
                rim_grad[c, row_block(step + k * rim_half), :] = gathered[c]
        return 0

    lax.fori_loop(0, rim_half, rim_back, 0)

    def main_y(step, _):
        cells = [[[] for _ in range(4)] for _ in range(4)]
        cots = [[[] for _ in range(4)] for _ in range(2)]
        for k in range(PAIR):
            group = step + k * half
            rows = row_block(group)
            seg = group // rim_groups
            rim_at = row_block(group - seg * rim_groups)
            to_low = ny - (seg * SEG + 3 * RIM)
            to_high = lax.rem(ny - 1 - (seg * SEG + RIM - 1) + ny, ny)
            for c in range(4):
                value = middle[c, rows, :]
                rim_value = rim_middle[c, rim_at, :]
                low = jnp.where(lane < 2, pltpu.roll(rim_value, to_low, 1), value)
                high = jnp.where(lane == ny - 1, pltpu.roll(rim_value, to_high, 1), value)
                cells[0][c].append(turn(high, 1, 1))
                cells[1][c].append(value)
                cells[2][c].append(turn(jnp.where(lane < 1, low, value), -1, 1))
                cells[3][c].append(turn(low, -2, 1))
                value = cot[c, rows, :]
                rim_value = rim_cot[c, rim_at, :]
                low = jnp.where(lane < 1, pltpu.roll(rim_value, to_low, 1), value)
                cots[0][c].append(value)
                cots[1][c].append(turn(low, -1, 1))
        cells = [y_order([side(one) for one in row]) for row in cells]
        cots = [y_order([side(one) for one in row]) for row in cots]
        parts = y_step(cells, cots, None, refs, (acc_y, acc_mid, acc_out, acc_out_bias), hid)
        for k in range(PAIR):
            group = step + k * half
            rows = row_block(group)
            seg = group // rim_groups
            rim_at = row_block(group - seg * rim_groups)
            own_parts = [[one[:, k * ny : (k + 1) * ny] for one in row] for row in parts]
            gathered = y_order(y_gather(own_parts, ny))
            to_low = ny - (seg * SEG + RIM)
            to_high = lax.rem(ny - 1 - (seg * SEG + 3 * RIM - 1) + ny, ny)
            for c in range(4):
                rim_value = rim_grad[c, rim_at, :]
                from_rim = jnp.where(
                    lane < 2,
                    pltpu.roll(rim_value, to_low, 1),
                    jnp.where(lane == ny - 1, pltpu.roll(rim_value, to_high, 1), 0.0),
                )
                d_middle[c, rows, :] = cot[c, rows, :] + gathered[c] + from_rim
        return 0

    lax.fori_loop(0, half, main_y, 0)

    planes = [state.at[c] for c in range(4)]
    d_planes = [d_middle.at[c] for c in range(4)]

    def main_x(step, carry):
        tiles = pair_tiles(planes, step, half)
        d_tiles = pair_tiles(d_planes, step, half)
        gates = gates_in[step]
        h1_pair = (h1_hi[step], h1_lo[step])
        h2_pair = (h2_hi[step], h2_lo[step])
        h2 = h2_pair[0].astype(F32) + h2_pair[1].astype(F32)
        cells = x_cells(tiles)
        left, right = edge_states(cells, gates)
        d_flux = [courant * (turn(d, -2, 0)[:FACES] - turn(d, -1, 0)[:FACES]) for d in d_tiles]
        d_left, d_right = face_flux_backward(left, right, d_flux)
        d3_full, direct = edge_backward(cells, gates, d_left, d_right)
        d1_full = limiter_backward(
            d3_full, slope1[step], 1.0 - h2 * h2, h1_pair, h2_pair, out_back, mid_back, (acc_x, acc_mid, acc_out, acc_out_bias), hid
        )
        d1 = split(d1_full)
        d1_hi[step], d1_lo[step] = d1
        add_first_grads([split(one) for one in x_windows(tiles)], d1, acc_x)
        later = []
        for c in range(4):
            nothing = jnp.zeros_like(direct[0][c])
            total = stack([direct[0][c], nothing])
            for s in range(1, 4):
                total = total + turn(stack([direct[s][c], nothing]), s, 0)
            now = total[:FACES] + d_tiles[c][:FACES] + carry[c]
            for k in range(PAIR):
                base[c, row_block(step + k * half), :] = now[:, k * ny : (k + 1) * ny]
            later.append(total[FACES:])
        return tuple(later)

    start = tuple(jnp.zeros((FACES, PAIR * ny), F32) for _ in range(4))
    last = lax.fori_loop(0, half, main_x, start)
    for c in range(4):
        for k in range(PAIR):
            at = (k + 1) % PAIR * half * FACES
            base[c, pl.ds(at, FACES), :] += last[c][:, k * ny : (k + 1) * ny]

    lanes = g_weights.shape[1]
    values = acc_mid[: 8 * hid, :]
    r, c = rows_cols(values.shape)
    same = rest(quot(r, hid), 4) == rest(quot(c, hid), 4)
    values = fold_rows(jnp.where(same, values, 0.0), hid)
    grad_mid = exact_nt(
        pick((hid, 8 * hid), lambda q, n: rest(n, hid) == q, F32),
        stack([values, jnp.zeros((lanes - hid, 8 * hid), F32)]),
    )
    grad_mid_bias = exact(
        acc_mid[8 * hid : 8 * hid + 8, :], pick((8 * hid, lanes), lambda q, n: rest(q, hid) == n, F32)
    )
    r, c = rows_cols(acc_x.shape)
    values, shift = acc_x[...], (r & 7) - rest(quot(c, hid), 4)
    found = [jnp.where((shift == s) & (r < 64), values, 0.0)[:64] for s in range(4)]
    found.append(values[64:])
    r, c = rows_cols(acc_y.shape)
    found.append(jnp.where(((r & 3) == rest(quot(c, hid), 4)) | (r >= 128), acc_y[...], 0.0))
    found = exact(
        stack(found),
        pick((8 * hid, lanes), lambda q, n: (rest(n - q, hid) == 0) & (n >= hid) & (n < 2 * hid), F32),
    )
    y_at = 4 * 64 + ONES

    def source(q, n):
        in_x = (n < 256) & (q == 4 * (n >> 6) + ((n & 31) >> 3))
        m = n - y_at
        in_y = (m >= 0) & (m < 128) & (q == y_column(m & 63))
        return in_x | in_y | ((n == 256) | (m == 128)) & (q == 24)

    beside = exact(pick((32, found.shape[0]), source, F32), found)
    r, c = rows_cols(acc_out.shape)
    found = fold_rows(jnp.where((c & 7) == rest(quot(r, hid), FACES), acc_out[...], 0.0), hid)
    beside = beside + exact_nt(
        pick((32, found.shape[1]), lambda q, n: q == 16 + ((n & 63) >> 3), F32),
        stack([jnp.zeros((hid, found.shape[1]), F32), found, jnp.zeros((lanes - 2 * hid, found.shape[1]), F32)]),
    )
    out_bias_rows = exact_nt(jnp.ones((8, acc_out_bias.shape[1]), F32), acc_out_bias[...])
    grad_out_bias = exact_nt(out_bias_rows, pick((lanes, 64), lambda q, n: (n >> 3) == q - hid, F32))
    r, c = rows_cols((8, lanes))
    g_weights[:hid, :] = grad_mid + beside
    g_weights[25:26, :] += grad_out_bias[:1]
    g_weights[hid:, :] = grad_mid_bias


def state_kernel(base, d1_hi, d1_lo, first_x_back, _, g_den, g_mom, g_tra):
    nx, ny = base.shape[1:]
    half = nx // FACES // PAIR
    grads = [g_den.at[0], g_mom.at[0, 0], g_mom.at[0, 1], g_tra.at[0]]
    upper = rows_cols((FACES, PAIR * ny))[0] < FACES // 2

    def step_of(step, carry):
        first, second = first_backward((d1_hi[step], d1_lo[step]), first_x_back)
        later = []
        for c in range(4):
            rows = slice(FACES * c, FACES * (c + 1))
            moved = turn(second[rows], FACES // 2, 0)
            now = first[rows] + jnp.where(upper, 0.0, moved) + carry[c]
            for k in range(PAIR):
                at = row_block(step + k * half)
                grads[c][at, :] = base[c, at, :] + now[:, k * ny : (k + 1) * ny]
            later.append(jnp.where(upper, moved, 0.0))
        return tuple(later)

    start = tuple(jnp.zeros((FACES, PAIR * ny), F32) for _ in range(4))
    last = lax.fori_loop(0, half, step_of, start)
    for c in range(4):
        for k in range(PAIR):
            at = (k + 1) % PAIR * half * FACES
            grads[c][pl.ds(at, FACES), :] += last[c][:, k * ny : (k + 1) * ny]


def finish_kernel(total, g_w_in, g_b_in, g_w_mid, g_b_mid, g_w_out, g_b_out):
    hid = g_w_mid.shape[0]
    g_w_mid[...] = total[:hid, :hid]
    beside = total[:hid, hid : 2 * hid]
    g_w_in[...] = beside[:16]
    g_w_out[...] = beside[16:24]
    g_b_in[...] = beside[24:25]
    g_b_out[...] = beside[25:26, :8]
    g_b_mid[...] = total[hid : hid + 1, :hid]


def whole(count, space=pltpu.VMEM):
    return [pl.BlockSpec(memory_space=space)] * count


def call(kernel, outs, operands, out_spaces=None, in_spaces=None, scratch=(), flops=0, moved=0):
    return pl.pallas_call(
        kernel,
        out_shape=outs,
        in_specs=in_spaces or whole(len(operands)),
        out_specs=out_spaces or whole(len(outs)),
        scratch_shapes=list(scratch),
        compiler_params=pltpu.CompilerParams(vmem_limit_bytes=VMEM_BYTES),
        cost_estimate=pl.CostEstimate(flops=flops, bytes_accessed=moved, transcendentals=0),
    )(*operands)


def sum_rounds(values, sizes):
    axes, size = tuple(sizes), 1
    for one in sizes.values():
        size *= one
    if size & (size - 1):
        return [values, lax.psum(values, axes)]
    bits = [1 << k for k in range(size.bit_length() - 1)]
    core = size // sizes["traj"]
    others = [bit for bit in reversed(bits) if bit != core]
    found = [values]
    for masks in [[core]] * (core in bits) + [others[k : k + 2] for k in range(0, len(others), 2)]:
        partners = [0]
        for mask in masks:
            partners = partners + [one ^ mask for one in partners]
        parts = [
            lax.ppermute(values, axes, [(i, i ^ one) for i in range(size)]) if one else values for one in partners
        ]
        while len(parts) > 1:
            parts = [parts[k] + parts[k + 1] for k in range(0, len(parts), 2)]
        values = parts[0]
        found.append(values)
    return found


def body(sizes, density, momentum, tracer, cotangent, w_in, b_in, w_mid, b_mid, w_out, b_out):
    nx, ny = density.shape[1:]
    hid = w_in.shape[0]
    wide = FACES * hid
    groups = nx // FACES
    half = groups // PAIR
    lanes = PAIR * ny
    segs = ny // SEG
    rim_rows = nx // segs
    ring = sizes["tx"] * sizes["ty"]
    shape = jax.ShapeDtypeStruct

    operands = [
        density, momentum, tracer, cotangent, w_in.T, b_in[None], w_mid, b_mid[None], w_out, b_out[None]
    ]
    rim, to_first, to_second, state, cots, *matrices = call(
        pack_kernel,
        [
            shape((8, rim_rows, ny), F32),
            shape((8, FACES, ny), F32),
            shape((8, FACES, ny), F32),
            shape((4, nx, ny), F32),
            shape((4, nx, ny), F32),
            shape((wide // 2, 6 * 32 + ONES), BF16),
            shape((wide, 4 * 64), BF16),
            shape((wide // 2, ny), F32),
            shape((4 * hid, 8 * hid), BF16),
            shape((2 * hid, ny), F32),
            shape((192, wide), BF16),
            shape((64, ny), F32),
            shape((wide, 192), BF16),
            shape((2 * hid, 6 * hid), BF16),
            shape((64, wide), BF16),
            shape((128, wide), BF16),
        ],
        [pltpu.with_memory_space_constraint(one, pltpu.HBM) for one in operands],
        in_spaces=whole(10, pltpu.HBM),
        scratch=[pltpu.VMEM(one.shape, F32) for one in operands[4:]] + [pltpu.SemaphoreType.DMA((10,))],
    )
    axes = ("tx", "ty")
    swaps = [[(i, (i + 1 if (i + first) % 2 == 0 else i - 1) % ring) for i in range(ring)] for first in range(2)]
    from_first, from_second = (
        lax.ppermute(one, axes, swap) for one, swap in zip((to_first, to_second), swaps)
    )

    middle, *kept = call(
        x_forward_kernel,
        [shape((4, nx, ny), F32)]
        + [shape((half, wide, lanes), BF16)] * 4
        + [shape((half, wide, lanes), F32)]
        + [shape((half, 64, lanes), F32)],
        [state, matrices[0]] + matrices[3:7],
        scratch=[pltpu.VMEM((4, nx + FACES, ny), F32)],
        flops=10**10,
        moved=10**7,
    )
    first_x_back = matrices.pop(-2)
    *found, g_weights = call(
        back_kernel,
        [
            shape((4, nx, ny), F32),
            shape((half, wide, lanes), BF16),
            shape((half, wide, lanes), BF16),
            shape((hid + 8, 128), F32),
        ],
        [state, cots, middle, rim, from_first, from_second] + matrices + kept,
        scratch=[
            pltpu.VMEM((4, rim_rows + FACES, ny), F32),
            pltpu.VMEM((4, rim_rows, ny), F32),
            pltpu.VMEM((4, rim_rows + FACES, ny), F32),
            pltpu.VMEM((4, rim_rows, ny), F32),
            pltpu.VMEM((4, rim_rows, ny), F32),
            pltpu.VMEM((4, nx, ny), F32),
            pltpu.VMEM((2 * 32 + ONES, wide), F32),
            pltpu.VMEM((2 * 64 + ONES, wide), F32),
            pltpu.VMEM((8 * hid + ONES, 8 * hid), F32),
            pltpu.VMEM((2 * wide, 128), F32),
            pltpu.VMEM((64, lanes), F32),
        ],
        flops=4 * 10**10,
        moved=2 * 10**7,
    )
    rounds = sum_rounds(g_weights, sizes)
    g_den, g_mom, g_tra = call(
        state_kernel,
        [shape(density.shape, F32), shape(momentum.shape, F32), shape(tracer.shape, F32)],
        found + [first_x_back, rounds[min(1, len(rounds) - 1)]],
        flops=2 * 10**9,
        moved=10**6,
    )
    total = rounds[-1]
    g_w_in, g_b_in, g_w_mid, g_b_mid, g_w_out, g_b_out = call(
        finish_kernel,
        [
            shape((w_in.shape[1], hid), F32),
            shape((1, hid), F32),
            shape(w_mid.shape, F32),
            shape((1, hid), F32),
            shape(w_out.shape, F32),
            shape((1, b_out.shape[0]), F32),
        ],
        [total],
    )
    return (g_den, g_mom, g_tra, g_w_in.T, g_b_in[0], g_w_mid, g_b_mid[0], g_w_out, g_b_out[0])


def solution(mesh):
    flow = P("traj", None, ("tx", "ty"))
    deep = P("traj", None, None, ("tx", "ty"))
    return jax.shard_map(
        functools.partial(body, dict(mesh.shape)),
        mesh=mesh,
        in_specs=(flow, deep, flow, deep) + (P(),) * 6,
        out_specs=(flow, deep, flow) + (P(),) * 6,
        check_vma=False,
    )
```

```python
import functools

import jax
import jax.numpy as jnp
from jax import lax
from jax.experimental import pallas as pl
from jax.experimental.pallas import tpu as pltpu
from jax.sharding import PartitionSpec as P

courant = 0.1
slope_gain = 0.25
F32 = jnp.float32
BF16 = jnp.bfloat16
FACES = 8
SEG = 16
RIM = 4
PAIR = 8
RIM_PAIR = 4
ONES = 16
VMEM_BYTES = 32 * 2**20


def dot(a, b):
    return lax.dot_general(a, b, (((1,), (0,)), ((), ())), preferred_element_type=F32)


def dot_nt(a, b):
    return lax.dot_general(a, b, (((1,), (1,)), ((), ())), preferred_element_type=F32)


def exact(a, b):
    return lax.dot_general(
        a, b, (((1,), (0,)), ((), ())), precision=lax.Precision.HIGHEST, preferred_element_type=F32
    )


def exact_nt(a, b):
    return lax.dot_general(
        a, b, (((1,), (1,)), ((), ())), precision=lax.Precision.HIGHEST, preferred_element_type=F32
    )


def split(values):
    high = values.astype(BF16)
    return high, (values - high.astype(F32)).astype(BF16)


def split3(values):
    high = values.astype(BF16)
    rest = values - high.astype(F32)
    middle = rest.astype(BF16)
    return high, middle, (rest - middle.astype(F32)).astype(BF16)


def rows_cols(shape):
    return lax.broadcasted_iota(jnp.int32, shape, 0), lax.broadcasted_iota(jnp.int32, shape, 1)


def quot(values, n):
    return values >> (n.bit_length() - 1) if n & (n - 1) == 0 else values // n


def rest(values, n):
    return values & (n - 1) if n & (n - 1) == 0 else values % n


def pick(shape, test, dtype=BF16):
    r, c = rows_cols(shape)
    return jnp.where(test(r, c), 1.0, 0.0).astype(dtype)


def stack(parts):
    return jnp.concatenate(parts, 0)


def side(parts):
    return jnp.concatenate(parts, 1)


STACKED = (0, 0, 0, 1, 1, 2)


def stacked(parts):
    return [parts[0], parts[1], parts[2], parts[0], parts[1], parts[0]]


def level_of(block):
    return jnp.where(block < 3, 0, jnp.where(block < 5, 1, 2))


def choose(values, levels):
    parts = [part.astype(F32) for part in split3(values)]
    total = jnp.zeros(values.shape, F32)
    for k, part in enumerate(parts):
        total = jnp.where(levels == k, part, total)
    return total


def y_column(m):
    return 4 * (2 * (m >> 5) + ((m & 7) >> 2)) + ((m & 31) >> 3)


def build_first(w, b, hid):
    x_cols, y_cols, step = 6 * 32 + ONES, 4 * 64, 256

    def source(q, n):
        s = n >> 8
        m = n & (step - 1)
        in_x = (s < 4) & (m < 192) & (q == 4 * s + ((m & 31) >> 3))
        in_y = (s == 4) & (q == y_column(m & 63))
        return in_x | in_y

    values = exact(w, pick((16, 4 * step + y_cols), source, F32))
    _, n = rows_cols(values.shape)
    for_x = choose(values, level_of((n & (step - 1)) >> 5))
    for_y = values[:, 4 * step :]
    block = n[:, :y_cols] >> 6
    upper = choose(for_y, jnp.where(block < 3, 0, 2))
    lower = choose(for_y, jnp.where(block < 2, 1, -1))

    at, _ = rows_cols((x_cols, hid))
    rows = jnp.zeros((x_cols, hid), F32)
    for k, level in enumerate(split3(b)):
        rows = jnp.where(at == 192 + k, jnp.broadcast_to(level.astype(F32), (x_cols, hid)), rows)
    bias = dot_nt(pick((hid, hid), lambda q, n: q == n), rows.astype(BF16))

    half = FACES // 2
    r, c = rows_cols((half * hid, x_cols))
    shift = jnp.where(c < 192, (c & 7) - quot(r, hid), -1)
    first_x = stack([bias] * half)
    for s in range(4):
        part = for_x[:, s * step : s * step + x_cols]
        first_x = jnp.where(shift == s, stack([part] * half), first_x)
    r, c = rows_cols((2 * half * hid, y_cols))
    keep = (c & 3) == rest(quot(r, hid), half)
    first_y = jnp.where(keep, stack([upper] * half + [lower] * half), 0.0)
    return first_x.astype(BF16), first_y.astype(BF16)


def build_first_back(w_t, hid):
    wide = FACES // 2 * hid

    def source(q, n):
        in_x = (q < 128) & (n == 4 * (q >> 5) + ((q & 31) >> 3))
        in_y = (q >= 128) & (n == y_column(q - 128))
        return in_x | in_y

    rows = exact(pick((128 + 64, 16), source, F32), w_t)
    right = pick((hid, 2 * wide), lambda q, n: rest(n, hid) == q)
    high, low = (dot(part, right) for part in split(rows))
    r, c = rows_cols(high.shape)
    low = jnp.where(c < wide, low, 0.0)
    face = quot(rest(c, wide), hid)
    shift = (r & 7) - face
    upper = lower = jnp.zeros((32, 2 * wide), F32)
    for s in range(4):
        keep = shift[:32] == s
        upper = jnp.where(keep, high[32 * s : 32 * (s + 1)], upper)
        lower = jnp.where(keep, low[32 * s : 32 * (s + 1)], lower)
    keep = ((r & 3) == face)[128:]
    back_y = stack([jnp.where(keep, high[128:], 0.0), jnp.where(keep, low[128:], 0.0)])
    return stack([upper, lower]).astype(BF16), back_y.astype(BF16)


def build_mid(w, hid):
    block = 2 * hid
    tiled = exact(w, pick((hid, 4 * block), lambda q, n: rest(n, hid) == q, F32))
    _, n = rows_cols(tiled.shape)
    upper = choose(tiled, jnp.where(n < 3 * block, 0, 2))
    lower = choose(tiled, jnp.where(n < 2 * block, 1, -1))
    r, c = rows_cols((2 * block, 4 * block))
    keep = quot(rest(r, block), hid) == quot(rest(c, block), hid)
    return jnp.where(keep, stack([upper, upper, lower, lower]), 0.0).astype(BF16)


def build_mid_back(w, hid):
    block = 2 * hid
    turned = exact_nt(pick((hid, hid), lambda q, n: q == n, F32), w)
    tiled = exact(turned, pick((hid, 3 * block), lambda q, n: rest(n, hid) == q, F32))
    _, n = rows_cols(tiled.shape)
    tiled = choose(tiled, jnp.where(quot(n, block) == 1, 1, 0))
    r, c = rows_cols((block, 3 * block))
    keep = quot(r, hid) == quot(rest(c, block), hid)
    return jnp.where(keep, stack([tiled] * 2), 0.0).astype(BF16)


def build_out(w, hid):
    wide = FACES * hid
    rows = exact(pick((64, 8), lambda q, n: (q >> 3) == n, F32), w)
    tiled = dot(stack(list(split3(rows))), pick((hid, wide), lambda q, n: rest(n, hid) == q))
    r, c = rows_cols(tiled.shape)
    return jnp.where((r & 7) == quot(c, hid), tiled, 0.0).astype(BF16)


def build_out_back(w, hid):
    wide = FACES * hid
    turned = exact_nt(pick((hid, hid), lambda q, n: q == n, F32), w)
    tiled = exact(turned, pick((8, 192), lambda q, n: ((n & 63) >> 3) == q, F32))
    _, n = rows_cols(tiled.shape)
    tiled = choose(tiled, jnp.where((n >> 6) == 1, 1, 0))
    r, c = rows_cols((wide, 192))
    return jnp.where(quot(r, hid) == (c & 7), stack([tiled] * FACES), 0.0).astype(BF16)


def spread_bias(b, lanes, copies):
    n = b.shape[1]
    rows = exact_nt(pick((n, n), lambda q, m: q == m, F32), jnp.broadcast_to(b, (lanes, n)))
    return stack([rows] * copies)


def spread(bias_ref, width):
    return side([bias_ref[...]] * (width // bias_ref.shape[1]))


def limiter_forward(first, weights, hid):
    first_ref, first_bias_ref, mid_ref, mid_bias_ref, out_ref, out_bias_ref = weights
    width = first[0][0].shape[1]
    ones = [jnp.ones((ONES, width), BF16)]
    firsts = []
    for one in first:
        if first_bias_ref is None:
            firsts.append(dot(first_ref[...], stack(stacked(one) + ones)))
        else:
            high, middle, low = one
            both = dot(first_ref[...], stack([high, middle, low, high]))
            half = both.shape[0] // 2
            firsts.append(both[:half] + both[half:] + spread(first_bias_ref, width))
    block = 2 * hid
    h1, h1_parts, h2, h2_parts = [], [], [], []
    for values in firsts:
        for at in range(0, values.shape[0], block):
            h1.append(jnp.tanh(values[at : at + block]))
            high, middle, low = split3(h1[-1])
            h1_parts.append((high, middle))
            both = dot(mid_ref[...], stack([high, middle, low, high]))
            h2.append(jnp.tanh(both[:block] + both[block:] + spread(mid_bias_ref, width)))
            h2_parts.append(split3(h2[-1]))
    h1, h2 = stack(h1), stack(h2)
    h1_parts = tuple(stack([one[k] for one in h1_parts]) for k in range(2))
    h2_parts = tuple(stack([one[k] for one in h2_parts]) for k in range(3))
    rows = 8 * FACES
    a = dot(out_ref[...], h2_parts[0])
    b = dot(out_ref[: 2 * rows, :], h2_parts[1])
    c = dot(out_ref[:rows, :], h2_parts[2])
    gates = jnp.tanh(
        ((a[2 * rows :] + b[rows:] + c) + (a[rows : 2 * rows] + b[:rows])) + a[:rows] + spread(out_bias_ref, width)
    )
    return h1, h1_parts, h2, h2_parts[:2], gates


def limiter_backward(d3, h1, h2, h1_pair, h2_pair, out_back_ref, mid_back_ref, acc, hid):
    d3_hi, d3_lo = split(d3)
    dh2 = dot(out_back_ref[...], stack([d3_hi, d3_hi, d3_lo]))
    if acc is not None:
        acc[2][...] += dot_nt(stack(list(h2_pair)), stack([d3_hi, d3_lo]))
        acc[3][...] += d3
    block = 2 * hid
    d2, d1 = [], []
    for at in range(0, FACES * hid, block):
        one1, one2 = h1[at : at + block], h2[at : at + block]
        high, low = split(dh2[at : at + block] * (1.0 - one2 * one2))
        d2.append((high, low))
        d1.append(split(dot(mid_back_ref[...], stack([high, high, low])) * (1.0 - one1 * one1)))
    d2_hi, d2_lo = (stack([one[k] for one in d2]) for k in range(2))
    if acc is not None:
        ones = jnp.ones((ONES, d3.shape[1]), BF16)
        lefts, rights = [], []
        for at in range(0, FACES * hid, 2 * block):
            lefts.append(stack([part[at : at + 2 * block] for part in h1_pair] + [ones]))
            rights.append(stack([part[at : at + 2 * block] for part in (d2_hi, d2_lo)]))
        acc[1][...] += dot_nt(side(lefts), side(rights))
    return tuple(stack([one[k] for one in d1]) for k in range(2))


def first_backward(d1, back_ref):
    wide = d1[0].shape[0] // 2
    found = []
    for at in (0, wide):
        both = dot(back_ref[...], stack([part[at : at + wide] for part in d1]))
        half = both.shape[0] // 2
        found.append(both[:half] + both[half:])
    return found


def add_first_grads(first, d1, acc_in):
    ones = jnp.ones((ONES, d1[0].shape[1]), BF16)
    wide = d1[0].shape[0] // 2
    lefts = [stack([one[0], one[1], ones]) for one in first]
    rights = [stack([part[at : at + wide] for part in d1]) for at in (0, wide)]
    acc_in[...] += dot_nt(side(lefts), side(rights))


def edge_states(cells, gates):
    left, right = [], []
    for c in range(4):
        low = gates[FACES * c : FACES * (c + 1)]
        high = gates[FACES * (c + 4) : FACES * (c + 5)]
        left.append(cells[1][c] + slope_gain * low * (cells[2][c] - cells[0][c]))
        right.append(cells[2][c] - slope_gain * high * (cells[3][c] - cells[1][c]))
    return left, right


def face_flux(left, right):
    ul = left[1] / left[0]
    ur = right[1] / right[0]
    half_speed = 0.5 * (jnp.maximum(jnp.abs(ul), jnp.abs(ur)) + 1.0)
    fl = [left[1], left[1] * ul + left[0], left[2] * ul, left[3] * ul]
    fr = [right[1], right[1] * ur + right[0], right[2] * ur, right[3] * ur]
    return [0.5 * (fl[c] + fr[c]) - half_speed * (right[c] - left[c]) for c in range(4)]


def sign_of(values):
    return jnp.where(values > 0.0, 1.0, jnp.where(values < 0.0, -1.0, 0.0))


def face_flux_backward(left, right, d_flux):
    inv_l, inv_r = 1.0 / left[0], 1.0 / right[0]
    ul, ur = left[1] / left[0], right[1] / right[0]
    al, ar = jnp.abs(ul), jnp.abs(ur)
    half_speed = 0.5 * (jnp.maximum(al, ar) + 1.0)
    d_speed = -0.5 * sum(d_flux[c] * (right[c] - left[c]) for c in range(4))
    share = jnp.where(al > ar, 1.0, jnp.where(al < ar, 0.0, 0.5))
    half = [0.5 * d for d in d_flux]
    spread = [half_speed * d for d in d_flux]

    def one(state, u, inv, speed_part, sign):
        du = half[1] * state[1] + half[2] * state[2] + half[3] * state[3] + speed_part * sign_of(u)
        over = du * inv
        return [
            half[1] - over * u + sign * spread[0],
            half[0] + half[1] * u + over + sign * spread[1],
            half[2] * u + sign * spread[2],
            half[3] * u + sign * spread[3],
        ]

    return (
        one(left, ul, inv_l, d_speed * share, 1.0),
        one(right, ur, inv_r, d_speed * (1.0 - share), -1.0),
    )


def edge_backward(cells, gates, d_left, d_right):
    lows, highs = [], []
    direct = [[None] * 4 for _ in range(4)]
    for c in range(4):
        low = gates[FACES * c : FACES * (c + 1)]
        high = gates[FACES * (c + 4) : FACES * (c + 5)]
        lows.append(slope_gain * (cells[2][c] - cells[0][c]) * d_left[c])
        highs.append(-slope_gain * (cells[3][c] - cells[1][c]) * d_right[c])
        low_part = slope_gain * low * d_left[c]
        high_part = slope_gain * high * d_right[c]
        direct[0][c] = -low_part
        direct[1][c] = d_left[c] + high_part
        direct[2][c] = d_right[c] + low_part
        direct[3][c] = -high_part
    return stack(lows + highs) * (1.0 - gates * gates), direct


def turn(values, shift, axis):
    size = values.shape[axis]
    return values if shift % size == 0 else pltpu.roll(values, shift % size, axis)


def x_cells(tiles):
    return [[turn(t, -s, 0)[:FACES] for t in tiles] for s in range(4)]


def pack_kernel(den, mom, tra, cot, w_in, b_in, w_mid, b_mid, w_out, b_out,
                rim, to_first, to_second, state, cots, first_x, first_y, first_bias, mid, mid_bias, out, out_bias,
                out_back, mid_back, first_x_back, first_y_back, *scratch):
    *small, sems = scratch
    nx, ny = den.shape[1:]
    segs = ny // SEG
    rows = nx // segs
    hid = w_in.shape[1]
    copies = [
        pltpu.make_async_copy(source, target, sems.at[k])
        for k, (source, target) in enumerate(
            list(zip([w_in, b_in, w_mid, b_mid, w_out, b_out], small))
            + [
                (den.at[0], state.at[0]),
                (mom.at[0], state.at[pl.ds(1, 2)]),
                (tra.at[0], state.at[3]),
                (cot.at[0], cots),
            ]
        )
    ]
    for one in copies:
        one.start()
    for one in copies[:6]:
        one.wait()
    w_in, b_in, w_mid, b_mid, w_out, b_out = small
    lanes = out_bias.shape[1]
    w_in_rows = exact_nt(pick((hid, hid), lambda q, n: q == n, F32), w_in[...])
    first_x[...], first_y[...] = build_first(w_in_rows, b_in[...], hid)
    first_bias[...] = spread_bias(b_in[...], lanes, FACES // 2)
    mid[...] = build_mid(w_mid[...], hid)
    mid_bias[...] = spread_bias(b_mid[...], lanes, 2)
    out[...] = build_out(w_out[...], hid)
    out_bias[...] = exact_nt(
        pick((64, 8), lambda q, n: (q >> 3) == n, F32), jnp.broadcast_to(b_out[...], (lanes, 8))
    )
    out_back[...] = build_out_back(w_out[...], hid)
    mid_back[...] = build_mid_back(w_mid[...], hid)
    first_x_back[...], first_y_back[...] = build_first_back(w_in[...], hid)

    for one in copies[6:]:
        one.wait()
    lane = lane_index(ny)
    for v in range(8):
        plane = state.at[v] if v < 4 else cots.at[v - 4]
        for at in range(0, rows, FACES):
            total = jnp.zeros((FACES, ny), F32)
            for s in range(segs):
                first = s * SEG + RIM
                moved = turn(plane[pl.ds(s * rows + at, FACES), :], first + RIM, 1)
                total = jnp.where((lane >= first) & (lane < first + 2 * RIM), moved, total)
            rim[v, pl.ds(at, FACES), :] = total
    is_odd = odd_mask(ny)
    spot = lane & (SEG - 1)
    for v in range(8):
        sides = []
        for first in (2 * RIM, RIM):
            total = jnp.zeros((FACES, ny), F32)
            for g in range(rows // FACES):
                moved = turn(rim[v, pl.ds(g * FACES, FACES), :], g * RIM - first, 1)
                total = jnp.where((spot >= g * RIM) & (spot < (g + 1) * RIM), moved, total)
            sides.append(total)
        to_first[v] = jnp.where(is_odd, sides[0], sides[1])
        to_second[v] = jnp.where(is_odd, sides[1], sides[0])


def odd_mask(ny):
    return jnp.full((FACES, ny), lax.rem(lax.axis_index(("tx", "ty")), 2), jnp.int32) == 1


def row_block(at):
    return pl.ds(pl.multiple_of(at * FACES, FACES), FACES)


def x_tiles(planes, group, groups):
    after = jnp.where(group + 1 == groups, 0, group + 1)
    return [stack([plane[row_block(group), :], plane[row_block(after), :]]) for plane in planes]


def pair_tiles(planes, step, half):
    sets = [x_tiles(planes, step + k * half, PAIR * half) for k in range(PAIR)]
    return [side([one[c] for one in sets]) for c in range(len(planes))]


def x_windows(tiles):
    half = FACES // 2
    return [stack([turn(tile, -at, 0)[:FACES] for tile in tiles]) for at in (0, half)]


def swap_halves(first, second):
    half = FACES // 2
    upper = rows_cols(first.shape)[0] < half
    return jnp.where(upper, first, turn(second, half, 0)), jnp.where(upper, turn(first, half, 0), second)


def y_windows(cells):
    pairs = [swap_halves(cells[s][c], cells[s + 1][c]) for s in (0, 2) for c in range(4)]
    return [stack([one[k] for one in pairs]) for k in range(2)]


def y_unwindow(parts):
    found = [[None] * 4 for _ in range(4)]
    for s in (0, 2):
        for c in range(4):
            at = FACES * (2 * s + c)
            found[s][c], found[s + 1][c] = swap_halves(parts[0][at : at + FACES], parts[1][at : at + FACES])
    return found


def x_forward(tiles, weights, hid):
    h1, h1_pair, h2, h2_pair, gates = limiter_forward([split3(one) for one in x_windows(tiles)], weights, hid)
    cells = x_cells(tiles)
    return h1_pair, h2_pair, gates, face_flux(*edge_states(cells, gates))


def update_cells(plane_rows, flux_rows):
    upper = turn(flux_rows, -7, 0)[:FACES]
    lower = turn(flux_rows, -6, 0)[:FACES]
    return plane_rows - courant * (upper - lower)


def x_forward_kernel(state, first_x, mid, mid_bias, out, out_bias,
                     middle, h1_hi, h1_lo, h2_hi, h2_lo, gates_out, flux):
    nx, ny = state.shape[1:]
    groups = nx // FACES
    half = groups // PAIR
    hid = mid.shape[0] // 4
    x_weights = (first_x, None, mid, mid_bias, out, out_bias)
    planes = [state.at[c] for c in range(4)]

    def step_of(step, _):
        tiles = pair_tiles(planes, step, half)
        h1_pair, h2_pair, gates, fluxes = x_forward(tiles, x_weights, hid)
        for target, value in zip((h1_hi, h1_lo, h2_hi, h2_lo, gates_out), h1_pair + h2_pair + (gates,)):
            target[step] = value
        for c in range(4):
            for k in range(PAIR):
                flux[c, row_block(step + k * half + 1), :] = fluxes[c][:, k * ny : (k + 1) * ny]
        return 0

    lax.fori_loop(0, half, step_of, 0)
    for c in range(4):
        flux[c, :FACES, :] = flux[c, nx : nx + FACES, :]

    def update(group, _):
        for c in range(4):
            both = stack([flux[c, row_block(group), :], flux[c, row_block(group + 1), :]])
            middle[c, row_block(group), :] = update_cells(planes[c][row_block(group), :], both)
        return 0

    lax.fori_loop(0, groups, update, 0)


def y_order(planes):
    return [planes[0], planes[2], planes[1], planes[3]]


def lane_index(width):
    return lax.broadcasted_iota(jnp.int32, (FACES, width), 1)


def y_step(cells, cots, halo_mask, refs, acc, hid):
    weights, out_back, mid_back, first_y_back = refs
    window = [split3(one) for one in y_windows(cells)]
    h1, h1_pair, h2, h2_pair, gates = limiter_forward(window, weights, hid)
    left, right = edge_states(cells, gates)
    d_flux = [courant * (cots[1][c] - cots[0][c]) for c in range(4)]
    d_left, d_right = face_flux_backward(left, right, d_flux)
    if halo_mask is not None:
        d_left = [jnp.where(halo_mask, d, 0.0) for d in d_left]
        d_right = [jnp.where(halo_mask, d, 0.0) for d in d_right]
    d3_full, direct = edge_backward(cells, gates, d_left, d_right)
    d1 = limiter_backward(d3_full, h1, h2, h1_pair, h2_pair, out_back, mid_back, acc, hid)
    d_window = y_unwindow(first_backward(d1, first_y_back))
    if acc is not None:
        add_first_grads(window, d1, acc[0])
    return [
        [d_window[s][c] + direct[s][c] for c in range(4)]
        for s in range(4)
    ]


def y_gather(parts, ny):
    lane = lane_index(ny)
    out = []
    for c in range(4):
        a = turn(jnp.where(lane >= 1, parts[0][c], 0.0), -1, 1)
        b = turn(jnp.where(lane < ny - 1, parts[2][c], 0.0), 1, 1)
        d = turn(jnp.where(lane < ny - 2, parts[3][c], 0.0), 2, 1)
        out.append(parts[1][c] + a + b + d)
    return out


def fold_rows(values, hid):
    return sum(values[at : at + hid] for at in range(0, values.shape[0], hid))


def back_kernel(state, cot, middle, own, from_first, from_second,
                first_x, first_y, first_bias, mid, mid_bias, out, out_bias,
                out_back, mid_back, first_y_back,
                h1_hi, h1_lo, h2_hi, h2_lo, gates_in,
                base, d1_hi, d1_lo, g_weights,
                rim_state, rim_cot, rim_flux, rim_middle, rim_grad, d_middle,
                acc_x, acc_y, acc_mid, acc_out, acc_out_bias):
    nx, ny = state.shape[1:]
    groups = nx // FACES
    half = groups // PAIR
    hid = mid.shape[0] // 4
    x_weights = (first_x, None, mid, mid_bias, out, out_bias)
    segs = ny // SEG
    rim_rows = nx // segs
    rim_groups = rim_rows // FACES
    rim_half = rim_groups // RIM_PAIR

    for acc in (acc_x, acc_y, acc_mid, acc_out, acc_out_bias):
        acc[...] = jnp.zeros(acc.shape, F32)

    lane = lane_index(ny)
    spot = lane & (SEG - 1)
    is_odd = odd_mask(ny)
    for v in range(8):
        for g in range(rim_groups):
            rows = pl.ds(g * FACES, FACES)
            mine, first, second = own[v, rows, :], from_first[v], from_second[v]
            left, right = jnp.where(is_odd, first, second), jnp.where(is_odd, second, first)
            value = jnp.where(
                spot < RIM,
                turn(left, -g * RIM, 1),
                jnp.where(
                    spot < 2 * RIM,
                    turn(mine, -RIM, 1),
                    jnp.where(spot < 3 * RIM, turn(mine, RIM, 1), turn(right, (3 - g) * RIM, 1)),
                ),
            )
            if v < 4:
                rim_state[v, rows, :] = value
                if g == 0:
                    rim_state[v, pl.ds(rim_rows, FACES), :] = turn(value, -SEG, 1)
            else:
                rim_cot[v - 4, rows, :] = value

    def rim_forward(step, _):
        sets = [
            [
                stack([
                    rim_state[c, row_block(step + k * rim_half), :],
                    rim_state[c, row_block(step + k * rim_half + 1), :],
                ])
                for c in range(4)
            ]
            for k in range(RIM_PAIR)
        ]
        tiles = [side([one[c] for one in sets]) for c in range(4)]
        fluxes = x_forward(tiles, x_weights, hid)[3]
        for c in range(4):
            for k in range(RIM_PAIR):
                rim_flux[c, row_block(step + k * rim_half + 1), :] = fluxes[c][:, k * ny : (k + 1) * ny]
        return 0

    lax.fori_loop(0, rim_half, rim_forward, 0)
    for c in range(4):
        rim_flux[c, :FACES, :] = turn(rim_flux[c, rim_rows : rim_rows + FACES, :], SEG, 1)
        for g in range(rim_groups):
            rows = pl.ds(g * FACES, FACES)
            both = stack([rim_flux[c, rows, :], rim_flux[c, pl.ds((g + 1) * FACES, FACES), :]])
            rim_middle[c, rows, :] = update_cells(rim_state[c, rows, :], both)

    refs = ((first_y, first_bias, mid, mid_bias, out, out_bias), out_back, mid_back, first_y_back)
    spot_wide = lane_index(RIM_PAIR * ny) & (SEG - 1)
    rim_faces = (spot_wide == RIM - 2) | (spot_wide == RIM - 1) | (spot_wide == 3 * RIM)

    def rim_back(step, _):
        cells = [[[] for _ in range(4)] for _ in range(4)]
        cots = [[[] for _ in range(4)] for _ in range(2)]
        for k in range(RIM_PAIR):
            rows = row_block(step + k * rim_half)
            for c in range(4):
                value = rim_middle[c, rows, :]
                for s in range(4):
                    cells[s][c].append(turn(value, 1 - s, 1))
                value = rim_cot[c, rows, :]
                for s in range(2):
                    cots[s][c].append(turn(value, -s, 1))
        cells = [y_order([side(one) for one in row]) for row in cells]
        cots = [y_order([side(one) for one in row]) for row in cots]
        parts = y_step(cells, cots, rim_faces, refs, None, hid)
        for k in range(RIM_PAIR):
            own_parts = [[one[:, k * ny : (k + 1) * ny] for one in row] for row in parts]
            gathered = y_order(y_gather(own_parts, ny))
            for c in range(4):
                rim_grad[c, row_block(step + k * rim_half), :] = gathered[c]
        return 0

    lax.fori_loop(0, rim_half, rim_back, 0)

    def main_y(step, _):
        cells = [[[] for _ in range(4)] for _ in range(4)]
        cots = [[[] for _ in range(4)] for _ in range(2)]
        for k in range(PAIR):
            group = step + k * half
            rows = row_block(group)
            seg = group // rim_groups
            rim_at = row_block(group - seg * rim_groups)
            to_low = ny - (seg * SEG + 3 * RIM)
            to_high = lax.rem(ny - 1 - (seg * SEG + RIM - 1) + ny, ny)
            for c in range(4):
                value = middle[c, rows, :]
                rim_value = rim_middle[c, rim_at, :]
                low = jnp.where(lane < 2, pltpu.roll(rim_value, to_low, 1), value)
                high = jnp.where(lane == ny - 1, pltpu.roll(rim_value, to_high, 1), value)
                cells[0][c].append(turn(high, 1, 1))
                cells[1][c].append(value)
                cells[2][c].append(turn(jnp.where(lane < 1, low, value), -1, 1))
                cells[3][c].append(turn(low, -2, 1))
                value = cot[c, rows, :]
                rim_value = rim_cot[c, rim_at, :]
                low = jnp.where(lane < 1, pltpu.roll(rim_value, to_low, 1), value)
                cots[0][c].append(value)
                cots[1][c].append(turn(low, -1, 1))
        cells = [y_order([side(one) for one in row]) for row in cells]
        cots = [y_order([side(one) for one in row]) for row in cots]
        parts = y_step(cells, cots, None, refs, (acc_y, acc_mid, acc_out, acc_out_bias), hid)
        for k in range(PAIR):
            group = step + k * half
            rows = row_block(group)
            seg = group // rim_groups
            rim_at = row_block(group - seg * rim_groups)
            own_parts = [[one[:, k * ny : (k + 1) * ny] for one in row] for row in parts]
            gathered = y_order(y_gather(own_parts, ny))
            to_low = ny - (seg * SEG + RIM)
            to_high = lax.rem(ny - 1 - (seg * SEG + 3 * RIM - 1) + ny, ny)
            for c in range(4):
                rim_value = rim_grad[c, rim_at, :]
                from_rim = jnp.where(
                    lane < 2,
                    pltpu.roll(rim_value, to_low, 1),
                    jnp.where(lane == ny - 1, pltpu.roll(rim_value, to_high, 1), 0.0),
                )
                d_middle[c, rows, :] = cot[c, rows, :] + gathered[c] + from_rim
        return 0

    lax.fori_loop(0, half, main_y, 0)

    planes = [state.at[c] for c in range(4)]
    d_planes = [d_middle.at[c] for c in range(4)]

    def main_x(step, carry):
        tiles = pair_tiles(planes, step, half)
        d_tiles = pair_tiles(d_planes, step, half)
        gates = gates_in[step]
        h1_pair = (h1_hi[step], h1_lo[step])
        h2_pair = (h2_hi[step], h2_lo[step])
        h1 = h1_pair[0].astype(F32) + h1_pair[1].astype(F32)
        h2 = h2_pair[0].astype(F32) + h2_pair[1].astype(F32)
        cells = x_cells(tiles)
        left, right = edge_states(cells, gates)
        d_flux = [courant * (turn(d, -2, 0)[:FACES] - turn(d, -1, 0)[:FACES]) for d in d_tiles]
        d_left, d_right = face_flux_backward(left, right, d_flux)
        d3_full, direct = edge_backward(cells, gates, d_left, d_right)
        d1 = limiter_backward(
            d3_full, h1, h2, h1_pair, h2_pair, out_back, mid_back, (acc_x, acc_mid, acc_out, acc_out_bias), hid
        )
        d1_hi[step], d1_lo[step] = d1
        add_first_grads([split(one) for one in x_windows(tiles)], d1, acc_x)
        later = []
        for c in range(4):
            nothing = jnp.zeros_like(direct[0][c])
            total = stack([direct[0][c], nothing])
            for s in range(1, 4):
                total = total + turn(stack([direct[s][c], nothing]), s, 0)
            now = total[:FACES] + d_tiles[c][:FACES] + carry[c]
            for k in range(PAIR):
                base[c, row_block(step + k * half), :] = now[:, k * ny : (k + 1) * ny]
            later.append(total[FACES:])
        return tuple(later)

    start = tuple(jnp.zeros((FACES, PAIR * ny), F32) for _ in range(4))
    last = lax.fori_loop(0, half, main_x, start)
    for c in range(4):
        for k in range(PAIR):
            at = (k + 1) % PAIR * half * FACES
            base[c, pl.ds(at, FACES), :] += last[c][:, k * ny : (k + 1) * ny]

    lanes = g_weights.shape[1]
    values = acc_mid[: 8 * hid, :]
    r, c = rows_cols(values.shape)
    same = rest(quot(r, hid), 4) == rest(quot(c, hid), 4)
    values = fold_rows(jnp.where(same, values, 0.0), hid)
    grad_mid = exact_nt(
        pick((hid, 8 * hid), lambda q, n: rest(n, hid) == q, F32),
        stack([values, jnp.zeros((lanes - hid, 8 * hid), F32)]),
    )
    grad_mid_bias = exact(
        acc_mid[8 * hid : 8 * hid + 8, :], pick((8 * hid, lanes), lambda q, n: rest(q, hid) == n, F32)
    )
    r, c = rows_cols(acc_x.shape)
    values, shift = acc_x[...], (r & 7) - rest(quot(c, hid), 4)
    found = [jnp.where((shift == s) & (r < 64), values, 0.0)[:64] for s in range(4)]
    found.append(values[64:])
    r, c = rows_cols(acc_y.shape)
    found.append(jnp.where(((r & 3) == rest(quot(c, hid), 4)) | (r >= 128), acc_y[...], 0.0))
    found = exact(
        stack(found),
        pick((8 * hid, lanes), lambda q, n: (rest(n - q, hid) == 0) & (n >= hid) & (n < 2 * hid), F32),
    )
    y_at = 4 * 64 + ONES

    def source(q, n):
        in_x = (n < 256) & (q == 4 * (n >> 6) + ((n & 31) >> 3))
        m = n - y_at
        in_y = (m >= 0) & (m < 128) & (q == y_column(m & 63))
        return in_x | in_y | ((n == 256) | (m == 128)) & (q == 24)

    beside = exact(pick((32, found.shape[0]), source, F32), found)
    r, c = rows_cols(acc_out.shape)
    found = fold_rows(jnp.where((c & 7) == rest(quot(r, hid), FACES), acc_out[...], 0.0), hid)
    beside = beside + exact_nt(
        pick((32, found.shape[1]), lambda q, n: q == 16 + ((n & 63) >> 3), F32),
        stack([jnp.zeros((hid, found.shape[1]), F32), found, jnp.zeros((lanes - 2 * hid, found.shape[1]), F32)]),
    )
    out_bias_rows = exact_nt(jnp.ones((8, acc_out_bias.shape[1]), F32), acc_out_bias[...])
    grad_out_bias = exact_nt(out_bias_rows, pick((lanes, 64), lambda q, n: (n >> 3) == q - hid, F32))
    r, c = rows_cols((8, lanes))
    g_weights[:hid, :] = grad_mid + beside
    g_weights[25:26, :] += grad_out_bias[:1]
    g_weights[hid:, :] = grad_mid_bias


def state_kernel(base, d1_hi, d1_lo, first_x_back, _, g_den, g_mom, g_tra):
    nx, ny = base.shape[1:]
    half = nx // FACES // PAIR
    grads = [g_den.at[0], g_mom.at[0, 0], g_mom.at[0, 1], g_tra.at[0]]
    upper = rows_cols((FACES, PAIR * ny))[0] < FACES // 2

    def step_of(step, carry):
        first, second = first_backward((d1_hi[step], d1_lo[step]), first_x_back)
        later = []
        for c in range(4):
            rows = slice(FACES * c, FACES * (c + 1))
            moved = turn(second[rows], FACES // 2, 0)
            now = first[rows] + jnp.where(upper, 0.0, moved) + carry[c]
            for k in range(PAIR):
                at = row_block(step + k * half)
                grads[c][at, :] = base[c, at, :] + now[:, k * ny : (k + 1) * ny]
            later.append(jnp.where(upper, moved, 0.0))
        return tuple(later)

    start = tuple(jnp.zeros((FACES, PAIR * ny), F32) for _ in range(4))
    last = lax.fori_loop(0, half, step_of, start)
    for c in range(4):
        for k in range(PAIR):
            at = (k + 1) % PAIR * half * FACES
            grads[c][pl.ds(at, FACES), :] += last[c][:, k * ny : (k + 1) * ny]


def finish_kernel(total, g_w_in, g_b_in, g_w_mid, g_b_mid, g_w_out, g_b_out):
    hid = g_w_mid.shape[0]
    g_w_mid[...] = total[:hid, :hid]
    beside = total[:hid, hid : 2 * hid]
    g_w_in[...] = beside[:16]
    g_w_out[...] = beside[16:24]
    g_b_in[...] = beside[24:25]
    g_b_out[...] = beside[25:26, :8]
    g_b_mid[...] = total[hid : hid + 1, :hid]


def whole(count, space=pltpu.VMEM):
    return [pl.BlockSpec(memory_space=space)] * count


def call(kernel, outs, operands, out_spaces=None, in_spaces=None, scratch=(), flops=0, moved=0):
    return pl.pallas_call(
        kernel,
        out_shape=outs,
        in_specs=in_spaces or whole(len(operands)),
        out_specs=out_spaces or whole(len(outs)),
        scratch_shapes=list(scratch),
        compiler_params=pltpu.CompilerParams(vmem_limit_bytes=VMEM_BYTES),
        cost_estimate=pl.CostEstimate(flops=flops, bytes_accessed=moved, transcendentals=0),
    )(*operands)


def sum_rounds(values, sizes):
    axes, size = tuple(sizes), 1
    for one in sizes.values():
        size *= one
    if size & (size - 1):
        return [values, lax.psum(values, axes)]
    bits = [1 << k for k in range(size.bit_length() - 1)]
    core = size // sizes["traj"]
    others = [bit for bit in reversed(bits) if bit != core]
    found = [values]
    for masks in [[core]] * (core in bits) + [others[k : k + 2] for k in range(0, len(others), 2)]:
        partners = [0]
        for mask in masks:
            partners = partners + [one ^ mask for one in partners]
        parts = [
            lax.ppermute(values, axes, [(i, i ^ one) for i in range(size)]) if one else values for one in partners
        ]
        while len(parts) > 1:
            parts = [parts[k] + parts[k + 1] for k in range(0, len(parts), 2)]
        values = parts[0]
        found.append(values)
    return found


def body(sizes, density, momentum, tracer, cotangent, w_in, b_in, w_mid, b_mid, w_out, b_out):
    nx, ny = density.shape[1:]
    hid = w_in.shape[0]
    wide = FACES * hid
    groups = nx // FACES
    half = groups // PAIR
    lanes = PAIR * ny
    segs = ny // SEG
    rim_rows = nx // segs
    ring = sizes["tx"] * sizes["ty"]
    shape = jax.ShapeDtypeStruct

    operands = [
        density, momentum, tracer, cotangent, w_in.T, b_in[None], w_mid, b_mid[None], w_out, b_out[None]
    ]
    rim, to_first, to_second, state, cots, *matrices = call(
        pack_kernel,
        [
            shape((8, rim_rows, ny), F32),
            shape((8, FACES, ny), F32),
            shape((8, FACES, ny), F32),
            shape((4, nx, ny), F32),
            shape((4, nx, ny), F32),
            shape((wide // 2, 6 * 32 + ONES), BF16),
            shape((wide, 4 * 64), BF16),
            shape((wide // 2, ny), F32),
            shape((4 * hid, 8 * hid), BF16),
            shape((2 * hid, ny), F32),
            shape((192, wide), BF16),
            shape((64, ny), F32),
            shape((wide, 192), BF16),
            shape((2 * hid, 6 * hid), BF16),
            shape((64, wide), BF16),
            shape((128, wide), BF16),
        ],
        [pltpu.with_memory_space_constraint(one, pltpu.HBM) for one in operands],
        in_spaces=whole(10, pltpu.HBM),
        scratch=[pltpu.VMEM(one.shape, F32) for one in operands[4:]] + [pltpu.SemaphoreType.DMA((10,))],
    )
    axes = ("tx", "ty")
    swaps = [[(i, (i + 1 if (i + first) % 2 == 0 else i - 1) % ring) for i in range(ring)] for first in range(2)]
    from_first, from_second = (
        lax.ppermute(one, axes, swap) for one, swap in zip((to_first, to_second), swaps)
    )

    middle, *kept = call(
        x_forward_kernel,
        [shape((4, nx, ny), F32)]
        + [shape((half, wide, lanes), BF16)] * 4
        + [shape((half, 64, lanes), F32)],
        [state, matrices[0]] + matrices[3:7],
        scratch=[pltpu.VMEM((4, nx + FACES, ny), F32)],
        flops=10**10,
        moved=10**7,
    )
    first_x_back = matrices.pop(-2)
    *found, g_weights = call(
        back_kernel,
        [
            shape((4, nx, ny), F32),
            shape((half, wide, lanes), BF16),
            shape((half, wide, lanes), BF16),
            shape((hid + 8, 128), F32),
        ],
        [state, cots, middle, rim, from_first, from_second] + matrices + kept,
        scratch=[
            pltpu.VMEM((4, rim_rows + FACES, ny), F32),
            pltpu.VMEM((4, rim_rows, ny), F32),
            pltpu.VMEM((4, rim_rows + FACES, ny), F32),
            pltpu.VMEM((4, rim_rows, ny), F32),
            pltpu.VMEM((4, rim_rows, ny), F32),
            pltpu.VMEM((4, nx, ny), F32),
            pltpu.VMEM((2 * 32 + ONES, wide), F32),
            pltpu.VMEM((2 * 64 + ONES, wide), F32),
            pltpu.VMEM((8 * hid + ONES, 8 * hid), F32),
            pltpu.VMEM((2 * wide, 128), F32),
            pltpu.VMEM((64, lanes), F32),
        ],
        flops=4 * 10**10,
        moved=2 * 10**7,
    )
    rounds = sum_rounds(g_weights, sizes)
    g_den, g_mom, g_tra = call(
        state_kernel,
        [shape(density.shape, F32), shape(momentum.shape, F32), shape(tracer.shape, F32)],
        found + [first_x_back, rounds[min(1, len(rounds) - 1)]],
        flops=2 * 10**9,
        moved=10**6,
    )
    total = rounds[-1]
    g_w_in, g_b_in, g_w_mid, g_b_mid, g_w_out, g_b_out = call(
        finish_kernel,
        [
            shape((w_in.shape[1], hid), F32),
            shape((1, hid), F32),
            shape(w_mid.shape, F32),
            shape((1, hid), F32),
            shape(w_out.shape, F32),
            shape((1, b_out.shape[0]), F32),
        ],
        [total],
    )
    return (g_den, g_mom, g_tra, g_w_in.T, g_b_in[0], g_w_mid, g_b_mid[0], g_w_out, g_b_out[0])


def solution(mesh):
    flow = P("traj", None, ("tx", "ty"))
    deep = P("traj", None, None, ("tx", "ty"))
    return jax.shard_map(
        functools.partial(body, dict(mesh.shape)),
        mesh=mesh,
        in_specs=(flow, deep, flow, deep) + (P(),) * 6,
        out_specs=(flow, deep, flow) + (P(),) * 6,
        check_vma=False,
    )
```

```python
import functools

import jax
import jax.numpy as jnp
from jax import lax
from jax.experimental import pallas as pl
from jax.experimental.pallas import tpu as pltpu
from jax.sharding import PartitionSpec as P

courant = 0.1
slope_gain = 0.25
F32 = jnp.float32
BF16 = jnp.bfloat16
FACES = 8
SEG = 16
RIM = 4
PAIR = 8
RIM_PAIR = 4
ONES = 16
VMEM_BYTES = 32 * 2**20


def dot(a, b):
    return lax.dot_general(a, b, (((1,), (0,)), ((), ())), preferred_element_type=F32)


def dot_nt(a, b):
    return lax.dot_general(a, b, (((1,), (1,)), ((), ())), preferred_element_type=F32)


def exact(a, b):
    return lax.dot_general(
        a, b, (((1,), (0,)), ((), ())), precision=lax.Precision.HIGHEST, preferred_element_type=F32
    )


def exact_nt(a, b):
    return lax.dot_general(
        a, b, (((1,), (1,)), ((), ())), precision=lax.Precision.HIGHEST, preferred_element_type=F32
    )


def split(values):
    high = values.astype(BF16)
    return high, (values - high.astype(F32)).astype(BF16)


def split3(values):
    high = values.astype(BF16)
    rest = values - high.astype(F32)
    middle = rest.astype(BF16)
    return high, middle, (rest - middle.astype(F32)).astype(BF16)


def rows_cols(shape):
    return lax.broadcasted_iota(jnp.int32, shape, 0), lax.broadcasted_iota(jnp.int32, shape, 1)


def quot(values, n):
    return values >> (n.bit_length() - 1) if n & (n - 1) == 0 else values // n


def rest(values, n):
    return values & (n - 1) if n & (n - 1) == 0 else values % n


def pick(shape, test, dtype=BF16):
    r, c = rows_cols(shape)
    return jnp.where(test(r, c), 1.0, 0.0).astype(dtype)


def stack(parts):
    return jnp.concatenate(parts, 0)


def side(parts):
    return jnp.concatenate(parts, 1)


STACKED = (0, 0, 0, 1, 1, 2)


def stacked(parts):
    return [parts[0], parts[1], parts[2], parts[0], parts[1], parts[0]]


def level_of(block):
    return jnp.where(block < 3, 0, jnp.where(block < 5, 1, 2))


def choose(values, levels):
    parts = [part.astype(F32) for part in split3(values)]
    total = jnp.zeros(values.shape, F32)
    for k, part in enumerate(parts):
        total = jnp.where(levels == k, part, total)
    return total


def y_column(m):
    return 4 * (2 * (m >> 5) + ((m & 7) >> 2)) + ((m & 31) >> 3)


def build_first(w, b, hid):
    x_cols, y_cols, step = 6 * 32 + ONES, 4 * 64, 256

    def source(q, n):
        s = n >> 8
        m = n & (step - 1)
        in_x = (s < 4) & (m < 192) & (q == 4 * s + ((m & 31) >> 3))
        in_y = (s == 4) & (q == y_column(m & 63))
        return in_x | in_y

    values = exact(w, pick((16, 4 * step + y_cols), source, F32))
    _, n = rows_cols(values.shape)
    for_x = choose(values, level_of((n & (step - 1)) >> 5))
    for_y = values[:, 4 * step :]
    block = n[:, :y_cols] >> 6
    upper = choose(for_y, jnp.where(block < 3, 0, 2))
    lower = choose(for_y, jnp.where(block < 2, 1, -1))

    at, _ = rows_cols((x_cols, hid))
    rows = jnp.zeros((x_cols, hid), F32)
    for k, level in enumerate(split3(b)):
        rows = jnp.where(at == 192 + k, jnp.broadcast_to(level.astype(F32), (x_cols, hid)), rows)
    bias = dot_nt(pick((hid, hid), lambda q, n: q == n), rows.astype(BF16))

    half = FACES // 2
    r, c = rows_cols((half * hid, x_cols))
    shift = jnp.where(c < 192, (c & 7) - quot(r, hid), -1)
    first_x = stack([bias] * half)
    for s in range(4):
        part = for_x[:, s * step : s * step + x_cols]
        first_x = jnp.where(shift == s, stack([part] * half), first_x)
    r, c = rows_cols((2 * half * hid, y_cols))
    keep = (c & 3) == rest(quot(r, hid), half)
    first_y = jnp.where(keep, stack([upper] * half + [lower] * half), 0.0)
    return first_x.astype(BF16), first_y.astype(BF16)


def build_first_back(w_t, hid):
    wide = FACES // 2 * hid

    def source(q, n):
        in_x = (q < 128) & (n == 4 * (q >> 5) + ((q & 31) >> 3))
        in_y = (q >= 128) & (n == y_column(q - 128))
        return in_x | in_y

    rows = exact(pick((128 + 64, 16), source, F32), w_t)
    right = pick((hid, 2 * wide), lambda q, n: rest(n, hid) == q)
    high, low = (dot(part, right) for part in split(rows))
    r, c = rows_cols(high.shape)
    low = jnp.where(c < wide, low, 0.0)
    face = quot(rest(c, wide), hid)
    shift = (r & 7) - face
    upper = lower = jnp.zeros((32, 2 * wide), F32)
    for s in range(4):
        keep = shift[:32] == s
        upper = jnp.where(keep, high[32 * s : 32 * (s + 1)], upper)
        lower = jnp.where(keep, low[32 * s : 32 * (s + 1)], lower)
    keep = ((r & 3) == face)[128:]
    back_y = stack([jnp.where(keep, high[128:], 0.0), jnp.where(keep, low[128:], 0.0)])
    return stack([upper, lower]).astype(BF16), back_y.astype(BF16)


def build_mid(w, hid):
    block = 2 * hid
    tiled = exact(w, pick((hid, 4 * block), lambda q, n: rest(n, hid) == q, F32))
    _, n = rows_cols(tiled.shape)
    upper = choose(tiled, jnp.where(n < 3 * block, 0, 2))
    lower = choose(tiled, jnp.where(n < 2 * block, 1, -1))
    r, c = rows_cols((2 * block, 4 * block))
    keep = quot(rest(r, block), hid) == quot(rest(c, block), hid)
    return jnp.where(keep, stack([upper, upper, lower, lower]), 0.0).astype(BF16)


def build_mid_back(w, hid):
    block = 2 * hid
    turned = exact_nt(pick((hid, hid), lambda q, n: q == n, F32), w)
    tiled = exact(turned, pick((hid, 3 * block), lambda q, n: rest(n, hid) == q, F32))
    _, n = rows_cols(tiled.shape)
    tiled = choose(tiled, jnp.where(quot(n, block) == 1, 1, 0))
    r, c = rows_cols((block, 3 * block))
    keep = quot(r, hid) == quot(rest(c, block), hid)
    return jnp.where(keep, stack([tiled] * 2), 0.0).astype(BF16)


def build_out(w, hid):
    wide = FACES * hid
    rows = exact(pick((64, 8), lambda q, n: (q >> 3) == n, F32), w)
    tiled = dot(stack(list(split3(rows))), pick((hid, wide), lambda q, n: rest(n, hid) == q))
    r, c = rows_cols(tiled.shape)
    return jnp.where((r & 7) == quot(c, hid), tiled, 0.0).astype(BF16)


def build_out_back(w, hid):
    wide = FACES * hid
    turned = exact_nt(pick((hid, hid), lambda q, n: q == n, F32), w)
    tiled = exact(turned, pick((8, 192), lambda q, n: ((n & 63) >> 3) == q, F32))
    _, n = rows_cols(tiled.shape)
    tiled = choose(tiled, jnp.where((n >> 6) == 1, 1, 0))
    r, c = rows_cols((wide, 192))
    return jnp.where(quot(r, hid) == (c & 7), stack([tiled] * FACES), 0.0).astype(BF16)


def spread_bias(b, lanes, copies):
    n = b.shape[1]
    rows = exact_nt(pick((n, n), lambda q, m: q == m, F32), jnp.broadcast_to(b, (lanes, n)))
    return stack([rows] * copies)


def spread(bias_ref, width):
    return side([bias_ref[...]] * (width // bias_ref.shape[1]))


def limiter_forward(first, weights, hid):
    first_ref, first_bias_ref, mid_ref, mid_bias_ref, out_ref, out_bias_ref = weights
    width = first[0][0].shape[1]
    ones = [jnp.ones((ONES, width), BF16)]
    firsts = []
    for one in first:
        if first_bias_ref is None:
            firsts.append(dot(first_ref[...], stack(stacked(one) + ones)))
        else:
            high, middle, low = one
            both = dot(first_ref[...], stack([high, middle, low, high]))
            half = both.shape[0] // 2
            firsts.append(both[:half] + both[half:] + spread(first_bias_ref, width))
    block = 2 * hid
    h1, h1_parts, h2, h2_parts = [], [], [], []
    for values in firsts:
        for at in range(0, values.shape[0], block):
            h1.append(jnp.tanh(values[at : at + block]))
            high, middle, low = split3(h1[-1])
            h1_parts.append((high, middle))
            both = dot(mid_ref[...], stack([high, middle, low, high]))
            h2.append(jnp.tanh(both[:block] + both[block:] + spread(mid_bias_ref, width)))
            h2_parts.append(split3(h2[-1]))
    h1, h2 = stack(h1), stack(h2)
    h1_parts = tuple(stack([one[k] for one in h1_parts]) for k in range(2))
    h2_parts = tuple(stack([one[k] for one in h2_parts]) for k in range(3))
    rows = 8 * FACES
    a = dot(out_ref[...], h2_parts[0])
    b = dot(out_ref[: 2 * rows, :], h2_parts[1])
    c = dot(out_ref[:rows, :], h2_parts[2])
    gates = jnp.tanh(
        ((a[2 * rows :] + b[rows:] + c) + (a[rows : 2 * rows] + b[:rows])) + a[:rows] + spread(out_bias_ref, width)
    )
    return h1, h1_parts, h2, h2_parts[:2], gates


def limiter_backward(d3, h1, h2, h1_pair, h2_pair, out_back_ref, mid_back_ref, acc, hid):
    d3_hi, d3_lo = split(d3)
    dh2 = dot(out_back_ref[...], stack([d3_hi, d3_hi, d3_lo]))
    if acc is not None:
        acc[2][...] += dot_nt(stack(list(h2_pair)), stack([d3_hi, d3_lo]))
        acc[3][...] += d3
    block = 2 * hid
    d2, d1 = [], []
    for at in range(0, FACES * hid, block):
        one1, one2 = h1[at : at + block], h2[at : at + block]
        high, low = split(dh2[at : at + block] * (1.0 - one2 * one2))
        d2.append((high, low))
        d1.append(split(dot(mid_back_ref[...], stack([high, high, low])) * (1.0 - one1 * one1)))
    d2_hi, d2_lo = (stack([one[k] for one in d2]) for k in range(2))
    if acc is not None:
        ones = jnp.ones((ONES, d3.shape[1]), BF16)
        lefts, rights = [], []
        for at in range(0, FACES * hid, 2 * block):
            lefts.append(stack([part[at : at + 2 * block] for part in h1_pair] + [ones]))
            rights.append(stack([part[at : at + 2 * block] for part in (d2_hi, d2_lo)]))
        acc[1][...] += dot_nt(side(lefts), side(rights))
    return tuple(stack([one[k] for one in d1]) for k in range(2))


def first_backward(d1, back_ref):
    wide = d1[0].shape[0] // 2
    found = []
    for at in (0, wide):
        both = dot(back_ref[...], stack([part[at : at + wide] for part in d1]))
        half = both.shape[0] // 2
        found.append(both[:half] + both[half:])
    return found


def add_first_grads(first, d1, acc_in):
    ones = jnp.ones((ONES, d1[0].shape[1]), BF16)
    wide = d1[0].shape[0] // 2
    lefts = [stack([one[0], one[1], ones]) for one in first]
    rights = [stack([part[at : at + wide] for part in d1]) for at in (0, wide)]
    acc_in[...] += dot_nt(side(lefts), side(rights))


def edge_states(cells, gates):
    left, right = [], []
    for c in range(4):
        low = gates[FACES * c : FACES * (c + 1)]
        high = gates[FACES * (c + 4) : FACES * (c + 5)]
        left.append(cells[1][c] + slope_gain * low * (cells[2][c] - cells[0][c]))
        right.append(cells[2][c] - slope_gain * high * (cells[3][c] - cells[1][c]))
    return left, right


def face_flux(left, right):
    ul = left[1] / left[0]
    ur = right[1] / right[0]
    half_speed = 0.5 * (jnp.maximum(jnp.abs(ul), jnp.abs(ur)) + 1.0)
    fl = [left[1], left[1] * ul + left[0], left[2] * ul, left[3] * ul]
    fr = [right[1], right[1] * ur + right[0], right[2] * ur, right[3] * ur]
    return [0.5 * (fl[c] + fr[c]) - half_speed * (right[c] - left[c]) for c in range(4)]


def sign_of(values):
    return jnp.where(values > 0.0, 1.0, jnp.where(values < 0.0, -1.0, 0.0))


def face_flux_backward(left, right, d_flux):
    inv_l, inv_r = 1.0 / left[0], 1.0 / right[0]
    ul, ur = left[1] / left[0], right[1] / right[0]
    al, ar = jnp.abs(ul), jnp.abs(ur)
    half_speed = 0.5 * (jnp.maximum(al, ar) + 1.0)
    d_speed = -0.5 * sum(d_flux[c] * (right[c] - left[c]) for c in range(4))
    share = jnp.where(al > ar, 1.0, jnp.where(al < ar, 0.0, 0.5))
    half = [0.5 * d for d in d_flux]
    spread = [half_speed * d for d in d_flux]

    def one(state, u, inv, speed_part, sign):
        du = half[1] * state[1] + half[2] * state[2] + half[3] * state[3] + speed_part * sign_of(u)
        over = du * inv
        return [
            half[1] - over * u + sign * spread[0],
            half[0] + half[1] * u + over + sign * spread[1],
            half[2] * u + sign * spread[2],
            half[3] * u + sign * spread[3],
        ]

    return (
        one(left, ul, inv_l, d_speed * share, 1.0),
        one(right, ur, inv_r, d_speed * (1.0 - share), -1.0),
    )


def edge_backward(cells, gates, d_left, d_right):
    lows, highs = [], []
    direct = [[None] * 4 for _ in range(4)]
    for c in range(4):
        low = gates[FACES * c : FACES * (c + 1)]
        high = gates[FACES * (c + 4) : FACES * (c + 5)]
        lows.append(slope_gain * (cells[2][c] - cells[0][c]) * d_left[c])
        highs.append(-slope_gain * (cells[3][c] - cells[1][c]) * d_right[c])
        low_part = slope_gain * low * d_left[c]
        high_part = slope_gain * high * d_right[c]
        direct[0][c] = -low_part
        direct[1][c] = d_left[c] + high_part
        direct[2][c] = d_right[c] + low_part
        direct[3][c] = -high_part
    return stack(lows + highs) * (1.0 - gates * gates), direct


def turn(values, shift, axis):
    size = values.shape[axis]
    return values if shift % size == 0 else pltpu.roll(values, shift % size, axis)


def x_cells(tiles):
    return [[turn(t, -s, 0)[:FACES] for t in tiles] for s in range(4)]


def pack_kernel(den, mom, tra, cot, w_in, b_in, w_mid, b_mid, w_out, b_out,
                rim, to_first, to_second, state, cots, first_x, first_y, first_bias, mid, mid_bias, out, out_bias,
                out_back, mid_back, first_x_back, first_y_back, *scratch):
    *small, sems = scratch
    nx, ny = den.shape[1:]
    segs = ny // SEG
    rows = nx // segs
    hid = w_in.shape[1]
    copies = [
        pltpu.make_async_copy(source, target, sems.at[k])
        for k, (source, target) in enumerate(
            list(zip([w_in, b_in, w_mid, b_mid, w_out, b_out], small))
            + [
                (den.at[0], state.at[0]),
                (mom.at[0], state.at[pl.ds(1, 2)]),
                (tra.at[0], state.at[3]),
                (cot.at[0], cots),
            ]
        )
    ]
    for one in copies:
        one.start()
    for one in copies[:6]:
        one.wait()
    w_in, b_in, w_mid, b_mid, w_out, b_out = small
    lanes = out_bias.shape[1]
    w_in_rows = exact_nt(pick((hid, hid), lambda q, n: q == n, F32), w_in[...])
    first_x[...], first_y[...] = build_first(w_in_rows, b_in[...], hid)
    first_bias[...] = spread_bias(b_in[...], lanes, FACES // 2)
    mid[...] = build_mid(w_mid[...], hid)
    mid_bias[...] = spread_bias(b_mid[...], lanes, 2)
    out[...] = build_out(w_out[...], hid)
    out_bias[...] = exact_nt(
        pick((64, 8), lambda q, n: (q >> 3) == n, F32), jnp.broadcast_to(b_out[...], (lanes, 8))
    )
    out_back[...] = build_out_back(w_out[...], hid)
    mid_back[...] = build_mid_back(w_mid[...], hid)
    first_x_back[...], first_y_back[...] = build_first_back(w_in[...], hid)

    for one in copies[6:]:
        one.wait()
    lane = lane_index(ny)
    for v in range(8):
        plane = state.at[v] if v < 4 else cots.at[v - 4]
        for at in range(0, rows, FACES):
            total = jnp.zeros((FACES, ny), F32)
            for s in range(segs):
                first = s * SEG + RIM
                moved = turn(plane[pl.ds(s * rows + at, FACES), :], first + RIM, 1)
                total = jnp.where((lane >= first) & (lane < first + 2 * RIM), moved, total)
            rim[v, pl.ds(at, FACES), :] = total
    is_odd = odd_mask(ny)
    spot = lane & (SEG - 1)
    for v in range(8):
        sides = []
        for first in (2 * RIM, RIM):
            total = jnp.zeros((FACES, ny), F32)
            for g in range(rows // FACES):
                moved = turn(rim[v, pl.ds(g * FACES, FACES), :], g * RIM - first, 1)
                total = jnp.where((spot >= g * RIM) & (spot < (g + 1) * RIM), moved, total)
            sides.append(total)
        to_first[v] = jnp.where(is_odd, sides[0], sides[1])
        to_second[v] = jnp.where(is_odd, sides[1], sides[0])


def odd_mask(ny):
    return jnp.full((FACES, ny), lax.rem(lax.axis_index(("tx", "ty")), 2), jnp.int32) == 1


def row_block(at):
    return pl.ds(pl.multiple_of(at * FACES, FACES), FACES)


def x_tiles(planes, group, groups):
    after = jnp.where(group + 1 == groups, 0, group + 1)
    return [stack([plane[row_block(group), :], plane[row_block(after), :]]) for plane in planes]


def pair_tiles(planes, step, half):
    sets = [x_tiles(planes, step + k * half, PAIR * half) for k in range(PAIR)]
    return [side([one[c] for one in sets]) for c in range(len(planes))]


def x_windows(tiles):
    half = FACES // 2
    return [stack([turn(tile, -at, 0)[:FACES] for tile in tiles]) for at in (0, half)]


def swap_halves(first, second):
    half = FACES // 2
    upper = rows_cols(first.shape)[0] < half
    return jnp.where(upper, first, turn(second, half, 0)), jnp.where(upper, turn(first, half, 0), second)


def y_windows(cells):
    pairs = [swap_halves(cells[s][c], cells[s + 1][c]) for s in (0, 2) for c in range(4)]
    return [stack([one[k] for one in pairs]) for k in range(2)]


def y_unwindow(parts):
    found = [[None] * 4 for _ in range(4)]
    for s in (0, 2):
        for c in range(4):
            at = FACES * (2 * s + c)
            found[s][c], found[s + 1][c] = swap_halves(parts[0][at : at + FACES], parts[1][at : at + FACES])
    return found


def x_forward(tiles, weights, hid):
    h1, h1_pair, h2, h2_pair, gates = limiter_forward([split3(one) for one in x_windows(tiles)], weights, hid)
    cells = x_cells(tiles)
    return h1_pair, h2_pair, gates, face_flux(*edge_states(cells, gates))


def update_cells(plane_rows, flux_rows):
    upper = turn(flux_rows, -7, 0)[:FACES]
    lower = turn(flux_rows, -6, 0)[:FACES]
    return plane_rows - courant * (upper - lower)


def x_forward_kernel(state, first_x, mid, mid_bias, out, out_bias,
                     middle, h1_hi, h1_lo, h2_hi, h2_lo, gates_out, flux):
    nx, ny = state.shape[1:]
    groups = nx // FACES
    half = groups // PAIR
    hid = mid.shape[0] // 4
    x_weights = (first_x, None, mid, mid_bias, out, out_bias)
    planes = [state.at[c] for c in range(4)]

    def step_of(step, _):
        tiles = pair_tiles(planes, step, half)
        h1_pair, h2_pair, gates, fluxes = x_forward(tiles, x_weights, hid)
        for target, value in zip((h1_hi, h1_lo, h2_hi, h2_lo, gates_out), h1_pair + h2_pair + (gates,)):
            target[step] = value
        for c in range(4):
            for k in range(PAIR):
                flux[c, row_block(step + k * half + 1), :] = fluxes[c][:, k * ny : (k + 1) * ny]
        return 0

    lax.fori_loop(0, half, step_of, 0, unroll=2)
    for c in range(4):
        flux[c, :FACES, :] = flux[c, nx : nx + FACES, :]

    def update(group, _):
        for c in range(4):
            both = stack([flux[c, row_block(group), :], flux[c, row_block(group + 1), :]])
            middle[c, row_block(group), :] = update_cells(planes[c][row_block(group), :], both)
        return 0

    lax.fori_loop(0, groups, update, 0, unroll=4)


def y_order(planes):
    return [planes[0], planes[2], planes[1], planes[3]]


def lane_index(width):
    return lax.broadcasted_iota(jnp.int32, (FACES, width), 1)


def y_step(cells, cots, halo_mask, refs, acc, hid):
    weights, out_back, mid_back, first_y_back = refs
    window = [split3(one) for one in y_windows(cells)]
    h1, h1_pair, h2, h2_pair, gates = limiter_forward(window, weights, hid)
    left, right = edge_states(cells, gates)
    d_flux = [courant * (cots[1][c] - cots[0][c]) for c in range(4)]
    d_left, d_right = face_flux_backward(left, right, d_flux)
    if halo_mask is not None:
        d_left = [jnp.where(halo_mask, d, 0.0) for d in d_left]
        d_right = [jnp.where(halo_mask, d, 0.0) for d in d_right]
    d3_full, direct = edge_backward(cells, gates, d_left, d_right)
    d1 = limiter_backward(d3_full, h1, h2, h1_pair, h2_pair, out_back, mid_back, acc, hid)
    d_window = y_unwindow(first_backward(d1, first_y_back))
    if acc is not None:
        add_first_grads(window, d1, acc[0])
    return [
        [d_window[s][c] + direct[s][c] for c in range(4)]
        for s in range(4)
    ]


def y_gather(parts, ny):
    lane = lane_index(ny)
    out = []
    for c in range(4):
        a = turn(jnp.where(lane >= 1, parts[0][c], 0.0), -1, 1)
        b = turn(jnp.where(lane < ny - 1, parts[2][c], 0.0), 1, 1)
        d = turn(jnp.where(lane < ny - 2, parts[3][c], 0.0), 2, 1)
        out.append(parts[1][c] + a + b + d)
    return out


def fold_rows(values, hid):
    return sum(values[at : at + hid] for at in range(0, values.shape[0], hid))


def back_kernel(state, cot, middle, own, from_first, from_second,
                first_x, first_y, first_bias, mid, mid_bias, out, out_bias,
                out_back, mid_back, first_y_back,
                h1_hi, h1_lo, h2_hi, h2_lo, gates_in,
                base, d1_hi, d1_lo, g_weights,
                rim_state, rim_cot, rim_flux, rim_middle, rim_grad, d_middle,
                acc_x, acc_y, acc_mid, acc_out, acc_out_bias):
    nx, ny = state.shape[1:]
    groups = nx // FACES
    half = groups // PAIR
    hid = mid.shape[0] // 4
    x_weights = (first_x, None, mid, mid_bias, out, out_bias)
    segs = ny // SEG
    rim_rows = nx // segs
    rim_groups = rim_rows // FACES
    rim_half = rim_groups // RIM_PAIR

    for acc in (acc_x, acc_y, acc_mid, acc_out, acc_out_bias):
        acc[...] = jnp.zeros(acc.shape, F32)

    lane = lane_index(ny)
    spot = lane & (SEG - 1)
    is_odd = odd_mask(ny)
    for v in range(8):
        for g in range(rim_groups):
            rows = pl.ds(g * FACES, FACES)
            mine, first, second = own[v, rows, :], from_first[v], from_second[v]
            left, right = jnp.where(is_odd, first, second), jnp.where(is_odd, second, first)
            value = jnp.where(
                spot < RIM,
                turn(left, -g * RIM, 1),
                jnp.where(
                    spot < 2 * RIM,
                    turn(mine, -RIM, 1),
                    jnp.where(spot < 3 * RIM, turn(mine, RIM, 1), turn(right, (3 - g) * RIM, 1)),
                ),
            )
            if v < 4:
                rim_state[v, rows, :] = value
                if g == 0:
                    rim_state[v, pl.ds(rim_rows, FACES), :] = turn(value, -SEG, 1)
            else:
                rim_cot[v - 4, rows, :] = value

    def rim_forward(step, _):
        sets = [
            [
                stack([
                    rim_state[c, row_block(step + k * rim_half), :],
                    rim_state[c, row_block(step + k * rim_half + 1), :],
                ])
                for c in range(4)
            ]
            for k in range(RIM_PAIR)
        ]
        tiles = [side([one[c] for one in sets]) for c in range(4)]
        fluxes = x_forward(tiles, x_weights, hid)[3]
        for c in range(4):
            for k in range(RIM_PAIR):
                rim_flux[c, row_block(step + k * rim_half + 1), :] = fluxes[c][:, k * ny : (k + 1) * ny]
        return 0

    lax.fori_loop(0, rim_half, rim_forward, 0)
    for c in range(4):
        rim_flux[c, :FACES, :] = turn(rim_flux[c, rim_rows : rim_rows + FACES, :], SEG, 1)
        for g in range(rim_groups):
            rows = pl.ds(g * FACES, FACES)
            both = stack([rim_flux[c, rows, :], rim_flux[c, pl.ds((g + 1) * FACES, FACES), :]])
            rim_middle[c, rows, :] = update_cells(rim_state[c, rows, :], both)

    refs = ((first_y, first_bias, mid, mid_bias, out, out_bias), out_back, mid_back, first_y_back)
    spot_wide = lane_index(RIM_PAIR * ny) & (SEG - 1)
    rim_faces = (spot_wide == RIM - 2) | (spot_wide == RIM - 1) | (spot_wide == 3 * RIM)

    def rim_back(step, _):
        cells = [[[] for _ in range(4)] for _ in range(4)]
        cots = [[[] for _ in range(4)] for _ in range(2)]
        for k in range(RIM_PAIR):
            rows = row_block(step + k * rim_half)
            for c in range(4):
                value = rim_middle[c, rows, :]
                for s in range(4):
                    cells[s][c].append(turn(value, 1 - s, 1))
                value = rim_cot[c, rows, :]
                for s in range(2):
                    cots[s][c].append(turn(value, -s, 1))
        cells = [y_order([side(one) for one in row]) for row in cells]
        cots = [y_order([side(one) for one in row]) for row in cots]
        parts = y_step(cells, cots, rim_faces, refs, None, hid)
        for k in range(RIM_PAIR):
            own_parts = [[one[:, k * ny : (k + 1) * ny] for one in row] for row in parts]
            gathered = y_order(y_gather(own_parts, ny))
            for c in range(4):
                rim_grad[c, row_block(step + k * rim_half), :] = gathered[c]
        return 0

    lax.fori_loop(0, rim_half, rim_back, 0)

    def main_y(step, _):
        cells = [[[] for _ in range(4)] for _ in range(4)]
        cots = [[[] for _ in range(4)] for _ in range(2)]
        for k in range(PAIR):
            group = step + k * half
            rows = row_block(group)
            seg = group // rim_groups
            rim_at = row_block(group - seg * rim_groups)
            to_low = ny - (seg * SEG + 3 * RIM)
            to_high = lax.rem(ny - 1 - (seg * SEG + RIM - 1) + ny, ny)
            for c in range(4):
                value = middle[c, rows, :]
                rim_value = rim_middle[c, rim_at, :]
                low = jnp.where(lane < 2, pltpu.roll(rim_value, to_low, 1), value)
                high = jnp.where(lane == ny - 1, pltpu.roll(rim_value, to_high, 1), value)
                cells[0][c].append(turn(high, 1, 1))
                cells[1][c].append(value)
                cells[2][c].append(turn(jnp.where(lane < 1, low, value), -1, 1))
                cells[3][c].append(turn(low, -2, 1))
                value = cot[c, rows, :]
                rim_value = rim_cot[c, rim_at, :]
                low = jnp.where(lane < 1, pltpu.roll(rim_value, to_low, 1), value)
                cots[0][c].append(value)
                cots[1][c].append(turn(low, -1, 1))
        cells = [y_order([side(one) for one in row]) for row in cells]
        cots = [y_order([side(one) for one in row]) for row in cots]
        parts = y_step(cells, cots, None, refs, (acc_y, acc_mid, acc_out, acc_out_bias), hid)
        for k in range(PAIR):
            group = step + k * half
            rows = row_block(group)
            seg = group // rim_groups
            rim_at = row_block(group - seg * rim_groups)
            own_parts = [[one[:, k * ny : (k + 1) * ny] for one in row] for row in parts]
            gathered = y_order(y_gather(own_parts, ny))
            to_low = ny - (seg * SEG + RIM)
            to_high = lax.rem(ny - 1 - (seg * SEG + 3 * RIM - 1) + ny, ny)
            for c in range(4):
                rim_value = rim_grad[c, rim_at, :]
                from_rim = jnp.where(
                    lane < 2,
                    pltpu.roll(rim_value, to_low, 1),
                    jnp.where(lane == ny - 1, pltpu.roll(rim_value, to_high, 1), 0.0),
                )
                d_middle[c, rows, :] = cot[c, rows, :] + gathered[c] + from_rim
        return 0

    lax.fori_loop(0, half, main_y, 0, unroll=2)

    planes = [state.at[c] for c in range(4)]
    d_planes = [d_middle.at[c] for c in range(4)]

    def main_x(step, carry):
        tiles = pair_tiles(planes, step, half)
        d_tiles = pair_tiles(d_planes, step, half)
        gates = gates_in[step]
        h1_pair = (h1_hi[step], h1_lo[step])
        h2_pair = (h2_hi[step], h2_lo[step])
        h1 = h1_pair[0].astype(F32) + h1_pair[1].astype(F32)
        h2 = h2_pair[0].astype(F32) + h2_pair[1].astype(F32)
        cells = x_cells(tiles)
        left, right = edge_states(cells, gates)
        d_flux = [courant * (turn(d, -2, 0)[:FACES] - turn(d, -1, 0)[:FACES]) for d in d_tiles]
        d_left, d_right = face_flux_backward(left, right, d_flux)
        d3_full, direct = edge_backward(cells, gates, d_left, d_right)
        d1 = limiter_backward(
            d3_full, h1, h2, h1_pair, h2_pair, out_back, mid_back, (acc_x, acc_mid, acc_out, acc_out_bias), hid
        )
        d1_hi[step], d1_lo[step] = d1
        add_first_grads([split(one) for one in x_windows(tiles)], d1, acc_x)
        later = []
        for c in range(4):
            nothing = jnp.zeros_like(direct[0][c])
            total = stack([direct[0][c], nothing])
            for s in range(1, 4):
                total = total + turn(stack([direct[s][c], nothing]), s, 0)
            now = total[:FACES] + d_tiles[c][:FACES] + carry[c]
            for k in range(PAIR):
                base[c, row_block(step + k * half), :] = now[:, k * ny : (k + 1) * ny]
            later.append(total[FACES:])
        return tuple(later)

    start = tuple(jnp.zeros((FACES, PAIR * ny), F32) for _ in range(4))
    last = lax.fori_loop(0, half, main_x, start, unroll=2)
    for c in range(4):
        for k in range(PAIR):
            at = (k + 1) % PAIR * half * FACES
            base[c, pl.ds(at, FACES), :] += last[c][:, k * ny : (k + 1) * ny]

    lanes = g_weights.shape[1]
    values = acc_mid[: 8 * hid, :]
    r, c = rows_cols(values.shape)
    same = rest(quot(r, hid), 4) == rest(quot(c, hid), 4)
    values = fold_rows(jnp.where(same, values, 0.0), hid)
    grad_mid = exact_nt(
        pick((hid, 8 * hid), lambda q, n: rest(n, hid) == q, F32),
        stack([values, jnp.zeros((lanes - hid, 8 * hid), F32)]),
    )
    grad_mid_bias = exact(
        acc_mid[8 * hid : 8 * hid + 8, :], pick((8 * hid, lanes), lambda q, n: rest(q, hid) == n, F32)
    )
    r, c = rows_cols(acc_x.shape)
    values, shift = acc_x[...], (r & 7) - rest(quot(c, hid), 4)
    found = [jnp.where((shift == s) & (r < 64), values, 0.0)[:64] for s in range(4)]
    found.append(values[64:])
    r, c = rows_cols(acc_y.shape)
    found.append(jnp.where(((r & 3) == rest(quot(c, hid), 4)) | (r >= 128), acc_y[...], 0.0))
    found = exact(
        stack(found),
        pick((8 * hid, lanes), lambda q, n: (rest(n - q, hid) == 0) & (n >= hid) & (n < 2 * hid), F32),
    )
    y_at = 4 * 64 + ONES

    def source(q, n):
        in_x = (n < 256) & (q == 4 * (n >> 6) + ((n & 31) >> 3))
        m = n - y_at
        in_y = (m >= 0) & (m < 128) & (q == y_column(m & 63))
        return in_x | in_y | ((n == 256) | (m == 128)) & (q == 24)

    beside = exact(pick((32, found.shape[0]), source, F32), found)
    r, c = rows_cols(acc_out.shape)
    found = fold_rows(jnp.where((c & 7) == rest(quot(r, hid), FACES), acc_out[...], 0.0), hid)
    beside = beside + exact_nt(
        pick((32, found.shape[1]), lambda q, n: q == 16 + ((n & 63) >> 3), F32),
        stack([jnp.zeros((hid, found.shape[1]), F32), found, jnp.zeros((lanes - 2 * hid, found.shape[1]), F32)]),
    )
    out_bias_rows = exact_nt(jnp.ones((8, acc_out_bias.shape[1]), F32), acc_out_bias[...])
    grad_out_bias = exact_nt(out_bias_rows, pick((lanes, 64), lambda q, n: (n >> 3) == q - hid, F32))
    r, c = rows_cols((8, lanes))
    g_weights[:hid, :] = grad_mid + beside
    g_weights[25:26, :] += grad_out_bias[:1]
    g_weights[hid:, :] = grad_mid_bias


def state_kernel(base, d1_hi, d1_lo, first_x_back, _, g_den, g_mom, g_tra):
    nx, ny = base.shape[1:]
    half = nx // FACES // PAIR
    grads = [g_den.at[0], g_mom.at[0, 0], g_mom.at[0, 1], g_tra.at[0]]
    upper = rows_cols((FACES, PAIR * ny))[0] < FACES // 2

    def step_of(step, carry):
        first, second = first_backward((d1_hi[step], d1_lo[step]), first_x_back)
        later = []
        for c in range(4):
            rows = slice(FACES * c, FACES * (c + 1))
            moved = turn(second[rows], FACES // 2, 0)
            now = first[rows] + jnp.where(upper, 0.0, moved) + carry[c]
            for k in range(PAIR):
                at = row_block(step + k * half)
                grads[c][at, :] = base[c, at, :] + now[:, k * ny : (k + 1) * ny]
            later.append(jnp.where(upper, moved, 0.0))
        return tuple(later)

    start = tuple(jnp.zeros((FACES, PAIR * ny), F32) for _ in range(4))
    last = lax.fori_loop(0, half, step_of, start)
    for c in range(4):
        for k in range(PAIR):
            at = (k + 1) % PAIR * half * FACES
            grads[c][pl.ds(at, FACES), :] += last[c][:, k * ny : (k + 1) * ny]


def finish_kernel(total, g_w_in, g_b_in, g_w_mid, g_b_mid, g_w_out, g_b_out):
    hid = g_w_mid.shape[0]
    g_w_mid[...] = total[:hid, :hid]
    beside = total[:hid, hid : 2 * hid]
    g_w_in[...] = beside[:16]
    g_w_out[...] = beside[16:24]
    g_b_in[...] = beside[24:25]
    g_b_out[...] = beside[25:26, :8]
    g_b_mid[...] = total[hid : hid + 1, :hid]


def whole(count, space=pltpu.VMEM):
    return [pl.BlockSpec(memory_space=space)] * count


def call(kernel, outs, operands, out_spaces=None, in_spaces=None, scratch=(), flops=0, moved=0):
    return pl.pallas_call(
        kernel,
        out_shape=outs,
        in_specs=in_spaces or whole(len(operands)),
        out_specs=out_spaces or whole(len(outs)),
        scratch_shapes=list(scratch),
        compiler_params=pltpu.CompilerParams(vmem_limit_bytes=VMEM_BYTES),
        cost_estimate=pl.CostEstimate(flops=flops, bytes_accessed=moved, transcendentals=0),
    )(*operands)


def sum_rounds(values, sizes):
    axes, size = tuple(sizes), 1
    for one in sizes.values():
        size *= one
    if size & (size - 1):
        return [values, lax.psum(values, axes)]
    bits = [1 << k for k in range(size.bit_length() - 1)]
    core = size // sizes["traj"]
    others = [bit for bit in reversed(bits) if bit != core]
    found = [values]
    for masks in [[core]] * (core in bits) + [others[k : k + 2] for k in range(0, len(others), 2)]:
        partners = [0]
        for mask in masks:
            partners = partners + [one ^ mask for one in partners]
        parts = [
            lax.ppermute(values, axes, [(i, i ^ one) for i in range(size)]) if one else values for one in partners
        ]
        while len(parts) > 1:
            parts = [parts[k] + parts[k + 1] for k in range(0, len(parts), 2)]
        values = parts[0]
        found.append(values)
    return found


def body(sizes, density, momentum, tracer, cotangent, w_in, b_in, w_mid, b_mid, w_out, b_out):
    nx, ny = density.shape[1:]
    hid = w_in.shape[0]
    wide = FACES * hid
    groups = nx // FACES
    half = groups // PAIR
    lanes = PAIR * ny
    segs = ny // SEG
    rim_rows = nx // segs
    ring = sizes["tx"] * sizes["ty"]
    shape = jax.ShapeDtypeStruct

    operands = [
        density, momentum, tracer, cotangent, w_in.T, b_in[None], w_mid, b_mid[None], w_out, b_out[None]
    ]
    rim, to_first, to_second, state, cots, *matrices = call(
        pack_kernel,
        [
            shape((8, rim_rows, ny), F32),
            shape((8, FACES, ny), F32),
            shape((8, FACES, ny), F32),
            shape((4, nx, ny), F32),
            shape((4, nx, ny), F32),
            shape((wide // 2, 6 * 32 + ONES), BF16),
            shape((wide, 4 * 64), BF16),
            shape((wide // 2, ny), F32),
            shape((4 * hid, 8 * hid), BF16),
            shape((2 * hid, ny), F32),
            shape((192, wide), BF16),
            shape((64, ny), F32),
            shape((wide, 192), BF16),
            shape((2 * hid, 6 * hid), BF16),
            shape((64, wide), BF16),
            shape((128, wide), BF16),
        ],
        [pltpu.with_memory_space_constraint(one, pltpu.HBM) for one in operands],
        in_spaces=whole(10, pltpu.HBM),
        scratch=[pltpu.VMEM(one.shape, F32) for one in operands[4:]] + [pltpu.SemaphoreType.DMA((10,))],
    )
    axes = ("tx", "ty")
    swaps = [[(i, (i + 1 if (i + first) % 2 == 0 else i - 1) % ring) for i in range(ring)] for first in range(2)]
    from_first, from_second = (
        lax.ppermute(one, axes, swap) for one, swap in zip((to_first, to_second), swaps)
    )

    middle, *kept = call(
        x_forward_kernel,
        [shape((4, nx, ny), F32)]
        + [shape((half, wide, lanes), BF16)] * 4
        + [shape((half, 64, lanes), F32)],
        [state, matrices[0]] + matrices[3:7],
        scratch=[pltpu.VMEM((4, nx + FACES, ny), F32)],
        flops=10**10,
        moved=10**7,
    )
    first_x_back = matrices.pop(-2)
    *found, g_weights = call(
        back_kernel,
        [
            shape((4, nx, ny), F32),
            shape((half, wide, lanes), BF16),
            shape((half, wide, lanes), BF16),
            shape((hid + 8, 128), F32),
        ],
        [state, cots, middle, rim, from_first, from_second] + matrices + kept,
        scratch=[
            pltpu.VMEM((4, rim_rows + FACES, ny), F32),
            pltpu.VMEM((4, rim_rows, ny), F32),
            pltpu.VMEM((4, rim_rows + FACES, ny), F32),
            pltpu.VMEM((4, rim_rows, ny), F32),
            pltpu.VMEM((4, rim_rows, ny), F32),
            pltpu.VMEM((4, nx, ny), F32),
            pltpu.VMEM((2 * 32 + ONES, wide), F32),
            pltpu.VMEM((2 * 64 + ONES, wide), F32),
            pltpu.VMEM((8 * hid + ONES, 8 * hid), F32),
            pltpu.VMEM((2 * wide, 128), F32),
            pltpu.VMEM((64, lanes), F32),
        ],
        flops=4 * 10**10,
        moved=2 * 10**7,
    )
    rounds = sum_rounds(g_weights, sizes)
    g_den, g_mom, g_tra = call(
        state_kernel,
        [shape(density.shape, F32), shape(momentum.shape, F32), shape(tracer.shape, F32)],
        found + [first_x_back, rounds[min(1, len(rounds) - 1)]],
        flops=2 * 10**9,
        moved=10**6,
    )
    total = rounds[-1]
    g_w_in, g_b_in, g_w_mid, g_b_mid, g_w_out, g_b_out = call(
        finish_kernel,
        [
            shape((w_in.shape[1], hid), F32),
            shape((1, hid), F32),
            shape(w_mid.shape, F32),
            shape((1, hid), F32),
            shape(w_out.shape, F32),
            shape((1, b_out.shape[0]), F32),
        ],
        [total],
    )
    return (g_den, g_mom, g_tra, g_w_in.T, g_b_in[0], g_w_mid, g_b_mid[0], g_w_out, g_b_out[0])


def solution(mesh):
    flow = P("traj", None, ("tx", "ty"))
    deep = P("traj", None, None, ("tx", "ty"))
    return jax.shard_map(
        functools.partial(body, dict(mesh.shape)),
        mesh=mesh,
        in_specs=(flow, deep, flow, deep) + (P(),) * 6,
        out_specs=(flow, deep, flow) + (P(),) * 6,
        check_vma=False,
    )
```
